32 devices in a mesh: wide: 8 (over z, y), narrow: 4 (over x, core).
Axes of the slice: x: 2, y: 2, z: 4, core: 2. Of those that a mesh axis runs over, the one named last changes fastest.
Arguments:
- tokens: bfloat16 [64, 512, 768], P('wide', 'narrow'), may hold values from -6 to 6
- lengths: int32 [64], P('wide'), may hold values from 16 to 512, as said below
- routes: int32 [64, 512, 1], P('wide', 'narrow'), may hold values from 0 to 7
- bucket_table: int32 [1023], replicated, may hold values from 0 to 31, as said below
- attn_gain: bfloat16 [768], replicated, may hold values from 0.5 to 1.5
- query_weight: bfloat16 [768, 768], replicated, may hold values from -0.0546875 to 0.0546875
- key_weight: bfloat16 [768, 768], replicated, may hold values from -0.21875 to 0.21875
- value_weight: bfloat16 [768, 768], replicated, may hold values from -0.21875 to 0.21875
- output_weight: bfloat16 [768, 768], replicated, may hold values from -1.25 to 1.25
- relative_bias: bfloat16 [32, 12], replicated, may hold values from -3 to 3
- expert_gain: bfloat16 [768], replicated, may hold values from 0.5 to 1.5
- router_weight: bfloat16 [768, 8], replicated, may hold values from -0.15625 to 0.15625
- experts_in: bfloat16 [8, 768, 3072], P('wide'), may hold values from -0.21875 to 0.21875
- experts_out: bfloat16 [8, 3072, 768], P('wide'), may hold values from -0.875 to 0.875
- cotangent: bfloat16 [64, 512, 768], P('wide', 'narrow'), may hold values from -6 to 6
Outputs:
- layer_output: float32 [64, 512, 768], P('wide', 'narrow')
- input_grad: float32 [64, 512, 768], P('wide', 'narrow')
- grad_attn_gain: float32 [768], P('narrow')
- grad_query: float32 [768, 768], P('narrow')
- grad_key: float32 [768, 768], P('narrow')
- grad_value: float32 [768, 768], P('narrow')
- grad_output_weight: float32 [768, 768], P('narrow')
- grad_relative: float32 [32, 12], P('narrow')
- grad_expert_gain: float32 [768], P('narrow')
- grad_router: float32 [768, 8], P('narrow')
- grad_experts_in: float32 [8, 768, 3072], P('wide', 'narrow')
- grad_experts_out: float32 [8, 3072, 768], P('wide', 'narrow')
The draws below stay inside these ranges and needn't reach their ends.
Inputs may be any that keep to these rules, and one draw needn't show every extreme that they name: lengths[s] counts the valid leading positions of sequence s; some sequence is full in every draw. bucket_table[j - i + 511] is the bucket of key position j seen from query position i.
All inputs are finite; a program needn't handle non-finite values.
Results may differ from the reference program's by a relative error of at most 0.018.
Values may be sent and summed in bfloat16 or wider, within the bound.
A program may use at most 192 MiB of HBM per device.

```python
import jax
import jax.numpy as jnp
from jax import lax

D = 768
HEADS = 12
HEAD = 64
FF = 3072
BUCKETS = 32
SEQLEN = 512
SEQ_DEV = 8
SPAN = 128
SEQS = 64
TOK_DEV = 1024
EXPERTS = 8
CAP = 160
N_WIDE = 8
N_NARROW = 4


def draw_lengths(key, part):
    first_key, second_key = jax.random.split(jax.random.fold_in(key, 11))
    drawn = jax.random.randint(first_key, (SEQS,), 16, SEQLEN + 1, dtype=jnp.int32)
    full_one = jax.random.randint(second_key, (), 0, SEQS, dtype=jnp.int32)
    return jnp.where(jnp.arange(SEQS, dtype=jnp.int32) == full_one, SEQLEN, drawn).astype(jnp.int32)


def draw_bucket_table(key, part):
    drawn = jax.random.randint(jax.random.fold_in(key, 23), (2 * SEQLEN - 1,), 0, BUCKETS, dtype=jnp.int32)
    index_row = jnp.arange(2 * SEQLEN - 1, dtype=jnp.int32)
    drawn = jnp.where(index_row == 0, BUCKETS - 1, drawn)
    drawn = jnp.where(index_row == 1, 0, drawn)
    return drawn.astype(jnp.int32)


def shard_levels(stream_key, dims, cuts, smallest, largest):
    factor_of, own = 1.0, jax.random.fold_in(stream_key, 6)
    for axis_at, parts in cuts:
        draws = jnp.exp(jax.random.uniform(jax.random.fold_in(own, axis_at), (parts,), jnp.float32, smallest / len(cuts), largest / len(cuts)))
        factor_of = factor_of * jnp.repeat(draws, dims[axis_at] // parts).reshape([-1 if axis == axis_at else 1 for axis in range(len(dims))])
    return factor_of


def picks_of(stream_key, rows, number_of, top, lift):
    ranking = jax.random.permutation(jax.random.fold_in(stream_key, 1), number_of)
    favour = ranking
    for power in range(3):
        favour = favour * favour // number_of
    favour = favour * lift // number_of
    lots = jax.random.randint(jax.random.fold_in(stream_key, 2), (rows, number_of), 0, 4096) + favour
    fixed_rows = jax.random.permutation(jax.random.fold_in(stream_key, 3), rows)[jnp.arange(number_of) % rows]
    lots = jnp.where(jnp.arange(rows)[:, None] == fixed_rows[None, :], 1 << 14, lots)
    priority = lots * number_of + jnp.arange(number_of)
    return lax.top_k(priority.astype(jnp.int32), top)[1].astype(jnp.int32)


def noise(rng, dims, width, limit, cuts=(), kind=jnp.bfloat16):
    factor_of = shard_levels(rng, dims, cuts, -0.22, 0.18) if cuts else 1.0
    entries = jax.random.normal(rng, dims, jnp.float32) * width * factor_of
    return jnp.minimum(jnp.maximum(entries, -limit), limit).astype(kind)


def setup_inputs(seed: int = 0) -> dict:
    streams_of = jax.random.split(jax.random.key(seed), 16)
    return {
        "tokens": noise(streams_of[0], (SEQS, SEQLEN, D), 1.0, 6.0, ((0, 8), (1, 4))),
        "lengths": draw_lengths(jax.random.fold_in(streams_of[15], 71), 0),
        "routes": picks_of(streams_of[2], SEQS * SEQLEN, EXPERTS, 1, 1024).reshape((SEQS, SEQLEN, 1)),
        "bucket_table": draw_bucket_table(jax.random.fold_in(streams_of[15], 71), 0),
        "attn_gain": jnp.clip(1.0 + 0.1 * jax.random.normal(streams_of[4], (D,), jnp.float32), 0.5, 1.5).astype(jnp.bfloat16),
        "query_weight": noise(streams_of[5], (D, D), (16 * D) ** -0.5, 0.0546875),
        "key_weight": noise(streams_of[6], (D, D), D ** -0.5, 0.21875),
        "value_weight": noise(streams_of[7], (D, D), D ** -0.5, 0.21875),
        "output_weight": noise(streams_of[8], (D, D), (D // 32) ** -0.5, 1.25),
        "relative_bias": noise(streams_of[9], (BUCKETS, HEADS), 0.5, 3.0),
        "expert_gain": jnp.clip(1.0 + 0.1 * jax.random.normal(streams_of[10], (D,), jnp.float32), 0.5, 1.5).astype(jnp.bfloat16),
        "router_weight": noise(streams_of[11], (D, EXPERTS), (2 * D) ** -0.5, 0.15625),
        "experts_in": noise(streams_of[12], (EXPERTS, D, FF), D ** -0.5, 0.21875, ((0, 8),)),
        "experts_out": noise(streams_of[13], (EXPERTS, FF, D), (max(1, FF // (EXPERTS * EXPERTS))) ** -0.5, 0.875, ((0, 8),)),
        "cotangent": noise(streams_of[14], (SEQS, SEQLEN, D), 1.0, 6.0, ((0, 8), (1, 4))),
    }


epsilon = 1e-06
highest_precision = lax.Precision.HIGHEST

@jax.custom_vjp
def low(v):
    return lax.optimization_barrier(v.astype(jnp.bfloat16)).astype(jnp.float32)

@jax.custom_vjp
def low_back(v):
    return v

def low_keep(v):
    return (low(v), None)

def low_pass(kept, grad):
    return (grad,)

def back_keep(v):
    return (v, None)

def back_low(kept, grad):
    return (low(grad),)
low.defvjp(low_keep, low_pass)
low_back.defvjp(back_keep, back_low)

def rms_norm(field, gain_vec):
    return field * lax.rsqrt(lax.optimization_barrier(jnp.mean(field * field, axis=-1, keepdims=True)) + epsilon) * gain_vec

def to_groups(array):
    depth = array.shape[-1]
    shaped = array.reshape(N_WIDE, SEQ_DEV, N_NARROW, SPAN, depth).transpose(0, 2, 1, 3, 4)
    return shaped.reshape(N_WIDE * N_NARROW, TOK_DEV, depth)

def from_groups(array):
    depth = array.shape[-1]
    shaped = array.reshape(N_WIDE, N_NARROW, SEQ_DEV, SPAN, depth).transpose(0, 2, 1, 3, 4)
    return shaped.reshape(SEQS, SEQLEN, depth)

def routing(routes):
    grouped = to_groups(routes)[..., 0].astype(jnp.int32)
    onehot = grouped[..., None] == jnp.arange(EXPERTS, dtype=jnp.int32)
    counts = jnp.cumsum(onehot.astype(jnp.int32), axis=1).astype(jnp.int32)
    position = lax.optimization_barrier(jnp.sum(jnp.where(onehot, counts - 1, 0), axis=-1)).astype(jnp.int32)
    kept_mask = position < CAP
    slot_index = jnp.where(kept_mask, grouped * CAP + position, EXPERTS * CAP).astype(jnp.int32)
    return (onehot, kept_mask, slot_index)

def make_forward(key_valid, bucket_full, onehot, kept_mask, slot_index):
    group_count = N_WIDE * N_NARROW

    def forward(tokens, attn_gain, query_weight, key_weight, value_weight, output_weight, relative_bias, expert_gain, router_weight, experts_in, experts_out):
        normed = low(rms_norm(tokens, attn_gain))
        queries = low(low_back(jnp.dot(normed, query_weight, precision=highest_precision)))
        keys_all = low(low_back(jnp.dot(normed, key_weight, precision=highest_precision)))
        values_all = low(low_back(jnp.dot(normed, value_weight, precision=highest_precision)))
        score_bias = jnp.take(relative_bias, bucket_full, axis=0).transpose(2, 0, 1)

        def one_sequence(item):
            seq_query, seq_keys, seq_values, seq_valid = item
            split_q = seq_query.reshape(SEQLEN, HEADS, HEAD)
            split_k = seq_keys.reshape(SEQLEN, HEADS, HEAD)
            split_v = seq_values.reshape(SEQLEN, HEADS, HEAD)
            scores = jnp.einsum('ihd,jhd->hij', split_q, split_k, precision=highest_precision) + score_bias
            scores = low_back(scores)
            scores = jnp.where(seq_valid[None, None, :], scores, -1e+30)
            prob_rows = jax.nn.softmax(scores, axis=-1)
            mixed = jnp.einsum('hij,jhd->ihd', low(prob_rows), split_v, precision=highest_precision)
            return mixed.reshape(SEQLEN, D)
        attended = lax.map(jax.checkpoint(one_sequence), (queries, keys_all, values_all, key_valid))
        attended = low(low_back(attended))
        branch = low_back(jnp.dot(attended, output_weight, precision=highest_precision))
        hidden = tokens + branch
        routed = low(rms_norm(hidden, expert_gain))
        logits = low_back(jnp.dot(routed, router_weight, precision=highest_precision))
        prob_rows = jax.nn.softmax(to_groups(logits), axis=-1)
        gate = lax.optimization_barrier(jnp.sum(jnp.where(onehot, prob_rows, 0.0), axis=-1))
        grouped = to_groups(routed)
        group_ids = jnp.arange(group_count, dtype=jnp.int32)[:, None]
        dispatched = jnp.zeros((group_count, EXPERTS * CAP, D), jnp.float32)
        dispatched = dispatched.at[group_ids, slot_index].set(grouped, mode='drop')
        dispatched = low_back(dispatched)
        per_expert = dispatched.reshape(group_count, EXPERTS, CAP, D).transpose(1, 0, 2, 3)
        per_expert = per_expert.reshape(EXPERTS, group_count * CAP, D)

        def one_expert(item):
            expert_rows, first_weight, second_weight = item
            pre_act = low_back(jnp.dot(expert_rows, first_weight, precision=highest_precision))
            activation = low(jax.nn.gelu(pre_act))
            return low(low_back(jnp.dot(activation, second_weight, precision=highest_precision)))
        results = lax.map(jax.checkpoint(one_expert), (per_expert, experts_in, experts_out))
        back_groups = results.reshape(EXPERTS, group_count, CAP, D).transpose(1, 0, 2, 3)
        back_groups = back_groups.reshape(group_count, EXPERTS * CAP, D)
        safe_index = jnp.minimum(slot_index, EXPERTS * CAP - 1).astype(jnp.int32)
        picked = jnp.take_along_axis(back_groups, safe_index[..., None], axis=1)
        picked = jnp.where(kept_mask[..., None], picked, 0.0)
        return hidden + from_groups(gate[..., None] * picked)
    return forward

def reference(tokens, lengths, routes, bucket_table, attn_gain, query_weight, key_weight, value_weight, output_weight, relative_bias, expert_gain, router_weight, experts_in, experts_out, cotangent):
    positions = jnp.arange(SEQLEN, dtype=jnp.int32)
    key_valid = positions[None, :] < lengths[:, None]
    bucket_full = bucket_table[(positions[None, :] - positions[:, None] + SEQLEN - 1).astype(jnp.int32)]
    onehot, kept_mask, slot_index = routing(routes)
    forward = make_forward(key_valid, bucket_full, onehot, kept_mask, slot_index)
    primals = (tokens, attn_gain, query_weight, key_weight, value_weight, output_weight, relative_bias, expert_gain, router_weight, experts_in, experts_out)
    primals = tuple((item.astype(jnp.float32) for item in primals))
    layer_output, pull = jax.vjp(forward, *primals)
    grads = pull(cotangent.astype(jnp.float32))
    return (layer_output, grads[0], grads[1], grads[2], grads[3], grads[4], grads[5], grads[6], grads[7], grads[8], grads[9], grads[10])
```

```python
import functools

import jax
import jax.numpy as jnp
from jax import lax
from jax.experimental import pallas as pl
from jax.experimental.pallas import tpu as pltpu
from jax.sharding import PartitionSpec as P

f32, bf16 = jnp.float32, jnp.bfloat16
epsilon = 1e-06
VMEM_BYTES = 60 * 1024 * 1024
NN = (((1,), (0,)), ((), ()))
NT = (((1,), (1,)), ((), ()))
TN = (((0,), (0,)), ((), ()))


def dot(a, b, dims=NN):
    return lax.dot_general(a, b, dims, preferred_element_type=f32)


def vmem():
    return pl.BlockSpec(memory_space=pltpu.VMEM)


def params(**kw):
    return pltpu.CompilerParams(vmem_limit_bytes=VMEM_BYTES, **kw)


def inverse_rms(field):
    return lax.rsqrt(jnp.mean(field * field, axis=-1, keepdims=True) + epsilon)


def half_masks(pair_width):
    lane = lax.broadcasted_iota(jnp.int32, (1, pair_width), 1)
    low = lane < pair_width // 2
    return low, (low.astype(f32).astype(bf16), (~low).astype(f32).astype(bf16))


def attention_forward_kernel(
    lens_ref, tok_ref, diag_ref, gain_ref, wq_ref, wk_ref, wv_ref,
    att_ref, q_ref, k_ref, v_ref, p_ref, strip_ref,
):
    pair = pl.program_id(0)
    parts, seqs, span, width = tok_ref.shape
    total = parts * span
    table = diag_ref.shape[-1]
    me = lax.axis_index("narrow")

    @pl.when(pair == 0)
    def _():
        gain = gain_ref[...]

        def project(step, carry):
            s, n = step // (parts // 2), step % (parts // 2)
            x = tok_ref[pl.ds(2 * n, 2), s].reshape(2 * span, width).astype(f32)
            normed = (x * inverse_rms(x) * gain).astype(bf16)
            rows = pl.ds(pl.multiple_of(n * 2 * span, 2 * span), 2 * span)
            q_ref[s, rows, :] = dot(normed, wq_ref[...]).astype(bf16)
            k_ref[s, rows, :] = dot(normed, wk_ref[...]).astype(bf16)
            v_ref[s, rows, :] = dot(normed, wv_ref[...]).astype(bf16)
            return carry

        lax.fori_loop(0, seqs * (parts // 2), project, 0)

    low, masks = half_masks(128)
    for hh in range(2):
        row = diag_ref[0, hh : hh + 1, :]
        strip_ref[hh] = pltpu.roll(
            jnp.broadcast_to(row, (span, table)), table - span + 1, 1, stride=1, stride_axis=0
        )
    lanes = pl.ds(pl.multiple_of(pair * 128, 128), 128)
    cols = lax.broadcasted_iota(jnp.int32, (1, total), 1)

    def one_sequence(s, carry):
        kp = k_ref[s, :, lanes]
        vp = v_ref[s, :, lanes]
        length = lens_ref[me * seqs + s]
        push = jnp.where(cols < length, 0.0, -1e30)
        for block in range(parts // 2):
            rows = slice(block * 2 * span, (block + 1) * 2 * span)
            qp = q_ref[s, rows, lanes]
            mixed = None
            for hh in range(2):
                bias = jnp.concatenate(
                    [
                        strip_ref[hh, :, (parts - 1 - r) * span : (parts - 1 - r) * span + total]
                        for r in (2 * block, 2 * block + 1)
                    ],
                    axis=0,
                )
                scores = dot(qp * masks[hh], kp, NT) + bias + push
                raised = jnp.exp(scores - jnp.max(scores, axis=-1, keepdims=True))
                prob = raised * (1.0 / jnp.sum(raised, axis=-1, keepdims=True))
                prob = prob.astype(bf16)
                p_ref[s, hh, rows, :] = prob
                part = dot(prob, vp)
                mixed = part if hh == 0 else jnp.where(low, mixed, part)
            mixed = mixed.astype(bf16)
            for r in range(2):
                att_ref[2 * block + r, s, :, lanes] = mixed[r * span : (r + 1) * span]
        return carry

    lax.fori_loop(0, seqs, one_sequence, 0)


def attention_forward(lens, tok, diag, gain, wq, wk, wv):
    parts, seqs, span, width = tok.shape
    pairs, _, table = diag.shape
    total = parts * span
    rows = jax.ShapeDtypeStruct((seqs, total, width), bf16)
    return pl.pallas_call(
        attention_forward_kernel,
        grid=(pairs,),
        in_specs=[
            pl.BlockSpec(memory_space=pltpu.SMEM),
            vmem(),
            pl.BlockSpec((1, 2, table), lambda i: (i, 0, 0)),
            vmem(), vmem(), vmem(), vmem(),
        ],
        out_specs=[
            vmem(), vmem(), vmem(), vmem(),
            pl.BlockSpec((seqs, 2, total, total), lambda i: (0, i, 0, 0)),
        ],
        out_shape=[
            jax.ShapeDtypeStruct((parts, seqs, span, width), bf16),
            rows, rows, rows,
            jax.ShapeDtypeStruct((seqs, 2 * pairs, total, total), bf16),
        ],
        scratch_shapes=[pltpu.VMEM((2, span, table), f32)],
        compiler_params=params(),
        name="attention_forward",
    )(lens, tok, diag, gain, wq, wk, wv)


def mix_kernel(att_ref, tok_ref, slot_ref, wo_ref, gain_ref, hid_ref, send_ref, routed_ref):
    tokens, width = att_ref.shape
    slots = send_ref.shape[0]
    step = 256
    gain = gain_ref[...]

    def mix(i, carry):
        rows = pl.ds(pl.multiple_of(i * step, step), step)
        hidden = tok_ref[rows, :].astype(f32) + dot(att_ref[rows, :], wo_ref[...])
        hid_ref[rows, :] = hidden
        routed_ref[rows, :] = (hidden * inverse_rms(hidden) * gain).astype(bf16)
        return carry

    lax.fori_loop(0, tokens // step, mix, 0)

    def place(i, carry):
        rows = pl.ds(pl.multiple_of(i * step, step), step)
        ids = lax.broadcasted_iota(jnp.int32, (step, tokens), 0) + i * step
        pick = (ids == slot_ref[...]).astype(f32).astype(bf16)
        send_ref[rows, :] = dot(pick, routed_ref[...]).astype(bf16)
        return carry

    lax.fori_loop(0, slots // step, place, 0)


def mix(att, tok, slot_row, wo, gain, slots):
    tokens, width = att.shape
    return pl.pallas_call(
        mix_kernel,
        in_specs=[vmem()] * 5,
        out_specs=[vmem()] * 2,
        out_shape=[
            jax.ShapeDtypeStruct((tokens, width), f32),
            jax.ShapeDtypeStruct((slots, width), bf16),
        ],
        scratch_shapes=[pltpu.VMEM((tokens, width), bf16)],
        compiler_params=params(),
        name="mix",
    )(att, tok, slot_row, wo, gain)


def expert_kernel(
    experts, rows_ref, cot_ref, win_ref, wout_ref, wr_ref,
    res_ref, back_ref, gin_ref, gout_ref, grouter_ref,
    act_ref, pg_ref, push_ref, acc_res, acc_back,
):
    step_id = pl.program_id(0)
    chunk_rows = acc_res.shape[0]
    chunks = rows_ref.shape[0] // chunk_rows

    @pl.when(step_id < chunks)
    def _():
        expert_chunk(
            experts, step_id, rows_ref, cot_ref, win_ref, wout_ref, wr_ref, res_ref, back_ref,
            grouter_ref, act_ref, pg_ref, push_ref, acc_res, acc_back,
        )

    @pl.when(step_id >= chunks)
    def _():
        tile = gin_ref.shape[1]
        cols = pl.ds(pl.multiple_of((step_id - chunks) * tile, tile), tile)
        gin_ref[...] = dot(rows_ref[...], pg_ref[:, cols], TN).astype(bf16)
        gout_ref[...] = dot(act_ref[:, cols], push_ref[...], TN).astype(bf16)


def expert_chunk(
    experts, chunk, rows_ref, cot_ref, win_ref, wout_ref, wr_ref, res_ref, back_ref,
    grouter_ref, act_ref, pg_ref, push_ref, acc_res, acc_back,
):
    hidden_units = win_ref.shape[1]
    tile = 512
    chunk_rows = acc_res.shape[0]
    mine = lax.axis_index("wide")
    here = pl.ds(pl.multiple_of(chunk * chunk_rows, chunk_rows), chunk_rows)
    x = rows_ref[here, :]
    cot = cot_ref[here, :].astype(f32)
    lane = lax.broadcasted_iota(jnp.int32, (1, wr_ref.shape[1]), 1)
    logits = jnp.where(lane < experts, dot(x, wr_ref[...]), -1e30)
    raised = jnp.exp(logits - jnp.max(logits, axis=-1, keepdims=True))
    probs = raised * (1.0 / jnp.sum(raised, axis=-1, keepdims=True))
    hot = lane == mine
    gate = jnp.sum(jnp.where(hot, probs, 0.0), axis=-1, keepdims=True)
    push = (gate * cot).astype(bf16)
    push_ref[here, :] = push
    acc_res[...] = jnp.zeros_like(acc_res)
    acc_back[...] = jnp.zeros_like(acc_back)
    c0 = 0.7978845608028654
    c1 = c0 * 0.044715

    def units(t, carry):
        cols = pl.ds(pl.multiple_of(t * tile, tile), tile)
        pre = dot(x, win_ref[:, cols])
        ag = dot(push, wout_ref[cols, :], NT)
        sq = pre * pre
        th = jnp.tanh(pre * (c0 + c1 * sq))
        half = 0.5 + 0.5 * th
        act = (pre * half).astype(bf16)
        slope = half + pre * (0.5 - 0.5 * th * th) * (c0 + 3.0 * c1 * sq)
        pg = (ag * slope).astype(bf16)
        act_ref[here, cols] = act
        pg_ref[here, cols] = pg
        acc_res[...] += dot(act, wout_ref[cols, :])
        acc_back[...] += dot(pg, win_ref[:, cols], NT)
        return carry

    lax.fori_loop(0, hidden_units // tile, units, 0)
    result = acc_res[...].astype(bf16).astype(f32)
    res_ref[here, :] = (gate * result).astype(bf16)
    gate_grad = jnp.sum(cot * result, axis=-1, keepdims=True)
    logit_grad = probs * (jnp.where(hot, gate_grad, 0.0) - gate * gate_grad)
    logit_grad = logit_grad.astype(bf16)
    back = acc_back[...].astype(bf16).astype(f32) + dot(logit_grad, wr_ref[...], NT)
    back_ref[here, :] = back.astype(bf16)
    part = dot(x, logit_grad, TN)

    @pl.when(chunk == 0)
    def _():
        grouter_ref[...] = part

    @pl.when(chunk > 0)
    def _():
        grouter_ref[...] += part


def run_experts(rows, cot_rows, win, wout, wr, experts):
    count, width = rows.shape
    units = win.shape[1]
    chunks, tile = 4, 512
    step = count // chunks
    same = jax.ShapeDtypeStruct((count, width), bf16)
    return pl.pallas_call(
        functools.partial(expert_kernel, experts),
        grid=(chunks + units // tile,),
        in_specs=[vmem()] * 5,
        out_specs=[
            vmem(),
            vmem(),
            pl.BlockSpec((width, tile), lambda i: (0, jnp.maximum(i - chunks, 0))),
            pl.BlockSpec((tile, width), lambda i: (jnp.maximum(i - chunks, 0), 0)),
            vmem(),
        ],
        out_shape=[
            same,
            same,
            jax.ShapeDtypeStruct((width, units), bf16),
            jax.ShapeDtypeStruct((units, width), bf16),
            jax.ShapeDtypeStruct((width, wr.shape[1]), f32),
        ],
        scratch_shapes=[
            pltpu.VMEM((count, units), bf16),
            pltpu.VMEM((count, units), bf16),
            pltpu.VMEM((count, width), bf16),
            pltpu.VMEM((step, width), f32),
            pltpu.VMEM((step, width), f32),
        ],
        compiler_params=params(),
        name="experts",
    )(rows, cot_rows, win, wout, wr)


def hidden_back_kernel(
    back_ref, slot_ref, hid_ref, cot_ref, att_ref, wo_ref, gain_ref,
    hg_ref, ag_ref, gwo_ref, ggain_ref, branch_ref,
):
    tokens, width = hid_ref.shape
    slots = back_ref.shape[0]
    step = 256
    gain = gain_ref[...]
    ggain_ref[...] = jnp.zeros_like(ggain_ref)

    def pull(i, carry):
        rows = pl.ds(pl.multiple_of(i * step, step), step)
        ids = lax.broadcasted_iota(jnp.int32, (step, slots), 1)
        pick = (ids == slot_ref[rows, :]).astype(f32).astype(bf16)
        upstream = dot(pick, back_ref[...])
        hidden = hid_ref[rows, :]
        inv = inverse_rms(hidden)
        scaled = upstream * gain
        inner = jnp.mean(scaled * hidden, axis=-1, keepdims=True)
        grad = cot_ref[rows, :].astype(f32) + inv * scaled - hidden * (inv * inv * inv * inner)
        ggain_ref[...] += jnp.sum(upstream * hidden * inv, axis=0, keepdims=True)
        hg_ref[rows, :] = grad
        low = grad.astype(bf16)
        branch_ref[rows, :] = low
        ag_ref[rows, :] = dot(low, wo_ref[...], NT).astype(bf16)
        return carry

    lax.fori_loop(0, tokens // step, pull, 0)

    def weight(i, carry):
        cols = pl.ds(pl.multiple_of(i * 256, 256), 256)
        gwo_ref[:, cols] = dot(att_ref[...], branch_ref[:, cols], TN).astype(bf16)
        return carry

    lax.fori_loop(0, width // 256, weight, 0)


def hidden_back(back, slot_col, hid, cot, att, wo, gain):
    tokens, width = hid.shape
    return pl.pallas_call(
        hidden_back_kernel,
        in_specs=[vmem()] * 7,
        out_specs=[vmem()] * 4,
        out_shape=[
            jax.ShapeDtypeStruct((tokens, width), f32),
            jax.ShapeDtypeStruct((tokens, width), bf16),
            jax.ShapeDtypeStruct((width, width), bf16),
            jax.ShapeDtypeStruct((1, width), f32),
        ],
        scratch_shapes=[pltpu.VMEM((tokens, width), bf16)],
        compiler_params=params(),
        name="hidden_back",
    )(back, slot_col, hid, cot, att, wo, gain)


def attention_backward_kernel(
    ag_ref, p_ref, q_ref, k_ref, v_ref, tok_ref, gain_ref, wq_ref, wk_ref, wv_ref,
    gq_ref, gk_ref, gv_ref, part_ref, ggain_ref, diag_ref,
    dq_ref, dk_ref, dv_ref, strip_ref, normed_ref,
):
    pair = pl.program_id(0)
    parts, seqs, span, width = tok_ref.shape
    total = parts * span
    table = diag_ref.shape[-1]
    low, masks = half_masks(128)
    lanes = pl.ds(pl.multiple_of(pair * 128, 128), 128)
    strip_ref[...] = jnp.zeros_like(strip_ref)

    def one_sequence(s, carry):
        kp = k_ref[s, :, lanes]
        vp = v_ref[s, :, lanes]
        rows_all = pl.ds(pl.multiple_of(s * total, total), total)
        dk = [0.0, 0.0]
        dv = [0.0, 0.0]
        for block in range(parts // 2):
            rows = slice(block * 2 * span, (block + 1) * 2 * span)
            qp = q_ref[s, rows, lanes]
            gp = ag_ref[2 * block : 2 * block + 2, s, :, lanes].reshape(2 * span, 128)
            dq = None
            for hh in range(2):
                prob_low = p_ref[s, hh, rows, :]
                prob = prob_low.astype(f32)
                prob_grad = dot(gp * masks[hh], vp, NT)
                delta = jnp.sum(prob * prob_grad, axis=-1, keepdims=True)
                score_grad = prob * (prob_grad - delta)
                for r in range(2):
                    at = (parts - 1 - (2 * block + r)) * span
                    strip_ref[hh, :, at : at + total] += score_grad[r * span : (r + 1) * span]
                score_grad = score_grad.astype(bf16)
                part = dot(score_grad, kp)
                dq = part if hh == 0 else jnp.where(low, dq, part)
                dk[hh] = dk[hh] + dot(score_grad, qp, TN)
                dv[hh] = dv[hh] + dot(prob_low, gp, TN)
            at_rows = pl.ds(pl.multiple_of(s * total + block * 2 * span, 2 * span), 2 * span)
            dq_ref[at_rows, lanes] = dq.astype(bf16)
        dk_ref[rows_all, lanes] = jnp.where(low, dk[0], dk[1]).astype(bf16)
        dv_ref[rows_all, lanes] = jnp.where(low, dv[0], dv[1]).astype(bf16)
        return carry

    lax.fori_loop(0, seqs, one_sequence, 0)
    back = lax.broadcasted_iota(jnp.int32, (span, span), 0)
    flip = (back + lax.broadcasted_iota(jnp.int32, (span, span), 1) == span - 1).astype(f32)
    for hh in range(2):
        turned = lax.dot_general(
            flip, strip_ref[hh], NN, precision=lax.Precision.HIGHEST, preferred_element_type=f32
        )
        turned = pltpu.roll(turned, 0, 1, stride=1, stride_axis=0)
        diag_ref[0, hh : hh + 1, :] = jnp.sum(turned, axis=0, keepdims=True)

    @pl.when(pair == pl.num_programs(0) - 1)
    def _():
        gain = gain_ref[...]
        ggain_ref[...] = jnp.zeros_like(ggain_ref)

        def pull(step, carry):
            s, n = step // (parts // 2), step % (parts // 2)
            x = tok_ref[pl.ds(2 * n, 2), s].reshape(2 * span, width).astype(f32)
            inv = inverse_rms(x)
            rows = pl.ds(pl.multiple_of(step * 2 * span, 2 * span), 2 * span)
            normed_ref[rows, :] = (x * inv * gain).astype(bf16)
            upstream = dot(dq_ref[rows, :], wq_ref[...], NT)
            upstream += dot(dk_ref[rows, :], wk_ref[...], NT)
            upstream += dot(dv_ref[rows, :], wv_ref[...], NT)
            scaled = upstream * gain
            inner = jnp.mean(scaled * x, axis=-1, keepdims=True)
            grad = inv * scaled - x * (inv * inv * inv * inner)
            ggain_ref[...] += jnp.sum(upstream * x * inv, axis=0, keepdims=True)
            grad = grad.astype(bf16).reshape(2, span, width)
            part_ref[pl.ds(2 * n, 2), s] = grad
            return carry

        lax.fori_loop(0, seqs * (parts // 2), pull, 0)

        def weight(i, carry):
            cols = pl.ds(pl.multiple_of(i * 256, 256), 256)
            gq_ref[:, cols] = dot(normed_ref[...], dq_ref[:, cols], TN).astype(bf16)
            gk_ref[:, cols] = dot(normed_ref[...], dk_ref[:, cols], TN).astype(bf16)
            gv_ref[:, cols] = dot(normed_ref[...], dv_ref[:, cols], TN).astype(bf16)
            return carry

        lax.fori_loop(0, width // 256, weight, 0)


def attention_backward(ag, p, q, k, v, tok, gain, wq, wk, wv, table):
    parts, seqs, span, width = tok.shape
    total = parts * span
    pairs = p.shape[1] // 2
    square = jax.ShapeDtypeStruct((width, width), bf16)
    rows = pltpu.VMEM((seqs * total, width), bf16)
    return pl.pallas_call(
        attention_backward_kernel,
        grid=(pairs,),
        in_specs=[
            vmem(),
            pl.BlockSpec((seqs, 2, total, total), lambda i: (0, i, 0, 0)),
        ]
        + [vmem()] * 8,
        out_specs=[vmem()] * 5 + [pl.BlockSpec((1, 2, table), lambda i: (i, 0, 0))],
        out_shape=[
            square, square, square,
            jax.ShapeDtypeStruct((parts, seqs, span, width), bf16),
            jax.ShapeDtypeStruct((1, width), f32),
            jax.ShapeDtypeStruct((pairs, 2, table), f32),
        ],
        scratch_shapes=[rows, rows, rows, pltpu.VMEM((2, span, table), f32), rows],
        compiler_params=params(),
        name="attention_backward",
    )(ag, p, q, k, v, tok, gain, wq, wk, wv)


def finish_kernel(res_ref, slot_ref, hid_ref, out_ref):
    tokens, width = hid_ref.shape
    slots = res_ref.shape[0]
    step = 256

    def add(i, carry):
        rows = pl.ds(pl.multiple_of(i * step, step), step)
        ids = lax.broadcasted_iota(jnp.int32, (step, slots), 1)
        pick = (ids == slot_ref[rows, :]).astype(f32).astype(bf16)
        out_ref[rows, :] = hid_ref[rows, :] + dot(pick, res_ref[...])
        return carry

    lax.fori_loop(0, tokens // step, add, 0)


def finish(res, slot_col, hid):
    return pl.pallas_call(
        finish_kernel,
        in_specs=[vmem()] * 3,
        out_specs=vmem(),
        out_shape=jax.ShapeDtypeStruct(hid.shape, f32),
        compiler_params=params(),
        name="finish",
    )(res, slot_col, hid)


def body(
    tokens, lengths, routes, bucket_table, attn_gain, query_weight, key_weight, value_weight,
    output_weight, relative_bias, expert_gain, router_weight, experts_in, experts_out, cotangent,
):
    seq_count, span, width = tokens.shape
    narrow_n = lax.axis_size("narrow")
    wide_n = lax.axis_size("wide")
    seqs = seq_count // narrow_n
    heads = relative_bias.shape[1]
    buckets = relative_bias.shape[0]
    experts = router_weight.shape[1]
    tok_count = seq_count * span
    capacity = 5 * tok_count // (4 * experts)
    cap = -(-capacity // 16) * 16
    slots = experts * cap
    table = 2 * span * narrow_n
    gain_a = attn_gain.astype(f32).reshape(1, width)
    gain_e = expert_gain.astype(f32).reshape(1, width)
    router = jnp.pad(router_weight, ((0, 0), (0, -experts % 128)))

    def swap(array):
        return lax.all_to_all(array, "narrow", split_axis=0, concat_axis=0, tiled=True)

    def trade(array):
        array = array.reshape(wide_n, -1, width)
        return lax.all_to_all(array, "wide", split_axis=0, concat_axis=0, tiled=True).reshape(
            -1, width
        )

    table_ids = jnp.pad(bucket_table, (0, 1))
    offset_hot = (table_ids[None, :] == jnp.arange(buckets, dtype=jnp.int32)[:, None]).astype(bf16)
    diag = dot(relative_bias, offset_hot, TN).reshape(heads // 2, 2, table)
    route_ids = routes.reshape(tok_count)
    onehot = route_ids[:, None] == jnp.arange(experts, dtype=jnp.int32)[None, :]
    counts = jnp.cumsum(onehot.astype(jnp.int32), axis=0)
    position = jnp.sum(jnp.where(onehot, counts - 1, 0), axis=-1)
    slot = jnp.where(position < capacity, route_ids * cap + position, slots)
    slot_row, slot_col = slot.reshape(1, tok_count), slot.reshape(tok_count, 1)

    flat_cot = cotangent.reshape(tok_count, width)
    pick = (jnp.arange(slots, dtype=jnp.int32)[:, None] == slot_row).astype(bf16)
    cot_rows = trade(dot(pick, flat_cot).astype(bf16))

    tok_seq = swap(tokens).reshape(narrow_n, seqs, span, width)
    att_seq, q, k, v, probs = attention_forward(
        lengths, tok_seq, diag, gain_a, query_weight, key_weight, value_weight
    )
    attended = swap(att_seq.reshape(seq_count, span, width)).reshape(tok_count, width)
    flat_tok = tokens.reshape(tok_count, width)
    hidden, send_rows = mix(attended, flat_tok, slot_row, output_weight, gain_e, slots)
    rows = trade(send_rows)
    res, back, term_in, term_out, router_grad = run_experts(
        rows, cot_rows, experts_in[0], experts_out[0], router, experts
    )
    back_rows = trade(back)
    res_rows = trade(res)
    hidden_grad, att_grad, output_grad, gain_second = hidden_back(
        back_rows, slot_col, hidden, flat_cot, attended, output_weight, gain_e
    )
    layer_output = finish(res_rows, slot_col, hidden).reshape(seq_count, span, width)
    ag_seq = swap(att_grad.reshape(seq_count, span, width)).reshape(narrow_n, seqs, span, width)
    grad_query, grad_key, grad_value, part, gain_first, diag_grad = attention_backward(
        ag_seq, probs, q, k, v, tok_seq, gain_a, query_weight, key_weight, value_weight, table
    )
    part = swap(part.reshape(seq_count, span, width))
    input_grad = hidden_grad.reshape(seq_count, span, width) + part.astype(f32)
    relative_grad = lax.dot_general(
        offset_hot.astype(f32),
        diag_grad.reshape(heads, table),
        NT,
        precision=lax.Precision.HIGHEST,
        preferred_element_type=f32,
    )

    def scatter(array, dim=0):
        return lax.psum_scatter(
            array.astype(bf16), "narrow", scatter_dimension=dim, tiled=True
        ).astype(f32)

    grad_experts_in = scatter(term_in)[None]
    grad_experts_out = scatter(term_out)[None]
    shares = tuple(
        scatter(item)
        for item in (
            grad_query, grad_key, grad_value, output_grad, router_grad[:, :experts],
            relative_grad, gain_first[0], gain_second[0],
        )
    )
    totals = lax.psum(shares, "wide")
    return (
        layer_output,
        input_grad,
        totals[6],
        totals[0],
        totals[1],
        totals[2],
        totals[3],
        totals[5],
        totals[7],
        totals[4],
        grad_experts_in,
        grad_experts_out,
    )


def solution(mesh):
    token = P("wide", "narrow", None)
    expert = P("wide", None, None)
    row, vector = P("narrow", None), P("narrow")
    return jax.shard_map(
        body,
        mesh=mesh,
        in_specs=(token, P("wide"), token) + (P(),) * 9 + (expert, expert, token),
        out_specs=(
            token, token, vector, row, row, row, row, row, vector, row,
            P("wide", "narrow", None), P("wide", "narrow", None),
        ),
        check_vma=False,
    )
```

```python
import functools

import jax
import jax.numpy as jnp
from jax import lax
from jax.experimental import pallas as pl
from jax.experimental.pallas import tpu as pltpu
from jax.sharding import PartitionSpec as P

f32, bf16 = jnp.float32, jnp.bfloat16
epsilon = 1e-06
VMEM_BYTES = 60 * 1024 * 1024
NN = (((1,), (0,)), ((), ()))
NT = (((1,), (1,)), ((), ()))
TN = (((0,), (0,)), ((), ()))


def dot(a, b, dims=NN):
    return lax.dot_general(a, b, dims, preferred_element_type=f32)


def vmem():
    return pl.BlockSpec(memory_space=pltpu.VMEM)


def params(**kw):
    return pltpu.CompilerParams(vmem_limit_bytes=VMEM_BYTES, **kw)


def inverse_rms(field):
    return lax.rsqrt(jnp.mean(field * field, axis=-1, keepdims=True) + epsilon)


def half_masks(pair_width):
    lane = lax.broadcasted_iota(jnp.int32, (1, pair_width), 1)
    low = lane < pair_width // 2
    return low, (low.astype(f32).astype(bf16), (~low).astype(f32).astype(bf16))


MESH = pl.DeviceIdType.MESH
LOG2E = 1.4426950408889634


def hbm():
    return pl.BlockSpec(memory_space=pl.ANY)


def flipped(me, k, size):
    out, bit = me, 1
    while bit < size:
        out = out + ((k // bit) % 2) * (bit - 2 * bit * ((me // bit) % 2))
        bit *= 2
    return out


def remote(src, dst, sems, k, axis, peer):
    return pltpu.make_async_remote_copy(
        src_ref=src,
        dst_ref=dst,
        send_sem=sems.at[0, k],
        recv_sem=sems.at[1, k],
        device_id={axis: peer},
        device_id_type=MESH,
    )


def enter(narrow_n, wide_n):
    barrier = pltpu.get_barrier_semaphore()
    count = 0
    for axis, size in (("narrow", narrow_n), ("wide", wide_n)):
        if size > 1:
            me = lax.axis_index(axis)

            def greet(k, carry, axis=axis, size=size, me=me):
                pl.semaphore_signal(
                    barrier, inc=1, device_id={axis: flipped(me, k, size)}, device_id_type=MESH
                )
                return carry

            lax.fori_loop(1, size, greet, 0)
            count += size - 1
    pl.semaphore_wait(barrier, count)


def expert_pick(expert, cap, slot_row):
    ids = lax.broadcasted_iota(jnp.int32, (cap, slot_row.shape[1]), 0) + expert * cap
    return (ids == slot_row).astype(f32).astype(bf16)


def forward_kernel(
    wide_n, lens_ref, tok_any, cot_ref, slot_ref, diag_ref, gain_a_ref, gain_e_ref,
    wq_ref, wk_ref, wv_ref, wo_ref,
    tokseq_any, attseq_any, att_any, hid_any, routed_any, cotrows_any, q_any, k_any, v_any, invl_any, p_any,
    tokbuf, tokpos, q_ref, k_ref, v_ref, invl_ref, attseq, attpos, hid_ref, routed_ref, cotsend,
    strip_ref, pbuf, vext, kext, toksem, attsem, cotsem, psem, outsem,
):
    parts, seqs, span, width = tokbuf.shape
    total = parts * span
    pairs, _, table = diag_ref.shape
    cap = cotsend.shape[1]
    n = lax.axis_index("narrow")
    w = lax.axis_index("wide")
    own = pltpu.make_async_copy(tok_any.at[n], tokbuf.at[n], outsem.at[0])
    own.start()
    position = pltpu.make_async_copy(tok_any, tokpos, outsem.at[1])
    position.start()
    enter(parts, wide_n)

    def tok_copy(k):
        peer = flipped(n, k, parts)
        return remote(tok_any.at[peer], tokbuf.at[n], toksem, k, "narrow", peer)

    for k in range(parts - 1, 0, -1):
        tok_copy(k).start()

    def cot_copy(k):
        peer = flipped(w, k, wide_n)
        return remote(cotsend.at[k], cotrows_any.at[k], cotsem, k, "wide", peer)

    def cot_block(k):
        pick = expert_pick(flipped(w, k, wide_n), cap, slot_ref[...])
        cotsend[k] = dot(pick, cot_ref[...]).astype(bf16)

    def cot_step(i, carry):
        k = wide_n - 1 - i
        cot_block(k)
        cot_copy(k).start()
        return carry

    lax.fori_loop(0, wide_n - 1, cot_step, 0)
    cot_block(0)
    cot_own = pltpu.make_async_copy(cotsend.at[0], cotrows_any.at[0], outsem.at[2])
    cot_own.start()

    gain = gain_a_ref[...]
    own.wait()
    for k in range(parts):
        src = flipped(n, k, parts)
        if k > 0:
            tok_copy(k).wait_recv()
        x = tokbuf[src].reshape(seqs * span, width).astype(f32)
        normed = (x * inverse_rms(x) * gain).astype(bf16)
        shape = (seqs, span, width)
        q_ref[src] = (dot(normed, wq_ref[...]) * LOG2E).astype(bf16).reshape(shape)
        k_ref[src] = dot(normed, wk_ref[...]).astype(bf16).reshape(shape)
        v_ref[src] = dot(normed, wv_ref[...]).astype(bf16).reshape(shape)
    outs = [
        pltpu.make_async_copy(a, b, outsem.at[i])
        for a, b, i in (
            (tokbuf, tokseq_any, 3), (q_ref, q_any, 4), (k_ref, k_any, 5), (v_ref, v_any, 6),
        )
    ]
    for copy in outs:
        copy.start()

    low, masks = half_masks(128)
    lane = lax.broadcasted_iota(jnp.int32, (1, 128), 1)
    hot = [(lane == 64).astype(f32).astype(bf16), (lane == 0).astype(f32).astype(bf16)]
    for hh in range(2):
        ones = jnp.broadcast_to(masks[hh], (total, 128))
        vext[hh * total : (hh + 1) * total, 128:] = ones

    def att_copy(k, lanes):
        peer = flipped(n, k, parts)
        return remote(
            attseq.at[peer, :, :, lanes], attpos.at[n, :, :, lanes], attsem, k, "narrow", peer
        )

    def one_pair(pair, carry):
        lanes = pl.ds(pl.multiple_of(pair * 128, 128), 128)
        for hh in range(2):
            row = diag_ref[pair, hh : hh + 1, :]
            strip_ref[hh] = pltpu.roll(
                jnp.broadcast_to(row, (span, table)), table - span + 1, 1, stride=1, stride_axis=0
            )

        def one_sequence(s, inner):
            vp = v_ref[:, s, :, lanes].reshape(total, 128)
            kp = k_ref[:, s, :, lanes].reshape(total, 128).astype(f32)
            ids = lax.broadcasted_iota(jnp.int32, (total, 128), 0)
            push = jnp.where(ids < lens_ref[n * seqs + s], 0.0, -1e30)
            for hh in range(2):
                vext[hh * total : (hh + 1) * total, :128] = vp * masks[hh]
                kext[hh] = jnp.where(lane == 64 - 64 * hh, push, kp).astype(bf16)

            @pl.when(pair > 0)
            def _():
                pltpu.make_async_copy(pbuf.at[s], p_any.at[pair, s], psem.at[s]).wait()

            for block in range(parts // 2):
                rows = slice(block * 2 * span, (block + 1) * 2 * span)
                both = slice(2 * block, 2 * block + 2)
                qp = q_ref[both, s, :, lanes].reshape(2 * span, 128)
                for hh in range(2):
                    bias = jnp.concatenate(
                        [
                            strip_ref[hh, :, (parts - 1 - r) * span : (parts - 1 - r) * span + total]
                            for r in (2 * block, 2 * block + 1)
                        ],
                        axis=0,
                    )
                    scores = dot(qp * masks[hh] + hot[hh], kext[hh], NT) + bias
                    raised = jnp.exp2(scores - jnp.max(scores, axis=-1, keepdims=True))
                    pbuf[s, rows, hh * total : (hh + 1) * total] = raised.astype(bf16)
                mixed = dot(pbuf[s, rows, :], vext[...])
                inv = 1.0 / mixed[:, 128:]
                invl_ref[both, s, :, lanes] = inv.reshape(2, span, 128)
                attseq[both, s, :, lanes] = (mixed[:, :128] * inv).astype(bf16).reshape(2, span, 128)
            pltpu.make_async_copy(pbuf.at[s], p_any.at[pair, s], psem.at[s]).start()
            return inner

        lax.fori_loop(0, seqs, one_sequence, 0)
        for k in range(parts - 1, 0, -1):
            att_copy(k, lanes).start()
        return carry

    lax.fori_loop(0, pairs, one_pair, 0)
    copy = pltpu.make_async_copy(invl_ref, invl_any, outsem.at[7])
    copy.start()
    outs.append(copy)
    position.wait()
    gain = gain_e_ref[...]
    for k in range(parts):
        src = flipped(n, k, parts)
        if k > 0:
            att_copy(k, slice(None)).wait_recv()
            att = attpos[src].reshape(seqs * span, width)
        else:
            attpos[src] = attseq[src]
            att = attseq[src].reshape(seqs * span, width)
        rows = pl.ds(pl.multiple_of(src * seqs * span, seqs * span), seqs * span)
        hidden = tokpos[src].reshape(seqs * span, width).astype(f32) + dot(att, wo_ref[...])
        hid_ref[rows, :] = hidden
        routed_ref[rows, :] = (hidden * inverse_rms(hidden) * gain).astype(bf16)
    for a, b, i in ((attpos, att_any, 8), (hid_ref, hid_any, 9), (routed_ref, routed_any, 10),
                    (attseq, attseq_any, 11)):
        copy = pltpu.make_async_copy(a, b, outsem.at[i])
        copy.start()
        outs.append(copy)
    for k in range(1, parts):
        tok_copy(k).wait_send()
        att_copy(k, slice(None)).wait_send()
    for s in range(seqs):
        pltpu.make_async_copy(pbuf.at[s], p_any.at[0, s], psem.at[s]).wait()
    cot_own.wait()

    def cot_wait(k, carry):
        cot_copy(k).wait()
        return carry

    lax.fori_loop(1, wide_n, cot_wait, 0)
    for copy in outs:
        copy.wait()


def forward(lens, tok, cot, slot_row, diag, gain_a, gain_e, wq, wk, wv, wo, wide_n, cap):
    parts, seqs, span, width = tok.shape
    pairs, _, table = diag.shape
    total = parts * span
    tokens = parts * seqs * span
    quad = (parts, seqs, span, width)
    shapes = [
        (quad, bf16), (quad, bf16), (quad, bf16), ((tokens, width), f32), ((tokens, width), bf16),
        ((wide_n, cap, width), bf16), (quad, bf16), (quad, bf16), (quad, bf16), (quad, f32),
        ((pairs, seqs, total, 2 * total), bf16),
    ]
    return pl.pallas_call(
        functools.partial(forward_kernel, wide_n),
        in_specs=[pl.BlockSpec(memory_space=pltpu.SMEM), hbm()] + [vmem()] * 9,
        out_specs=[hbm()] * len(shapes),
        out_shape=[jax.ShapeDtypeStruct(*item) for item in shapes],
        scratch_shapes=[
            pltpu.VMEM(quad, bf16),
            pltpu.VMEM(quad, bf16),
            pltpu.VMEM(quad, bf16),
            pltpu.VMEM(quad, bf16),
            pltpu.VMEM(quad, bf16),
            pltpu.VMEM(quad, f32),
            pltpu.VMEM(quad, bf16),
            pltpu.VMEM(quad, bf16),
            pltpu.VMEM((tokens, width), f32),
            pltpu.VMEM((tokens, width), bf16),
            pltpu.VMEM((wide_n, cap, width), bf16),
            pltpu.VMEM((2, span, table), f32),
            pltpu.VMEM((seqs, total, 2 * total), bf16),
            pltpu.VMEM((2 * total, 256), bf16),
            pltpu.VMEM((2, total, 128), bf16),
            pltpu.SemaphoreType.DMA((2, parts)),
            pltpu.SemaphoreType.DMA((2, parts)),
            pltpu.SemaphoreType.DMA((2, wide_n)),
            pltpu.SemaphoreType.DMA((seqs,)),
            pltpu.SemaphoreType.DMA((12,)),
        ],
        compiler_params=params(collective_id=1, has_side_effects=True),
        name="forward",
    )(lens, tok, cot, slot_row, diag, gain_a, gain_e, wq, wk, wv, wo)


def expert_kernel(
    experts, chunks, routed_ref, slot_ref, wr_ref, cot_any, win_any, wout_any,
    res_any, back_any, gin_any, gout_any, grouter_ref,
    send_ref, recv_ref, cot_ref, push_ref, win_ref, wout_ref, act_ref, pg_ref, bsend_ref, res_ref,
    acc_res, acc_back, sendsem, backsem, sem,
):
    wide_n, cap, width = send_ref.shape
    units = win_ref.shape[1]
    tile = 512
    w = lax.axis_index("wide")
    per = wide_n // chunks
    chunk_rows = per * cap
    loads = [
        pltpu.make_async_copy(a, b, sem.at[i])
        for i, (a, b) in enumerate(((cot_any, cot_ref), (win_any, win_ref), (wout_any, wout_ref)))
    ]
    for copy in loads:
        copy.start()
    enter(1, wide_n)

    def send_copy(k):
        return remote(
            send_ref.at[k], recv_ref.at[k], sendsem, k, "wide", flipped(w, k, wide_n)
        )

    def back_copy(k):
        return remote(
            bsend_ref.at[k], back_any.at[w], backsem, k, "wide", flipped(w, k, wide_n)
        )

    def send_step(i, carry):
        k = wide_n - 1 - i
        pick = expert_pick(flipped(w, k, wide_n), cap, slot_ref[...])
        send_ref[k] = dot(pick, routed_ref[...]).astype(bf16)
        send_copy(k).start()
        return carry

    lax.fori_loop(0, wide_n - 1, send_step, 0)
    pick = expert_pick(w, cap, slot_ref[...])
    recv_ref[0] = dot(pick, routed_ref[...]).astype(bf16)
    for copy in loads:
        copy.wait()
    lane = lax.broadcasted_iota(jnp.int32, (1, wr_ref.shape[1]), 1)
    hot = lane == w
    c0 = 0.7978845608028654
    c1 = c0 * 0.044715
    grouter_ref[...] = jnp.zeros_like(grouter_ref)

    def one_chunk(chunk, carry):
        first = chunk * per

        def arrive(j, inner):
            @pl.when(first + j > 0)
            def _():
                send_copy(first + j).wait_recv()

            return inner

        lax.fori_loop(0, per, arrive, 0)
        sources = pl.ds(first, per)
        here = pl.ds(pl.multiple_of(chunk * chunk_rows, chunk_rows), chunk_rows)
        x = recv_ref[sources].reshape(chunk_rows, width)
        cot = cot_ref[sources].reshape(chunk_rows, width).astype(f32)
        logits = jnp.where(lane < experts, dot(x, wr_ref[...]), -1e30)
        raised = jnp.exp(logits - jnp.max(logits, axis=-1, keepdims=True))
        probs = raised * (1.0 / jnp.sum(raised, axis=-1, keepdims=True))
        gate = jnp.sum(jnp.where(hot, probs, 0.0), axis=-1, keepdims=True)
        push_ref[here, :] = (gate * cot).astype(bf16)
        acc_res[...] = jnp.zeros_like(acc_res)
        acc_back[...] = jnp.zeros_like(acc_back)

        def hidden_tile(t, inner):
            cols = pl.ds(pl.multiple_of(t * tile, tile), tile)
            pre = dot(recv_ref[sources].reshape(chunk_rows, width), win_ref[:, cols])
            ag = dot(push_ref[here, :], wout_ref[cols, :], NT)
            sq = pre * pre
            th = jnp.tanh(pre * (c0 + c1 * sq))
            half = 0.5 + 0.5 * th
            act = (pre * half).astype(bf16)
            slope = half + pre * (0.5 - 0.5 * th * th) * (c0 + 3.0 * c1 * sq)
            pg = (ag * slope).astype(bf16)
            act_ref[here, cols] = act
            pg_ref[here, cols] = pg
            acc_res[...] += dot(act, wout_ref[cols, :])
            acc_back[...] += dot(pg, win_ref[:, cols], NT)
            return inner

        lax.fori_loop(0, units // tile, hidden_tile, 0)
        result = acc_res[...].astype(bf16).astype(f32)
        res_ref[sources] = (gate * result).astype(bf16).reshape(per, cap, width)
        gate_grad = jnp.sum(cot * result, axis=-1, keepdims=True)
        logit_grad = probs * (jnp.where(hot, gate_grad, 0.0) - gate * gate_grad)
        logit_grad = logit_grad.astype(bf16)
        back = acc_back[...].astype(bf16).astype(f32) + dot(logit_grad, wr_ref[...], NT)
        bsend_ref[sources] = back.astype(bf16).reshape(per, cap, width)
        grouter_ref[...] += dot(x, logit_grad, TN)

        def give(j, inner):
            @pl.when(first + j > 0)
            def _():
                back_copy(first + j).start()

            return inner

        lax.fori_loop(0, per, give, 0)
        return carry

    lax.fori_loop(0, chunks, one_chunk, 0)
    own = pltpu.make_async_copy(bsend_ref.at[0], back_any.at[w], sem.at[0])
    own.start()
    res_copy = pltpu.make_async_copy(res_ref, res_any, sem.at[1])
    res_copy.start()

    def weight_tile(t, carry):
        cols = pl.ds(pl.multiple_of(t * tile, tile), tile)
        win_ref[:, cols] = dot(
            recv_ref[...].reshape(wide_n * cap, width), pg_ref[:, cols], TN
        ).astype(bf16)
        wout_ref[cols, :] = dot(act_ref[:, cols], push_ref[...], TN).astype(bf16)
        return carry

    lax.fori_loop(0, units // tile, weight_tile, 0)
    gin_copy = pltpu.make_async_copy(win_ref, gin_any, sem.at[2])
    gin_copy.start()
    gout_copy = pltpu.make_async_copy(wout_ref, gout_any, sem.at[3])
    gout_copy.start()

    def finish_step(k, carry):
        send_copy(k).wait_send()
        back_copy(k).wait()
        return carry

    lax.fori_loop(1, wide_n, finish_step, 0)
    own.wait()
    res_copy.wait()
    gin_copy.wait()
    gout_copy.wait()


def run_experts(routed, slot_row, wr, cot_rows, win, wout, experts):
    wide_n, cap, width = cot_rows.shape
    units = win.shape[1]
    chunks = 4
    slots = wide_n * cap
    block = (wide_n, cap, width)
    step = slots // chunks
    return pl.pallas_call(
        functools.partial(expert_kernel, experts, chunks),
        in_specs=[vmem()] * 3 + [hbm()] * 3,
        out_specs=[hbm()] * 4 + [vmem()],
        out_shape=[
            jax.ShapeDtypeStruct(block, bf16),
            jax.ShapeDtypeStruct(block, bf16),
            jax.ShapeDtypeStruct((width, units), bf16),
            jax.ShapeDtypeStruct((units, width), bf16),
            jax.ShapeDtypeStruct((width, wr.shape[1]), f32),
        ],
        scratch_shapes=[
            pltpu.VMEM(block, bf16),
            pltpu.VMEM(block, bf16),
            pltpu.VMEM(block, bf16),
            pltpu.VMEM((slots, width), bf16),
            pltpu.VMEM((width, units), bf16),
            pltpu.VMEM((units, width), bf16),
            pltpu.VMEM((slots, units), bf16),
            pltpu.VMEM((slots, units), bf16),
            pltpu.VMEM(block, bf16),
            pltpu.VMEM(block, bf16),
            pltpu.VMEM((step, width), f32),
            pltpu.VMEM((step, width), f32),
            pltpu.SemaphoreType.DMA((2, wide_n)),
            pltpu.SemaphoreType.DMA((2, wide_n)),
            pltpu.SemaphoreType.DMA((4,)),
        ],
        compiler_params=params(collective_id=2, has_side_effects=True),
        name="experts",
    )(routed, slot_row, wr, cot_rows, win, wout)


def hidden_back_kernel(
    back_ref, slot_ref, hid_ref, cot_ref, att_ref, wo_ref, gain_ref,
    hg_ref, ag_ref, gwo_ref, ggain_ref, branch_ref,
):
    tokens, width = hid_ref.shape
    slots = back_ref.shape[0]
    step = 256
    gain = gain_ref[...]
    ggain_ref[...] = jnp.zeros_like(ggain_ref)

    def pull(i, carry):
        rows = pl.ds(pl.multiple_of(i * step, step), step)
        ids = lax.broadcasted_iota(jnp.int32, (step, slots), 1)
        pick = (ids == slot_ref[rows, :]).astype(f32).astype(bf16)
        upstream = dot(pick, back_ref[...])
        hidden = hid_ref[rows, :]
        inv = inverse_rms(hidden)
        scaled = upstream * gain
        inner = jnp.mean(scaled * hidden, axis=-1, keepdims=True)
        grad = cot_ref[rows, :].astype(f32) + inv * scaled - hidden * (inv * inv * inv * inner)
        ggain_ref[...] += jnp.sum(upstream * hidden * inv, axis=0, keepdims=True)
        hg_ref[rows, :] = grad
        low = grad.astype(bf16)
        branch_ref[rows, :] = low
        ag_ref[rows, :] = dot(low, wo_ref[...], NT).astype(bf16)
        return carry

    lax.fori_loop(0, tokens // step, pull, 0)

    def weight(i, carry):
        cols = pl.ds(pl.multiple_of(i * 256, 256), 256)
        gwo_ref[:, cols] = dot(att_ref[...], branch_ref[:, cols], TN).astype(bf16)
        return carry

    lax.fori_loop(0, width // 256, weight, 0)


def hidden_back(back, slot_col, hid, cot, att, wo, gain):
    tokens, width = hid.shape
    return pl.pallas_call(
        hidden_back_kernel,
        in_specs=[vmem()] * 7,
        out_specs=[vmem()] * 4,
        out_shape=[
            jax.ShapeDtypeStruct((tokens, width), f32),
            jax.ShapeDtypeStruct((tokens, width), bf16),
            jax.ShapeDtypeStruct((width, width), bf16),
            jax.ShapeDtypeStruct((1, width), f32),
        ],
        scratch_shapes=[pltpu.VMEM((tokens, width), bf16)],
        compiler_params=params(),
        name="hidden_back",
    )(back, slot_col, hid, cot, att, wo, gain)


def attention_backward_kernel(
    ag_ref, att_ref, p_ref, invl_ref, q_ref, k_ref, v_ref, tok_ref, gain_ref,
    wq_ref, wk_ref, wv_ref, gq_ref, gk_ref, gv_ref, part_ref, ggain_ref, diag_ref,
    dq_ref, dk_ref, dv_ref, strip_ref, normed_ref, kmask_ref, vext_ref, ds_ref,
):
    pair = pl.program_id(0)
    parts, seqs, span, width = tok_ref.shape
    total = parts * span
    table = diag_ref.shape[-1]
    low, masks = half_masks(128)
    lane = lax.broadcasted_iota(jnp.int32, (1, 128), 1)
    lanes = pl.ds(pl.multiple_of(pair * 128, 128), 128)
    strip_ref[...] = jnp.zeros_like(strip_ref)

    def one_sequence(s, carry):
        kp = k_ref[:, s, :, lanes].reshape(total, 128)
        vp = v_ref[:, s, :, lanes].reshape(total, 128)
        for hh in range(2):
            ones = (lane // 2 == 32 - 32 * hh).astype(f32)
            kmask_ref[hh * total : (hh + 1) * total, :] = kp * masks[hh]
            vext_ref[hh] = jnp.where(ones > 0, ones, vp.astype(f32)).astype(bf16)
        dk = [0.0, 0.0]
        dv = [0.0, 0.0]
        for block in range(parts // 2):
            rows = slice(block * 2 * span, (block + 1) * 2 * span)
            both = slice(2 * block, 2 * block + 2)
            qp = q_ref[both, s, :, lanes].reshape(2 * span, 128)
            inv = invl_ref[both, s, :, lanes].reshape(2 * span, 128)
            gp = ag_ref[both, s, :, lanes].reshape(2 * span, 128).astype(f32)
            gp = (gp * inv).astype(bf16)
            gf = gp.astype(f32)
            agree = gf * att_ref[both, s, :, lanes].reshape(2 * span, 128).astype(f32)
            for hh in range(2):
                delta = -jnp.sum(
                    jnp.where(low if hh == 0 else ~low, agree, 0.0), axis=-1, keepdims=True
                )
                high = delta.astype(bf16).astype(f32)
                ext = jnp.where(lane == 64 - 64 * hh, high, 0.0)
                ext = jnp.where(lane == 65 - 64 * hh, delta - high, ext)
                ext = jnp.where(low if hh == 0 else ~low, gf, ext).astype(bf16)
                raised = p_ref[0, s, rows, hh * total : (hh + 1) * total]
                score_grad = raised.astype(f32) * dot(ext, vext_ref[hh], NT)
                for r in range(2):
                    at = (parts - 1 - (2 * block + r)) * span
                    strip_ref[hh, :, at : at + total] += score_grad[r * span : (r + 1) * span]
                score_grad = score_grad.astype(bf16)
                ds_ref[:, hh * total : (hh + 1) * total] = score_grad
                dk[hh] = dk[hh] + dot(score_grad, qp, TN)
                dv[hh] = dv[hh] + dot(raised, gp, TN)
            dq = dot(ds_ref[...], kmask_ref[...])
            at_rows = pl.ds(pl.multiple_of(s * total + block * 2 * span, 2 * span), 2 * span)
            dq_ref[at_rows, lanes] = dq.astype(bf16)
        rows_all = pl.ds(pl.multiple_of(s * total, total), total)
        dk_ref[rows_all, lanes] = (jnp.where(low, dk[0], dk[1]) * (1.0 / LOG2E)).astype(bf16)
        dv_ref[rows_all, lanes] = jnp.where(low, dv[0], dv[1]).astype(bf16)
        return carry

    lax.fori_loop(0, seqs, one_sequence, 0)
    back = lax.broadcasted_iota(jnp.int32, (span, span), 0)
    flip = (back + lax.broadcasted_iota(jnp.int32, (span, span), 1) == span - 1).astype(f32)
    for hh in range(2):
        turned = lax.dot_general(
            flip, strip_ref[hh], NN, precision=lax.Precision.HIGHEST, preferred_element_type=f32
        )
        turned = pltpu.roll(turned, 0, 1, stride=1, stride_axis=0)
        diag_ref[0, hh : hh + 1, :] = jnp.sum(turned, axis=0, keepdims=True)

    @pl.when(pair == pl.num_programs(0) - 1)
    def _():
        gain = gain_ref[...]
        ggain_ref[...] = jnp.zeros_like(ggain_ref)

        def pull(step, carry):
            s, n = step // (parts // 2), step % (parts // 2)
            x = tok_ref[pl.ds(2 * n, 2), s].reshape(2 * span, width).astype(f32)
            inv = inverse_rms(x)
            rows = pl.ds(pl.multiple_of(step * 2 * span, 2 * span), 2 * span)
            normed_ref[rows, :] = (x * inv * gain).astype(bf16)
            upstream = dot(dq_ref[rows, :], wq_ref[...], NT)
            upstream += dot(dk_ref[rows, :], wk_ref[...], NT)
            upstream += dot(dv_ref[rows, :], wv_ref[...], NT)
            scaled = upstream * gain
            inner = jnp.mean(scaled * x, axis=-1, keepdims=True)
            grad = inv * scaled - x * (inv * inv * inv * inner)
            ggain_ref[...] += jnp.sum(upstream * x * inv, axis=0, keepdims=True)
            grad = grad.astype(bf16).reshape(2, span, width)
            part_ref[pl.ds(2 * n, 2), s] = grad
            return carry

        lax.fori_loop(0, seqs * (parts // 2), pull, 0)

        def weight(i, carry):
            cols = pl.ds(pl.multiple_of(i * 256, 256), 256)
            gq_ref[:, cols] = dot(normed_ref[...], dq_ref[:, cols], TN).astype(bf16)
            gk_ref[:, cols] = dot(normed_ref[...], dk_ref[:, cols], TN).astype(bf16)
            gv_ref[:, cols] = dot(normed_ref[...], dv_ref[:, cols], TN).astype(bf16)
            return carry

        lax.fori_loop(0, width // 256, weight, 0)


def attention_backward(ag, att, p, invl, q, k, v, tok, gain, wq, wk, wv, table):
    parts, seqs, span, width = tok.shape
    total = parts * span
    pairs = p.shape[0]
    square = jax.ShapeDtypeStruct((width, width), bf16)
    rows = pltpu.VMEM((seqs * total, width), bf16)
    return pl.pallas_call(
        attention_backward_kernel,
        grid=(pairs,),
        in_specs=[
            vmem(),
            vmem(),
            pl.BlockSpec((1, seqs, total, 2 * total), lambda i: (i, 0, 0, 0)),
        ]
        + [vmem()] * 9,
        out_specs=[vmem()] * 5 + [pl.BlockSpec((1, 2, table), lambda i: (i, 0, 0))],
        out_shape=[
            square, square, square,
            jax.ShapeDtypeStruct((parts, seqs, span, width), bf16),
            jax.ShapeDtypeStruct((1, width), f32),
            jax.ShapeDtypeStruct((pairs, 2, table), f32),
        ],
        scratch_shapes=[
            rows, rows, rows, pltpu.VMEM((2, span, table), f32), rows,
            pltpu.VMEM((2 * total, 128), bf16),
            pltpu.VMEM((2, total, 128), bf16),
            pltpu.VMEM((2 * span, 2 * total), bf16),
        ],
        compiler_params=params(),
        name="attention_backward",
    )(ag, att, p, invl, q, k, v, tok, gain, wq, wk, wv)


def finish_kernel(res_ref, slot_ref, hid_ref, out_ref):
    tokens, width = hid_ref.shape
    slots = res_ref.shape[0]
    step = 256

    def add(i, carry):
        rows = pl.ds(pl.multiple_of(i * step, step), step)
        ids = lax.broadcasted_iota(jnp.int32, (step, slots), 1)
        pick = (ids == slot_ref[rows, :]).astype(f32).astype(bf16)
        out_ref[rows, :] = hid_ref[rows, :] + dot(pick, res_ref[...])
        return carry

    lax.fori_loop(0, tokens // step, add, 0)


def finish(res, slot_col, hid):
    return pl.pallas_call(
        finish_kernel,
        in_specs=[vmem()] * 3,
        out_specs=vmem(),
        out_shape=jax.ShapeDtypeStruct(hid.shape, f32),
        compiler_params=params(),
        name="finish",
    )(res, slot_col, hid)


def body(
    tokens, lengths, routes, bucket_table, attn_gain, query_weight, key_weight, value_weight,
    output_weight, relative_bias, expert_gain, router_weight, experts_in, experts_out, cotangent,
):
    seq_count, span, width = tokens.shape
    narrow_n = lax.axis_size("narrow")
    wide_n = lax.axis_size("wide")
    seqs = seq_count // narrow_n
    heads = relative_bias.shape[1]
    buckets = relative_bias.shape[0]
    experts = router_weight.shape[1]
    tok_count = seq_count * span
    capacity = 5 * tok_count // (4 * experts)
    cap = -(-capacity // 16) * 16
    slots = experts * cap
    table = 2 * span * narrow_n
    gain_a = attn_gain.astype(f32).reshape(1, width)
    gain_e = expert_gain.astype(f32).reshape(1, width)
    router = jnp.pad(router_weight, ((0, 0), (0, -experts % 128)))

    def swap(array):
        return lax.all_to_all(array, "narrow", split_axis=0, concat_axis=0, tiled=True)

    def trade(array):
        array = array.reshape(wide_n, -1, width)
        return lax.all_to_all(array, "wide", split_axis=0, concat_axis=0, tiled=True).reshape(
            -1, width
        )

    table_ids = jnp.pad(bucket_table, (0, 1))
    offset_hot = (table_ids[None, :] == jnp.arange(buckets, dtype=jnp.int32)[:, None]).astype(bf16)
    diag = dot(relative_bias, offset_hot, TN).reshape(heads // 2, 2, table)
    route_ids = routes.reshape(tok_count)
    onehot = route_ids[:, None] == jnp.arange(experts, dtype=jnp.int32)[None, :]
    counts = jnp.cumsum(onehot.astype(jnp.int32), axis=0)
    position = jnp.sum(jnp.where(onehot, counts - 1, 0), axis=-1)
    slot = jnp.where(position < capacity, route_ids * cap + position, slots)
    slot_row, slot_col = slot.reshape(1, tok_count), slot.reshape(tok_count, 1)

    flat_cot = cotangent.reshape(tok_count, width)
    tok_quad = tokens.reshape(narrow_n, seqs, span, width)
    tok_seq, att_seq, att_pos, hidden, routed, cot_rows, q, k, v, invl, probs = forward(
        lengths, tok_quad, flat_cot, slot_row, diag * LOG2E, gain_a, gain_e,
        query_weight, key_weight, value_weight, output_weight, wide_n, cap,
    )
    attended = att_pos.reshape(tok_count, width)
    res, back_rows, term_in, term_out, router_grad = run_experts(
        routed, slot_row, router, cot_rows, experts_in[0], experts_out[0], experts
    )
    back_rows = back_rows.reshape(slots, width)
    me = lax.axis_index("wide")
    order = jnp.arange(wide_n, dtype=jnp.int32) ^ me
    res_rows = trade(res[order])
    hidden_grad, att_grad, output_grad, gain_second = hidden_back(
        back_rows, slot_col, hidden, flat_cot, attended, output_weight, gain_e
    )
    layer_output = finish(res_rows, slot_col, hidden).reshape(seq_count, span, width)
    ag_seq = swap(att_grad.reshape(seq_count, span, width)).reshape(narrow_n, seqs, span, width)
    grad_query, grad_key, grad_value, part, gain_first, diag_grad = attention_backward(
        ag_seq, att_seq, probs, invl, q, k, v, tok_seq, gain_a, query_weight, key_weight, value_weight, table
    )
    part = swap(part.reshape(seq_count, span, width))
    input_grad = hidden_grad.reshape(seq_count, span, width) + part.astype(f32)
    relative_grad = lax.dot_general(
        offset_hot.astype(f32),
        diag_grad.reshape(heads, table),
        NT,
        precision=lax.Precision.HIGHEST,
        preferred_element_type=f32,
    )

    def scatter(array, dim=0):
        return lax.psum_scatter(
            array.astype(bf16), "narrow", scatter_dimension=dim, tiled=True
        ).astype(f32)

    grad_experts_in = scatter(term_in)[None]
    grad_experts_out = scatter(term_out)[None]
    shares = tuple(
        scatter(item)
        for item in (
            grad_query, grad_key, grad_value, output_grad, router_grad[:, :experts],
            relative_grad, gain_first[0], gain_second[0],
        )
    )
    totals = lax.psum(shares, "wide")
    return (
        layer_output,
        input_grad,
        totals[6],
        totals[0],
        totals[1],
        totals[2],
        totals[3],
        totals[5],
        totals[7],
        totals[4],
        grad_experts_in,
        grad_experts_out,
    )


def solution(mesh):
    token = P("wide", "narrow", None)
    expert = P("wide", None, None)
    row, vector = P("narrow", None), P("narrow")
    return jax.shard_map(
        body,
        mesh=mesh,
        in_specs=(token, P("wide"), token) + (P(),) * 9 + (expert, expert, token),
        out_specs=(
            token, token, vector, row, row, row, row, row, vector, row,
            P("wide", "narrow", None), P("wide", "narrow", None),
        ),
        check_vma=False,
    )
```

```python
import functools

import jax
import jax.numpy as jnp
from jax import lax
from jax.experimental import pallas as pl
from jax.experimental.pallas import tpu as pltpu
from jax.sharding import PartitionSpec as P

f32, bf16 = jnp.float32, jnp.bfloat16
epsilon = 1e-06
VMEM_BYTES = 60 * 1024 * 1024
NN = (((1,), (0,)), ((), ()))
NT = (((1,), (1,)), ((), ()))
TN = (((0,), (0,)), ((), ()))


def dot(a, b, dims=NN):
    return lax.dot_general(a, b, dims, preferred_element_type=f32)


def vmem():
    return pl.BlockSpec(memory_space=pltpu.VMEM)


def params(**kw):
    return pltpu.CompilerParams(vmem_limit_bytes=VMEM_BYTES, **kw)


def inverse_rms(field):
    return lax.rsqrt(jnp.mean(field * field, axis=-1, keepdims=True) + epsilon)


def half_masks(pair_width):
    lane = lax.broadcasted_iota(jnp.int32, (1, pair_width), 1)
    low = lane < pair_width // 2
    return low, (low.astype(f32).astype(bf16), (~low).astype(f32).astype(bf16))


MESH = pl.DeviceIdType.MESH
LOG2E = 1.4426950408889634


def hbm():
    return pl.BlockSpec(memory_space=pl.ANY)


def flipped(me, k, size):
    out, bit = me, 1
    while bit < size:
        out = out + ((k // bit) % 2) * (bit - 2 * bit * ((me // bit) % 2))
        bit *= 2
    return out


def remote(src, dst, sems, k, axis, peer):
    return pltpu.make_async_remote_copy(
        src_ref=src,
        dst_ref=dst,
        send_sem=sems.at[0, k],
        recv_sem=sems.at[1, k],
        device_id={axis: peer},
        device_id_type=MESH,
    )


def enter(narrow_n, wide_n):
    barrier = pltpu.get_barrier_semaphore()
    count = 0
    for axis, size in (("narrow", narrow_n), ("wide", wide_n)):
        if size > 1:
            me = lax.axis_index(axis)

            def greet(k, carry, axis=axis, size=size, me=me):
                pl.semaphore_signal(
                    barrier, inc=1, device_id={axis: flipped(me, k, size)}, device_id_type=MESH
                )
                return carry

            lax.fori_loop(1, size, greet, 0)
            count += size - 1
    pl.semaphore_wait(barrier, count)


def expert_pick(expert, cap, slot_row):
    ids = lax.broadcasted_iota(jnp.int32, (cap, slot_row.shape[1]), 0) + expert * cap
    return (ids == slot_row).astype(f32).astype(bf16)


def forward_kernel(
    wide_n, lens_ref, tok_any, cot_ref, slot_ref, diag_ref, gain_a_ref, gain_e_ref,
    wq_ref, wk_ref, wv_ref, wo_ref,
    tokseq_any, attseq_any, att_any, hid_any, routed_any, cotrows_any, q_any, k_any, v_any, invl_any, p_any,
    tokbuf, tokpos, q_ref, k_ref, v_ref, invl_ref, attseq, attpos, hid_ref, routed_ref, cotsend,
    strip_ref, pbuf, vext, kext, toksem, attsem, cotsem, psem, outsem,
):
    parts, seqs, span, width = tokbuf.shape
    total = parts * span
    pairs, _, table = diag_ref.shape
    cap = cotsend.shape[1]
    n = lax.axis_index("narrow")
    w = lax.axis_index("wide")
    own = pltpu.make_async_copy(tok_any.at[n], tokbuf.at[n], outsem.at[0])
    own.start()
    position = pltpu.make_async_copy(tok_any, tokpos, outsem.at[1])
    position.start()
    enter(parts, wide_n)

    def tok_copy(k):
        peer = flipped(n, k, parts)
        return remote(tok_any.at[peer], tokbuf.at[n], toksem, k, "narrow", peer)

    for k in range(parts - 1, 0, -1):
        tok_copy(k).start()

    def cot_copy(k):
        peer = flipped(w, k, wide_n)
        return remote(cotsend.at[k], cotrows_any.at[k], cotsem, k, "wide", peer)

    def cot_block(k):
        pick = expert_pick(flipped(w, k, wide_n), cap, slot_ref[...])
        cotsend[k] = dot(pick, cot_ref[...]).astype(bf16)

    def cot_step(i, carry):
        k = wide_n - 1 - i
        cot_block(k)
        cot_copy(k).start()
        return carry

    lax.fori_loop(0, wide_n - 1, cot_step, 0)
    cot_block(0)
    cot_own = pltpu.make_async_copy(cotsend.at[0], cotrows_any.at[0], outsem.at[2])
    cot_own.start()

    gain = gain_a_ref[...]
    own.wait()
    for k in range(parts):
        src = flipped(n, k, parts)
        if k > 0:
            tok_copy(k).wait_recv()
        x = tokbuf[src].reshape(seqs * span, width).astype(f32)
        normed = (x * inverse_rms(x) * gain).astype(bf16)
        shape = (seqs, span, width)
        q_ref[src] = (dot(normed, wq_ref[...]) * LOG2E).astype(bf16).reshape(shape)
        k_ref[src] = dot(normed, wk_ref[...]).astype(bf16).reshape(shape)
        v_ref[src] = dot(normed, wv_ref[...]).astype(bf16).reshape(shape)
    outs = [
        pltpu.make_async_copy(a, b, outsem.at[i])
        for a, b, i in (
            (tokbuf, tokseq_any, 3), (q_ref, q_any, 4), (k_ref, k_any, 5), (v_ref, v_any, 6),
        )
    ]
    for copy in outs:
        copy.start()

    low, masks = half_masks(128)
    lane = lax.broadcasted_iota(jnp.int32, (1, 128), 1)
    hot = [(lane == 64).astype(f32).astype(bf16), (lane == 0).astype(f32).astype(bf16)]
    for hh in range(2):
        ones = jnp.broadcast_to(masks[hh], (total, 128))
        vext[hh * total : (hh + 1) * total, 128:] = ones

    def att_copy(k, lanes):
        peer = flipped(n, k, parts)
        return remote(
            attseq.at[peer, :, :, lanes], attpos.at[n, :, :, lanes], attsem, k, "narrow", peer
        )

    def one_pair(pair, carry):
        lanes = pl.ds(pl.multiple_of(pair * 128, 128), 128)
        for hh in range(2):
            row = diag_ref[pair, hh : hh + 1, :]
            strip_ref[hh] = pltpu.roll(
                jnp.broadcast_to(row, (span, table)), table - span + 1, 1, stride=1, stride_axis=0
            )

        def one_sequence(s, inner):
            vp = v_ref[:, s, :, lanes].reshape(total, 128)
            kp = k_ref[:, s, :, lanes].reshape(total, 128).astype(f32)
            ids = lax.broadcasted_iota(jnp.int32, (total, 128), 0)
            push = jnp.where(ids < lens_ref[n * seqs + s], 0.0, -1e30)
            for hh in range(2):
                vext[hh * total : (hh + 1) * total, :128] = vp * masks[hh]
                kext[hh] = jnp.where(lane == 64 - 64 * hh, push, kp).astype(bf16)

            @pl.when(pair > 0)
            def _():
                pltpu.make_async_copy(pbuf.at[s], p_any.at[pair, s], psem.at[s]).wait()

            for block in range(parts // 2):
                rows = slice(block * 2 * span, (block + 1) * 2 * span)
                both = slice(2 * block, 2 * block + 2)
                qp = q_ref[both, s, :, lanes].reshape(2 * span, 128)
                for hh in range(2):
                    bias = jnp.concatenate(
                        [
                            strip_ref[hh, :, (parts - 1 - r) * span : (parts - 1 - r) * span + total]
                            for r in (2 * block, 2 * block + 1)
                        ],
                        axis=0,
                    )
                    scores = dot(qp * masks[hh] + hot[hh], kext[hh], NT) + bias
                    raised = jnp.exp2(scores - jnp.max(scores, axis=-1, keepdims=True))
                    pbuf[s, rows, hh * total : (hh + 1) * total] = raised.astype(bf16)
                mixed = dot(pbuf[s, rows, :], vext[...])
                inv = 1.0 / mixed[:, 128:]
                invl_ref[both, s, :, lanes] = inv.astype(bf16).reshape(2, span, 128)
                attseq[both, s, :, lanes] = (mixed[:, :128] * inv).astype(bf16).reshape(2, span, 128)
            pltpu.make_async_copy(pbuf.at[s], p_any.at[pair, s], psem.at[s]).start()
            return inner

        lax.fori_loop(0, seqs, one_sequence, 0)
        for k in range(parts - 1, 0, -1):
            att_copy(k, lanes).start()
        return carry

    lax.fori_loop(0, pairs, one_pair, 0)
    copy = pltpu.make_async_copy(invl_ref, invl_any, outsem.at[7])
    copy.start()
    outs.append(copy)
    position.wait()
    gain = gain_e_ref[...]
    for k in range(parts):
        src = flipped(n, k, parts)
        if k > 0:
            att_copy(k, slice(None)).wait_recv()
            att = attpos[src].reshape(seqs * span, width)
        else:
            attpos[src] = attseq[src]
            att = attseq[src].reshape(seqs * span, width)
        rows = pl.ds(pl.multiple_of(src * seqs * span, seqs * span), seqs * span)
        hidden = tokpos[src].reshape(seqs * span, width).astype(f32) + dot(att, wo_ref[...])
        hid_ref[rows, :] = hidden
        routed_ref[rows, :] = (hidden * inverse_rms(hidden) * gain).astype(bf16)
    for a, b, i in ((attpos, att_any, 8), (hid_ref, hid_any, 9), (routed_ref, routed_any, 10),
                    (attseq, attseq_any, 11)):
        copy = pltpu.make_async_copy(a, b, outsem.at[i])
        copy.start()
        outs.append(copy)
    for k in range(1, parts):
        tok_copy(k).wait_send()
        att_copy(k, slice(None)).wait_send()
    for s in range(seqs):
        pltpu.make_async_copy(pbuf.at[s], p_any.at[0, s], psem.at[s]).wait()
    cot_own.wait()

    def cot_wait(k, carry):
        cot_copy(k).wait()
        return carry

    lax.fori_loop(1, wide_n, cot_wait, 0)
    for copy in outs:
        copy.wait()


def forward(lens, tok, cot, slot_row, diag, gain_a, gain_e, wq, wk, wv, wo, wide_n, cap):
    parts, seqs, span, width = tok.shape
    pairs, _, table = diag.shape
    total = parts * span
    tokens = parts * seqs * span
    quad = (parts, seqs, span, width)
    shapes = [
        (quad, bf16), (quad, bf16), (quad, bf16), ((tokens, width), f32), ((tokens, width), bf16),
        ((wide_n, cap, width), bf16), (quad, bf16), (quad, bf16), (quad, bf16), (quad, bf16),
        ((pairs, seqs, total, 2 * total), bf16),
    ]
    return pl.pallas_call(
        functools.partial(forward_kernel, wide_n),
        in_specs=[pl.BlockSpec(memory_space=pltpu.SMEM), hbm()] + [vmem()] * 9,
        out_specs=[hbm()] * len(shapes),
        out_shape=[jax.ShapeDtypeStruct(*item) for item in shapes],
        scratch_shapes=[
            pltpu.VMEM(quad, bf16),
            pltpu.VMEM(quad, bf16),
            pltpu.VMEM(quad, bf16),
            pltpu.VMEM(quad, bf16),
            pltpu.VMEM(quad, bf16),
            pltpu.VMEM(quad, bf16),
            pltpu.VMEM(quad, bf16),
            pltpu.VMEM(quad, bf16),
            pltpu.VMEM((tokens, width), f32),
            pltpu.VMEM((tokens, width), bf16),
            pltpu.VMEM((wide_n, cap, width), bf16),
            pltpu.VMEM((2, span, table), f32),
            pltpu.VMEM((seqs, total, 2 * total), bf16),
            pltpu.VMEM((2 * total, 256), bf16),
            pltpu.VMEM((2, total, 128), bf16),
            pltpu.SemaphoreType.DMA((2, parts)),
            pltpu.SemaphoreType.DMA((2, parts)),
            pltpu.SemaphoreType.DMA((2, wide_n)),
            pltpu.SemaphoreType.DMA((seqs,)),
            pltpu.SemaphoreType.DMA((12,)),
        ],
        compiler_params=params(collective_id=1, has_side_effects=True),
        name="forward",
    )(lens, tok, cot, slot_row, diag, gain_a, gain_e, wq, wk, wv, wo)


def expert_kernel(
    experts, chunks, routed_ref, slot_ref, wr_ref, cot_any, win_any, wout_any,
    res_any, back_any, gin_any, gout_any, grouter_ref,
    send_ref, recv_ref, cot_ref, push_ref, win_ref, wout_ref, act_ref, pg_ref, bsend_ref, res_ref,
    acc_res, acc_back, sendsem, backsem, sem,
):
    wide_n, cap, width = send_ref.shape
    units = win_ref.shape[1]
    tile = 512
    w = lax.axis_index("wide")
    per = wide_n // chunks
    chunk_rows = per * cap
    loads = [
        pltpu.make_async_copy(a, b, sem.at[i])
        for i, (a, b) in enumerate(((cot_any, cot_ref), (win_any, win_ref), (wout_any, wout_ref)))
    ]
    for copy in loads:
        copy.start()
    enter(1, wide_n)

    def send_copy(k):
        return remote(
            send_ref.at[k], recv_ref.at[k], sendsem, k, "wide", flipped(w, k, wide_n)
        )

    def back_copy(k):
        return remote(
            bsend_ref.at[k], back_any.at[w], backsem, k, "wide", flipped(w, k, wide_n)
        )

    def send_step(i, carry):
        k = wide_n - 1 - i
        pick = expert_pick(flipped(w, k, wide_n), cap, slot_ref[...])
        send_ref[k] = dot(pick, routed_ref[...]).astype(bf16)
        send_copy(k).start()
        return carry

    lax.fori_loop(0, wide_n - 1, send_step, 0)
    pick = expert_pick(w, cap, slot_ref[...])
    recv_ref[0] = dot(pick, routed_ref[...]).astype(bf16)
    for copy in loads:
        copy.wait()
    lane = lax.broadcasted_iota(jnp.int32, (1, wr_ref.shape[1]), 1)
    hot = lane == w
    c0 = 0.7978845608028654
    c1 = c0 * 0.044715
    grouter_ref[...] = jnp.zeros_like(grouter_ref)

    def one_chunk(chunk, carry):
        first = chunk * per

        def arrive(j, inner):
            @pl.when(first + j > 0)
            def _():
                send_copy(first + j).wait_recv()

            return inner

        lax.fori_loop(0, per, arrive, 0)
        sources = pl.ds(first, per)
        here = pl.ds(pl.multiple_of(chunk * chunk_rows, chunk_rows), chunk_rows)
        x = recv_ref[sources].reshape(chunk_rows, width)
        cot = cot_ref[sources].reshape(chunk_rows, width).astype(f32)
        logits = jnp.where(lane < experts, dot(x, wr_ref[...]), -1e30)
        raised = jnp.exp(logits - jnp.max(logits, axis=-1, keepdims=True))
        probs = raised * (1.0 / jnp.sum(raised, axis=-1, keepdims=True))
        gate = jnp.sum(jnp.where(hot, probs, 0.0), axis=-1, keepdims=True)
        push_ref[here, :] = (gate * cot).astype(bf16)
        acc_res[...] = jnp.zeros_like(acc_res)
        acc_back[...] = jnp.zeros_like(acc_back)

        def hidden_tile(t, inner):
            cols = pl.ds(pl.multiple_of(t * tile, tile), tile)
            pre = dot(recv_ref[sources].reshape(chunk_rows, width), win_ref[:, cols])
            ag = dot(push_ref[here, :], wout_ref[cols, :], NT)
            sq = pre * pre
            th = jnp.tanh(pre * (c0 + c1 * sq))
            half = 0.5 + 0.5 * th
            act = (pre * half).astype(bf16)
            slope = half + pre * (0.5 - 0.5 * th * th) * (c0 + 3.0 * c1 * sq)
            pg = (ag * slope).astype(bf16)
            act_ref[here, cols] = act
            pg_ref[here, cols] = pg
            acc_res[...] += dot(act, wout_ref[cols, :])
            acc_back[...] += dot(pg, win_ref[:, cols], NT)
            return inner

        lax.fori_loop(0, units // tile, hidden_tile, 0)
        result = acc_res[...].astype(bf16).astype(f32)
        res_ref[sources] = (gate * result).astype(bf16).reshape(per, cap, width)
        gate_grad = jnp.sum(cot * result, axis=-1, keepdims=True)
        logit_grad = probs * (jnp.where(hot, gate_grad, 0.0) - gate * gate_grad)
        logit_grad = logit_grad.astype(bf16)
        back = acc_back[...].astype(bf16).astype(f32) + dot(logit_grad, wr_ref[...], NT)
        bsend_ref[sources] = back.astype(bf16).reshape(per, cap, width)
        grouter_ref[...] += dot(x, logit_grad, TN)

        def give(j, inner):
            @pl.when(first + j > 0)
            def _():
                back_copy(first + j).start()

            return inner

        lax.fori_loop(0, per, give, 0)
        return carry

    lax.fori_loop(0, chunks, one_chunk, 0)
    own = pltpu.make_async_copy(bsend_ref.at[0], back_any.at[w], sem.at[0])
    own.start()
    res_copy = pltpu.make_async_copy(res_ref, res_any, sem.at[1])
    res_copy.start()

    def weight_tile(t, carry):
        cols = pl.ds(pl.multiple_of(t * tile, tile), tile)
        win_ref[:, cols] = dot(
            recv_ref[...].reshape(wide_n * cap, width), pg_ref[:, cols], TN
        ).astype(bf16)
        wout_ref[cols, :] = dot(act_ref[:, cols], push_ref[...], TN).astype(bf16)
        return carry

    lax.fori_loop(0, units // tile, weight_tile, 0)
    gin_copy = pltpu.make_async_copy(win_ref, gin_any, sem.at[2])
    gin_copy.start()
    gout_copy = pltpu.make_async_copy(wout_ref, gout_any, sem.at[3])
    gout_copy.start()

    def finish_step(k, carry):
        send_copy(k).wait_send()
        back_copy(k).wait()
        return carry

    lax.fori_loop(1, wide_n, finish_step, 0)
    own.wait()
    res_copy.wait()
    gin_copy.wait()
    gout_copy.wait()


def run_experts(routed, slot_row, wr, cot_rows, win, wout, experts):
    wide_n, cap, width = cot_rows.shape
    units = win.shape[1]
    chunks = 4
    slots = wide_n * cap
    block = (wide_n, cap, width)
    step = slots // chunks
    return pl.pallas_call(
        functools.partial(expert_kernel, experts, chunks),
        in_specs=[vmem()] * 3 + [hbm()] * 3,
        out_specs=[hbm()] * 4 + [vmem()],
        out_shape=[
            jax.ShapeDtypeStruct(block, bf16),
            jax.ShapeDtypeStruct(block, bf16),
            jax.ShapeDtypeStruct((width, units), bf16),
            jax.ShapeDtypeStruct((units, width), bf16),
            jax.ShapeDtypeStruct((width, wr.shape[1]), f32),
        ],
        scratch_shapes=[
            pltpu.VMEM(block, bf16),
            pltpu.VMEM(block, bf16),
            pltpu.VMEM(block, bf16),
            pltpu.VMEM((slots, width), bf16),
            pltpu.VMEM((width, units), bf16),
            pltpu.VMEM((units, width), bf16),
            pltpu.VMEM((slots, units), bf16),
            pltpu.VMEM((slots, units), bf16),
            pltpu.VMEM(block, bf16),
            pltpu.VMEM(block, bf16),
            pltpu.VMEM((step, width), f32),
            pltpu.VMEM((step, width), f32),
            pltpu.SemaphoreType.DMA((2, wide_n)),
            pltpu.SemaphoreType.DMA((2, wide_n)),
            pltpu.SemaphoreType.DMA((4,)),
        ],
        compiler_params=params(collective_id=2, has_side_effects=True),
        name="experts",
    )(routed, slot_row, wr, cot_rows, win, wout)


def link(src, dst, send_sem, recv_sem, axis, peer):
    return pltpu.make_async_remote_copy(
        src_ref=src,
        dst_ref=dst,
        send_sem=send_sem,
        recv_sem=recv_sem,
        device_id={axis: peer},
        device_id_type=MESH,
    )


def padded(v):
    return -(-v // 16) * 16


class Sums:
    def __init__(self, wide_n, refs, sems):
        self.terms, self.near, self.far, self.mine, self.given, self.whole = refs
        self.near_sem, self.far_sem, self.piece_sem, self.gather_sem = sems
        self.wide_n = wide_n
        self.n, self.w = lax.axis_index("narrow"), lax.axis_index("wide")
        self.core, self.half = self.n % 2, self.n // 2
        _, _, self.blocks, self.rows, _ = self.terms.shape
        self.piece = self.given.shape[2]

    def near_copy(self, g, side):
        return link(
            self.terms.at[g, 2 * side + 1 - self.core], self.near.at[g, side],
            self.near_sem.at[0, g, side], self.near_sem.at[1, g, side],
            "narrow", flipped(self.n, 1, 4),
        )

    def far_copy(self, g):
        return link(
            self.terms.at[g, 2 * (1 - self.half) + self.core], self.far.at[g],
            self.far_sem.at[0, g], self.far_sem.at[1, g], "narrow", flipped(self.n, 2, 4),
        )

    def piece_copy(self, g, k):
        peer = flipped(self.w, k, self.wide_n)
        at = pl.ds(pl.multiple_of(peer * self.piece, 16), self.piece)
        return link(
            self.mine.at[g, at], self.given.at[g, k],
            self.piece_sem.at[0, g, k], self.piece_sem.at[1, g, k], "wide", peer,
        )

    def gather_copy(self, g, k):
        at = pl.ds(pl.multiple_of(self.w * self.piece, 16), self.piece)
        return link(
            self.whole.at[g, at], self.whole.at[g, at],
            self.gather_sem.at[0, g, k], self.gather_sem.at[1, g, k],
            "wide", flipped(self.w, k, self.wide_n),
        )

    def each(self, f):
        def step(k, carry):
            f(k)
            return carry

        lax.fori_loop(1, self.wide_n, step, 0)

    def start(self, g):
        for side in (0, 1):
            self.near_copy(g, side).start()

    def to_far(self, g):
        for side in (1 - self.half, self.half):
            self.near_copy(g, side).wait()
            at = 2 * side + self.core
            total = self.terms[g, at].astype(f32) + self.near[g, side].astype(f32)
            self.terms[g, at] = total.astype(bf16)
            if side is not self.half:
                self.far_copy(g).start()

    def to_pieces(self, g):
        self.far_copy(g).wait()
        total = self.terms[g, 2 * self.half + self.core].astype(f32) + self.far[g].astype(f32)
        rows = self.blocks * self.rows
        self.mine[g, :rows] = total.astype(bf16).reshape(rows, 128)
        self.each(lambda k: self.piece_copy(g, k).start())

    def to_gather(self, g):
        at = pl.ds(pl.multiple_of(self.w * self.piece, 16), self.piece)
        self.each(lambda k: self.piece_copy(g, k).wait())

        def add(k, total):
            return total + self.given[g, k].astype(f32)

        total = lax.fori_loop(1, self.wide_n, add, self.mine[g, at].astype(f32))
        self.whole[g, at] = total.astype(bf16)
        self.each(lambda k: self.gather_copy(g, k).start())

    def finish(self, g):
        self.each(lambda k: self.gather_copy(g, k).wait())

    @staticmethod
    def scratch(groups, blocks, rows, wide_n):
        piece = padded(-(-blocks * rows // wide_n))
        return [
            pltpu.VMEM((groups, 4, blocks, rows, 128), bf16),
            pltpu.VMEM((groups, 2, blocks, rows, 128), bf16),
            pltpu.VMEM((groups, blocks, rows, 128), bf16),
            pltpu.VMEM((groups, wide_n * piece, 128), bf16),
            pltpu.VMEM((groups, wide_n, piece, 128), bf16),
            pltpu.VMEM((groups, wide_n * piece, 128), bf16),
        ], [
            pltpu.SemaphoreType.DMA((2, groups, 2)),
            pltpu.SemaphoreType.DMA((2, groups)),
            pltpu.SemaphoreType.DMA((2, groups, wide_n)),
            pltpu.SemaphoreType.DMA((2, groups, wide_n)),
        ]


def backward_kernel(
    wide_n, back_any, slot_ref, hid_any, cot_any, att_any, attseq_any, p_any, invl_any,
    q_any, k_any, v_any, tok_any, res_any, wo_ref, wq_ref, wk_ref, wv_ref, gain_a_ref, gain_e_ref,
    router_ref, hot_ref,
    out_any, igrad_any, big_any, small_any, resland_any,
    back_ref, hid_ref, cot_ref, att_ref, attseq_ref, invl_ref, q_ref, k_ref, v_ref, tok_ref,
    agsend, agbuf, partbuf, turned_ref, dk_ref, dv_ref, pbuf, acc_ref, diag_ref,
    kmask_ref, vext_ref, ds_ref, gains_ref, smallout, loadsem, psem, agsem, partsem,
    ressem, *rest,
):
    parts, seqs, span, width = tok_ref.shape
    total = parts * span
    block_rows = seqs * span
    pairs = width // 128
    slots = back_ref.shape[0] * back_ref.shape[1]
    rows_n = width // parts
    n, w = lax.axis_index("narrow"), lax.axis_index("wide")
    big = Sums(wide_n, rest[0:6], rest[12:16])
    small = Sums(wide_n, rest[6:12], rest[16:20])
    loads = [
        pltpu.make_async_copy(a, b, loadsem.at[i])
        for i, (a, b) in enumerate(
            (
                (back_any, back_ref), (hid_any, hid_ref), (cot_any, cot_ref), (att_any, att_ref),
                (attseq_any, attseq_ref), (invl_any, invl_ref), (q_any, q_ref), (k_any, k_ref),
                (v_any, v_ref), (tok_any, tok_ref),
            )
        )
    ]
    for copy in loads:
        copy.start()

    def block_of(phase):
        return n // 2 + phase * (1 - 2 * (n // 2))

    def p_copy(i):
        at = pl.ds(pl.multiple_of(block_of(i // pairs) * 2 * span, 2 * span), 2 * span)
        return pltpu.make_async_copy(p_any.at[i % pairs, :, at], pbuf.at[i % 2], psem.at[i % 2])

    p_copy(0).start()
    enter(parts, wide_n)

    def res_copy(k):
        return remote(
            res_any.at[k], resland_any.at[w], ressem, k, "wide", flipped(w, k, wide_n)
        )

    def res_start(k, carry):
        res_copy(k).start()
        return carry

    lax.fori_loop(1, wide_n, res_start, 0)
    res_own = pltpu.make_async_copy(res_any.at[0], resland_any.at[w], loadsem.at[10])
    res_own.start()

    def ag_copy(k):
        peer = flipped(n, k, parts)
        return remote(agsend.at[peer], agbuf.at[n], agsem, k, "narrow", peer)

    def rows_of(src):
        return pl.ds(pl.multiple_of(src * block_rows, block_rows), block_rows)

    def picked(rows):
        ids = lax.broadcasted_iota(jnp.int32, (block_rows, slots), 1)
        pick = (ids == slot_ref[rows, :]).astype(f32).astype(bf16)
        return dot(pick, back_ref[...].reshape(slots, width))

    gain_a, gain_e = gain_a_ref[...], gain_e_ref[...]
    gains_ref[...] = jnp.zeros_like(gains_ref)
    for copy in loads[:3]:
        copy.wait()
    for k in range(parts - 1, -1, -1):
        src = flipped(n, k, parts)
        rows = rows_of(src)
        upstream = picked(rows)
        hidden = hid_ref[rows, :]
        inv = inverse_rms(hidden)
        scaled = upstream * gain_e
        inner = jnp.mean(scaled * hidden, axis=-1, keepdims=True)
        grad = cot_ref[rows, :].astype(f32) + inv * scaled - hidden * (inv * inv * inv * inner)
        gains_ref[1:2, :] += jnp.sum(upstream * hidden * inv, axis=0, keepdims=True)
        hid_ref[rows, :] = grad
        grad = grad.astype(bf16)
        cot_ref[rows, :] = grad
        grad = dot(grad, wo_ref[...], NT).astype(bf16).reshape(seqs, span, width)
        if k > 0:
            agsend[src] = grad
            ag_copy(k).start()
        else:
            agbuf[src] = grad
    loads[3].wait()
    for h in range(2):
        cols = slice(h * 2 * rows_n, (h + 1) * 2 * rows_n)
        grad = dot(att_ref[...].reshape(parts * block_rows, width)[:, cols], cot_ref[...], TN)
        grad = grad.astype(bf16)
        for t in range(2):
            for b in range(pairs):
                big.terms[0, 2 * h + t, b] = grad[
                    t * rows_n : (t + 1) * rows_n, b * 128 : (b + 1) * 128
                ]
    big.start(0)
    for copy in loads[4:]:
        copy.wait()
    for b in range(parts):
        x = tok_ref[b].reshape(block_rows, width).astype(f32)
        normed = x * inverse_rms(x) * gain_a
        turned_ref[:, b * block_rows : (b + 1) * block_rows] = normed.T.astype(bf16)
    diag_ref[...] = jnp.zeros_like(diag_ref)

    low, masks = half_masks(128)
    lane = lax.broadcasted_iota(jnp.int32, (1, 128), 1)
    strip = (parts + 2) * span

    def attention_pair(phase, pair):
        i = phase * pairs + pair
        slot = i % 2
        block = block_of(phase)
        both = pl.ds(2 * block, 2)
        lanes = pl.ds(pl.multiple_of(pair * 128, 128), 128)
        p_copy(i).wait()

        @pl.when(i + 1 < 2 * pairs)
        def _():
            p_copy(i + 1).start()

        for s in range(seqs):
            kp = k_ref[:, s, :, lanes].reshape(total, 128)
            vp = v_ref[:, s, :, lanes].reshape(total, 128)
            for hh in range(2):
                ones = (lane // 2 == 32 - 32 * hh).astype(f32)
                kmask_ref[hh * total : (hh + 1) * total, :] = kp * masks[hh]
                vext_ref[hh] = jnp.where(ones > 0, ones, vp.astype(f32)).astype(bf16)
            dk = [0.0, 0.0]
            dv = [0.0, 0.0]
            qp = q_ref[both, s, :, lanes].reshape(2 * span, 128)
            inv = invl_ref[both, s, :, lanes].reshape(2 * span, 128).astype(f32)
            gp = agbuf[both, s, :, lanes].reshape(2 * span, 128).astype(f32)
            gp = (gp * inv).astype(bf16)
            gf = gp.astype(f32)
            agree = gf * attseq_ref[both, s, :, lanes].reshape(2 * span, 128).astype(f32)
            for hh in range(2):
                side = low if hh == 0 else ~low
                delta = -jnp.sum(jnp.where(side, agree, 0.0), axis=-1, keepdims=True)
                high = delta.astype(bf16).astype(f32)
                ext = jnp.where(lane == 64 - 64 * hh, high, 0.0)
                ext = jnp.where(lane == 65 - 64 * hh, delta - high, ext)
                ext = jnp.where(side, gf, ext).astype(bf16)
                raised = pbuf[slot, s, :, hh * total : (hh + 1) * total]
                score_grad = raised.astype(f32) * dot(ext, vext_ref[hh], NT)
                if s == 0:
                    acc_ref[hh] = score_grad
                else:
                    acc_ref[hh] += score_grad
                score_grad = score_grad.astype(bf16)
                ds_ref[:, hh * total : (hh + 1) * total] = score_grad
                dk[hh] = dot(score_grad, qp, TN)
                dv[hh] = dot(raised, gp, TN)
            dq = dot(ds_ref[...], kmask_ref[...])
            q_ref[both, s, :, lanes] = dq.astype(bf16).reshape(2, span, 128)
            dk = jnp.where(low, dk[0], dk[1]) * (1.0 / LOG2E)
            dv = jnp.where(low, dv[0], dv[1])
            here = slice(s * total, (s + 1) * total)
            if phase == 0:
                dk_ref[here, lanes] = dk
                dv_ref[here, lanes] = dv
            else:
                dk = dk + dk_ref[here, lanes]
                dv = dv + dv_ref[here, lanes]
                k_ref[:, s, :, lanes] = dk.astype(bf16).reshape(parts, span, 128)
                v_ref[:, s, :, lanes] = dv.astype(bf16).reshape(parts, span, 128)
        base = pl.multiple_of((parts - 2 - 2 * block) * span, span)
        for hh in range(2):
            upper, lower = acc_ref[hh, :span, :], acc_ref[hh, span:, :]
            zero = jnp.zeros((span, span), f32)
            upper = jnp.concatenate([zero, upper, zero], axis=1)
            lower = jnp.concatenate([lower, zero, zero], axis=1)
            both_rows = upper + lower
            small_sum = jnp.zeros((8, strip), f32)
            for a in range(span // 8):
                shift = span - 8 - 8 * a
                rows8 = both_rows[8 * a : 8 * a + 8]
                small_sum += rows8 if shift == 0 else pltpu.roll(rows8, shift, 1)
            line = small_sum[7:8]
            for a in range(7):
                line = line + pltpu.roll(small_sum[a : a + 1], 7 - a, 1)
            diag_ref[pl.ds(112 + 2 * pair + hh, 1), pl.ds(base, strip)] += line

    ag_copy(1).wait_recv()

    def first_phase(pair, carry):
        attention_pair(0, pair)

        @pl.when(pair == 1)
        def _():
            big.to_far(0)

        @pl.when(pair == 4)
        def _():
            big.to_pieces(0)

        return carry

    lax.fori_loop(0, pairs, first_phase, 0)
    for k in range(2, parts):
        ag_copy(k).wait_recv()

    def second_phase(j, carry):
        def inner(t, carry):
            attention_pair(1, 2 * j + t)

            @pl.when(t == 0)
            def _():
                @pl.when(j > 0)
                def _():
                    big.to_far(j)

            return carry

        lax.fori_loop(0, 2, inner, 0)
        cols = pl.ds(pl.multiple_of(j * 256, 256), 256)
        for i, ref in enumerate((q_ref, k_ref, v_ref)):
            field = ref[:, :, :, cols].reshape(parts * block_rows, 256)
            grad = dot(turned_ref[...], field).astype(bf16)
            for part in range(parts):
                for t in range(2):
                    big.terms[1 + j, part, 2 * i + t] = grad[
                        part * rows_n : (part + 1) * rows_n, t * 128 : (t + 1) * 128
                    ]
        big.start(1 + j)

        @pl.when(j == 0)
        def _():
            big.to_gather(0)

        @pl.when(j > 0)
        def _():
            big.to_pieces(j)

        return carry

    lax.fori_loop(0, pairs // 2, second_phase, 0)

    def part_copy(k):
        peer = flipped(n, k, parts)
        return remote(agsend.at[peer], partbuf.at[n], partsem, k, "narrow", peer)

    for k in range(1, parts):
        ag_copy(k).wait_send()
    for k in range(parts - 1, -1, -1):
        src = flipped(n, k, parts)
        x = tok_ref[src].reshape(block_rows, width).astype(f32)
        inv = inverse_rms(x)
        upstream = dot(q_ref[src].reshape(block_rows, width), wq_ref[...], NT)
        upstream += dot(k_ref[src].reshape(block_rows, width), wk_ref[...], NT)
        upstream += dot(v_ref[src].reshape(block_rows, width), wv_ref[...], NT)
        scaled = upstream * gain_a
        inner = jnp.mean(scaled * x, axis=-1, keepdims=True)
        grad = inv * scaled - x * (inv * inv * inv * inner)
        gains_ref[0:1, :] += jnp.sum(upstream * x * inv, axis=0, keepdims=True)
        grad = grad.astype(bf16).reshape(seqs, span, width)
        if k > 0:
            agsend[src] = grad
            part_copy(k).start()
        else:
            partbuf[src] = grad
        if k == 2:
            big.to_far(3)
        if k == 1:
            big.to_gather(1)

    pack = router_ref[...]
    for i in range(2):
        column = jnp.broadcast_to(gains_ref[i : i + 1, :], (128, width)).T
        pack = pack + jnp.where(lane == 126 + i, column, 0.0)
    relative = lax.dot_general(
        hot_ref[...].astype(f32), diag_ref[...], NT,
        precision=lax.Precision.HIGHEST, preferred_element_type=f32,
    )
    share = relative.shape[0] // parts
    for part in range(parts):
        slab = pack[part * rows_n : (part + 1) * rows_n]
        head = slab[:share] + relative[part * share : (part + 1) * share]
        small.terms[0, part, 0] = jnp.concatenate([head, slab[share:]], axis=0).astype(bf16)
    small.start(0)
    big.to_gather(2)

    res_own.wait()

    def res_wait(k, carry):
        res_copy(k).wait()
        return carry

    lax.fori_loop(1, wide_n, res_wait, 0)
    again = [
        pltpu.make_async_copy(resland_any, back_ref, loadsem.at[0]),
        pltpu.make_async_copy(hid_any, dk_ref, loadsem.at[1]),
    ]
    for copy in again:
        copy.start()
    small.to_far(0)
    big.to_pieces(3)
    for copy in again:
        copy.wait()
    outs = []
    for b in range(parts):
        rows = pl.ds(b * block_rows, block_rows)
        dk_ref[rows, :] += picked(rows)
        copy = pltpu.make_async_copy(dk_ref.at[rows], out_any.at[rows], loadsem.at[2 + b])
        copy.start()
        outs.append(copy)
        if b == 0:
            small.to_pieces(0)
        if b == 2:
            big.to_gather(3)
    small.to_gather(0)
    for k in range(parts):
        src = flipped(n, k, parts)
        rows = rows_of(src)
        if k > 0:
            part_copy(k).wait()
        hid_ref[rows, :] += partbuf[src].reshape(block_rows, width).astype(f32)
        copy = pltpu.make_async_copy(hid_ref.at[rows], igrad_any.at[rows], loadsem.at[6 + k])
        copy.start()
        outs.append(copy)
    for g in range(4):
        big.finish(g)
        for b in range(pairs):
            value = big.whole[g, b * rows_n : (b + 1) * rows_n, :].astype(f32)
            i, at = (3, b) if g == 0 else (b // 2, 2 * (g - 1) + b % 2)
            dv_ref[i * rows_n : (i + 1) * rows_n, at * 128 : (at + 1) * 128] = value
    small.finish(0)
    smallout[...] = small.whole[0, :rows_n, :].astype(f32)
    for a, b, i in ((dv_ref.at[: 4 * rows_n], big_any, 11), (smallout, small_any, 12)):
        copy = pltpu.make_async_copy(a, b, loadsem.at[i])
        copy.start()
        outs.append(copy)
    for copy in outs:
        copy.wait()


def backward(args, wide_n, quad, slots_shape, table):
    parts, seqs, span, width = quad
    total, tokens = parts * span, parts * seqs * span
    rows_n = width // parts
    square = pltpu.VMEM((tokens, width), f32)
    big_refs, big_sems = Sums.scratch(4, width // 128, rows_n, wide_n)
    small_refs, small_sems = Sums.scratch(1, 1, rows_n, wide_n)
    return pl.pallas_call(
        functools.partial(backward_kernel, wide_n),
        in_specs=[hbm(), vmem()] + [hbm()] * 11 + [vmem()] * 8,
        out_specs=[hbm()] * 5,
        out_shape=[
            jax.ShapeDtypeStruct((tokens, width), f32),
            jax.ShapeDtypeStruct((tokens, width), f32),
            jax.ShapeDtypeStruct((4 * rows_n, width), f32),
            jax.ShapeDtypeStruct((rows_n, 128), f32),
            jax.ShapeDtypeStruct(slots_shape, bf16),
        ],
        scratch_shapes=[
            pltpu.VMEM(slots_shape, bf16),
            square,
            pltpu.VMEM((tokens, width), bf16),
            pltpu.VMEM(quad, bf16),
            pltpu.VMEM(quad, bf16),
            pltpu.VMEM(quad, bf16),
            pltpu.VMEM(quad, bf16),
            pltpu.VMEM(quad, bf16),
            pltpu.VMEM(quad, bf16),
            pltpu.VMEM(quad, bf16),
            pltpu.VMEM(quad, bf16),
            pltpu.VMEM(quad, bf16),
            pltpu.VMEM(quad, bf16),
            pltpu.VMEM((width, tokens), bf16),
            square,
            square,
            pltpu.VMEM((2, seqs, 2 * span, 2 * total), bf16),
            pltpu.VMEM((2, 2 * span, total), f32),
            pltpu.VMEM((128, table), f32),
            pltpu.VMEM((2 * total, 128), bf16),
            pltpu.VMEM((2, total, 128), bf16),
            pltpu.VMEM((2 * span, 2 * total), bf16),
            pltpu.VMEM((8, width), f32),
            pltpu.VMEM((rows_n, 128), f32),
            pltpu.SemaphoreType.DMA((13,)),
            pltpu.SemaphoreType.DMA((2,)),
            pltpu.SemaphoreType.DMA((2, parts)),
            pltpu.SemaphoreType.DMA((2, parts)),
            pltpu.SemaphoreType.DMA((2, wide_n)),
        ]
        + big_refs
        + small_refs
        + big_sems
        + small_sems,
        compiler_params=params(collective_id=3, has_side_effects=True),
        name="backward",
    )(*args)


def body(
    tokens, lengths, routes, bucket_table, attn_gain, query_weight, key_weight, value_weight,
    output_weight, relative_bias, expert_gain, router_weight, experts_in, experts_out, cotangent,
):
    seq_count, span, width = tokens.shape
    narrow_n = lax.axis_size("narrow")
    wide_n = lax.axis_size("wide")
    seqs = seq_count // narrow_n
    heads = relative_bias.shape[1]
    buckets = relative_bias.shape[0]
    experts = router_weight.shape[1]
    tok_count = seq_count * span
    capacity = 5 * tok_count // (4 * experts)
    cap = -(-capacity // 16) * 16
    slots = experts * cap
    table = 2 * span * narrow_n
    gain_a = attn_gain.astype(f32).reshape(1, width)
    gain_e = expert_gain.astype(f32).reshape(1, width)
    router = jnp.pad(router_weight, ((0, 0), (0, -experts % 128)))

    table_ids = jnp.pad(bucket_table, (0, 1))
    offset_hot = (table_ids[None, :] == jnp.arange(buckets, dtype=jnp.int32)[:, None]).astype(bf16)
    diag = dot(relative_bias, offset_hot, TN).reshape(heads // 2, 2, table)
    route_ids = routes.reshape(tok_count)
    onehot = route_ids[:, None] == jnp.arange(experts, dtype=jnp.int32)[None, :]
    counts = jnp.cumsum(onehot.astype(jnp.int32), axis=0)
    position = jnp.sum(jnp.where(onehot, counts - 1, 0), axis=-1)
    slot = jnp.where(position < capacity, route_ids * cap + position, slots)
    slot_row, slot_col = slot.reshape(1, tok_count), slot.reshape(tok_count, 1)

    flat_cot = cotangent.reshape(tok_count, width)
    tok_quad = tokens.reshape(narrow_n, seqs, span, width)
    tok_seq, att_seq, att_pos, hidden, routed, cot_rows, q, k, v, invl, probs = forward(
        lengths, tok_quad, flat_cot, slot_row, diag * LOG2E, gain_a, gain_e,
        query_weight, key_weight, value_weight, output_weight, wide_n, cap,
    )
    res, back_rows, term_in, term_out, router_grad = run_experts(
        routed, slot_row, router, cot_rows, experts_in[0], experts_out[0], experts
    )
    layer_output, input_grad, big, small, _ = backward(
        (
            back_rows, slot_col, hidden, flat_cot, att_pos, att_seq, probs, invl, q, k, v, tok_seq,
            res, output_weight, query_weight, key_weight, value_weight, gain_a, gain_e,
            router_grad, offset_hot,
        ),
        wide_n, tok_quad.shape, res.shape, table,
    )

    def scatter(array, dim=0):
        return lax.psum_scatter(
            array.astype(bf16), "narrow", scatter_dimension=dim, tiled=True
        ).astype(f32)

    return (
        layer_output.reshape(seq_count, span, width),
        input_grad.reshape(seq_count, span, width),
        small[:, 126],
        *big.reshape(narrow_n, -1, width),
        small[: buckets // narrow_n, 112 : 112 + heads],
        small[:, 127],
        small[:, :experts],
        scatter(term_in)[None],
        scatter(term_out)[None],
    )


def solution(mesh):
    token = P("wide", "narrow", None)
    expert = P("wide", None, None)
    row, vector = P("narrow", None), P("narrow")
    return jax.shard_map(
        body,
        mesh=mesh,
        in_specs=(token, P("wide"), token) + (P(),) * 9 + (expert, expert, token),
        out_specs=(
            token, token, vector, row, row, row, row, row, vector, row,
            P("wide", "narrow", None), P("wide", "narrow", None),
        ),
        check_vma=False,
    )
```

```python
import functools

import jax
import jax.numpy as jnp
from jax import lax
from jax.experimental import pallas as pl
from jax.experimental.pallas import tpu as pltpu
from jax.sharding import PartitionSpec as P

f32, bf16 = jnp.float32, jnp.bfloat16
epsilon = 1e-06
VMEM_BYTES = 62 * 1024 * 1024
NN = (((1,), (0,)), ((), ()))
NT = (((1,), (1,)), ((), ()))
TN = (((0,), (0,)), ((), ()))


def dot(a, b, dims=NN):
    return lax.dot_general(a, b, dims, preferred_element_type=f32)


def vmem():
    return pl.BlockSpec(memory_space=pltpu.VMEM)


def params(**kw):
    return pltpu.CompilerParams(vmem_limit_bytes=VMEM_BYTES, **kw)


def inverse_rms(field):
    return lax.rsqrt(jnp.mean(field * field, axis=-1, keepdims=True) + epsilon)


def half_masks(pair_width):
    lane = lax.broadcasted_iota(jnp.int32, (1, pair_width), 1)
    low = lane < pair_width // 2
    return low, (low.astype(f32).astype(bf16), (~low).astype(f32).astype(bf16))


MESH = pl.DeviceIdType.MESH
LOG2E = 1.4426950408889634


def hbm():
    return pl.BlockSpec(memory_space=pl.ANY)


def flipped(me, k, size):
    out, bit = me, 1
    while bit < size:
        out = out + ((k // bit) % 2) * (bit - 2 * bit * ((me // bit) % 2))
        bit *= 2
    return out


def remote(src, dst, sems, k, axis, peer):
    return pltpu.make_async_remote_copy(
        src_ref=src,
        dst_ref=dst,
        send_sem=sems.at[0, k],
        recv_sem=sems.at[1, k],
        device_id={axis: peer},
        device_id_type=MESH,
    )


def enter(narrow_n, wide_n):
    barrier = pltpu.get_barrier_semaphore()
    count = 0
    for axis, size in (("narrow", narrow_n), ("wide", wide_n)):
        if size > 1:
            me = lax.axis_index(axis)

            def greet(k, carry, axis=axis, size=size, me=me):
                pl.semaphore_signal(
                    barrier, inc=1, device_id={axis: flipped(me, k, size)}, device_id_type=MESH
                )
                return carry

            lax.fori_loop(1, size, greet, 0)
            count += size - 1
    pl.semaphore_wait(barrier, count)


def expert_pick(expert, cap, slot_row):
    ids = lax.broadcasted_iota(jnp.int32, (cap, slot_row.shape[1]), 0) + expert * cap
    return (ids == slot_row).astype(f32).astype(bf16)


def token_slots(routes_ref, column_ref, experts, capacity, cap):
    seqs, span = routes_ref.shape
    routes = routes_ref[...]
    hot = jnp.concatenate([(routes == e).astype(f32) for e in range(experts)], axis=0)
    row = lax.broadcasted_iota(jnp.int32, (span, span), 0)
    ahead = (row < lax.broadcasted_iota(jnp.int32, (span, span), 1)).astype(f32).astype(bf16)
    size = experts * seqs
    row = lax.broadcasted_iota(jnp.int32, (size, size), 0)
    col = lax.broadcasted_iota(jnp.int32, (size, size), 1)
    above = ((row // seqs == col // seqs) & (col < row)).astype(f32).astype(bf16)
    counts = jnp.broadcast_to(jnp.sum(hot, axis=-1, keepdims=True), hot.shape).astype(bf16)
    position = dot(hot.astype(bf16), ahead) + dot(above, counts)
    slot = jnp.zeros((seqs, span), f32)
    for e in range(experts):
        here = position[e * seqs : (e + 1) * seqs]
        here = jnp.where(here < capacity, here + e * cap, experts * cap)
        slot = slot + hot[e * seqs : (e + 1) * seqs] * here
    turned = jnp.concatenate([slot] * (span // seqs), axis=0).T
    for s in range(seqs):
        column_ref[s * span : (s + 1) * span, :] = turned[:, s : s + 1].astype(jnp.int32)
    return jnp.concatenate([slot[s : s + 1] for s in range(seqs)], axis=1).astype(jnp.int32)


def forward_kernel(
    wide_n, capacity, lens_ref, tok_any, cot_ref, routes_ref, table_ref, bias_ref, gain_a_ref, gain_e_ref,
    wq_ref, wk_ref, wv_ref, wo_ref,
    tokseq_any, attseq_any, att_any, hid_any, routed_any, cotrows_any, q_any, k_any, v_any, invl_any, p_any,
    slot_row_ref, slot_col_ref, hot_ref,
    tokbuf, tokpos, q_ref, k_ref, v_ref, invl_ref, attseq, attpos, hid_ref, routed_ref, cotsend,
    strip_ref, pbuf, vext, kext, diag_ref, toksem, attsem, cotsem, psem, outsem,
):
    parts, seqs, span, width = tokbuf.shape
    total = parts * span
    heads = bias_ref.shape[1]
    pairs, table = heads // 2, diag_ref.shape[1]
    cap = cotsend.shape[1]
    n = lax.axis_index("narrow")
    w = lax.axis_index("wide")
    own = pltpu.make_async_copy(tok_any.at[n], tokbuf.at[n], outsem.at[0])
    own.start()
    position = pltpu.make_async_copy(tok_any, tokpos, outsem.at[1])
    position.start()
    enter(parts, wide_n)

    def tok_copy(k):
        peer = flipped(n, k, parts)
        return remote(tok_any.at[peer], tokbuf.at[n], toksem, k, "narrow", peer)

    for k in range(parts - 1, 0, -1):
        tok_copy(k).start()

    slot_row_ref[...] = token_slots(routes_ref, slot_col_ref, wide_n, capacity, cap)

    def cot_copy(k):
        peer = flipped(w, k, wide_n)
        return remote(cotsend.at[k], cotrows_any.at[k], cotsem, k, "wide", peer)

    def cot_block(k):
        pick = expert_pick(flipped(w, k, wide_n), cap, slot_row_ref[...])
        cotsend[k] = dot(pick, cot_ref[...]).astype(bf16)

    def cot_step(i, carry):
        k = wide_n - 1 - i
        cot_block(k)
        cot_copy(k).start()
        return carry

    lax.fori_loop(0, wide_n - 1, cot_step, 0)
    cot_block(0)
    cot_own = pltpu.make_async_copy(cotsend.at[0], cotrows_any.at[0], outsem.at[2])
    cot_own.start()

    gain = gain_a_ref[...].astype(f32).reshape(1, width)
    own.wait()
    for k in range(parts):
        src = flipped(n, k, parts)
        if k > 0:
            tok_copy(k).wait_recv()
        x = tokbuf[src].reshape(seqs * span, width).astype(f32)
        normed = (x * inverse_rms(x) * gain).astype(bf16)
        shape = (seqs, span, width)
        q_ref[src] = (dot(normed, wq_ref[...]) * LOG2E).astype(bf16).reshape(shape)
        k_ref[src] = dot(normed, wk_ref[...]).astype(bf16).reshape(shape)
        v_ref[src] = dot(normed, wv_ref[...]).astype(bf16).reshape(shape)
    outs = [
        pltpu.make_async_copy(a, b, outsem.at[i])
        for a, b, i in (
            (tokbuf, tokseq_any, 3), (q_ref, q_any, 4), (k_ref, k_any, 5), (v_ref, v_any, 6),
        )
    ]
    for copy in outs:
        copy.start()

    buckets, offsets = bias_ref.shape[0], table_ref.shape[0]
    ids = lax.broadcasted_iota(jnp.int32, (buckets, offsets), 0)
    found = (ids == table_ref[...].reshape(1, offsets)).astype(f32).astype(bf16)
    hot_ref[...] = jnp.zeros_like(hot_ref)
    hot_ref[:, :offsets] = found
    diag_ref[:heads, :] = dot(bias_ref[...], hot_ref[...], TN) * LOG2E

    low, masks = half_masks(128)
    lane = lax.broadcasted_iota(jnp.int32, (1, 128), 1)
    hot = [(lane == 64).astype(f32).astype(bf16), (lane == 0).astype(f32).astype(bf16)]
    for hh in range(2):
        ones = jnp.broadcast_to(masks[hh], (total, 128))
        vext[hh * total : (hh + 1) * total, 128:] = ones

    def att_copy(k, lanes):
        peer = flipped(n, k, parts)
        return remote(
            attseq.at[peer, :, :, lanes], attpos.at[n, :, :, lanes], attsem, k, "narrow", peer
        )

    def one_pair(pair, carry):
        lanes = pl.ds(pl.multiple_of(pair * 128, 128), 128)
        for hh in range(2):
            row = diag_ref[pl.ds(2 * pair + hh, 1), :]
            strip_ref[hh] = pltpu.roll(
                jnp.broadcast_to(row, (span, table)), table - span + 1, 1, stride=1, stride_axis=0
            )

        def one_sequence(s, inner):
            vp = v_ref[:, s, :, lanes].reshape(total, 128)
            kp = k_ref[:, s, :, lanes].reshape(total, 128).astype(f32)
            ids = lax.broadcasted_iota(jnp.int32, (total, 128), 0)
            push = jnp.where(ids < lens_ref[n * seqs + s], 0.0, -1e30)
            for hh in range(2):
                vext[hh * total : (hh + 1) * total, :128] = vp * masks[hh]
                kext[hh] = jnp.where(lane == 64 - 64 * hh, push, kp).astype(bf16)

            @pl.when(pair > 0)
            def _():
                pltpu.make_async_copy(pbuf.at[s], p_any.at[pair, s], psem.at[s]).wait()

            for block in range(parts // 2):
                rows = slice(block * 2 * span, (block + 1) * 2 * span)
                both = slice(2 * block, 2 * block + 2)
                qp = q_ref[both, s, :, lanes].reshape(2 * span, 128)
                for hh in range(2):
                    bias = jnp.concatenate(
                        [
                            strip_ref[hh, :, (parts - 1 - r) * span : (parts - 1 - r) * span + total]
                            for r in (2 * block, 2 * block + 1)
                        ],
                        axis=0,
                    )
                    scores = dot(qp * masks[hh] + hot[hh], kext[hh], NT) + bias
                    raised = jnp.exp2(scores - jnp.max(scores, axis=-1, keepdims=True))
                    pbuf[s, rows, hh * total : (hh + 1) * total] = raised.astype(bf16)
                mixed = dot(pbuf[s, rows, :], vext[...])
                inv = 1.0 / mixed[:, 128:]
                invl_ref[both, s, :, lanes] = inv.astype(bf16).reshape(2, span, 128)
                attseq[both, s, :, lanes] = (mixed[:, :128] * inv).astype(bf16).reshape(2, span, 128)
            pltpu.make_async_copy(pbuf.at[s], p_any.at[pair, s], psem.at[s]).start()
            return inner

        lax.fori_loop(0, seqs, one_sequence, 0)
        for k in range(parts - 1, 0, -1):
            att_copy(k, lanes).start()
        return carry

    lax.fori_loop(0, pairs, one_pair, 0)
    copy = pltpu.make_async_copy(invl_ref, invl_any, outsem.at[7])
    copy.start()
    outs.append(copy)
    position.wait()
    gain = gain_e_ref[...].astype(f32).reshape(1, width)
    for k in range(parts):
        src = flipped(n, k, parts)
        if k > 0:
            att_copy(k, slice(None)).wait_recv()
            att = attpos[src].reshape(seqs * span, width)
        else:
            attpos[src] = attseq[src]
            att = attseq[src].reshape(seqs * span, width)
        rows = pl.ds(pl.multiple_of(src * seqs * span, seqs * span), seqs * span)
        hidden = tokpos[src].reshape(seqs * span, width).astype(f32) + dot(att, wo_ref[...])
        hid_ref[rows, :] = hidden
        routed_ref[rows, :] = (hidden * inverse_rms(hidden) * gain).astype(bf16)
    for a, b, i in ((attpos, att_any, 8), (hid_ref, hid_any, 9), (routed_ref, routed_any, 10),
                    (attseq, attseq_any, 11)):
        copy = pltpu.make_async_copy(a, b, outsem.at[i])
        copy.start()
        outs.append(copy)
    for k in range(1, parts):
        tok_copy(k).wait_send()
        att_copy(k, slice(None)).wait_send()
    for s in range(seqs):
        pltpu.make_async_copy(pbuf.at[s], p_any.at[0, s], psem.at[s]).wait()
    cot_own.wait()

    def cot_wait(k, carry):
        cot_copy(k).wait()
        return carry

    lax.fori_loop(1, wide_n, cot_wait, 0)
    for copy in outs:
        copy.wait()


def forward(args, wide_n, capacity, cap, quad, table):
    parts, seqs, span, width = quad
    buckets, heads = args[5].shape
    pairs = heads // 2
    total = parts * span
    tokens = parts * seqs * span
    shapes = [
        (quad, bf16), (quad, bf16), (quad, bf16), ((tokens, width), f32), ((tokens, width), bf16),
        ((wide_n, cap, width), bf16), (quad, bf16), (quad, bf16), (quad, bf16), (quad, bf16),
        ((pairs, seqs, total, 2 * total), bf16),
    ]
    small = [((1, tokens), jnp.int32), ((tokens, 1), jnp.int32), ((buckets, table), bf16)]
    return pl.pallas_call(
        functools.partial(forward_kernel, wide_n, capacity),
        in_specs=[pl.BlockSpec(memory_space=pltpu.SMEM), hbm()] + [vmem()] * 10,
        out_specs=[hbm()] * len(shapes) + [vmem()] * 3,
        out_shape=[jax.ShapeDtypeStruct(*item) for item in shapes + small],
        scratch_shapes=[
            pltpu.VMEM(quad, bf16),
            pltpu.VMEM(quad, bf16),
            pltpu.VMEM(quad, bf16),
            pltpu.VMEM(quad, bf16),
            pltpu.VMEM(quad, bf16),
            pltpu.VMEM(quad, bf16),
            pltpu.VMEM(quad, bf16),
            pltpu.VMEM(quad, bf16),
            pltpu.VMEM((tokens, width), f32),
            pltpu.VMEM((tokens, width), bf16),
            pltpu.VMEM((wide_n, cap, width), bf16),
            pltpu.VMEM((2, span, table), f32),
            pltpu.VMEM((seqs, total, 2 * total), bf16),
            pltpu.VMEM((2 * total, 256), bf16),
            pltpu.VMEM((2, total, 128), bf16),
            pltpu.VMEM((16, table), f32),
            pltpu.SemaphoreType.DMA((2, parts)),
            pltpu.SemaphoreType.DMA((2, parts)),
            pltpu.SemaphoreType.DMA((2, wide_n)),
            pltpu.SemaphoreType.DMA((seqs,)),
            pltpu.SemaphoreType.DMA((12,)),
        ],
        compiler_params=params(collective_id=1, has_side_effects=True),
        name="forward",
    )(*args)


def expert_kernel(
    experts, chunks, split, routed_ref, slot_ref, router_ref, cot_any, win_any, wout_any,
    res_any, back_any, gin_any, ginfar_any, ginsend_any, gout_any, goutsend_any, grouter_ref,
    send_ref, recv_ref, cot_ref, push_ref, win_ref, wout_ref, act_ref, pg_ref, res_ref,
    acc_res, acc_back, nearin_ref, nearout_ref, wr_ref, sendsem, backsem, sem, gradsem,
):
    wide_n, cap, width = send_ref.shape
    units = win_ref.shape[1]
    tile = 512
    w = lax.axis_index("wide")
    per = wide_n // chunks
    chunk_rows = per * cap
    loads = [
        pltpu.make_async_copy(a, b, sem.at[i])
        for i, (a, b) in enumerate(((cot_any, cot_ref), (win_any, win_ref), (wout_any, wout_ref)))
    ]
    for copy in loads:
        copy.start()
    enter(4, wide_n)

    def send_copy(k):
        return remote(
            send_ref.at[k], recv_ref.at[k], sendsem, k, "wide", flipped(w, k, wide_n)
        )

    def back_copy(k):
        return remote(
            cot_ref.at[k], back_any.at[w], backsem, k, "wide", flipped(w, k, wide_n)
        )

    def turn(i):
        return (i % 2) * 2 + i // 2

    def send_step(i, carry):
        k = turn(i // per) * per + i % per
        pick = expert_pick(flipped(w, k, wide_n), cap, slot_ref[...])
        send_ref[k] = dot(pick, routed_ref[...]).astype(bf16)
        send_copy(k).start()
        return carry

    lax.fori_loop(1, wide_n, send_step, 0)
    pick = expert_pick(w, cap, slot_ref[...])
    recv_ref[0] = dot(pick, routed_ref[...]).astype(bf16)
    for copy in loads:
        copy.wait()
    wr_ref[...] = jnp.zeros_like(wr_ref)
    wr_ref[:, :experts] = router_ref[...]
    lane = lax.broadcasted_iota(jnp.int32, (1, wr_ref.shape[1]), 1)
    hot = lane == w
    c0 = 0.7978845608028654
    c1 = c0 * 0.044715
    grouter_ref[...] = jnp.zeros_like(grouter_ref)

    def give(first):
        def one(j, carry):
            @pl.when(first + j > 0)
            def _():
                back_copy(first + j).start()

            return carry

        return one

    def one_chunk(step, carry):
        chunk = turn(step)
        first = chunk * per

        def arrive(j, inner):
            @pl.when(first + j > 0)
            def _():
                send_copy(first + j).wait_recv()

            return inner

        lax.fori_loop(0, per, arrive, 0)

        @pl.when(step == chunks - 1)
        def _():
            for earlier in (2, 1, 0):
                lax.fori_loop(0, per, give(earlier * per), 0)

        sources = pl.ds(first, per)
        here = pl.ds(pl.multiple_of(chunk * chunk_rows, chunk_rows), chunk_rows)
        x = recv_ref[sources].reshape(chunk_rows, width)
        cot = cot_ref[sources].reshape(chunk_rows, width).astype(f32)
        logits = jnp.where(lane < experts, dot(x, wr_ref[...]), -1e30)
        raised = jnp.exp(logits - jnp.max(logits, axis=-1, keepdims=True))
        probs = raised * (1.0 / jnp.sum(raised, axis=-1, keepdims=True))
        gate = jnp.sum(jnp.where(hot, probs, 0.0), axis=-1, keepdims=True)
        push_ref[here, :] = (gate * cot).astype(bf16)
        acc_res[...] = jnp.zeros_like(acc_res)
        acc_back[...] = jnp.zeros_like(acc_back)

        def hidden_tile(t, inner):
            cols = pl.ds(pl.multiple_of(t * tile, tile), tile)
            pre = dot(recv_ref[sources].reshape(chunk_rows, width), win_ref[:, cols])
            ag = dot(push_ref[here, :], wout_ref[cols, :], NT)
            sq = pre * pre
            th = jnp.tanh(pre * (c0 + c1 * sq))
            half = 0.5 + 0.5 * th
            act = (pre * half).astype(bf16)
            slope = half + pre * (0.5 - 0.5 * th * th) * (c0 + 3.0 * c1 * sq)
            pg = (ag * slope).astype(bf16)
            act_ref[here, cols] = act
            pg_ref[here, cols] = pg
            acc_res[...] += dot(act, wout_ref[cols, :])
            acc_back[...] += dot(pg, win_ref[:, cols], NT)
            return inner

        lax.fori_loop(0, units // tile, hidden_tile, 0)
        result = acc_res[...].astype(bf16).astype(f32)
        res_ref[sources] = (gate * result).astype(bf16).reshape(per, cap, width)
        gate_grad = jnp.sum(cot * result, axis=-1, keepdims=True)
        logit_grad = probs * (jnp.where(hot, gate_grad, 0.0) - gate * gate_grad)
        logit_grad = logit_grad.astype(bf16)
        back = acc_back[...].astype(bf16).astype(f32) + dot(logit_grad, wr_ref[...], NT)
        cot_ref[sources] = back.astype(bf16).reshape(per, cap, width)
        grouter_ref[...] += dot(x, logit_grad, TN)

        @pl.when(step == chunks - 1)
        def _():
            lax.fori_loop(0, per, give(first), 0)

        return carry

    lax.fori_loop(0, chunks, one_chunk, 0)
    own = pltpu.make_async_copy(cot_ref.at[0], back_any.at[w], sem.at[0])
    own.start()
    res_copy = pltpu.make_async_copy(res_ref, res_any, sem.at[1])
    res_copy.start()

    n = lax.axis_index("narrow")
    core, half = n % 2, n // 2
    in_rows, out_rows = width // 4, units // 4

    def slice_at(index, rows):
        return pl.ds(pl.multiple_of(index * rows, rows), rows)

    def near_copy(ref, near, rows, side, i, cols=slice(None)):
        return link(
            ref.at[slice_at(2 * side + 1 - core, rows), cols], near.at[side, :, cols],
            gradsem.at[0, i + side], gradsem.at[1, i + side], "narrow", flipped(n, 1, 4),
        )

    def near_add(ref, near, rows, side, i, cols=slice(None)):
        near_copy(ref, near, rows, side, i, cols).wait()
        at = slice_at(2 * side + core, rows)
        ref[at, cols] = (ref[at, cols].astype(f32) + near[side, :, cols].astype(f32)).astype(bf16)
        return at

    early, late = slice(0, split), slice(split, units)
    gin_far = link(
        win_ref.at[slice_at(2 * (1 - half) + core, in_rows), early], ginfar_any,
        gradsem.at[0, 6], gradsem.at[1, 6], "narrow", flipped(n, 2, 4),
    )

    def in_tile(t, carry):
        cols = pl.ds(pl.multiple_of(t * tile, tile), tile)
        win_ref[:, cols] = dot(
            recv_ref[...].reshape(wide_n * cap, width), pg_ref[:, cols], TN
        ).astype(bf16)

        @pl.when(t == split // tile - 1)
        def _():
            for side in range(2):
                near_copy(win_ref, nearin_ref, in_rows, side, 0, early).start()

        return carry

    def out_tile(t, carry):
        cols = pl.ds(pl.multiple_of(t * tile, tile), tile)
        wout_ref[cols, :] = dot(act_ref[:, cols], push_ref[...], TN).astype(bf16)

        @pl.when(t == 1)
        def _():
            near_add(win_ref, nearin_ref, in_rows, 1 - half, 0, early)
            gin_far.start()

        return carry

    lax.fori_loop(0, units // tile, in_tile, 0)
    for side in range(2):
        near_copy(win_ref, nearin_ref, in_rows, side, 4, late).start()
    lax.fori_loop(0, units // tile, out_tile, 0)
    for side in range(2):
        near_copy(wout_ref, nearout_ref, out_rows, side, 2).start()
    near_add(win_ref, nearin_ref, in_rows, half, 0, early)
    at = near_add(win_ref, nearin_ref, in_rows, half, 4, late)
    ends = [pltpu.make_async_copy(win_ref.at[at], gin_any, sem.at[2])]
    at = near_add(win_ref, nearin_ref, in_rows, 1 - half, 4, late)
    ends.append(pltpu.make_async_copy(win_ref.at[at, late], ginsend_any, sem.at[5]))
    at = near_add(wout_ref, nearout_ref, out_rows, 1 - half, 2)
    ends.append(pltpu.make_async_copy(wout_ref.at[at], goutsend_any, sem.at[3]))
    at = near_add(wout_ref, nearout_ref, out_rows, half, 2)
    ends.append(pltpu.make_async_copy(wout_ref.at[at], gout_any, sem.at[4]))
    for copy in ends:
        copy.start()

    def finish_step(k, carry):
        send_copy(k).wait_send()
        back_copy(k).wait()
        return carry

    lax.fori_loop(1, wide_n, finish_step, 0)
    own.wait()
    res_copy.wait()
    gin_far.wait()
    for copy in ends:
        copy.wait()


def run_experts(routed, slot_row, wr, cot_rows, win, wout, experts):
    wide_n, cap, width = cot_rows.shape
    units = win.shape[1]
    chunks, split = 4, 2 * units // 3
    slots = wide_n * cap
    block = (wide_n, cap, width)
    step = slots // chunks
    return pl.pallas_call(
        functools.partial(expert_kernel, experts, chunks, split),
        in_specs=[vmem()] * 3 + [hbm()] * 3,
        out_specs=[hbm()] * 7 + [vmem()],
        out_shape=[
            jax.ShapeDtypeStruct(block, bf16),
            jax.ShapeDtypeStruct(block, bf16),
            jax.ShapeDtypeStruct((width // 4, units), bf16),
            jax.ShapeDtypeStruct((width // 4, split), bf16),
            jax.ShapeDtypeStruct((width // 4, units - split), bf16),
            jax.ShapeDtypeStruct((units // 4, width), bf16),
            jax.ShapeDtypeStruct((units // 4, width), bf16),
            jax.ShapeDtypeStruct((width, 128), f32),
        ],
        scratch_shapes=[
            pltpu.VMEM(block, bf16),
            pltpu.VMEM(block, bf16),
            pltpu.VMEM(block, bf16),
            pltpu.VMEM((slots, width), bf16),
            pltpu.VMEM((width, units), bf16),
            pltpu.VMEM((units, width), bf16),
            pltpu.VMEM((slots, units), bf16),
            pltpu.VMEM((slots, units), bf16),
            pltpu.VMEM(block, bf16),
            pltpu.VMEM((step, width), f32),
            pltpu.VMEM((step, width), f32),
            pltpu.VMEM((2, width // 4, units), bf16),
            pltpu.VMEM((2, units // 4, width), bf16),
            pltpu.VMEM((width, 128), bf16),
            pltpu.SemaphoreType.DMA((2, wide_n)),
            pltpu.SemaphoreType.DMA((2, wide_n)),
            pltpu.SemaphoreType.DMA((6,)),
            pltpu.SemaphoreType.DMA((2, 7)),
        ],
        compiler_params=params(collective_id=2, has_side_effects=True),
        name="experts",
    )(routed, slot_row, wr, cot_rows, win, wout)


def link(src, dst, send_sem, recv_sem, axis, peer):
    return pltpu.make_async_remote_copy(
        src_ref=src,
        dst_ref=dst,
        send_sem=send_sem,
        recv_sem=recv_sem,
        device_id={axis: peer},
        device_id_type=MESH,
    )


def padded(v):
    return -(-v // 16) * 16


class Sums:
    REFS = 7

    def __init__(self, wide_n, refs, sems):
        self.terms, self.near, self.mine, self.half_in, self.piece_in, self.cross_in, self.whole = refs
        self.narrow_sem, self.y_sem, self.z_sem = sems
        self.wide_n = wide_n
        self.n, self.w = lax.axis_index("narrow"), lax.axis_index("wide")
        self.core, self.side = self.n % 2, self.n // 2
        self.direct = self.mine.shape[0] == 1
        self.bit = 0 if self.direct else self.w % 2
        self.rank = self.w if self.direct else self.w // 2
        self.ranks = self.piece_in.shape[0]
        _, self.blocks, self.rows, _ = self.terms.shape
        self.piece = self.piece_in.shape[2]
        self.span = self.ranks * self.piece

    def near_copy(self, side):
        return link(
            self.terms.at[2 * side + 1 - self.core], self.near.at[side],
            self.narrow_sem.at[0, side], self.narrow_sem.at[1, side],
            "narrow", flipped(self.n, 1, 4),
        )

    def cross_copy(self):
        if self.direct:
            source = self.terms.at[2 * (1 - self.side) + self.core]
        else:
            source = self.mine.at[1 - self.side, self.piece_at(self.rank)]
        return link(
            source, self.cross_in,
            self.narrow_sem.at[0, 2], self.narrow_sem.at[1, 2], "narrow", flipped(self.n, 2, 4),
        )

    def half_at(self, bit):
        return pl.ds(pl.multiple_of(bit * self.span, 16), self.span)

    def piece_at(self, rank):
        return pl.ds(pl.multiple_of(self.bit * self.span + rank * self.piece, 16), self.piece)

    def half_copy(self):
        return link(
            self.mine.at[:, self.half_at(1 - self.bit)], self.half_in, self.y_sem.at[0, 0],
            self.y_sem.at[1, 0], "wide", flipped(self.w, 1, self.wide_n),
        )

    def piece_copy(self, k):
        peer = flipped(self.rank, k, self.ranks)
        return link(
            self.mine.at[:, self.piece_at(peer)], self.piece_in.at[k], self.z_sem.at[0, 0, k],
            self.z_sem.at[1, 0, k], "wide", peer if self.direct else 2 * peer + self.bit,
        )

    def piece_back(self, k):
        peer = flipped(self.rank, k, self.ranks)
        at = self.piece_at(self.rank)
        return link(
            self.whole.at[at], self.whole.at[at], self.z_sem.at[0, 1, k],
            self.z_sem.at[1, 1, k], "wide", peer if self.direct else 2 * peer + self.bit,
        )

    def half_back(self):
        at = self.half_at(self.bit)
        return link(
            self.whole.at[at], self.whole.at[at], self.y_sem.at[0, 1], self.y_sem.at[1, 1],
            "wide", flipped(self.w, 1, self.wide_n),
        )

    def each(self, f):
        def step(k, carry):
            f(k)
            return carry

        lax.fori_loop(1, self.ranks, step, 0)

    def start(self):
        for side in (0, 1):
            self.near_copy(side).start()

    def near_total(self, side):
        self.near_copy(side).wait()
        return self.terms[2 * side + self.core].astype(f32) + self.near[side].astype(f32)

    def place(self, i, total):
        rows = self.blocks * self.rows // 2
        total = total.astype(bf16).reshape(2 * rows, 128)
        if self.direct:
            self.mine[i, : 2 * rows] = total
            return
        self.mine[i, 0:rows] = total[:rows]
        self.mine[i, self.span : self.span + rows] = total[rows:]

    def to_far(self):
        total = self.near_total(1 - self.side)
        self.terms[2 * (1 - self.side) + self.core] = total.astype(bf16)
        self.cross_copy().start()

    def to_half(self):
        if self.direct:
            total = self.near_total(self.side)
            self.cross_copy().wait()
            self.place(0, total + self.cross_in[...].astype(f32))
            self.each(lambda k: self.piece_copy(k).start())
        else:
            for side in (0, 1):
                self.place(side, self.near_total(side))
            self.half_copy().start()

    def to_piece(self):
        self.half_copy().wait()
        at = self.half_at(self.bit)
        total = self.mine[:, at].astype(f32) + self.half_in[...].astype(f32)
        self.mine[:, at] = total.astype(bf16)
        self.each(lambda k: self.piece_copy(k).start())

    def pieces_total(self):
        self.each(lambda k: self.piece_copy(k).wait())

        def add(k, total):
            return total + self.piece_in[k].astype(f32)

        at = self.piece_at(self.rank)
        return lax.fori_loop(1, self.ranks, add, self.mine[:, at].astype(f32))

    def to_cross(self):
        self.mine[:, self.piece_at(self.rank)] = self.pieces_total().astype(bf16)
        self.cross_copy().start()

    def back_piece(self):
        at = self.piece_at(self.rank)
        if self.direct:
            total = self.pieces_total()[0]
        else:
            self.cross_copy().wait()
            total = self.mine[self.side, at].astype(f32) + self.cross_in[...].astype(f32)
        self.whole[at] = total.astype(bf16)
        self.each(lambda k: self.piece_back(k).start())

    def back_half(self):
        self.each(lambda k: self.piece_back(k).wait())
        self.half_back().start()

    def finish(self):
        if self.direct:
            self.each(lambda k: self.piece_back(k).wait())
        else:
            self.half_back().wait()

    def block(self, b):
        half = self.blocks * self.rows // 2
        first, last = b * self.rows, (b + 1) * self.rows
        if self.direct:
            return self.whole[first:last, :].astype(f32)
        pieces = []
        if first < half:
            pieces.append(self.whole[first : min(last, half), :])
        if last > half:
            at = self.span - half
            pieces.append(self.whole[at + max(first, half) : at + last, :])
        pieces = [piece.astype(f32) for piece in pieces]
        return pieces[0] if len(pieces) == 1 else jnp.concatenate(pieces, axis=0)

    @staticmethod
    def scratch(blocks, rows, wide_n, slices):
        ranks, halves = (wide_n, 1) if slices == 1 else (wide_n // 2, 2)
        piece = padded(-(-blocks * rows // (halves * ranks)))
        return [
            pltpu.VMEM((4, blocks, rows, 128), bf16),
            pltpu.VMEM((2, blocks, rows, 128), bf16),
            pltpu.VMEM((slices, halves * ranks * piece, 128), bf16),
            pltpu.VMEM((slices, 16 if slices == 1 else ranks * piece, 128), bf16),
            pltpu.VMEM((ranks, slices, piece, 128), bf16),
            pltpu.VMEM((blocks, rows, 128) if slices == 1 else (piece, 128), bf16),
            pltpu.VMEM((halves * ranks * piece, 128), bf16),
        ], [
            pltpu.SemaphoreType.DMA((2, 3)),
            pltpu.SemaphoreType.DMA((2, 2)),
            pltpu.SemaphoreType.DMA((2, 2, ranks)),
        ]


GROUPS = ((0, 6), (0, 3), (3, 5), (5, 6))


def backward_kernel(
    wide_n, experts, back_any, slot_ref, hid_any, cot_any, att_any, attseq_any, p_any, invl_any,
    q_any, k_any, v_any, tok_any, res_any, wo_ref, wq_ref, wk_ref, wv_ref, gain_a_ref, gain_e_ref,
    router_ref, hot_ref, gin_any, gout_any,
    out_any, igrad_any, big_any, small_any, resland_any, ginfar_any, goutfar_any,
    back_ref, hid_ref, cot_ref, attseq_ref, invl_ref, q_ref, k_ref, v_ref, tok_ref,
    agsend, agbuf, partbuf, turned_ref, dk_ref, dv_ref, pbuf, acc_ref, diag_ref,
    kmask_ref, vext_ref, ds_ref, gains_ref, smallout, loadsem, psem, agsem, partsem,
    ressem, gradsem, *rest,
):
    parts, seqs, span, width = tok_ref.shape
    total = parts * span
    block_rows = seqs * span
    pairs = width // 128
    slots = back_ref.shape[0] * back_ref.shape[1]
    rows_n = width // parts
    n, w = lax.axis_index("narrow"), lax.axis_index("wide")
    count = len(GROUPS)
    per = Sums.REFS
    group = [
        Sums(
            wide_n,
            rest[per * i : per * i + per],
            rest[per * count + 3 * i : per * count + 3 * i + 3],
        )
        for i in range(count)
    ]
    folds = 4 if experts <= 16 else 1
    fold_rows = rows_n // folds
    gain_lane = 30 if folds == 4 else 126
    small_terms, small_near, small_mine, small_in, small_sem, small_wide_sem = rest[
        per * count + 3 * count :
    ]

    def small_copy(k):
        peer = flipped(n, k, parts)
        return remote(small_terms.at[peer], small_near.at[k], small_sem, k, "narrow", peer)

    def small_wide(k):
        peer = flipped(w, k, wide_n)
        return remote(small_mine, small_in.at[k], small_wide_sem, k, "wide", peer)

    loads = [
        pltpu.make_async_copy(a, b, loadsem.at[i])
        for i, (a, b) in enumerate(
            (
                (back_any, back_ref), (hid_any, hid_ref), (cot_any, cot_ref), (att_any, k_ref),
                (attseq_any, attseq_ref), (invl_any, invl_ref), (q_any, q_ref), (v_any, v_ref),
                (tok_any, tok_ref),
            )
        )
    ]
    for copy in loads:
        copy.start()

    def block_of(phase):
        return n // 2 + phase * (1 - 2 * (n // 2))

    def step_of(i):
        late = i // 8
        phase = (1 - late) * (i // 4) + late * (i % 2)
        return phase, (1 - late) * (i % 4) + late * (i // 2)

    def p_copy(i):
        phase, pair = step_of(i)
        at = pl.ds(pl.multiple_of(block_of(phase) * 2 * span, 2 * span), 2 * span)
        return pltpu.make_async_copy(p_any.at[pair, :, at], pbuf.at[i % 2], psem.at[i % 2])

    grad_copies = [
        link(a, b, gradsem.at[0, i], gradsem.at[1, i], "narrow", flipped(n, 2, parts))
        for i, (a, b) in enumerate(((gin_any, ginfar_any), (gout_any, goutfar_any)))
    ]
    p_copy(0).start()
    enter(parts, wide_n)

    def res_copy(k):
        return remote(
            res_any.at[k], resland_any.at[w], ressem, k, "wide", flipped(w, k, wide_n)
        )

    def res_start(k, carry):
        res_copy(k).start()
        return carry

    lax.fori_loop(1, wide_n, res_start, 0)
    res_own = pltpu.make_async_copy(res_any.at[0], resland_any.at[w], loadsem.at[10])
    res_own.start()

    def ag_copy(k):
        peer = flipped(n, k, parts)
        return remote(agsend.at[peer], agbuf.at[n], agsem, k, "narrow", peer)

    def rows_of(src):
        return pl.ds(pl.multiple_of(src * block_rows, block_rows), block_rows)

    def picked(rows):
        ids = lax.broadcasted_iota(jnp.int32, (block_rows, slots), 1)
        pick = (ids == slot_ref[rows, :]).astype(f32).astype(bf16)
        return dot(pick, back_ref[...].reshape(slots, width))

    gain_a = gain_a_ref[...].astype(f32).reshape(1, width)
    gain_e = gain_e_ref[...].astype(f32).reshape(1, width)
    gains_ref[...] = jnp.zeros_like(gains_ref)
    for copy in loads[:3]:
        copy.wait()
    for k in range(parts - 1, -1, -1):
        src = flipped(n, k, parts)
        rows = rows_of(src)
        upstream = picked(rows)
        hidden = hid_ref[rows, :]
        inv = inverse_rms(hidden)
        scaled = upstream * gain_e
        inner = jnp.mean(scaled * hidden, axis=-1, keepdims=True)
        grad = cot_ref[rows, :].astype(f32) + inv * scaled - hidden * (inv * inv * inv * inner)
        gains_ref[1:2, :] += jnp.sum(upstream * hidden * inv, axis=0, keepdims=True)
        hid_ref[rows, :] = grad
        grad = grad.astype(bf16)
        cot_ref[rows, :] = grad
        grad = dot(grad, wo_ref[...], NT).astype(bf16).reshape(seqs, span, width)
        if k > 0:
            agsend[src] = grad
            ag_copy(k).start()
        else:
            agbuf[src] = grad
    for copy in grad_copies:
        copy.start()
    loads[3].wait()
    for h in range(2):
        cols = slice(h * 2 * rows_n, (h + 1) * 2 * rows_n)
        grad = dot(k_ref[...].reshape(parts * block_rows, width)[:, cols], cot_ref[...], TN)
        grad = grad.astype(bf16)
        for t in range(2):
            for b in range(pairs):
                group[0].terms[2 * h + t, b] = grad[
                    t * rows_n : (t + 1) * rows_n, b * 128 : (b + 1) * 128
                ]
    k_copy = pltpu.make_async_copy(k_any, k_ref, loadsem.at[9])
    k_copy.start()
    group[0].start()
    for copy in loads[4:]:
        copy.wait()
    for b in range(parts):
        x = tok_ref[b].reshape(block_rows, width).astype(f32)
        normed = x * inverse_rms(x) * gain_a
        turned_ref[:, b * block_rows : (b + 1) * block_rows] = normed.T.astype(bf16)
    diag_ref[...] = jnp.zeros_like(diag_ref)

    low, masks = half_masks(128)
    lane = lax.broadcasted_iota(jnp.int32, (1, 128), 1)
    strip = (parts + 2) * span

    def attention_pair(phase, pair, i):
        slot = i % 2
        block = block_of(phase)
        both = pl.ds(2 * block, 2)
        lanes = pl.ds(pl.multiple_of(pair * 128, 128), 128)
        p_copy(i).wait()

        @pl.when(i + 1 < 2 * pairs)
        def _():
            p_copy(i + 1).start()

        for s in range(seqs):
            kp = k_ref[:, s, :, lanes].reshape(total, 128)
            vp = v_ref[:, s, :, lanes].reshape(total, 128)
            for hh in range(2):
                ones = (lane // 2 == 32 - 32 * hh).astype(f32)
                kmask_ref[hh * total : (hh + 1) * total, :] = kp * masks[hh]
                vext_ref[hh] = jnp.where(ones > 0, ones, vp.astype(f32)).astype(bf16)
            dk = [0.0, 0.0]
            dv = [0.0, 0.0]
            qp = q_ref[both, s, :, lanes].reshape(2 * span, 128)
            inv = invl_ref[both, s, :, lanes].reshape(2 * span, 128).astype(f32)
            gp = agbuf[both, s, :, lanes].reshape(2 * span, 128).astype(f32)
            gp = (gp * inv).astype(bf16)
            gf = gp.astype(f32)
            agree = gf * attseq_ref[both, s, :, lanes].reshape(2 * span, 128).astype(f32)
            for hh in range(2):
                side = low if hh == 0 else ~low
                delta = -jnp.sum(jnp.where(side, agree, 0.0), axis=-1, keepdims=True)
                high = delta.astype(bf16).astype(f32)
                ext = jnp.where(lane == 64 - 64 * hh, high, 0.0)
                ext = jnp.where(lane == 65 - 64 * hh, delta - high, ext)
                ext = jnp.where(side, gf, ext).astype(bf16)
                raised = pbuf[slot, s, :, hh * total : (hh + 1) * total]
                score_grad = raised.astype(f32) * dot(ext, vext_ref[hh], NT)
                if s == 0:
                    acc_ref[hh] = score_grad
                else:
                    acc_ref[hh] += score_grad
                score_grad = score_grad.astype(bf16)
                ds_ref[:, hh * total : (hh + 1) * total] = score_grad
                dk[hh] = dot(score_grad, qp, TN)
                dv[hh] = dot(raised, gp, TN)
            dq = dot(ds_ref[...], kmask_ref[...])
            q_ref[both, s, :, lanes] = dq.astype(bf16).reshape(2, span, 128)
            dk = jnp.where(low, dk[0], dk[1]) * (1.0 / LOG2E)
            dv = jnp.where(low, dv[0], dv[1])
            here = slice(s * total, (s + 1) * total)
            if phase == 0:
                dk_ref[here, lanes] = dk
                dv_ref[here, lanes] = dv
            else:
                dk = dk + dk_ref[here, lanes]
                dv = dv + dv_ref[here, lanes]
                k_ref[:, s, :, lanes] = dk.astype(bf16).reshape(parts, span, 128)
                v_ref[:, s, :, lanes] = dv.astype(bf16).reshape(parts, span, 128)
        base = pl.multiple_of((parts - 2 - 2 * block) * span, span)
        for hh in range(2):
            upper, lower = acc_ref[hh, :span, :], acc_ref[hh, span:, :]
            zero = jnp.zeros((span, span), f32)
            upper = jnp.concatenate([zero, upper, zero], axis=1)
            lower = jnp.concatenate([lower, zero, zero], axis=1)
            both_rows = upper + lower
            small_sum = jnp.zeros((8, strip), f32)
            for a in range(span // 8):
                shift = span - 8 - 8 * a
                rows8 = both_rows[8 * a : 8 * a + 8]
                small_sum += rows8 if shift == 0 else pltpu.roll(rows8, shift, 1)
            line = small_sum[7:8]
            for a in range(7):
                line = line + pltpu.roll(small_sum[a : a + 1], 7 - a, 1)
            diag_ref[pl.ds(gain_lane - 14 + 2 * pair + hh, 1), pl.ds(base, strip)] += line

    k_copy.wait()
    ag_copy(1).wait_recv()

    def weight_group(g):
        first, last = GROUPS[g]
        cols = slice(first * 128, last * 128)
        size = last - first
        for i, ref in enumerate((q_ref, k_ref, v_ref)):
            field = ref[:, :, :, cols].reshape(parts * block_rows, size * 128)
            grad = dot(turned_ref[...], field).astype(bf16)
            for part in range(parts):
                for t in range(size):
                    group[g].terms[part, size * i + t] = grad[
                        part * rows_n : (part + 1) * rows_n, t * 128 : (t + 1) * 128
                    ]
        group[g].start()

    hooks = {
        1: [group[0].to_half],
        6: [lambda: weight_group(1)],
        7: [group[1].to_half, group[0].to_piece],
        9: [lambda: weight_group(2)],
        10: [group[2].to_half, group[1].to_piece],
    }

    def attention_step(i, carry):
        phase, pair = step_of(i)

        @pl.when(i == 4)
        def _():
            for k in range(2, parts):
                ag_copy(k).wait_recv()

        for which in range(2):

            @pl.when(phase == which)
            def _(which=which):
                attention_pair(which, pair, i)

        for at, calls in hooks.items():

            @pl.when(i == at)
            def _(calls=calls):
                for call in calls:
                    call()

        return carry

    lax.fori_loop(0, 2 * pairs, attention_step, 0)
    weight_group(3)
    group[0].to_cross()

    def part_copy(k):
        peer = flipped(n, k, parts)
        return remote(agsend.at[peer], partbuf.at[n], partsem, k, "narrow", peer)

    for k in range(1, parts):
        ag_copy(k).wait_send()
    for k in (0, 3, 1, 2):
        src = flipped(n, k, parts)
        x = tok_ref[src].reshape(block_rows, width).astype(f32)
        inv = inverse_rms(x)
        upstream = dot(q_ref[src].reshape(block_rows, width), wq_ref[...], NT)
        upstream += dot(k_ref[src].reshape(block_rows, width), wk_ref[...], NT)
        upstream += dot(v_ref[src].reshape(block_rows, width), wv_ref[...], NT)
        scaled = upstream * gain_a
        inner = jnp.mean(scaled * x, axis=-1, keepdims=True)
        grad = inv * scaled - x * (inv * inv * inv * inner)
        gains_ref[0:1, :] += jnp.sum(upstream * x * inv, axis=0, keepdims=True)
        grad = grad.astype(bf16).reshape(seqs, span, width)
        if k > 0:
            agsend[src] = grad
        else:
            partbuf[src] = grad
        if k == 0:
            group[3].to_far()
        if k in (1, 3):
            part_copy(k).start()
        if k == 3:
            group[2].to_piece()
        if k == 1:
            group[3].to_half()
            group[1].to_cross()

    pack = router_ref[...]
    for i in range(2):
        column = jnp.broadcast_to(gains_ref[i : i + 1, :], (128, width)).T
        pack = pack + jnp.where(lane == gain_lane + i, column, 0.0)
    relative = lax.dot_general(
        hot_ref[...].astype(f32), diag_ref[...], NT,
        precision=lax.Precision.HIGHEST, preferred_element_type=f32,
    )
    share = relative.shape[0] // parts
    for part in range(parts):
        slab = pack[part * rows_n : (part + 1) * rows_n]
        head = slab[:share] + relative[part * share : (part + 1) * share]
        slab = jnp.concatenate([head, slab[share:]], axis=0)
        folded = slab[:fold_rows]
        for fold in range(1, folds):
            folded += pltpu.roll(slab[fold * fold_rows : (fold + 1) * fold_rows], 32 * fold, 1)
        small_terms[part] = folded.astype(bf16)
    for k in range(1, parts):
        small_copy(k).start()
    part_copy(2).start()
    group[2].to_cross()
    group[0].back_piece()
    total = small_terms[n].astype(f32)
    for k in range(1, parts):
        small_copy(k).wait()
        total += small_near[k].astype(f32)
    small_mine[...] = total.astype(bf16)

    def small_send(k, carry):
        small_wide(k).start()
        return carry

    lax.fori_loop(1, wide_n, small_send, 0)

    res_own.wait()

    def res_wait(k, carry):
        res_copy(k).wait()
        return carry

    lax.fori_loop(1, wide_n, res_wait, 0)
    again = [
        pltpu.make_async_copy(resland_any, back_ref, loadsem.at[0]),
        pltpu.make_async_copy(hid_any, dk_ref, loadsem.at[1]),
    ]
    for copy in again:
        copy.start()
    group[3].back_piece()
    group[1].back_piece()
    for copy in again:
        copy.wait()
    outs = []
    for b in range(parts):
        rows = pl.ds(b * block_rows, block_rows)
        dk_ref[rows, :] += picked(rows)
        copy = pltpu.make_async_copy(dk_ref.at[rows], out_any.at[rows], loadsem.at[2 + b])
        copy.start()
        outs.append(copy)
        if b == 0:
            group[2].back_piece()
        if b == 1:
            group[0].back_half()
        if b == 2:
            group[1].back_half()
    group[2].back_half()
    for k in (0, 1, 3, 2):
        src = flipped(n, k, parts)
        rows = rows_of(src)
        if k > 0:
            part_copy(k).wait()
        hid_ref[rows, :] += partbuf[src].reshape(block_rows, width).astype(f32)
        copy = pltpu.make_async_copy(hid_ref.at[rows], igrad_any.at[rows], loadsem.at[6 + k])
        copy.start()
        outs.append(copy)
    for g in range(4):
        group[g].finish()
        first, last = GROUPS[g]
        size = last - first
        for b in range(group[g].blocks):
            i, at = (3, b) if g == 0 else (b // size, first + b % size)
            dv_ref[i * rows_n : (i + 1) * rows_n, at * 128 : (at + 1) * 128] = group[g].block(b)
    total = small_mine[...].astype(f32)
    for k in range(1, wide_n):
        small_wide(k).wait()
        total += small_in[k].astype(f32)
    for fold in range(folds):
        part = total if fold == 0 else pltpu.roll(total, 128 - 32 * fold, 1)
        smallout[fold * fold_rows : (fold + 1) * fold_rows, :] = part
    for copy in grad_copies:
        copy.wait()
    for a, b, i in ((dv_ref.at[: 4 * rows_n], big_any, 11), (smallout, small_any, 12)):
        copy = pltpu.make_async_copy(a, b, loadsem.at[i])
        copy.start()
        outs.append(copy)
    for copy in outs:
        copy.wait()


def backward(args, wide_n, experts, quad, slots_shape, table):
    parts, seqs, span, width = quad
    total, tokens = parts * span, parts * seqs * span
    rows_n = width // parts
    fold_rows = rows_n // (4 if experts <= 16 else 1)
    square = pltpu.VMEM((tokens, width), f32)
    sums = [
        Sums.scratch(
            (1 if g == 0 else 3) * (last - first), rows_n, wide_n, 1 if g == 3 else 2
        )
        for g, (first, last) in enumerate(GROUPS)
    ]
    return pl.pallas_call(
        functools.partial(backward_kernel, wide_n, experts),
        in_specs=[hbm(), vmem()] + [hbm()] * 11 + [vmem()] * 8 + [hbm()] * 2,
        out_specs=[hbm()] * 7,
        out_shape=[
            jax.ShapeDtypeStruct((tokens, width), f32),
            jax.ShapeDtypeStruct((tokens, width), f32),
            jax.ShapeDtypeStruct((4 * rows_n, width), f32),
            jax.ShapeDtypeStruct((rows_n, 128), f32),
            jax.ShapeDtypeStruct(slots_shape, bf16),
            jax.ShapeDtypeStruct(args[-2].shape, bf16),
            jax.ShapeDtypeStruct(args[-1].shape, bf16),
        ],
        scratch_shapes=[
            pltpu.VMEM(slots_shape, bf16),
            square,
            pltpu.VMEM((tokens, width), bf16),
            pltpu.VMEM(quad, bf16),
            pltpu.VMEM(quad, bf16),
            pltpu.VMEM(quad, bf16),
            pltpu.VMEM(quad, bf16),
            pltpu.VMEM(quad, bf16),
            pltpu.VMEM(quad, bf16),
            pltpu.VMEM(quad, bf16),
            pltpu.VMEM(quad, bf16),
            pltpu.VMEM(quad, bf16),
            pltpu.VMEM((width, tokens), bf16),
            square,
            square,
            pltpu.VMEM((2, seqs, 2 * span, 2 * total), bf16),
            pltpu.VMEM((2, 2 * span, total), f32),
            pltpu.VMEM((128, table), f32),
            pltpu.VMEM((2 * total, 128), bf16),
            pltpu.VMEM((2, total, 128), bf16),
            pltpu.VMEM((2 * span, 2 * total), bf16),
            pltpu.VMEM((8, width), f32),
            pltpu.VMEM((rows_n, 128), f32),
            pltpu.SemaphoreType.DMA((13,)),
            pltpu.SemaphoreType.DMA((2,)),
            pltpu.SemaphoreType.DMA((2, parts)),
            pltpu.SemaphoreType.DMA((2, parts)),
            pltpu.SemaphoreType.DMA((2, wide_n)),
            pltpu.SemaphoreType.DMA((2, 2)),
        ]
        + [ref for refs, _ in sums for ref in refs]
        + [sem for _, sems in sums for sem in sems]
        + [
            pltpu.VMEM((parts, fold_rows, 128), bf16),
            pltpu.VMEM((parts, fold_rows, 128), bf16),
            pltpu.VMEM((fold_rows, 128), bf16),
            pltpu.VMEM((wide_n, fold_rows, 128), bf16),
            pltpu.SemaphoreType.DMA((2, parts)),
            pltpu.SemaphoreType.DMA((2, wide_n)),
        ],
        compiler_params=params(collective_id=3, has_side_effects=True),
        name="backward",
    )(*args)


def body(
    tokens, lengths, routes, bucket_table, attn_gain, query_weight, key_weight, value_weight,
    output_weight, relative_bias, expert_gain, router_weight, experts_in, experts_out, cotangent,
):
    seq_count, span, width = tokens.shape
    narrow_n = lax.axis_size("narrow")
    wide_n = lax.axis_size("wide")
    seqs = seq_count // narrow_n
    heads = relative_bias.shape[1]
    buckets = relative_bias.shape[0]
    experts = router_weight.shape[1]
    tok_count = seq_count * span
    capacity = 5 * tok_count // (4 * experts)
    cap = -(-capacity // 16) * 16
    table = 2 * span * narrow_n
    flat_cot = cotangent.reshape(tok_count, width)
    tok_quad = tokens.reshape(narrow_n, seqs, span, width)
    (
        tok_seq, att_seq, att_pos, hidden, routed, cot_rows, q, k, v, invl, probs,
        slot_row, slot_col, offset_hot,
    ) = forward(
        (
            lengths, tok_quad, flat_cot, routes.reshape(seq_count, span), bucket_table,
            relative_bias, attn_gain, expert_gain,
            query_weight, key_weight, value_weight, output_weight,
        ),
        wide_n, capacity, cap, tok_quad.shape, table,
    )
    res, back_rows, gin, gin_early, gin_send, gout, gout_send, router_grad = run_experts(
        routed, slot_row, router_weight, cot_rows, experts_in[0], experts_out[0], experts
    )
    layer_output, input_grad, big, small, _, gin_late, gout_far = backward(
        (
            back_rows, slot_col, hidden, flat_cot, att_pos, att_seq, probs, invl, q, k, v, tok_seq,
            res, output_weight, query_weight, key_weight, value_weight, attn_gain, expert_gain,
            router_grad, offset_hot, gin_send, gout_send,
        ),
        wide_n, experts, tok_quad.shape, res.shape, table,
    )

    gain_lane = 30 if experts <= 16 else 126
    return (
        layer_output.reshape(seq_count, span, width),
        input_grad.reshape(seq_count, span, width),
        small[:, gain_lane],
        *big.reshape(narrow_n, -1, width),
        small[: buckets // narrow_n, gain_lane - 14 : gain_lane - 14 + heads],
        small[:, gain_lane + 1],
        small[:, :experts],
        (gin.astype(f32) + jnp.concatenate([gin_early, gin_late], axis=1).astype(f32))[None],
        (gout.astype(f32) + gout_far.astype(f32))[None],
    )


def solution(mesh):
    token = P("wide", "narrow", None)
    expert = P("wide", None, None)
    row, vector = P("narrow", None), P("narrow")
    return jax.shard_map(
        body,
        mesh=mesh,
        in_specs=(token, P("wide"), token) + (P(),) * 9 + (expert, expert, token),
        out_specs=(
            token, token, vector, row, row, row, row, row, vector, row,
            P("wide", "narrow", None), P("wide", "narrow", None),
        ),
        check_vma=False,
    )
```

```python
import functools

import jax
import jax.numpy as jnp
from jax import lax
from jax.experimental import pallas as pl
from jax.experimental.pallas import tpu as pltpu
from jax.sharding import PartitionSpec as P

f32, bf16 = jnp.float32, jnp.bfloat16
epsilon = 1e-06
VMEM_BYTES = 62 * 1024 * 1024
NN = (((1,), (0,)), ((), ()))
NT = (((1,), (1,)), ((), ()))
TN = (((0,), (0,)), ((), ()))


def dot(a, b, dims=NN):
    return lax.dot_general(a, b, dims, preferred_element_type=f32)


def vmem():
    return pl.BlockSpec(memory_space=pltpu.VMEM)


def params(**kw):
    return pltpu.CompilerParams(vmem_limit_bytes=VMEM_BYTES, **kw)


def inverse_rms(field):
    return lax.rsqrt(jnp.mean(field * field, axis=-1, keepdims=True) + epsilon)


def half_masks(pair_width):
    lane = lax.broadcasted_iota(jnp.int32, (1, pair_width), 1)
    low = lane < pair_width // 2
    return low, (low.astype(f32).astype(bf16), (~low).astype(f32).astype(bf16))


MESH = pl.DeviceIdType.MESH
LOG2E = 1.4426950408889634


def hbm():
    return pl.BlockSpec(memory_space=pl.ANY)


def flipped(me, k, size):
    out, bit = me, 1
    while bit < size:
        out = out + ((k // bit) % 2) * (bit - 2 * bit * ((me // bit) % 2))
        bit *= 2
    return out


def remote(src, dst, sems, k, axis, peer):
    return pltpu.make_async_remote_copy(
        src_ref=src,
        dst_ref=dst,
        send_sem=sems.at[0, k],
        recv_sem=sems.at[1, k],
        device_id={axis: peer},
        device_id_type=MESH,
    )


def greet(narrow_n, wide_n):
    barrier = pltpu.get_barrier_semaphore()
    count = 0
    for axis, size in (("narrow", narrow_n), ("wide", wide_n)):
        if size > 1:
            me = lax.axis_index(axis)

            def greet(k, carry, axis=axis, size=size, me=me):
                pl.semaphore_signal(
                    barrier, inc=1, device_id={axis: flipped(me, k, size)}, device_id_type=MESH
                )
                return carry

            lax.fori_loop(1, size, greet, 0)
            count += size - 1
    return count


def enter(narrow_n, wide_n):
    count = greet(narrow_n, wide_n)
    pl.semaphore_wait(pltpu.get_barrier_semaphore(), count)


def expert_pick(expert, cap, slot_row):
    ids = lax.broadcasted_iota(jnp.int32, (cap, slot_row.shape[1]), 0) + expert * cap
    return (ids == slot_row).astype(f32).astype(bf16)


def token_slots(routes_ref, column_ref, experts, capacity, cap):
    seqs, span = routes_ref.shape
    routes = routes_ref[...]
    hot = jnp.concatenate([(routes == e).astype(f32) for e in range(experts)], axis=0)
    row = lax.broadcasted_iota(jnp.int32, (span, span), 0)
    ahead = (row < lax.broadcasted_iota(jnp.int32, (span, span), 1)).astype(f32).astype(bf16)
    size = experts * seqs
    row = lax.broadcasted_iota(jnp.int32, (size, size), 0)
    col = lax.broadcasted_iota(jnp.int32, (size, size), 1)
    above = ((row // seqs == col // seqs) & (col < row)).astype(f32).astype(bf16)
    counts = jnp.broadcast_to(jnp.sum(hot, axis=-1, keepdims=True), hot.shape).astype(bf16)
    position = dot(hot.astype(bf16), ahead) + dot(above, counts)
    slot = jnp.zeros((seqs, span), f32)
    for e in range(experts):
        here = position[e * seqs : (e + 1) * seqs]
        here = jnp.where(here < capacity, here + e * cap, experts * cap)
        slot = slot + hot[e * seqs : (e + 1) * seqs] * here
    turned = jnp.concatenate([slot] * (span // seqs), axis=0).T
    for s in range(seqs):
        column_ref[s * span : (s + 1) * span, :] = turned[:, s : s + 1].astype(jnp.int32)
    return jnp.concatenate([slot[s : s + 1] for s in range(seqs)], axis=1).astype(jnp.int32)


def forward_kernel(
    wide_n, capacity, lens_ref, tok_any, cot_ref, routes_ref, table_ref, bias_ref, gain_a_ref, gain_e_ref,
    wq_ref, wk_ref, wv_ref, wo_ref,
    tokseq_any, attseq_any, att_any, hid_any, routed_any, cotrows_any, q_any, k_any, v_any, invl_any, p_any,
    slot_row_ref, slot_col_ref, hot_ref,
    tokbuf, tokpos, q_ref, k_ref, v_ref, invl_ref, attseq, attpos, hid_ref, routed_ref, cotsend,
    strip_ref, pbuf, vext, kext, diag_ref, toksem, attsem, cotsem, psem, outsem,
):
    parts, seqs, span, width = tokbuf.shape
    total = parts * span
    heads = bias_ref.shape[1]
    pairs, table = heads // 2, diag_ref.shape[1]
    cap = cotsend.shape[1]
    n = lax.axis_index("narrow")
    w = lax.axis_index("wide")
    own = pltpu.make_async_copy(tok_any.at[n], tokbuf.at[n], outsem.at[0])
    own.start()
    position = pltpu.make_async_copy(tok_any, tokpos, outsem.at[1])
    position.start()
    expected = greet(parts, wide_n)
    slot_row_ref[...] = token_slots(routes_ref, slot_col_ref, wide_n, capacity, cap)

    def cot_block(k):
        pick = expert_pick(flipped(w, k, wide_n), cap, slot_row_ref[...])
        cotsend[k] = dot(pick, cot_ref[...]).astype(bf16)

    def cot_early(k, carry):
        cot_block(k)
        return carry

    lax.fori_loop(wide_n // 2, wide_n, cot_early, 0)
    pl.semaphore_wait(pltpu.get_barrier_semaphore(), expected)

    def tok_copy(k):
        peer = flipped(n, k, parts)
        return remote(tok_any.at[peer], tokbuf.at[n], toksem, k, "narrow", peer)

    for k in range(parts - 1, 0, -1):
        tok_copy(k).start()

    def cot_copy(k):
        peer = flipped(w, k, wide_n)
        return remote(cotsend.at[k], cotrows_any.at[k], cotsem, k, "wide", peer)

    def cot_start(k, carry):
        cot_copy(k).start()
        return carry

    def cot_step(k, carry):
        cot_block(k)
        cot_copy(k).start()
        return carry

    lax.fori_loop(wide_n // 2, wide_n, cot_start, 0)
    lax.fori_loop(1, wide_n // 2, cot_step, 0)
    cot_block(0)
    cot_own = pltpu.make_async_copy(cotsend.at[0], cotrows_any.at[0], outsem.at[2])
    cot_own.start()

    gain = gain_a_ref[...].astype(f32).reshape(1, width)
    own.wait()
    for k in range(parts):
        src = flipped(n, k, parts)
        if k > 0:
            tok_copy(k).wait_recv()
        x = tokbuf[src].reshape(seqs * span, width).astype(f32)
        normed = (x * inverse_rms(x) * gain).astype(bf16)
        shape = (seqs, span, width)
        q_ref[src] = (dot(normed, wq_ref[...]) * LOG2E).astype(bf16).reshape(shape)
        k_ref[src] = dot(normed, wk_ref[...]).astype(bf16).reshape(shape)
        v_ref[src] = dot(normed, wv_ref[...]).astype(bf16).reshape(shape)
    outs = [
        pltpu.make_async_copy(a, b, outsem.at[i])
        for a, b, i in (
            (tokbuf, tokseq_any, 3), (q_ref, q_any, 4), (k_ref, k_any, 5), (v_ref, v_any, 6),
        )
    ]
    for copy in outs:
        copy.start()

    buckets, offsets = bias_ref.shape[0], table_ref.shape[0]
    ids = lax.broadcasted_iota(jnp.int32, (buckets, offsets), 0)
    found = (ids == table_ref[...].reshape(1, offsets)).astype(f32).astype(bf16)
    hot_ref[...] = jnp.zeros_like(hot_ref)
    hot_ref[:, :offsets] = found
    diag_ref[:heads, :] = dot(bias_ref[...], hot_ref[...], TN) * LOG2E

    low, masks = half_masks(128)
    lane = lax.broadcasted_iota(jnp.int32, (1, 128), 1)
    hot = [(lane == 64).astype(f32).astype(bf16), (lane == 0).astype(f32).astype(bf16)]
    for hh in range(2):
        ones = jnp.broadcast_to(masks[hh], (total, 128))
        vext[hh * total : (hh + 1) * total, 128:] = ones

    def att_copy(k, lanes):
        peer = flipped(n, k, parts)
        return remote(
            attseq.at[peer, :, :, lanes], attpos.at[n, :, :, lanes], attsem, k, "narrow", peer
        )

    def one_pair(pair, carry):
        lanes = pl.ds(pl.multiple_of(pair * 128, 128), 128)
        for hh in range(2):
            row = diag_ref[pl.ds(2 * pair + hh, 1), :]
            strip_ref[hh] = pltpu.roll(
                jnp.broadcast_to(row, (span, table)), table - span + 1, 1, stride=1, stride_axis=0
            )

        def one_sequence(s, inner):
            vp = v_ref[:, s, :, lanes].reshape(total, 128)
            kp = k_ref[:, s, :, lanes].reshape(total, 128).astype(f32)
            ids = lax.broadcasted_iota(jnp.int32, (total, 128), 0)
            push = jnp.where(ids < lens_ref[n * seqs + s], 0.0, -1e30)
            for hh in range(2):
                vext[hh * total : (hh + 1) * total, :128] = vp * masks[hh]
                kext[hh] = jnp.where(lane == 64 - 64 * hh, push, kp).astype(bf16)

            @pl.when(pair > 0)
            def _():
                pltpu.make_async_copy(pbuf.at[s], p_any.at[pair, s], psem.at[s]).wait()

            for block in range(parts // 2):
                rows = slice(block * 2 * span, (block + 1) * 2 * span)
                both = slice(2 * block, 2 * block + 2)
                qp = q_ref[both, s, :, lanes].reshape(2 * span, 128)
                for hh in range(2):
                    bias = jnp.concatenate(
                        [
                            strip_ref[hh, :, (parts - 1 - r) * span : (parts - 1 - r) * span + total]
                            for r in (2 * block, 2 * block + 1)
                        ],
                        axis=0,
                    )
                    scores = dot(qp * masks[hh] + hot[hh], kext[hh], NT) + bias
                    raised = jnp.exp2(scores - jnp.max(scores, axis=-1, keepdims=True))
                    pbuf[s, rows, hh * total : (hh + 1) * total] = raised.astype(bf16)
                mixed = dot(pbuf[s, rows, :], vext[...])
                inv = 1.0 / mixed[:, 128:]
                invl_ref[both, s, :, lanes] = inv.astype(bf16).reshape(2, span, 128)
                attseq[both, s, :, lanes] = (mixed[:, :128] * inv).astype(bf16).reshape(2, span, 128)
            pltpu.make_async_copy(pbuf.at[s], p_any.at[pair, s], psem.at[s]).start()
            return inner

        lax.fori_loop(0, seqs, one_sequence, 0)
        for k in range(parts - 1, 0, -1):
            att_copy(k, lanes).start()
        return carry

    lax.fori_loop(0, pairs, one_pair, 0)
    copy = pltpu.make_async_copy(invl_ref, invl_any, outsem.at[7])
    copy.start()
    outs.append(copy)
    position.wait()
    gain = gain_e_ref[...].astype(f32).reshape(1, width)
    for k in range(parts):
        src = flipped(n, k, parts)
        if k > 0:
            att_copy(k, slice(None)).wait_recv()
            att = attpos[src].reshape(seqs * span, width)
        else:
            attpos[src] = attseq[src]
            att = attseq[src].reshape(seqs * span, width)
        rows = pl.ds(pl.multiple_of(src * seqs * span, seqs * span), seqs * span)
        hidden = tokpos[src].reshape(seqs * span, width).astype(f32) + dot(att, wo_ref[...])
        hid_ref[rows, :] = hidden
        routed_ref[rows, :] = (hidden * inverse_rms(hidden) * gain).astype(bf16)
    for a, b, i in ((attpos, att_any, 8), (hid_ref, hid_any, 9), (routed_ref, routed_any, 10),
                    (attseq, attseq_any, 11)):
        copy = pltpu.make_async_copy(a, b, outsem.at[i])
        copy.start()
        outs.append(copy)
    for k in range(1, parts):
        tok_copy(k).wait_send()
        att_copy(k, slice(None)).wait_send()
    for s in range(seqs):
        pltpu.make_async_copy(pbuf.at[s], p_any.at[0, s], psem.at[s]).wait()
    cot_own.wait()

    def cot_wait(k, carry):
        cot_copy(k).wait()
        return carry

    lax.fori_loop(1, wide_n, cot_wait, 0)
    for copy in outs:
        copy.wait()


def forward(args, wide_n, capacity, cap, quad, table):
    parts, seqs, span, width = quad
    buckets, heads = args[5].shape
    pairs = heads // 2
    total = parts * span
    tokens = parts * seqs * span
    shapes = [
        (quad, bf16), (quad, bf16), (quad, bf16), ((tokens, width), f32), ((tokens, width), bf16),
        ((wide_n, cap, width), bf16), (quad, bf16), (quad, bf16), (quad, bf16), (quad, bf16),
        ((pairs, seqs, total, 2 * total), bf16),
    ]
    small = [((1, tokens), jnp.int32), ((tokens, 1), jnp.int32), ((buckets, table), bf16)]
    return pl.pallas_call(
        functools.partial(forward_kernel, wide_n, capacity),
        in_specs=[pl.BlockSpec(memory_space=pltpu.SMEM), hbm()] + [vmem()] * 10,
        out_specs=[hbm()] * len(shapes) + [vmem()] * 3,
        out_shape=[jax.ShapeDtypeStruct(*item) for item in shapes + small],
        scratch_shapes=[
            pltpu.VMEM(quad, bf16),
            pltpu.VMEM(quad, bf16),
            pltpu.VMEM(quad, bf16),
            pltpu.VMEM(quad, bf16),
            pltpu.VMEM(quad, bf16),
            pltpu.VMEM(quad, bf16),
            pltpu.VMEM(quad, bf16),
            pltpu.VMEM(quad, bf16),
            pltpu.VMEM((tokens, width), f32),
            pltpu.VMEM((tokens, width), bf16),
            pltpu.VMEM((wide_n, cap, width), bf16),
            pltpu.VMEM((2, span, table), f32),
            pltpu.VMEM((seqs, total, 2 * total), bf16),
            pltpu.VMEM((2 * total, 256), bf16),
            pltpu.VMEM((2, total, 128), bf16),
            pltpu.VMEM((16, table), f32),
            pltpu.SemaphoreType.DMA((2, parts)),
            pltpu.SemaphoreType.DMA((2, parts)),
            pltpu.SemaphoreType.DMA((2, wide_n)),
            pltpu.SemaphoreType.DMA((seqs,)),
            pltpu.SemaphoreType.DMA((12,)),
        ],
        compiler_params=params(collective_id=1, has_side_effects=True),
        name="forward",
    )(*args)


def expert_kernel(
    experts, chunks, split, routed_ref, slot_ref, router_ref, cot_any, win_any, wout_any,
    res_any, back_any, gin_any, ginfar_any, ginsend_any, gout_any, goutsend_any, grouter_ref,
    send_ref, recv_ref, cot_ref, push_ref, win_ref, wout_ref, act_ref, pg_ref, res_ref,
    acc_res, acc_back, nearin_ref, nearout_ref, wr_ref, sendsem, backsem, sem, gradsem,
):
    wide_n, cap, width = send_ref.shape
    units = win_ref.shape[1]
    tile = 512
    w = lax.axis_index("wide")
    per = wide_n // chunks
    chunk_rows = per * cap
    loads = [
        pltpu.make_async_copy(a, b, sem.at[i])
        for i, (a, b) in enumerate(((cot_any, cot_ref), (win_any, win_ref), (wout_any, wout_ref)))
    ]
    for copy in loads:
        copy.start()
    enter(4, wide_n)

    def send_copy(k):
        return remote(
            send_ref.at[k], recv_ref.at[k], sendsem, k, "wide", flipped(w, k, wide_n)
        )

    def back_copy(k):
        return remote(
            cot_ref.at[k], back_any.at[w], backsem, k, "wide", flipped(w, k, wide_n)
        )

    def turn(i):
        return (i % 2) * 2 + i // 2

    last = wide_n // 2 - 1
    inner = ((w // 2) % last + last - 1) // last

    def order(i):
        return i + inner * (turn(i) - i)

    def send_step(i, carry):
        k = turn(i // per) * per + i % per
        pick = expert_pick(flipped(w, k, wide_n), cap, slot_ref[...])
        send_ref[k] = dot(pick, routed_ref[...]).astype(bf16)
        send_copy(k).start()
        return carry

    lax.fori_loop(1, wide_n, send_step, 0)
    pick = expert_pick(w, cap, slot_ref[...])
    recv_ref[0] = dot(pick, routed_ref[...]).astype(bf16)
    for copy in loads:
        copy.wait()
    wr_ref[...] = jnp.zeros_like(wr_ref)
    wr_ref[:, :experts] = router_ref[...]
    lane = lax.broadcasted_iota(jnp.int32, (1, wr_ref.shape[1]), 1)
    hot = lane == w
    c0 = 0.7978845608028654
    c1 = c0 * 0.044715
    grouter_ref[...] = jnp.zeros_like(grouter_ref)

    def give(first):
        def one(j, carry):
            @pl.when(first + j > 0)
            def _():
                back_copy(first + j).start()

            return carry

        return one

    def one_chunk(step, carry):
        chunk = order(step)
        first = chunk * per

        def arrive(j, inner):
            @pl.when(first + j > 0)
            def _():
                send_copy(first + j).wait_recv()

            return inner

        lax.fori_loop(0, per, arrive, 0)

        @pl.when(inner * (step + 1) == chunks)
        def _():
            for earlier in (2, 1, 0):
                lax.fori_loop(0, per, give(earlier * per), 0)

        sources = pl.ds(first, per)
        here = pl.ds(pl.multiple_of(chunk * chunk_rows, chunk_rows), chunk_rows)
        x = recv_ref[sources].reshape(chunk_rows, width)
        cot = cot_ref[sources].reshape(chunk_rows, width).astype(f32)
        logits = jnp.where(lane < experts, dot(x, wr_ref[...]), -1e30)
        raised = jnp.exp(logits - jnp.max(logits, axis=-1, keepdims=True))
        probs = raised * (1.0 / jnp.sum(raised, axis=-1, keepdims=True))
        gate = jnp.sum(jnp.where(hot, probs, 0.0), axis=-1, keepdims=True)
        push_ref[here, :] = (gate * cot).astype(bf16)
        acc_res[...] = jnp.zeros_like(acc_res)
        acc_back[...] = jnp.zeros_like(acc_back)

        def hidden_tile(t, inner):
            cols = pl.ds(pl.multiple_of(t * tile, tile), tile)
            pre = dot(recv_ref[sources].reshape(chunk_rows, width), win_ref[:, cols])
            ag = dot(push_ref[here, :], wout_ref[cols, :], NT)
            sq = pre * pre
            th = jnp.tanh(pre * (c0 + c1 * sq))
            half = 0.5 + 0.5 * th
            act = (pre * half).astype(bf16)
            slope = half + pre * (0.5 - 0.5 * th * th) * (c0 + 3.0 * c1 * sq)
            pg = (ag * slope).astype(bf16)
            act_ref[here, cols] = act
            pg_ref[here, cols] = pg
            acc_res[...] += dot(act, wout_ref[cols, :])
            acc_back[...] += dot(pg, win_ref[:, cols], NT)
            return inner

        lax.fori_loop(0, units // tile, hidden_tile, 0)
        result = acc_res[...].astype(bf16).astype(f32)
        res_ref[sources] = (gate * result).astype(bf16).reshape(per, cap, width)
        gate_grad = jnp.sum(cot * result, axis=-1, keepdims=True)
        logit_grad = probs * (jnp.where(hot, gate_grad, 0.0) - gate * gate_grad)
        logit_grad = logit_grad.astype(bf16)
        back = acc_back[...].astype(bf16).astype(f32) + dot(logit_grad, wr_ref[...], NT)
        cot_ref[sources] = back.astype(bf16).reshape(per, cap, width)
        grouter_ref[...] += dot(x, logit_grad, TN)

        @pl.when(step == chunks - 1)
        def _():
            lax.fori_loop(0, per, give(first), 0)

        @pl.when((1 - inner) * (step + 1) == chunks)
        def _():
            for earlier in (2, 1, 0):
                lax.fori_loop(0, per, give(earlier * per), 0)

        return carry

    lax.fori_loop(0, chunks, one_chunk, 0)
    own = pltpu.make_async_copy(cot_ref.at[0], back_any.at[w], sem.at[0])
    own.start()
    res_copy = pltpu.make_async_copy(res_ref, res_any, sem.at[1])
    res_copy.start()

    n = lax.axis_index("narrow")
    core, half = n % 2, n // 2
    in_rows, out_rows = width // 4, units // 4

    def slice_at(index, rows):
        return pl.ds(pl.multiple_of(index * rows, rows), rows)

    def near_copy(ref, near, rows, side, i, cols=slice(None)):
        return link(
            ref.at[slice_at(2 * side + 1 - core, rows), cols], near.at[side, :, cols],
            gradsem.at[0, i + side], gradsem.at[1, i + side], "narrow", flipped(n, 1, 4),
        )

    def near_add(ref, near, rows, side, i, cols=slice(None)):
        near_copy(ref, near, rows, side, i, cols).wait()
        at = slice_at(2 * side + core, rows)
        ref[at, cols] = (ref[at, cols].astype(f32) + near[side, :, cols].astype(f32)).astype(bf16)
        return at

    early, late = slice(0, split), slice(split, units)
    gin_far = link(
        win_ref.at[slice_at(2 * (1 - half) + core, in_rows), early], ginfar_any,
        gradsem.at[0, 6], gradsem.at[1, 6], "narrow", flipped(n, 2, 4),
    )

    def in_tile(t, carry):
        cols = pl.ds(pl.multiple_of(t * tile, tile), tile)
        win_ref[:, cols] = dot(
            recv_ref[...].reshape(wide_n * cap, width), pg_ref[:, cols], TN
        ).astype(bf16)

        @pl.when(t == split // tile - 1)
        def _():
            for side in range(2):
                near_copy(win_ref, nearin_ref, in_rows, side, 0, early).start()

        return carry

    def out_tile(t, carry):
        cols = pl.ds(pl.multiple_of(t * tile, tile), tile)
        wout_ref[cols, :] = dot(act_ref[:, cols], push_ref[...], TN).astype(bf16)

        @pl.when(t == 1)
        def _():
            near_add(win_ref, nearin_ref, in_rows, 1 - half, 0, early)
            gin_far.start()

        return carry

    lax.fori_loop(0, units // tile, in_tile, 0)
    for side in range(2):
        near_copy(win_ref, nearin_ref, in_rows, side, 4, late).start()
    lax.fori_loop(0, units // tile, out_tile, 0)
    for side in range(2):
        near_copy(wout_ref, nearout_ref, out_rows, side, 2).start()
    near_add(win_ref, nearin_ref, in_rows, half, 0, early)
    at = near_add(win_ref, nearin_ref, in_rows, half, 4, late)
    ends = [pltpu.make_async_copy(win_ref.at[at], gin_any, sem.at[2])]
    at = near_add(win_ref, nearin_ref, in_rows, 1 - half, 4, late)
    ends.append(pltpu.make_async_copy(win_ref.at[at, late], ginsend_any, sem.at[5]))
    at = near_add(wout_ref, nearout_ref, out_rows, 1 - half, 2)
    ends.append(pltpu.make_async_copy(wout_ref.at[at], goutsend_any, sem.at[3]))
    at = near_add(wout_ref, nearout_ref, out_rows, half, 2)
    ends.append(pltpu.make_async_copy(wout_ref.at[at], gout_any, sem.at[4]))
    for copy in ends:
        copy.start()

    def finish_step(k, carry):
        send_copy(k).wait_send()
        back_copy(k).wait()
        return carry

    lax.fori_loop(1, wide_n, finish_step, 0)
    own.wait()
    res_copy.wait()
    gin_far.wait()
    for copy in ends:
        copy.wait()


def run_experts(routed, slot_row, wr, cot_rows, win, wout, experts):
    wide_n, cap, width = cot_rows.shape
    units = win.shape[1]
    chunks, split = 4, 2 * units // 3
    slots = wide_n * cap
    block = (wide_n, cap, width)
    step = slots // chunks
    return pl.pallas_call(
        functools.partial(expert_kernel, experts, chunks, split),
        in_specs=[vmem()] * 3 + [hbm()] * 3,
        out_specs=[hbm()] * 7 + [vmem()],
        out_shape=[
            jax.ShapeDtypeStruct(block, bf16),
            jax.ShapeDtypeStruct(block, bf16),
            jax.ShapeDtypeStruct((width // 4, units), bf16),
            jax.ShapeDtypeStruct((width // 4, split), bf16),
            jax.ShapeDtypeStruct((width // 4, units - split), bf16),
            jax.ShapeDtypeStruct((units // 4, width), bf16),
            jax.ShapeDtypeStruct((units // 4, width), bf16),
            jax.ShapeDtypeStruct((width, 128), f32),
        ],
        scratch_shapes=[
            pltpu.VMEM(block, bf16),
            pltpu.VMEM(block, bf16),
            pltpu.VMEM(block, bf16),
            pltpu.VMEM((slots, width), bf16),
            pltpu.VMEM((width, units), bf16),
            pltpu.VMEM((units, width), bf16),
            pltpu.VMEM((slots, units), bf16),
            pltpu.VMEM((slots, units), bf16),
            pltpu.VMEM(block, bf16),
            pltpu.VMEM((step, width), f32),
            pltpu.VMEM((step, width), f32),
            pltpu.VMEM((2, width // 4, units), bf16),
            pltpu.VMEM((2, units // 4, width), bf16),
            pltpu.VMEM((width, 128), bf16),
            pltpu.SemaphoreType.DMA((2, wide_n)),
            pltpu.SemaphoreType.DMA((2, wide_n)),
            pltpu.SemaphoreType.DMA((6,)),
            pltpu.SemaphoreType.DMA((2, 7)),
        ],
        compiler_params=params(collective_id=2, has_side_effects=True),
        name="experts",
    )(routed, slot_row, wr, cot_rows, win, wout)


def link(src, dst, send_sem, recv_sem, axis, peer):
    return pltpu.make_async_remote_copy(
        src_ref=src,
        dst_ref=dst,
        send_sem=send_sem,
        recv_sem=recv_sem,
        device_id={axis: peer},
        device_id_type=MESH,
    )


def padded(v):
    return -(-v // 16) * 16


class Sums:
    REFS = 8

    def __init__(self, wide_n, refs, sems):
        (
            self.terms, self.near, self.mine, self.half_in, self.quarter_in, self.piece_in,
            self.cross_in, self.whole,
        ) = refs
        self.narrow_sem, self.pair_sem, self.piece_sem, self.back_sem = sems
        self.wide_n = wide_n
        self.n, self.w = lax.axis_index("narrow"), lax.axis_index("wide")
        self.core, self.side = self.n % 2, self.n // 2
        self.ranks, slices, self.piece, _ = self.piece_in.shape
        self.direct = slices == 1
        self.cut = 1 if self.direct else 4
        self.rank = self.w // self.cut
        _, self.blocks, self.rows, _ = self.terms.shape
        self.total = self.mine.shape[1]

    def near_copy(self, side):
        return link(
            self.terms.at[2 * side + 1 - self.core], self.near.at[side],
            self.narrow_sem.at[0, side], self.narrow_sem.at[1, side],
            "narrow", flipped(self.n, 1, 4),
        )

    def cross_copy(self):
        if self.direct:
            source = self.terms.at[2 * (1 - self.side) + self.core]
        else:
            source = self.mine.at[1 - self.side, self.piece_at(self.rank)]
        return link(
            source, self.cross_in,
            self.narrow_sem.at[0, 2], self.narrow_sem.at[1, 2], "narrow", flipped(self.n, 2, 4),
        )

    def part_at(self, level, other):
        first, second = self.w % 2, (self.w // 2) % 2
        if level == 1:
            size, index = self.total // 2, first + other * (1 - 2 * first)
        else:
            size, index = self.total // 4, 2 * first + second + other * (1 - 2 * second)
        return pl.ds(pl.multiple_of(index * size, 16), size)

    def piece_at(self, rank):
        base = 0
        if not self.direct:
            base = (2 * (self.w % 2) + (self.w // 2) % 2) * (self.total // 4)
        return pl.ds(pl.multiple_of(base + rank * self.piece, 16), self.piece)

    def pair_copy(self, level):
        return link(
            self.mine.at[:, self.part_at(level, 1)],
            self.half_in if level == 1 else self.quarter_in,
            self.pair_sem.at[0, level - 1], self.pair_sem.at[1, level - 1],
            "wide", flipped(self.w, level, self.wide_n),
        )

    def peer(self, rank):
        return rank * self.cut + self.w % self.cut

    def piece_copy(self, k):
        rank = flipped(self.rank, k, self.ranks)
        return link(
            self.mine.at[:, self.piece_at(rank)], self.piece_in.at[k],
            self.piece_sem.at[0, k], self.piece_sem.at[1, k], "wide", self.peer(rank),
        )

    def piece_back(self, k):
        at = self.piece_at(self.rank)
        return link(
            self.whole.at[at], self.whole.at[at], self.back_sem.at[0, k], self.back_sem.at[1, k],
            "wide", flipped(self.w, k if self.direct else 2 * k, self.wide_n),
        )

    def pieces_back(self, f):
        self.each(f, self.wide_n if self.direct else self.wide_n // 2)

    def half_back(self):
        at = self.part_at(1, 0)
        return link(
            self.whole.at[at], self.whole.at[at], self.pair_sem.at[0, 2], self.pair_sem.at[1, 2],
            "wide", flipped(self.w, 1, self.wide_n),
        )

    def each(self, f, count=None):
        def step(k, carry):
            f(k)
            return carry

        lax.fori_loop(1, count or self.ranks, step, 0)

    def start(self):
        for side in (0, 1):
            self.near_copy(side).start()

    def near_total(self, side):
        self.near_copy(side).wait()
        return self.terms[2 * side + self.core].astype(f32) + self.near[side].astype(f32)

    def place(self, i, total):
        rows = self.blocks * self.rows
        self.mine[i, 0:rows] = total.astype(bf16).reshape(rows, 128)

    def to_far(self):
        total = self.near_total(1 - self.side)
        self.terms[2 * (1 - self.side) + self.core] = total.astype(bf16)
        self.cross_copy().start()

    def to_half(self):
        if self.direct:
            total = self.near_total(self.side)
            self.cross_copy().wait()
            self.place(0, total + self.cross_in[...].astype(f32))
            self.each(lambda k: self.piece_copy(k).start())
        else:
            for side in (0, 1):
                self.place(side, self.near_total(side))
            self.pair_copy(1).start()

    def take(self, level, ref):
        self.pair_copy(level).wait()
        at = self.part_at(level, 0)
        total = self.mine[:, at].astype(f32) + ref[...].astype(f32)
        self.mine[:, at] = total.astype(bf16)

    def to_quarter(self):
        self.take(1, self.half_in)
        self.pair_copy(2).start()

    def to_piece(self):
        self.take(2, self.quarter_in)
        self.each(lambda k: self.piece_copy(k).start())

    def pieces_total(self):
        self.each(lambda k: self.piece_copy(k).wait())

        def add(k, total):
            return total + self.piece_in[k].astype(f32)

        at = self.piece_at(self.rank)
        return lax.fori_loop(1, self.ranks, add, self.mine[:, at].astype(f32))

    def to_cross(self):
        self.mine[:, self.piece_at(self.rank)] = self.pieces_total().astype(bf16)
        self.cross_copy().start()

    def back_piece(self):
        at = self.piece_at(self.rank)
        if self.direct:
            total = self.pieces_total()[0]
        else:
            self.cross_copy().wait()
            total = self.mine[self.side, at].astype(f32) + self.cross_in[...].astype(f32)
        self.whole[at] = total.astype(bf16)
        self.pieces_back(lambda k: self.piece_back(k).start())

    def back_half(self):
        self.pieces_back(lambda k: self.piece_back(k).wait())
        self.half_back().start()

    def finish(self):
        if self.direct:
            self.pieces_back(lambda k: self.piece_back(k).wait())
        else:
            self.half_back().wait()

    def block(self, b):
        return self.whole[b * self.rows : (b + 1) * self.rows, :].astype(f32)

    @staticmethod
    def scratch(blocks, rows, wide_n, slices):
        cut = 1 if slices == 1 else 4
        ranks = wide_n // cut
        piece = padded(-(-blocks * rows // wide_n))
        total = wide_n * piece
        return [
            pltpu.VMEM((4, blocks, rows, 128), bf16),
            pltpu.VMEM((2, blocks, rows, 128), bf16),
            pltpu.VMEM((slices, total, 128), bf16),
            pltpu.VMEM((slices, 16 if slices == 1 else total // 2, 128), bf16),
            pltpu.VMEM((slices, 16 if slices == 1 else total // 4, 128), bf16),
            pltpu.VMEM((ranks, slices, piece, 128), bf16),
            pltpu.VMEM((blocks, rows, 128) if slices == 1 else (piece, 128), bf16),
            pltpu.VMEM((total, 128), bf16),
        ], [
            pltpu.SemaphoreType.DMA((2, 3)),
            pltpu.SemaphoreType.DMA((2, 3)),
            pltpu.SemaphoreType.DMA((2, ranks)),
            pltpu.SemaphoreType.DMA((2, wide_n)),
        ]


GROUPS = ((0, 6), (0, 2), (2, 4), (4, 5), (5, 6))


def backward_kernel(
    wide_n, experts, back_any, slot_ref, hid_any, cot_any, att_any, attseq_any, p_any, invl_any,
    q_any, k_any, v_any, tok_any, res_any, wo_ref, wq_ref, wk_ref, wv_ref, gain_a_ref, gain_e_ref,
    router_ref, hot_ref, gin_any, gout_any,
    out_any, hgrad_any, part_any, big_any, small_any, resland_any, ginfar_any, goutfar_any,
    back_ref, hid_ref, cot_ref, attseq_ref, invl_ref, q_ref, k_ref, v_ref, tok_ref,
    agsend, agbuf, turned_ref, dk_ref, dv_ref, pbuf, acc_ref, diag_ref,
    kmask_ref, vext_ref, ds_ref, gains_ref, smallout, loadsem, psem, agsem, partsem,
    ressem, gradsem, *rest,
):
    parts, seqs, span, width = tok_ref.shape
    total = parts * span
    block_rows = seqs * span
    pairs = width // 128
    slots = back_ref.shape[0] * back_ref.shape[1]
    rows_n = width // parts
    n, w = lax.axis_index("narrow"), lax.axis_index("wide")
    count = len(GROUPS)
    per = Sums.REFS
    group = [
        Sums(
            wide_n,
            rest[per * i : per * i + per],
            rest[per * count + 4 * i : per * count + 4 * i + 4],
        )
        for i in range(count)
    ]
    folds = 4 if experts <= 16 else 1
    fold_rows = rows_n // folds
    gain_lane = 30 if folds == 4 else 126
    small_terms, small_near, small_mine, small_in, small_sem, small_wide_sem = rest[
        per * count + 4 * count :
    ]

    def small_copy(k):
        peer = flipped(n, k, parts)
        return remote(small_terms.at[peer], small_near.at[k], small_sem, k, "narrow", peer)

    def small_wide(k):
        peer = flipped(w, k, wide_n)
        return remote(small_mine, small_in.at[k], small_wide_sem, k, "wide", peer)

    loads = [
        pltpu.make_async_copy(a, b, loadsem.at[i])
        for i, (a, b) in enumerate(
            (
                (back_any, back_ref), (hid_any, hid_ref), (cot_any, cot_ref), (att_any, k_ref),
                (attseq_any, attseq_ref), (invl_any, invl_ref), (q_any, q_ref), (v_any, v_ref),
                (tok_any, tok_ref),
            )
        )
    ]
    for copy in loads:
        copy.start()

    def block_of(phase):
        return n // 2 + phase * (1 - 2 * (n // 2))

    def step_of(i):
        late = i // 8
        phase = (1 - late) * (i // 4) + late * (i % 2)
        return phase, (1 - late) * (i % 4) + late * (i // 2)

    def p_copy(i):
        phase, pair = step_of(i)
        at = pl.ds(pl.multiple_of(block_of(phase) * 2 * span, 2 * span), 2 * span)
        return pltpu.make_async_copy(p_any.at[pair, :, at], pbuf.at[i % 2], psem.at[i % 2])

    out_half = gout_any.shape[0] // 2
    grad_copies = [
        link(a, b, gradsem.at[0, i], gradsem.at[1, i], "narrow", flipped(n, 2, parts))
        for i, (a, b) in enumerate(
            (
                (gin_any, ginfar_any),
                (gout_any.at[:out_half], goutfar_any.at[:out_half]),
                (gout_any.at[out_half:], goutfar_any.at[out_half:]),
            )
        )
    ]
    p_copy(0).start()
    expected = greet(parts, wide_n)

    def res_copy(k):
        return remote(
            res_any.at[k], resland_any.at[w], ressem, k, "wide", flipped(w, k, wide_n)
        )

    def res_start(k, carry):
        res_copy(k).start()
        return carry

    res_own = pltpu.make_async_copy(res_any.at[0], resland_any.at[w], loadsem.at[10])

    def ag_copy(k):
        peer = flipped(n, k, parts)
        return remote(agsend.at[peer], agbuf.at[n], agsem, k, "narrow", peer)

    def rows_of(src):
        return pl.ds(pl.multiple_of(src * block_rows, block_rows), block_rows)

    def picked(rows):
        ids = lax.broadcasted_iota(jnp.int32, (block_rows, slots), 1)
        pick = (ids == slot_ref[rows, :]).astype(f32).astype(bf16)
        return dot(pick, back_ref[...].reshape(slots, width))

    gain_a = gain_a_ref[...].astype(f32).reshape(1, width)
    gain_e = gain_e_ref[...].astype(f32).reshape(1, width)
    gains_ref[...] = jnp.zeros_like(gains_ref)
    for copy in loads[:3]:
        copy.wait()
    for k in range(parts - 1, -1, -1):
        src = flipped(n, k, parts)
        rows = rows_of(src)
        upstream = picked(rows)
        hidden = hid_ref[rows, :]
        inv = inverse_rms(hidden)
        scaled = upstream * gain_e
        inner = jnp.mean(scaled * hidden, axis=-1, keepdims=True)
        grad = cot_ref[rows, :].astype(f32) + inv * scaled - hidden * (inv * inv * inv * inner)
        gains_ref[1:2, :] += jnp.sum(upstream * hidden * inv, axis=0, keepdims=True)
        hid_ref[rows, :] = grad
        grad = grad.astype(bf16)
        cot_ref[rows, :] = grad
        grad = dot(grad, wo_ref[...], NT).astype(bf16).reshape(seqs, span, width)
        if k == parts - 1:
            pl.semaphore_wait(pltpu.get_barrier_semaphore(), expected)
        if k > 0:
            agsend[src] = grad
            ag_copy(k).start()
        else:
            agbuf[src] = grad
        if k == parts - 1:
            lax.fori_loop(1, wide_n, res_start, 0)
            res_own.start()
    for copy in grad_copies[:2]:
        copy.start()
    hid_copy = pltpu.make_async_copy(hid_ref, hgrad_any, loadsem.at[1])
    hid_copy.start()
    loads[3].wait()
    for h in range(2):
        cols = slice(h * 2 * rows_n, (h + 1) * 2 * rows_n)
        grad = dot(k_ref[...].reshape(parts * block_rows, width)[:, cols], cot_ref[...], TN)
        grad = grad.astype(bf16)
        for t in range(2):
            for b in range(pairs):
                group[0].terms[2 * h + t, b] = grad[
                    t * rows_n : (t + 1) * rows_n, b * 128 : (b + 1) * 128
                ]
    k_copy = pltpu.make_async_copy(k_any, k_ref, loadsem.at[9])
    k_copy.start()
    group[0].start()
    for copy in loads[4:]:
        copy.wait()
    for b in range(parts):
        x = tok_ref[b].reshape(block_rows, width).astype(f32)
        normed = x * inverse_rms(x) * gain_a
        turned_ref[:, b * block_rows : (b + 1) * block_rows] = normed.T.astype(bf16)
    diag_ref[...] = jnp.zeros_like(diag_ref)

    low, masks = half_masks(128)
    lane = lax.broadcasted_iota(jnp.int32, (1, 128), 1)
    strip = (parts + 2) * span

    def attention_pair(phase, pair, i):
        slot = i % 2
        block = block_of(phase)
        both = pl.ds(2 * block, 2)
        lanes = pl.ds(pl.multiple_of(pair * 128, 128), 128)
        p_copy(i).wait()

        @pl.when(i + 1 < 2 * pairs)
        def _():
            p_copy(i + 1).start()

        for s in range(seqs):
            kp = k_ref[:, s, :, lanes].reshape(total, 128)
            vp = v_ref[:, s, :, lanes].reshape(total, 128)
            for hh in range(2):
                ones = (lane // 2 == 32 - 32 * hh).astype(f32)
                kmask_ref[hh * total : (hh + 1) * total, :] = kp * masks[hh]
                vext_ref[hh] = jnp.where(ones > 0, ones, vp.astype(f32)).astype(bf16)
            dk = [0.0, 0.0]
            dv = [0.0, 0.0]
            qp = q_ref[both, s, :, lanes].reshape(2 * span, 128)
            inv = invl_ref[both, s, :, lanes].reshape(2 * span, 128).astype(f32)
            gp = agbuf[both, s, :, lanes].reshape(2 * span, 128).astype(f32)
            gp = (gp * inv).astype(bf16)
            gf = gp.astype(f32)
            agree = gf * attseq_ref[both, s, :, lanes].reshape(2 * span, 128).astype(f32)
            for hh in range(2):
                side = low if hh == 0 else ~low
                delta = -jnp.sum(jnp.where(side, agree, 0.0), axis=-1, keepdims=True)
                high = delta.astype(bf16).astype(f32)
                ext = jnp.where(lane == 64 - 64 * hh, high, 0.0)
                ext = jnp.where(lane == 65 - 64 * hh, delta - high, ext)
                ext = jnp.where(side, gf, ext).astype(bf16)
                raised = pbuf[slot, s, :, hh * total : (hh + 1) * total]
                score_grad = raised.astype(f32) * dot(ext, vext_ref[hh], NT)
                if s == 0:
                    acc_ref[hh] = score_grad
                else:
                    acc_ref[hh] += score_grad
                score_grad = score_grad.astype(bf16)
                ds_ref[:, hh * total : (hh + 1) * total] = score_grad
                dk[hh] = dot(score_grad, qp, TN)
                dv[hh] = dot(raised, gp, TN)
            dq = dot(ds_ref[...], kmask_ref[...])
            q_ref[both, s, :, lanes] = dq.astype(bf16).reshape(2, span, 128)
            dk = jnp.where(low, dk[0], dk[1]) * (1.0 / LOG2E)
            dv = jnp.where(low, dv[0], dv[1])
            here = slice(s * total, (s + 1) * total)
            if phase == 0:
                dk_ref[here, lanes] = dk
                dv_ref[here, lanes] = dv
            else:
                dk = dk + dk_ref[here, lanes]
                dv = dv + dv_ref[here, lanes]
                k_ref[:, s, :, lanes] = dk.astype(bf16).reshape(parts, span, 128)
                v_ref[:, s, :, lanes] = dv.astype(bf16).reshape(parts, span, 128)
        base = pl.multiple_of((parts - 2 - 2 * block) * span, span)
        for hh in range(2):
            upper, lower = acc_ref[hh, :span, :], acc_ref[hh, span:, :]
            zero = jnp.zeros((span, span), f32)
            upper = jnp.concatenate([zero, upper, zero], axis=1)
            lower = jnp.concatenate([lower, zero, zero], axis=1)
            both_rows = upper + lower
            small_sum = jnp.zeros((8, strip), f32)
            for a in range(span // 8):
                shift = span - 8 - 8 * a
                rows8 = both_rows[8 * a : 8 * a + 8]
                small_sum += rows8 if shift == 0 else pltpu.roll(rows8, shift, 1)
            line = small_sum[7:8]
            for a in range(7):
                line = line + pltpu.roll(small_sum[a : a + 1], 7 - a, 1)
            diag_ref[pl.ds(gain_lane - 14 + 2 * pair + hh, 1), pl.ds(base, strip)] += line

    k_copy.wait()
    ag_copy(1).wait_recv()

    def weight_group(g):
        first, last = GROUPS[g]
        cols = slice(first * 128, last * 128)
        size = last - first
        for i, ref in enumerate((q_ref, k_ref, v_ref)):
            field = ref[:, :, :, cols].reshape(parts * block_rows, size * 128)
            grad = dot(turned_ref[...], field).astype(bf16)
            for part in range(parts):
                for t in range(size):
                    group[g].terms[part, size * i + t] = grad[
                        part * rows_n : (part + 1) * rows_n, t * 128 : (t + 1) * 128
                    ]
        group[g].start()

    hooks = {
        1: [group[0].to_half],
        5: [lambda: weight_group(1)],
        6: [group[1].to_half],
        7: [lambda: weight_group(2), group[0].to_quarter, grad_copies[2].start],
        8: [group[2].to_half, group[1].to_quarter],
        9: [lambda: weight_group(3), group[0].to_piece],
        10: [group[3].to_half, group[2].to_quarter, group[1].to_piece],
        11: [group[0].to_cross],
    }

    def attention_step(i, carry):
        phase, pair = step_of(i)

        @pl.when(i == 4)
        def _():
            for k in range(2, parts):
                ag_copy(k).wait_recv()

        for which in range(2):

            @pl.when(phase == which)
            def _(which=which):
                attention_pair(which, pair, i)

        for at, calls in hooks.items():

            @pl.when(i == at)
            def _(calls=calls):
                for call in calls:
                    call()

        return carry

    lax.fori_loop(0, 2 * pairs, attention_step, 0)
    weight_group(4)

    def part_copy(k):
        peer = flipped(n, k, parts)
        return remote(agsend.at[peer], part_any.at[n], partsem, k, "narrow", peer)

    for k in range(1, parts):
        ag_copy(k).wait_send()
    for k in (0, 3, 1, 2):
        src = flipped(n, k, parts)
        x = tok_ref[src].reshape(block_rows, width).astype(f32)
        inv = inverse_rms(x)
        upstream = dot(q_ref[src].reshape(block_rows, width), wq_ref[...], NT)
        upstream += dot(k_ref[src].reshape(block_rows, width), wk_ref[...], NT)
        upstream += dot(v_ref[src].reshape(block_rows, width), wv_ref[...], NT)
        scaled = upstream * gain_a
        inner = jnp.mean(scaled * x, axis=-1, keepdims=True)
        grad = inv * scaled - x * (inv * inv * inv * inner)
        gains_ref[0:1, :] += jnp.sum(upstream * x * inv, axis=0, keepdims=True)
        grad = grad.astype(bf16).reshape(seqs, span, width)
        agsend[src] = grad
        if k == 0:
            part_own = pltpu.make_async_copy(agsend.at[src], part_any.at[n], loadsem.at[3])
            part_own.start()
            group[4].to_far()
            group[1].to_cross()
            group[3].to_quarter()
        if k in (1, 3):
            part_copy(k).start()
        if k == 3:
            group[2].to_piece()
            group[0].back_piece()
        if k == 1:
            group[4].to_half()
            group[3].to_piece()

    pack = router_ref[...]
    for i in range(2):
        column = jnp.broadcast_to(gains_ref[i : i + 1, :], (128, width)).T
        pack = pack + jnp.where(lane == gain_lane + i, column, 0.0)
    relative = lax.dot_general(
        hot_ref[...].astype(f32), diag_ref[...], NT,
        precision=lax.Precision.HIGHEST, preferred_element_type=f32,
    )
    share = relative.shape[0] // parts
    for part in range(parts):
        slab = pack[part * rows_n : (part + 1) * rows_n]
        head = slab[:share] + relative[part * share : (part + 1) * share]
        slab = jnp.concatenate([head, slab[share:]], axis=0)
        folded = slab[:fold_rows]
        for fold in range(1, folds):
            folded += pltpu.roll(slab[fold * fold_rows : (fold + 1) * fold_rows], 32 * fold, 1)
        small_terms[part] = folded.astype(bf16)
    for k in range(1, parts):
        small_copy(k).start()
    part_copy(2).start()
    group[2].to_cross()
    group[1].back_piece()
    res_own.wait()

    def res_wait(k, carry):
        res_copy(k).wait()
        return carry

    lax.fori_loop(1, wide_n, res_wait, 0)
    again = pltpu.make_async_copy(resland_any, back_ref, loadsem.at[0])
    again.start()

    def small_hop():
        total = small_terms[n].astype(f32)
        for k in range(1, parts):
            small_copy(k).wait()
            total += small_near[k].astype(f32)
        small_mine[...] = total.astype(bf16)

        def small_send(k, carry):
            small_wide(k).start()
            return carry

        lax.fori_loop(1, wide_n, small_send, 0)

    again.wait()
    outs = [part_own, hid_copy]
    for b in range(parts):
        rows = pl.ds(b * block_rows, block_rows)
        cot_ref[rows, :] = picked(rows).astype(bf16)
        if b == 0:
            group[4].back_piece()
            group[3].to_cross()
        if b == 1:
            small_hop()
            group[0].back_half()
        if b == 2:
            group[2].back_piece()
            group[1].back_half()
    copy = pltpu.make_async_copy(cot_ref, out_any, loadsem.at[2])
    copy.start()
    outs.append(copy)
    group[3].back_piece()

    def unpack(g):
        group[g].finish()
        first, last = GROUPS[g]
        size = last - first
        for b in range(group[g].blocks):
            i, at = (3, b) if g == 0 else (b // size, first + b % size)
            dv_ref[i * rows_n : (i + 1) * rows_n, at * 128 : (at + 1) * 128] = group[g].block(b)

    unpack(0)
    group[2].back_half()
    unpack(4)
    unpack(1)
    group[3].back_half()
    total = small_mine[...].astype(f32)
    for k in range(1, wide_n):
        small_wide(k).wait()
        total += small_in[k].astype(f32)
    for fold in range(folds):
        part = total if fold == 0 else pltpu.roll(total, 128 - 32 * fold, 1)
        smallout[fold * fold_rows : (fold + 1) * fold_rows, :] = part
    unpack(2)
    for k in range(1, parts):
        part_copy(k).wait()
    unpack(3)
    for copy in grad_copies:
        copy.wait()
    for a, b, i in ((dv_ref.at[: 4 * rows_n], big_any, 11), (smallout, small_any, 12)):
        copy = pltpu.make_async_copy(a, b, loadsem.at[i])
        copy.start()
        outs.append(copy)
    for copy in outs:
        copy.wait()


def backward(args, wide_n, experts, quad, slots_shape, table):
    parts, seqs, span, width = quad
    total, tokens = parts * span, parts * seqs * span
    rows_n = width // parts
    fold_rows = rows_n // (4 if experts <= 16 else 1)
    square = pltpu.VMEM((tokens, width), f32)
    sums = [
        Sums.scratch(
            (1 if g == 0 else 3) * (last - first), rows_n, wide_n, 1 if g == len(GROUPS) - 1 else 2
        )
        for g, (first, last) in enumerate(GROUPS)
    ]
    return pl.pallas_call(
        functools.partial(backward_kernel, wide_n, experts),
        in_specs=[hbm(), vmem()] + [hbm()] * 11 + [vmem()] * 8 + [hbm()] * 2,
        out_specs=[hbm()] * 8,
        out_shape=[
            jax.ShapeDtypeStruct((tokens, width), bf16),
            jax.ShapeDtypeStruct((tokens, width), f32),
            jax.ShapeDtypeStruct(quad, bf16),
            jax.ShapeDtypeStruct((4 * rows_n, width), f32),
            jax.ShapeDtypeStruct((rows_n, 128), f32),
            jax.ShapeDtypeStruct(slots_shape, bf16),
            jax.ShapeDtypeStruct(args[-2].shape, bf16),
            jax.ShapeDtypeStruct(args[-1].shape, bf16),
        ],
        scratch_shapes=[
            pltpu.VMEM(slots_shape, bf16),
            square,
            pltpu.VMEM((tokens, width), bf16),
            pltpu.VMEM(quad, bf16),
            pltpu.VMEM(quad, bf16),
            pltpu.VMEM(quad, bf16),
            pltpu.VMEM(quad, bf16),
            pltpu.VMEM(quad, bf16),
            pltpu.VMEM(quad, bf16),
            pltpu.VMEM(quad, bf16),
            pltpu.VMEM(quad, bf16),
            pltpu.VMEM((width, tokens), bf16),
            square,
            square,
            pltpu.VMEM((2, seqs, 2 * span, 2 * total), bf16),
            pltpu.VMEM((2, 2 * span, total), f32),
            pltpu.VMEM((128, table), f32),
            pltpu.VMEM((2 * total, 128), bf16),
            pltpu.VMEM((2, total, 128), bf16),
            pltpu.VMEM((2 * span, 2 * total), bf16),
            pltpu.VMEM((8, width), f32),
            pltpu.VMEM((rows_n, 128), f32),
            pltpu.SemaphoreType.DMA((13,)),
            pltpu.SemaphoreType.DMA((2,)),
            pltpu.SemaphoreType.DMA((2, parts)),
            pltpu.SemaphoreType.DMA((2, parts)),
            pltpu.SemaphoreType.DMA((2, wide_n)),
            pltpu.SemaphoreType.DMA((2, 3)),
        ]
        + [ref for refs, _ in sums for ref in refs]
        + [sem for _, sems in sums for sem in sems]
        + [
            pltpu.VMEM((parts, fold_rows, 128), bf16),
            pltpu.VMEM((parts, fold_rows, 128), bf16),
            pltpu.VMEM((fold_rows, 128), bf16),
            pltpu.VMEM((wide_n, fold_rows, 128), bf16),
            pltpu.SemaphoreType.DMA((2, parts)),
            pltpu.SemaphoreType.DMA((2, wide_n)),
        ],
        compiler_params=params(collective_id=3, has_side_effects=True),
        name="backward",
    )(*args)


def body(
    tokens, lengths, routes, bucket_table, attn_gain, query_weight, key_weight, value_weight,
    output_weight, relative_bias, expert_gain, router_weight, experts_in, experts_out, cotangent,
):
    seq_count, span, width = tokens.shape
    narrow_n = lax.axis_size("narrow")
    wide_n = lax.axis_size("wide")
    seqs = seq_count // narrow_n
    heads = relative_bias.shape[1]
    buckets = relative_bias.shape[0]
    experts = router_weight.shape[1]
    tok_count = seq_count * span
    capacity = 5 * tok_count // (4 * experts)
    cap = -(-capacity // 16) * 16
    table = 2 * span * narrow_n
    flat_cot = cotangent.reshape(tok_count, width)
    tok_quad = tokens.reshape(narrow_n, seqs, span, width)
    (
        tok_seq, att_seq, att_pos, hidden, routed, cot_rows, q, k, v, invl, probs,
        slot_row, slot_col, offset_hot,
    ) = forward(
        (
            lengths, tok_quad, flat_cot, routes.reshape(seq_count, span), bucket_table,
            relative_bias, attn_gain, expert_gain,
            query_weight, key_weight, value_weight, output_weight,
        ),
        wide_n, capacity, cap, tok_quad.shape, table,
    )
    res, back_rows, gin, gin_early, gin_send, gout, gout_send, router_grad = run_experts(
        routed, slot_row, router_weight, cot_rows, experts_in[0], experts_out[0], experts
    )
    picked_res, hidden_grad, part, big, small, _, gin_late, gout_far = backward(
        (
            back_rows, slot_col, hidden, flat_cot, att_pos, att_seq, probs, invl, q, k, v, tok_seq,
            res, output_weight, query_weight, key_weight, value_weight, attn_gain, expert_gain,
            router_grad, offset_hot, gin_send, gout_send,
        ),
        wide_n, experts, tok_quad.shape, res.shape, table,
    )

    gain_lane = 30 if experts <= 16 else 126
    return (
        (hidden + picked_res.astype(f32)).reshape(seq_count, span, width),
        (hidden_grad + part.reshape(tok_count, width).astype(f32)).reshape(seq_count, span, width),
        small[:, gain_lane],
        *big.reshape(narrow_n, -1, width),
        small[: buckets // narrow_n, gain_lane - 14 : gain_lane - 14 + heads],
        small[:, gain_lane + 1],
        small[:, :experts],
        (gin.astype(f32) + jnp.concatenate([gin_early, gin_late], axis=1).astype(f32))[None],
        (gout.astype(f32) + gout_far.astype(f32))[None],
    )


def solution(mesh):
    token = P("wide", "narrow", None)
    expert = P("wide", None, None)
    row, vector = P("narrow", None), P("narrow")
    return jax.shard_map(
        body,
        mesh=mesh,
        in_specs=(token, P("wide"), token) + (P(),) * 9 + (expert, expert, token),
        out_specs=(
            token, token, vector, row, row, row, row, row, vector, row,
            P("wide", "narrow", None), P("wide", "narrow", None),
        ),
        check_vma=False,
    )
```

```python
import functools

import jax
import jax.numpy as jnp
from jax import lax
from jax.experimental import pallas as pl
from jax.experimental.pallas import tpu as pltpu
from jax.sharding import PartitionSpec as P

f32, bf16 = jnp.float32, jnp.bfloat16
epsilon = 1e-06
VMEM_BYTES = 62 * 1024 * 1024
NN = (((1,), (0,)), ((), ()))
NT = (((1,), (1,)), ((), ()))
TN = (((0,), (0,)), ((), ()))


def dot(a, b, dims=NN):
    return lax.dot_general(a, b, dims, preferred_element_type=f32)


def vmem():
    return pl.BlockSpec(memory_space=pltpu.VMEM)


def params(**kw):
    return pltpu.CompilerParams(vmem_limit_bytes=VMEM_BYTES, **kw)


def inverse_rms(field):
    return lax.rsqrt(jnp.mean(field * field, axis=-1, keepdims=True) + epsilon)


def half_masks(pair_width):
    lane = lax.broadcasted_iota(jnp.int32, (1, pair_width), 1)
    low = lane < pair_width // 2
    return low, (low.astype(f32).astype(bf16), (~low).astype(f32).astype(bf16))


MESH = pl.DeviceIdType.MESH
LOG2E = 1.4426950408889634


def hbm():
    return pl.BlockSpec(memory_space=pl.ANY)


def flipped(me, k, size):
    out, bit = me, 1
    while bit < size:
        out = out + ((k // bit) % 2) * (bit - 2 * bit * ((me // bit) % 2))
        bit *= 2
    return out


def remote(src, dst, sems, k, axis, peer):
    return pltpu.make_async_remote_copy(
        src_ref=src,
        dst_ref=dst,
        send_sem=sems.at[0, k],
        recv_sem=sems.at[1, k],
        device_id={axis: peer},
        device_id_type=MESH,
    )


def greet(narrow_n, wide_n):
    barrier = pltpu.get_barrier_semaphore()
    count = 0
    for axis, size in (("narrow", narrow_n), ("wide", wide_n)):
        if size > 1:
            me = lax.axis_index(axis)

            def greet(k, carry, axis=axis, size=size, me=me):
                pl.semaphore_signal(
                    barrier, inc=1, device_id={axis: flipped(me, k, size)}, device_id_type=MESH
                )
                return carry

            lax.fori_loop(1, size, greet, 0)
            count += size - 1
    return count


def enter(narrow_n, wide_n):
    count = greet(narrow_n, wide_n)
    pl.semaphore_wait(pltpu.get_barrier_semaphore(), count)


def expert_pick(expert, cap, slot_row):
    ids = lax.broadcasted_iota(jnp.int32, (cap, slot_row.shape[1]), 0) + expert * cap
    return (ids == slot_row).astype(f32).astype(bf16)


def token_slots(routes_ref, column_ref, experts, capacity, cap):
    seqs, span = routes_ref.shape
    routes = routes_ref[...]
    hot = jnp.concatenate([(routes == e).astype(f32) for e in range(experts)], axis=0)
    row = lax.broadcasted_iota(jnp.int32, (span, span), 0)
    ahead = (row < lax.broadcasted_iota(jnp.int32, (span, span), 1)).astype(f32).astype(bf16)
    size = experts * seqs
    row = lax.broadcasted_iota(jnp.int32, (size, size), 0)
    col = lax.broadcasted_iota(jnp.int32, (size, size), 1)
    above = ((row // seqs == col // seqs) & (col < row)).astype(f32).astype(bf16)
    counts = jnp.broadcast_to(jnp.sum(hot, axis=-1, keepdims=True), hot.shape).astype(bf16)
    position = dot(hot.astype(bf16), ahead) + dot(above, counts)
    slot = jnp.zeros((seqs, span), f32)
    for e in range(experts):
        here = position[e * seqs : (e + 1) * seqs]
        here = jnp.where(here < capacity, here + e * cap, experts * cap)
        slot = slot + hot[e * seqs : (e + 1) * seqs] * here
    turned = jnp.concatenate([slot] * (span // seqs), axis=0).T
    for s in range(seqs):
        column_ref[s * span : (s + 1) * span, :] = turned[:, s : s + 1].astype(jnp.int32)
    return jnp.concatenate([slot[s : s + 1] for s in range(seqs)], axis=1).astype(jnp.int32)


def forward_kernel(
    wide_n, capacity, lens_ref, tok_any, cot_ref, routes_ref, table_ref, bias_ref, gain_a_ref, gain_e_ref,
    wq_ref, wk_ref, wv_ref, wo_ref,
    tokseq_any, attseq_any, att_any, hid_any, routed_any, cotrows_any, q_any, k_any, v_any, invl_any, p_any,
    slot_row_ref, slot_col_ref, hot_ref,
    tokbuf, tokpos, q_ref, k_ref, v_ref, invl_ref, attseq, attpos, hid_ref, routed_ref, cotsend,
    strip_ref, pbuf, vext, kext, diag_ref, toksem, attsem, cotsem, psem, outsem,
):
    parts, seqs, span, width = tokbuf.shape
    total = parts * span
    heads = bias_ref.shape[0]
    pairs, table = heads // 2, diag_ref.shape[1]
    cap = cotsend.shape[1]
    n = lax.axis_index("narrow")
    w = lax.axis_index("wide")
    own = pltpu.make_async_copy(tok_any.at[n], tokbuf.at[n], outsem.at[0])
    own.start()
    position = pltpu.make_async_copy(tok_any, tokpos, outsem.at[1])
    position.start()
    expected = greet(parts, wide_n)
    slot_row_ref[...] = token_slots(routes_ref, slot_col_ref, wide_n, capacity, cap)

    def cot_block(k):
        pick = expert_pick(flipped(w, k, wide_n), cap, slot_row_ref[...])
        cotsend[k] = dot(pick, cot_ref[...]).astype(bf16)

    def cot_early(k, carry):
        cot_block(k)
        return carry

    lax.fori_loop(wide_n // 2, wide_n, cot_early, 0)
    pl.semaphore_wait(pltpu.get_barrier_semaphore(), expected)

    def tok_copy(k):
        peer = flipped(n, k, parts)
        return remote(tok_any.at[peer], tokbuf.at[n], toksem, k, "narrow", peer)

    for k in (2, 3, 1):
        tok_copy(k).start()

    def cot_copy(k):
        peer = flipped(w, k, wide_n)
        return remote(cotsend.at[k], cotrows_any.at[k], cotsem, k, "wide", peer)

    def cot_start(k, carry):
        cot_copy(k).start()
        return carry

    def cot_step(k, carry):
        cot_block(k)
        cot_copy(k).start()
        return carry

    lax.fori_loop(wide_n // 2, wide_n, cot_start, 0)
    lax.fori_loop(1, wide_n // 2, cot_step, 0)
    cot_block(0)
    cot_own = pltpu.make_async_copy(cotsend.at[0], cotrows_any.at[0], outsem.at[2])
    cot_own.start()

    gain = gain_a_ref[...].astype(f32).reshape(1, width)
    own.wait()
    for k in range(parts):
        src = flipped(n, k, parts)
        if k > 0:
            tok_copy(k).wait_recv()
        x = tokbuf[src].reshape(seqs * span, width).astype(f32)
        normed = (x * inverse_rms(x) * gain).astype(bf16)
        shape = (seqs, span, width)
        q_ref[src] = (dot(normed, wq_ref[...]) * LOG2E).astype(bf16).reshape(shape)
        k_ref[src] = dot(normed, wk_ref[...]).astype(bf16).reshape(shape)
        v_ref[src] = dot(normed, wv_ref[...]).astype(bf16).reshape(shape)
    outs = [
        pltpu.make_async_copy(a, b, outsem.at[i])
        for a, b, i in (
            (tokbuf, tokseq_any, 3), (q_ref, q_any, 4), (k_ref, k_any, 5), (v_ref, v_any, 6),
        )
    ]
    for copy in outs:
        copy.start()

    buckets, offsets = bias_ref.shape[1], table_ref.shape[0]
    ids = lax.broadcasted_iota(jnp.int32, (buckets, offsets), 0)
    found = (ids == table_ref[...].reshape(1, offsets)).astype(f32).astype(bf16)
    hot_ref[...] = jnp.zeros_like(hot_ref)
    hot_ref[:, :offsets] = found
    diag_ref[:heads, :] = dot(bias_ref[...], hot_ref[...]) * LOG2E

    low, masks = half_masks(128)
    lane = lax.broadcasted_iota(jnp.int32, (1, 128), 1)
    hot = [(lane == 64).astype(f32).astype(bf16), (lane == 0).astype(f32).astype(bf16)]
    for hh in range(2):
        ones = jnp.broadcast_to(masks[hh], (total, 128))
        vext[hh * total : (hh + 1) * total, 128:] = ones

    def att_copy(k, lanes):
        peer = flipped(n, k, parts)
        return remote(
            attseq.at[peer, :, :, lanes], attpos.at[n, :, :, lanes], attsem, k, "narrow", peer
        )

    def one_pair(pair, carry):
        lanes = pl.ds(pl.multiple_of(pair * 128, 128), 128)
        for hh in range(2):
            row = diag_ref[pl.ds(2 * pair + hh, 1), :]
            strip_ref[hh] = pltpu.roll(
                jnp.broadcast_to(row, (span, table)), table - span + 1, 1, stride=1, stride_axis=0
            )

        def one_sequence(s, inner):
            vp = v_ref[:, s, :, lanes].reshape(total, 128)
            kp = k_ref[:, s, :, lanes].reshape(total, 128).astype(f32)
            ids = lax.broadcasted_iota(jnp.int32, (total, 128), 0)
            push = jnp.where(ids < lens_ref[n * seqs + s], 0.0, -1e30)
            for hh in range(2):
                vext[hh * total : (hh + 1) * total, :128] = vp * masks[hh]
                kext[hh] = jnp.where(lane == 64 - 64 * hh, push, kp).astype(bf16)

            @pl.when(pair > 0)
            def _():
                pltpu.make_async_copy(pbuf.at[s], p_any.at[pair, s], psem.at[s]).wait()

            for block in range(parts // 2):
                rows = slice(block * 2 * span, (block + 1) * 2 * span)
                both = slice(2 * block, 2 * block + 2)
                qp = q_ref[both, s, :, lanes].reshape(2 * span, 128)
                for hh in range(2):
                    bias = jnp.concatenate(
                        [
                            strip_ref[hh, :, (parts - 1 - r) * span : (parts - 1 - r) * span + total]
                            for r in (2 * block, 2 * block + 1)
                        ],
                        axis=0,
                    )
                    scores = dot(qp * masks[hh] + hot[hh], kext[hh], NT) + bias
                    raised = jnp.exp2(scores - jnp.max(scores, axis=-1, keepdims=True))
                    pbuf[s, rows, hh * total : (hh + 1) * total] = raised.astype(bf16)
                mixed = dot(pbuf[s, rows, :], vext[...])
                inv = 1.0 / mixed[:, 128:]
                invl_ref[both, s, :, lanes] = inv.astype(bf16).reshape(2, span, 128)
                attseq[both, s, :, lanes] = (mixed[:, :128] * inv).astype(bf16).reshape(2, span, 128)
            pltpu.make_async_copy(pbuf.at[s], p_any.at[pair, s], psem.at[s]).start()
            return inner

        lax.fori_loop(0, seqs, one_sequence, 0)
        for k in range(parts - 1, 0, -1):
            att_copy(k, lanes).start()
        return carry

    lax.fori_loop(0, pairs, one_pair, 0)
    for a, b, i in ((invl_ref, invl_any, 7), (attseq, attseq_any, 11)):
        copy = pltpu.make_async_copy(a, b, outsem.at[i])
        copy.start()
        outs.append(copy)
    position.wait()
    gain = gain_e_ref[...].astype(f32).reshape(1, width)
    for k in range(parts):
        src = flipped(n, k, parts)
        if k > 0:
            att_copy(k, slice(None)).wait_recv()
            att = attpos[src].reshape(seqs * span, width)
        else:
            attpos[src] = attseq[src]
            att = attseq[src].reshape(seqs * span, width)
        rows = pl.ds(pl.multiple_of(src * seqs * span, seqs * span), seqs * span)
        hidden = tokpos[src].reshape(seqs * span, width).astype(f32) + dot(att, wo_ref[...])
        hid_ref[rows, :] = hidden
        copy = pltpu.make_async_copy(hid_ref.at[rows], hid_any.at[rows], outsem.at[12 + k])
        copy.start()
        outs.append(copy)
        routed_ref[rows, :] = (hidden * inverse_rms(hidden) * gain).astype(bf16)
    for a, b, i in ((attpos, att_any, 8), (routed_ref, routed_any, 10)):
        copy = pltpu.make_async_copy(a, b, outsem.at[i])
        copy.start()
        outs.append(copy)
    for k in range(1, parts):
        tok_copy(k).wait_send()
        att_copy(k, slice(None)).wait_send()
    for s in range(seqs):
        pltpu.make_async_copy(pbuf.at[s], p_any.at[0, s], psem.at[s]).wait()
    cot_own.wait()

    def cot_wait(k, carry):
        cot_copy(k).wait()
        return carry

    lax.fori_loop(1, wide_n, cot_wait, 0)
    for copy in outs:
        copy.wait()


def forward(args, wide_n, capacity, cap, quad, table):
    parts, seqs, span, width = quad
    heads, buckets = args[5].shape
    pairs = heads // 2
    total = parts * span
    tokens = parts * seqs * span
    shapes = [
        (quad, bf16), (quad, bf16), (quad, bf16), ((tokens, width), f32), ((tokens, width), bf16),
        ((wide_n, cap, width), bf16), (quad, bf16), (quad, bf16), (quad, bf16), (quad, bf16),
        ((pairs, seqs, total, 2 * total), bf16),
    ]
    small = [((1, tokens), jnp.int32), ((tokens, 1), jnp.int32), ((buckets, table), bf16)]
    return pl.pallas_call(
        functools.partial(forward_kernel, wide_n, capacity),
        in_specs=[pl.BlockSpec(memory_space=pltpu.SMEM), hbm()] + [vmem()] * 10,
        out_specs=[hbm()] * len(shapes) + [vmem()] * 3,
        out_shape=[jax.ShapeDtypeStruct(*item) for item in shapes + small],
        scratch_shapes=[
            pltpu.VMEM(quad, bf16),
            pltpu.VMEM(quad, bf16),
            pltpu.VMEM(quad, bf16),
            pltpu.VMEM(quad, bf16),
            pltpu.VMEM(quad, bf16),
            pltpu.VMEM(quad, bf16),
            pltpu.VMEM(quad, bf16),
            pltpu.VMEM(quad, bf16),
            pltpu.VMEM((tokens, width), f32),
            pltpu.VMEM((tokens, width), bf16),
            pltpu.VMEM((wide_n, cap, width), bf16),
            pltpu.VMEM((2, span, table), f32),
            pltpu.VMEM((seqs, total, 2 * total), bf16),
            pltpu.VMEM((2 * total, 256), bf16),
            pltpu.VMEM((2, total, 128), bf16),
            pltpu.VMEM((16, table), f32),
            pltpu.SemaphoreType.DMA((2, parts)),
            pltpu.SemaphoreType.DMA((2, parts)),
            pltpu.SemaphoreType.DMA((2, wide_n)),
            pltpu.SemaphoreType.DMA((seqs,)),
            pltpu.SemaphoreType.DMA((16,)),
        ],
        compiler_params=params(collective_id=1, has_side_effects=True),
        name="forward",
    )(*args)


def expert_kernel(
    experts, chunks, split, routed_ref, slot_ref, router_ref, cot_any, win_any, wout_any,
    res_any, back_any, gin_any, ginfar_any, ginsend_any, gout_any, goutsend_any, grouter_ref,
    send_ref, recv_ref, cot_ref, push_ref, win_ref, wout_ref, act_ref, pg_ref, res_ref,
    acc_res, acc_back, nearin_ref, nearout_ref, wr_ref, sendsem, backsem, sem, gradsem,
):
    wide_n, cap, width = send_ref.shape
    units = win_ref.shape[1]
    tile = 512
    w = lax.axis_index("wide")
    per = wide_n // chunks
    chunk_rows = per * cap
    loads = [
        pltpu.make_async_copy(a, b, sem.at[i])
        for i, (a, b) in enumerate(((cot_any, cot_ref), (win_any, win_ref), (wout_any, wout_ref)))
    ]
    for copy in loads:
        copy.start()
    expected = greet(4, wide_n)

    def send_copy(k):
        return remote(
            send_ref.at[k], recv_ref.at[k], sendsem, k, "wide", flipped(w, k, wide_n)
        )

    def back_copy(k):
        return remote(
            cot_ref.at[k], back_any.at[w], backsem, k, "wide", flipped(w, k, wide_n)
        )

    def turn(i):
        return (i % 2) * 2 + i // 2

    last = wide_n // 2 - 1
    inner = ((w // 2) % last + last - 1) // last

    def order(i):
        return i + inner * (turn(i) - i)

    def make_rows(i, carry):
        k = turn(i // per) * per + i % per
        pick = expert_pick(flipped(w, k, wide_n), cap, slot_ref[...])
        send_ref[k] = dot(pick, routed_ref[...]).astype(bf16)
        return carry

    def send_rows(i, carry):
        send_copy(turn(i // per) * per + i % per).start()
        return carry

    def send_step(i, carry):
        return send_rows(i, make_rows(i, carry))

    lax.fori_loop(1, wide_n // 2, make_rows, 0)
    pl.semaphore_wait(pltpu.get_barrier_semaphore(), expected)
    lax.fori_loop(1, wide_n // 2, send_rows, 0)
    lax.fori_loop(wide_n // 2, wide_n, send_step, 0)
    pick = expert_pick(w, cap, slot_ref[...])
    recv_ref[0] = dot(pick, routed_ref[...]).astype(bf16)
    for copy in loads:
        copy.wait()
    router = router_ref[...].astype(f32)
    blank = jnp.zeros((wr_ref.shape[0] - experts, width), f32)
    wr_ref[...] = jnp.concatenate([router, blank], axis=0).astype(bf16)
    lane = lax.broadcasted_iota(jnp.int32, (1, wr_ref.shape[0]), 1)
    hot = lane == w
    c0 = 0.7978845608028654
    c1 = c0 * 0.044715
    grouter_ref[...] = jnp.zeros_like(grouter_ref)

    def give(first):
        def one(j, carry):
            @pl.when(first + j > 0)
            def _():
                back_copy(first + j).start()

            return carry

        return one

    def one_chunk(step, carry):
        chunk = order(step)
        first = chunk * per

        def arrive(j, inner):
            @pl.when(first + j > 0)
            def _():
                send_copy(first + j).wait_recv()

            return inner

        lax.fori_loop(0, per, arrive, 0)

        @pl.when(inner * (step + 1) == chunks)
        def _():
            for earlier in (2, 1, 0):
                lax.fori_loop(0, per, give(earlier * per), 0)

        sources = pl.ds(first, per)
        here = pl.ds(pl.multiple_of(chunk * chunk_rows, chunk_rows), chunk_rows)
        x = recv_ref[sources].reshape(chunk_rows, width)
        cot = cot_ref[sources].reshape(chunk_rows, width).astype(f32)
        logits = jnp.where(lane < experts, dot(x, wr_ref[...], NT), -1e30)
        raised = jnp.exp(logits - jnp.max(logits, axis=-1, keepdims=True))
        probs = raised * (1.0 / jnp.sum(raised, axis=-1, keepdims=True))
        gate = jnp.sum(jnp.where(hot, probs, 0.0), axis=-1, keepdims=True)
        push_ref[here, :] = (gate * cot).astype(bf16)
        acc_res[...] = jnp.zeros_like(acc_res)
        acc_back[...] = jnp.zeros_like(acc_back)

        def hidden_tile(t, inner):
            cols = pl.ds(pl.multiple_of(t * tile, tile), tile)
            pre = dot(recv_ref[sources].reshape(chunk_rows, width), win_ref[:, cols])
            ag = dot(push_ref[here, :], wout_ref[cols, :], NT)
            sq = pre * pre
            th = jnp.tanh(pre * (c0 + c1 * sq))
            half = 0.5 + 0.5 * th
            act = (pre * half).astype(bf16)
            slope = half + pre * (0.5 - 0.5 * th * th) * (c0 + 3.0 * c1 * sq)
            pg = (ag * slope).astype(bf16)
            act_ref[here, cols] = act
            pg_ref[here, cols] = pg
            acc_res[...] += dot(act, wout_ref[cols, :])
            acc_back[...] += dot(pg, win_ref[:, cols], NT)
            return inner

        lax.fori_loop(0, units // tile, hidden_tile, 0)
        result = acc_res[...].astype(bf16).astype(f32)
        res_ref[sources] = (gate * result).astype(bf16).reshape(per, cap, width)
        gate_grad = jnp.sum(cot * result, axis=-1, keepdims=True)
        logit_grad = probs * (jnp.where(hot, gate_grad, 0.0) - gate * gate_grad)
        logit_grad = logit_grad.astype(bf16)
        back = acc_back[...].astype(bf16).astype(f32) + dot(logit_grad, wr_ref[...])
        cot_ref[sources] = back.astype(bf16).reshape(per, cap, width)
        grouter_ref[...] += dot(x, logit_grad, TN)

        @pl.when(step == chunks - 1)
        def _():
            lax.fori_loop(0, per, give(first), 0)

        @pl.when((1 - inner) * (step + 1) == chunks)
        def _():
            for earlier in (2, 1, 0):
                lax.fori_loop(0, per, give(earlier * per), 0)

        return carry

    lax.fori_loop(0, chunks, one_chunk, 0)
    own = pltpu.make_async_copy(cot_ref.at[0], back_any.at[w], sem.at[0])
    own.start()
    res_copy = pltpu.make_async_copy(res_ref, res_any, sem.at[1])
    res_copy.start()

    n = lax.axis_index("narrow")
    core, half = n % 2, n // 2
    in_rows, out_rows = width // 4, units // 4

    def slice_at(index, rows):
        return pl.ds(pl.multiple_of(index * rows, rows), rows)

    def near_copy(ref, near, rows, side, i, cols=slice(None)):
        return link(
            ref.at[slice_at(2 * side + 1 - core, rows), cols], near.at[side, :, cols],
            gradsem.at[0, i + side], gradsem.at[1, i + side], "narrow", flipped(n, 1, 4),
        )

    def near_add(ref, near, rows, side, i, cols=slice(None)):
        near_copy(ref, near, rows, side, i, cols).wait()
        at = slice_at(2 * side + core, rows)
        ref[at, cols] = (ref[at, cols].astype(f32) + near[side, :, cols].astype(f32)).astype(bf16)
        return at

    early, late = slice(0, split), slice(split, units)
    gin_far = link(
        win_ref.at[slice_at(2 * (1 - half) + core, in_rows), early], ginfar_any,
        gradsem.at[0, 6], gradsem.at[1, 6], "narrow", flipped(n, 2, 4),
    )

    def in_tile(t, carry):
        cols = pl.ds(pl.multiple_of(t * tile, tile), tile)
        win_ref[:, cols] = dot(
            recv_ref[...].reshape(wide_n * cap, width), pg_ref[:, cols], TN
        ).astype(bf16)

        @pl.when(t == split // tile - 1)
        def _():
            for side in range(2):
                near_copy(win_ref, nearin_ref, in_rows, side, 0, early).start()

        return carry

    def out_tile(t, carry):
        cols = pl.ds(pl.multiple_of(t * tile, tile), tile)
        wout_ref[cols, :] = dot(act_ref[:, cols], push_ref[...], TN).astype(bf16)

        @pl.when(t == 1)
        def _():
            near_add(win_ref, nearin_ref, in_rows, 1 - half, 0, early)
            gin_far.start()

        return carry

    lax.fori_loop(0, units // tile, in_tile, 0)
    for side in range(2):
        near_copy(win_ref, nearin_ref, in_rows, side, 4, late).start()
    lax.fori_loop(0, units // tile, out_tile, 0)
    for side in range(2):
        near_copy(wout_ref, nearout_ref, out_rows, side, 2).start()
    near_add(win_ref, nearin_ref, in_rows, half, 0, early)
    at = near_add(win_ref, nearin_ref, in_rows, half, 4, late)
    ends = [pltpu.make_async_copy(win_ref.at[at], gin_any, sem.at[2])]
    at = near_add(win_ref, nearin_ref, in_rows, 1 - half, 4, late)
    ends.append(pltpu.make_async_copy(win_ref.at[at, late], ginsend_any, sem.at[5]))
    at = near_add(wout_ref, nearout_ref, out_rows, 1 - half, 2)
    ends.append(pltpu.make_async_copy(wout_ref.at[at], goutsend_any, sem.at[3]))
    at = near_add(wout_ref, nearout_ref, out_rows, half, 2)
    ends.append(pltpu.make_async_copy(wout_ref.at[at], gout_any, sem.at[4]))
    for copy in ends:
        copy.start()

    def finish_step(k, carry):
        send_copy(k).wait_send()
        back_copy(k).wait()
        return carry

    lax.fori_loop(1, wide_n, finish_step, 0)
    own.wait()
    res_copy.wait()
    gin_far.wait()
    for copy in ends:
        copy.wait()


def run_experts(routed, slot_row, wr, cot_rows, win, wout, experts):
    wide_n, cap, width = cot_rows.shape
    units = win.shape[1]
    chunks, split = 4, 2 * units // 3
    slots = wide_n * cap
    block = (wide_n, cap, width)
    step = slots // chunks
    return pl.pallas_call(
        functools.partial(expert_kernel, experts, chunks, split),
        in_specs=[vmem()] * 3 + [hbm()] * 3,
        out_specs=[hbm()] * 7 + [vmem()],
        out_shape=[
            jax.ShapeDtypeStruct(block, bf16),
            jax.ShapeDtypeStruct(block, bf16),
            jax.ShapeDtypeStruct((width // 4, units), bf16),
            jax.ShapeDtypeStruct((width // 4, split), bf16),
            jax.ShapeDtypeStruct((width // 4, units - split), bf16),
            jax.ShapeDtypeStruct((units // 4, width), bf16),
            jax.ShapeDtypeStruct((units // 4, width), bf16),
            jax.ShapeDtypeStruct((width, 128), f32),
        ],
        scratch_shapes=[
            pltpu.VMEM(block, bf16),
            pltpu.VMEM(block, bf16),
            pltpu.VMEM(block, bf16),
            pltpu.VMEM((slots, width), bf16),
            pltpu.VMEM((width, units), bf16),
            pltpu.VMEM((units, width), bf16),
            pltpu.VMEM((slots, units), bf16),
            pltpu.VMEM((slots, units), bf16),
            pltpu.VMEM(block, bf16),
            pltpu.VMEM((step, width), f32),
            pltpu.VMEM((step, width), f32),
            pltpu.VMEM((2, width // 4, units), bf16),
            pltpu.VMEM((2, units // 4, width), bf16),
            pltpu.VMEM((128, width), bf16),
            pltpu.SemaphoreType.DMA((2, wide_n)),
            pltpu.SemaphoreType.DMA((2, wide_n)),
            pltpu.SemaphoreType.DMA((6,)),
            pltpu.SemaphoreType.DMA((2, 7)),
        ],
        compiler_params=params(collective_id=2, has_side_effects=True),
        name="experts",
    )(routed, slot_row, wr, cot_rows, win, wout)


def link(src, dst, send_sem, recv_sem, axis, peer):
    return pltpu.make_async_remote_copy(
        src_ref=src,
        dst_ref=dst,
        send_sem=send_sem,
        recv_sem=recv_sem,
        device_id={axis: peer},
        device_id_type=MESH,
    )


def padded(v):
    return -(-v // 16) * 16


class Sums:
    REFS = 8

    def __init__(self, wide_n, refs, sems):
        (
            self.terms, self.near, self.mine, self.half_in, self.quarter_in, self.piece_in,
            self.cross_in, self.whole,
        ) = refs
        self.narrow_sem, self.pair_sem, self.piece_sem, self.back_sem = sems
        self.wide_n = wide_n
        self.n, self.w = lax.axis_index("narrow"), lax.axis_index("wide")
        self.core, self.side = self.n % 2, self.n // 2
        self.ranks, slices, self.piece, _ = self.piece_in.shape
        self.direct = slices == 1
        self.cut = 1 if self.direct else 4
        self.rank = self.w // self.cut
        _, self.blocks, self.rows, _ = self.terms.shape
        self.total = self.mine.shape[1]

    def near_copy(self, side):
        return link(
            self.terms.at[2 * side + 1 - self.core], self.near.at[side],
            self.narrow_sem.at[0, side], self.narrow_sem.at[1, side],
            "narrow", flipped(self.n, 1, 4),
        )

    def cross_copy(self):
        if self.direct:
            source = self.terms.at[2 * (1 - self.side) + self.core]
        else:
            source = self.mine.at[1 - self.side, self.piece_at(self.rank)]
        return link(
            source, self.cross_in,
            self.narrow_sem.at[0, 2], self.narrow_sem.at[1, 2], "narrow", flipped(self.n, 2, 4),
        )

    def part_at(self, level, other):
        first, second = self.w % 2, (self.w // 2) % 2
        if level == 1:
            size, index = self.total // 2, first + other * (1 - 2 * first)
        else:
            size, index = self.total // 4, 2 * first + second + other * (1 - 2 * second)
        return pl.ds(pl.multiple_of(index * size, 16), size)

    def piece_at(self, rank):
        base = 0
        if not self.direct:
            base = (2 * (self.w % 2) + (self.w // 2) % 2) * (self.total // 4)
        return pl.ds(pl.multiple_of(base + rank * self.piece, 16), self.piece)

    def pair_copy(self, level):
        return link(
            self.mine.at[:, self.part_at(level, 1)],
            self.half_in if level == 1 else self.quarter_in,
            self.pair_sem.at[0, level - 1], self.pair_sem.at[1, level - 1],
            "wide", flipped(self.w, level, self.wide_n),
        )

    def peer(self, rank):
        return rank * self.cut + self.w % self.cut

    def piece_copy(self, k):
        rank = flipped(self.rank, k, self.ranks)
        return link(
            self.mine.at[:, self.piece_at(rank)], self.piece_in.at[k],
            self.piece_sem.at[0, k], self.piece_sem.at[1, k], "wide", self.peer(rank),
        )

    def piece_back(self, k):
        at = self.piece_at(self.rank)
        return link(
            self.whole.at[at], self.whole.at[at], self.back_sem.at[0, k], self.back_sem.at[1, k],
            "wide", self.peer(flipped(self.rank, k, self.ranks)),
        )

    def pair_back(self, level):
        at = self.part_at(level, 0)
        return link(
            self.whole.at[at], self.whole.at[at],
            self.pair_sem.at[0, level + 1], self.pair_sem.at[1, level + 1],
            "wide", flipped(self.w, level, self.wide_n),
        )

    def each(self, f):
        def step(k, carry):
            f(k)
            return carry

        lax.fori_loop(1, self.ranks, step, 0)

    def start(self):
        for side in (0, 1):
            self.near_copy(side).start()

    def near_total(self, side):
        self.near_copy(side).wait()
        return self.terms[2 * side + self.core].astype(f32) + self.near[side].astype(f32)

    def place(self, i, total):
        rows = self.blocks * self.rows
        self.mine[i, 0:rows] = total.astype(bf16).reshape(rows, 128)

    def to_far(self):
        total = self.near_total(1 - self.side)
        self.terms[2 * (1 - self.side) + self.core] = total.astype(bf16)
        self.cross_copy().start()

    def to_half(self):
        if self.direct:
            total = self.near_total(self.side)
            self.cross_copy().wait()
            self.place(0, total + self.cross_in[...].astype(f32))
            self.each(lambda k: self.piece_copy(k).start())
        else:
            for side in (0, 1):
                self.place(side, self.near_total(side))
            self.pair_copy(1).start()

    def take(self, level, ref):
        self.pair_copy(level).wait()
        at = self.part_at(level, 0)
        total = self.mine[:, at].astype(f32) + ref[...].astype(f32)
        self.mine[:, at] = total.astype(bf16)

    def to_quarter(self):
        self.take(1, self.half_in)
        self.pair_copy(2).start()

    def to_piece(self):
        self.take(2, self.quarter_in)
        self.each(lambda k: self.piece_copy(k).start())

    def pieces_total(self):
        self.each(lambda k: self.piece_copy(k).wait())

        def add(k, total):
            return total + self.piece_in[k].astype(f32)

        at = self.piece_at(self.rank)
        return lax.fori_loop(1, self.ranks, add, self.mine[:, at].astype(f32))

    def to_cross(self):
        self.mine[:, self.piece_at(self.rank)] = self.pieces_total().astype(bf16)
        self.cross_copy().start()

    def back_piece(self):
        at = self.piece_at(self.rank)
        if self.direct:
            total = self.pieces_total()[0]
        else:
            self.cross_copy().wait()
            total = self.mine[self.side, at].astype(f32) + self.cross_in[...].astype(f32)
        self.whole[at] = total.astype(bf16)
        self.each(lambda k: self.piece_back(k).start())

    def back_quarter(self):
        self.each(lambda k: self.piece_back(k).wait())
        self.pair_back(2).start()

    def back_half(self):
        self.pair_back(2).wait()
        self.pair_back(1).start()

    def finish(self):
        if self.direct:
            self.each(lambda k: self.piece_back(k).wait())
        else:
            self.pair_back(1).wait()

    def block(self, b):
        return self.whole[b * self.rows : (b + 1) * self.rows, :].astype(f32)

    @staticmethod
    def scratch(blocks, rows, wide_n, slices):
        cut = 1 if slices == 1 else 4
        ranks = wide_n // cut
        piece = padded(-(-blocks * rows // wide_n))
        total = wide_n * piece
        return [
            pltpu.VMEM((4, blocks, rows, 128), bf16),
            pltpu.VMEM((2, blocks, rows, 128), bf16),
            pltpu.VMEM((slices, total, 128), bf16),
            pltpu.VMEM((slices, 16 if slices == 1 else total // 2, 128), bf16),
            pltpu.VMEM((slices, 16 if slices == 1 else total // 4, 128), bf16),
            pltpu.VMEM((ranks, slices, piece, 128), bf16),
            pltpu.VMEM((blocks, rows, 128) if slices == 1 else (piece, 128), bf16),
            pltpu.VMEM((total, 128), bf16),
        ], [
            pltpu.SemaphoreType.DMA((2, 3)),
            pltpu.SemaphoreType.DMA((2, 4)),
            pltpu.SemaphoreType.DMA((2, ranks)),
            pltpu.SemaphoreType.DMA((2, ranks)),
        ]


GROUPS = ((0, 6), (0, 2), (2, 4), (4, 5), (5, 6))


def backward_kernel(
    wide_n, experts, back_any, slot_ref, hid_any, cot_any, att_any, attseq_any, p_any, invl_any,
    q_any, k_any, v_any, tok_any, res_any, wo_ref, wq_ref, wk_ref, wv_ref, gain_a_ref, gain_e_ref,
    router_ref, hot_ref, gin_any, gout_any,
    out_any, hgrad_any, part_any, big_any, small_any, resland_any, ginfar_any, goutfar_any,
    back_ref, hid_ref, cot_ref, attseq_ref, invl_ref, q_ref, k_ref, v_ref, tok_ref,
    agsend, agbuf, turned_ref, dk_ref, dv_ref, pbuf, acc_ref, diag_ref,
    kmask_ref, vext_ref, ds_ref, gains_ref, smallout, loadsem, psem, agsem, partsem,
    ressem, gradsem, *rest,
):
    parts, seqs, span, width = tok_ref.shape
    total = parts * span
    block_rows = seqs * span
    pairs = width // 128
    slots = back_ref.shape[0] * back_ref.shape[1]
    rows_n = width // parts
    n, w = lax.axis_index("narrow"), lax.axis_index("wide")
    count = len(GROUPS)
    per = Sums.REFS
    group = [
        Sums(
            wide_n,
            rest[per * i : per * i + per],
            rest[per * count + 4 * i : per * count + 4 * i + 4],
        )
        for i in range(count)
    ]
    folds = 4 if experts <= 16 else 1
    fold_rows = rows_n // folds
    gain_lane = 30 if folds == 4 else 126
    small_terms, small_near, small_mine, small_in, small_sem, small_wide_sem = rest[
        per * count + 4 * count :
    ]

    def small_copy(k):
        peer = flipped(n, k, parts)
        return remote(small_terms.at[peer], small_near.at[k], small_sem, k, "narrow", peer)

    def small_wide(k):
        peer = flipped(w, k, wide_n)
        return remote(small_mine, small_in.at[k], small_wide_sem, k, "wide", peer)

    loads = [
        pltpu.make_async_copy(a, b, loadsem.at[i])
        for i, (a, b) in enumerate(
            (
                (back_any, back_ref), (hid_any, hid_ref), (cot_any, cot_ref), (att_any, k_ref),
                (attseq_any, attseq_ref), (invl_any, invl_ref), (q_any, q_ref), (v_any, v_ref),
                (tok_any, tok_ref),
            )
        )
    ]
    for copy in loads:
        copy.start()

    def block_of(phase):
        return n // 2 + phase * (1 - 2 * (n // 2))

    def step_of(i):
        late = i // 8
        phase = (1 - late) * (i // 4) + late * (i % 2)
        return phase, (1 - late) * (i % 4) + late * (i // 2)

    def p_copy(i):
        phase, pair = step_of(i)
        at = pl.ds(pl.multiple_of(block_of(phase) * 2 * span, 2 * span), 2 * span)
        return pltpu.make_async_copy(p_any.at[pair, :, at], pbuf.at[i % 2], psem.at[i % 2])

    out_half = gout_any.shape[0] // 2
    grad_copies = [
        link(a, b, gradsem.at[0, i], gradsem.at[1, i], "narrow", flipped(n, 2, parts))
        for i, (a, b) in enumerate(
            (
                (gin_any, ginfar_any),
                (gout_any.at[:out_half], goutfar_any.at[:out_half]),
                (gout_any.at[out_half:], goutfar_any.at[out_half:]),
            )
        )
    ]
    p_copy(0).start()
    expected = greet(parts, wide_n)

    def res_copy(k):
        return remote(
            res_any.at[k], resland_any.at[w], ressem, k, "wide", flipped(w, k, wide_n)
        )

    def res_start(k, carry):
        res_copy(k).start()
        return carry

    res_own = pltpu.make_async_copy(res_any.at[0], resland_any.at[w], loadsem.at[10])

    def ag_copy(k):
        peer = flipped(n, k, parts)
        return remote(agsend.at[peer], agbuf.at[n], agsem, k, "narrow", peer)

    def rows_of(src):
        return pl.ds(pl.multiple_of(src * block_rows, block_rows), block_rows)

    def picked(rows):
        ids = lax.broadcasted_iota(jnp.int32, (block_rows, slots), 1)
        pick = (ids == slot_ref[rows, :]).astype(f32).astype(bf16)
        return dot(pick, back_ref[...].reshape(slots, width))

    gain_a = gain_a_ref[...].astype(f32).reshape(1, width)
    gain_e = gain_e_ref[...].astype(f32).reshape(1, width)
    gains_ref[...] = jnp.zeros_like(gains_ref)
    for copy in loads[:3]:
        copy.wait()
    for k in range(parts - 1, -1, -1):
        src = flipped(n, k, parts)
        rows = rows_of(src)
        upstream = picked(rows)
        hidden = hid_ref[rows, :]
        inv = inverse_rms(hidden)
        scaled = upstream * gain_e
        inner = jnp.mean(scaled * hidden, axis=-1, keepdims=True)
        grad = cot_ref[rows, :].astype(f32) + inv * scaled - hidden * (inv * inv * inv * inner)
        gains_ref[1:2, :] += jnp.sum(upstream * hidden * inv, axis=0, keepdims=True)
        hid_ref[rows, :] = grad
        grad = grad.astype(bf16)
        cot_ref[rows, :] = grad
        grad = dot(grad, wo_ref[...], NT).astype(bf16).reshape(seqs, span, width)
        if k == parts - 1:
            pl.semaphore_wait(pltpu.get_barrier_semaphore(), expected)
        if k > 0:
            agsend[src] = grad
            ag_copy(k).start()
        else:
            agbuf[src] = grad
        if k == parts - 1:
            lax.fori_loop(1, wide_n, res_start, 0)
            res_own.start()
    for copy in grad_copies[:2]:
        copy.start()
    hid_copy = pltpu.make_async_copy(hid_ref, hgrad_any, loadsem.at[1])
    hid_copy.start()
    loads[3].wait()
    for h in range(2):
        cols = slice(h * 2 * rows_n, (h + 1) * 2 * rows_n)
        grad = dot(k_ref[...].reshape(parts * block_rows, width)[:, cols], cot_ref[...], TN)
        grad = grad.astype(bf16)
        for t in range(2):
            for b in range(pairs):
                group[0].terms[2 * h + t, b] = grad[
                    t * rows_n : (t + 1) * rows_n, b * 128 : (b + 1) * 128
                ]
    k_copy = pltpu.make_async_copy(k_any, k_ref, loadsem.at[9])
    k_copy.start()
    group[0].start()
    for copy in loads[4:]:
        copy.wait()
    for b in range(parts):
        x = tok_ref[b].reshape(block_rows, width).astype(f32)
        normed = x * inverse_rms(x) * gain_a
        turned_ref[:, b * block_rows : (b + 1) * block_rows] = normed.T.astype(bf16)
    diag_ref[...] = jnp.zeros_like(diag_ref)

    low, masks = half_masks(128)
    lane = lax.broadcasted_iota(jnp.int32, (1, 128), 1)
    strip = (parts + 2) * span

    def attention_pair(phase, pair, i):
        slot = i % 2
        block = block_of(phase)
        both = pl.ds(2 * block, 2)
        lanes = pl.ds(pl.multiple_of(pair * 128, 128), 128)
        p_copy(i).wait()

        @pl.when(i + 1 < 2 * pairs)
        def _():
            p_copy(i + 1).start()

        for s in range(seqs):
            kp = k_ref[:, s, :, lanes].reshape(total, 128)
            vp = v_ref[:, s, :, lanes].reshape(total, 128)
            for hh in range(2):
                ones = (lane // 2 == 32 - 32 * hh).astype(f32)
                kmask_ref[hh * total : (hh + 1) * total, :] = kp * masks[hh]
                vext_ref[hh] = jnp.where(ones > 0, ones, vp.astype(f32)).astype(bf16)
            dk = [0.0, 0.0]
            dv = [0.0, 0.0]
            qp = q_ref[both, s, :, lanes].reshape(2 * span, 128)
            inv = invl_ref[both, s, :, lanes].reshape(2 * span, 128).astype(f32)
            gp = agbuf[both, s, :, lanes].reshape(2 * span, 128).astype(f32)
            gp = (gp * inv).astype(bf16)
            gf = gp.astype(f32)
            agree = gf * attseq_ref[both, s, :, lanes].reshape(2 * span, 128).astype(f32)
            for hh in range(2):
                side = low if hh == 0 else ~low
                delta = -jnp.sum(jnp.where(side, agree, 0.0), axis=-1, keepdims=True)
                high = delta.astype(bf16).astype(f32)
                ext = jnp.where(lane == 64 - 64 * hh, high, 0.0)
                ext = jnp.where(lane == 65 - 64 * hh, delta - high, ext)
                ext = jnp.where(side, gf, ext).astype(bf16)
                raised = pbuf[slot, s, :, hh * total : (hh + 1) * total]
                score_grad = raised.astype(f32) * dot(ext, vext_ref[hh], NT)
                if s == 0:
                    acc_ref[hh] = score_grad
                else:
                    acc_ref[hh] += score_grad
                score_grad = score_grad.astype(bf16)
                ds_ref[:, hh * total : (hh + 1) * total] = score_grad
                dk[hh] = dot(score_grad, qp, TN)
                dv[hh] = dot(raised, gp, TN)
            dq = dot(ds_ref[...], kmask_ref[...])
            q_ref[both, s, :, lanes] = dq.astype(bf16).reshape(2, span, 128)
            dk = jnp.where(low, dk[0], dk[1]) * (1.0 / LOG2E)
            dv = jnp.where(low, dv[0], dv[1])
            here = slice(s * total, (s + 1) * total)
            if phase == 0:
                dk_ref[here, lanes] = dk
                dv_ref[here, lanes] = dv
            else:
                dk = dk + dk_ref[here, lanes]
                dv = dv + dv_ref[here, lanes]
                k_ref[:, s, :, lanes] = dk.astype(bf16).reshape(parts, span, 128)
                v_ref[:, s, :, lanes] = dv.astype(bf16).reshape(parts, span, 128)
        base = pl.multiple_of((parts - 2 - 2 * block) * span, span)
        for hh in range(2):
            upper, lower = acc_ref[hh, :span, :], acc_ref[hh, span:, :]
            zero = jnp.zeros((span, span), f32)
            upper = jnp.concatenate([zero, upper, zero], axis=1)
            lower = jnp.concatenate([lower, zero, zero], axis=1)
            both_rows = upper + lower
            small_sum = jnp.zeros((8, strip), f32)
            for a in range(span // 8):
                shift = span - 8 - 8 * a
                rows8 = both_rows[8 * a : 8 * a + 8]
                small_sum += rows8 if shift == 0 else pltpu.roll(rows8, shift, 1)
            line = small_sum[7:8]
            for a in range(7):
                line = line + pltpu.roll(small_sum[a : a + 1], 7 - a, 1)
            diag_ref[pl.ds(gain_lane - 14 + 2 * pair + hh, 1), pl.ds(base, strip)] += line

    k_copy.wait()
    ag_copy(1).wait_recv()

    def weight_group(g):
        first, last = GROUPS[g]
        cols = slice(first * 128, last * 128)
        size = last - first
        for i, ref in enumerate((q_ref, k_ref, v_ref)):
            field = ref[:, :, :, cols].reshape(parts * block_rows, size * 128)
            grad = dot(turned_ref[...], field).astype(bf16)
            for part in range(parts):
                for t in range(size):
                    group[g].terms[part, size * i + t] = grad[
                        part * rows_n : (part + 1) * rows_n, t * 128 : (t + 1) * 128
                    ]
        group[g].start()

    hooks = {
        1: [group[0].to_half],
        5: [lambda: weight_group(1)],
        6: [group[1].to_half],
        7: [lambda: weight_group(2), group[0].to_quarter, grad_copies[2].start],
        8: [group[2].to_half],
        9: [lambda: weight_group(3), group[0].to_piece, group[1].to_quarter],
        10: [group[3].to_half],
        11: [group[0].to_cross, group[2].to_quarter],
    }

    def attention_step(i, carry):
        phase, pair = step_of(i)

        @pl.when(i == 4)
        def _():
            for k in range(2, parts):
                ag_copy(k).wait_recv()

        for which in range(2):

            @pl.when(phase == which)
            def _(which=which):
                attention_pair(which, pair, i)

        for at, calls in hooks.items():

            @pl.when(i == at)
            def _(calls=calls):
                for call in calls:
                    call()

        return carry

    lax.fori_loop(0, 2 * pairs, attention_step, 0)
    weight_group(4)

    def part_copy(k):
        peer = flipped(n, k, parts)
        return remote(agsend.at[peer], part_any.at[n], partsem, k, "narrow", peer)

    for k in range(1, parts):
        ag_copy(k).wait_send()
    for k in (0, 3, 1, 2):
        src = flipped(n, k, parts)
        x = tok_ref[src].reshape(block_rows, width).astype(f32)
        inv = inverse_rms(x)
        upstream = dot(q_ref[src].reshape(block_rows, width), wq_ref[...], NT)
        upstream += dot(k_ref[src].reshape(block_rows, width), wk_ref[...], NT)
        upstream += dot(v_ref[src].reshape(block_rows, width), wv_ref[...], NT)
        scaled = upstream * gain_a
        inner = jnp.mean(scaled * x, axis=-1, keepdims=True)
        grad = inv * scaled - x * (inv * inv * inv * inner)
        gains_ref[0:1, :] += jnp.sum(upstream * x * inv, axis=0, keepdims=True)
        grad = grad.astype(bf16).reshape(seqs, span, width)
        agsend[src] = grad
        if k == 0:
            part_own = pltpu.make_async_copy(agsend.at[src], part_any.at[n], loadsem.at[3])
            part_own.start()
            group[4].to_far()
            group[1].to_piece()
        if k in (1, 3):
            part_copy(k).start()
        if k == 3:
            group[3].to_quarter()
            group[0].back_piece()
        if k == 1:
            group[4].to_half()
            group[2].to_piece()
            group[1].to_cross()

    pack = router_ref[...]
    for i in range(2):
        column = jnp.broadcast_to(gains_ref[i : i + 1, :], (128, width)).T
        pack = pack + jnp.where(lane == gain_lane + i, column, 0.0)
    relative = lax.dot_general(
        hot_ref[...].astype(f32), diag_ref[...], NT,
        precision=lax.Precision.HIGHEST, preferred_element_type=f32,
    )
    share = relative.shape[0] // parts
    for part in range(parts):
        slab = pack[part * rows_n : (part + 1) * rows_n]
        head = slab[:share] + relative[part * share : (part + 1) * share]
        slab = jnp.concatenate([head, slab[share:]], axis=0)
        folded = slab[:fold_rows]
        for fold in range(1, folds):
            folded += pltpu.roll(slab[fold * fold_rows : (fold + 1) * fold_rows], 32 * fold, 1)
        small_terms[part] = folded.astype(bf16)
    for k in range(1, parts):
        small_copy(k).start()
    part_copy(2).start()
    group[0].back_quarter()
    group[3].to_piece()
    res_own.wait()

    def res_wait(k, carry):
        res_copy(k).wait()
        return carry

    lax.fori_loop(1, wide_n, res_wait, 0)
    again = pltpu.make_async_copy(resland_any, back_ref, loadsem.at[0])
    again.start()

    def small_hop():
        total = small_terms[n].astype(f32)
        for k in range(1, parts):
            small_copy(k).wait()
            total += small_near[k].astype(f32)
        small_mine[...] = total.astype(bf16)

        def small_send(k, carry):
            small_wide(k).start()
            return carry

        lax.fori_loop(1, wide_n, small_send, 0)

    again.wait()
    outs = [part_own, hid_copy]
    for b in range(parts):
        rows = pl.ds(b * block_rows, block_rows)
        cot_ref[rows, :] = picked(rows).astype(bf16)
        if b == 0:
            group[4].back_piece()
            group[1].back_piece()
        if b == 1:
            small_hop()
            group[2].to_cross()
            group[0].back_half()
        if b == 2:
            group[1].back_quarter()
            group[3].to_cross()
    copy = pltpu.make_async_copy(cot_ref, out_any, loadsem.at[2])
    copy.start()
    outs.append(copy)
    group[2].back_piece()
    group[1].back_half()
    group[3].back_piece()

    def unpack(g):
        group[g].finish()
        first, last = GROUPS[g]
        size = last - first
        for b in range(group[g].blocks):
            i, at = (3, b) if g == 0 else (b // size, first + b % size)
            dv_ref[i * rows_n : (i + 1) * rows_n, at * 128 : (at + 1) * 128] = group[g].block(b)

    unpack(0)
    group[2].back_quarter()
    unpack(4)
    group[3].back_quarter()
    group[2].back_half()
    unpack(1)
    group[3].back_half()
    total = small_mine[...].astype(f32)
    for k in range(1, wide_n):
        small_wide(k).wait()
        total += small_in[k].astype(f32)
    for fold in range(folds):
        part = total if fold == 0 else pltpu.roll(total, 128 - 32 * fold, 1)
        smallout[fold * fold_rows : (fold + 1) * fold_rows, :] = part
    unpack(2)
    for k in range(1, parts):
        part_copy(k).wait()
    unpack(3)
    for copy in grad_copies:
        copy.wait()
    for a, b, i in ((dv_ref.at[: 4 * rows_n], big_any, 11), (smallout, small_any, 12)):
        copy = pltpu.make_async_copy(a, b, loadsem.at[i])
        copy.start()
        outs.append(copy)
    for copy in outs:
        copy.wait()


def backward(args, wide_n, experts, quad, slots_shape, table):
    parts, seqs, span, width = quad
    total, tokens = parts * span, parts * seqs * span
    rows_n = width // parts
    fold_rows = rows_n // (4 if experts <= 16 else 1)
    square = pltpu.VMEM((tokens, width), f32)
    sums = [
        Sums.scratch(
            (1 if g == 0 else 3) * (last - first), rows_n, wide_n, 1 if g == len(GROUPS) - 1 else 2
        )
        for g, (first, last) in enumerate(GROUPS)
    ]
    return pl.pallas_call(
        functools.partial(backward_kernel, wide_n, experts),
        in_specs=[hbm(), vmem()] + [hbm()] * 11 + [vmem()] * 8 + [hbm()] * 2,
        out_specs=[hbm()] * 8,
        out_shape=[
            jax.ShapeDtypeStruct((tokens, width), bf16),
            jax.ShapeDtypeStruct((tokens, width), f32),
            jax.ShapeDtypeStruct(quad, bf16),
            jax.ShapeDtypeStruct((4 * rows_n, width), f32),
            jax.ShapeDtypeStruct((rows_n, 128), f32),
            jax.ShapeDtypeStruct(slots_shape, bf16),
            jax.ShapeDtypeStruct(args[-2].shape, bf16),
            jax.ShapeDtypeStruct(args[-1].shape, bf16),
        ],
        scratch_shapes=[
            pltpu.VMEM(slots_shape, bf16),
            square,
            pltpu.VMEM((tokens, width), bf16),
            pltpu.VMEM(quad, bf16),
            pltpu.VMEM(quad, bf16),
            pltpu.VMEM(quad, bf16),
            pltpu.VMEM(quad, bf16),
            pltpu.VMEM(quad, bf16),
            pltpu.VMEM(quad, bf16),
            pltpu.VMEM(quad, bf16),
            pltpu.VMEM(quad, bf16),
            pltpu.VMEM((width, tokens), bf16),
            square,
            square,
            pltpu.VMEM((2, seqs, 2 * span, 2 * total), bf16),
            pltpu.VMEM((2, 2 * span, total), f32),
            pltpu.VMEM((128, table), f32),
            pltpu.VMEM((2 * total, 128), bf16),
            pltpu.VMEM((2, total, 128), bf16),
            pltpu.VMEM((2 * span, 2 * total), bf16),
            pltpu.VMEM((8, width), f32),
            pltpu.VMEM((rows_n, 128), f32),
            pltpu.SemaphoreType.DMA((13,)),
            pltpu.SemaphoreType.DMA((2,)),
            pltpu.SemaphoreType.DMA((2, parts)),
            pltpu.SemaphoreType.DMA((2, parts)),
            pltpu.SemaphoreType.DMA((2, wide_n)),
            pltpu.SemaphoreType.DMA((2, 3)),
        ]
        + [ref for refs, _ in sums for ref in refs]
        + [sem for _, sems in sums for sem in sems]
        + [
            pltpu.VMEM((parts, fold_rows, 128), bf16),
            pltpu.VMEM((parts, fold_rows, 128), bf16),
            pltpu.VMEM((fold_rows, 128), bf16),
            pltpu.VMEM((wide_n, fold_rows, 128), bf16),
            pltpu.SemaphoreType.DMA((2, parts)),
            pltpu.SemaphoreType.DMA((2, wide_n)),
        ],
        compiler_params=params(collective_id=3, has_side_effects=True),
        name="backward",
    )(*args)


def finish_kernel(
    heads, gain_lane, hid_ref, res_ref, hgrad_ref, part_ref, gin_ref, early_ref, late_ref,
    gout_ref, far_ref, big_ref, small_ref,
    out_ref, igrad_ref, gin_out, gout_out, wq_out, wk_out, wv_out, wo_out,
    router_out, relative_out, gain_a_out, gain_e_out,
):
    step = pl.program_id(0)
    out_ref[...] = hid_ref[...] + res_ref[...].astype(f32)
    igrad_ref[...] = hgrad_ref[...] + part_ref[...].astype(f32)
    split = early_ref.shape[1]
    gin = gin_ref[...].astype(f32)
    gin_out[:, :split] = gin[:, :split] + early_ref[...].astype(f32)
    gin_out[:, split:] = gin[:, split:] + late_ref[...].astype(f32)
    gout_out[...] = gout_ref[...].astype(f32) + far_ref[...].astype(f32)
    for i, ref in enumerate((wq_out, wk_out, wv_out, wo_out)):

        @pl.when(step == i)
        def _(ref=ref):
            ref[...] = big_ref[...]

    @pl.when(step == 0)
    def _():
        small = small_ref[...]
        share = relative_out.shape[0]
        relative_out[...] = small[:share, gain_lane - 14 : gain_lane - 14 + heads]
        rows = small.shape[0]
        turned = jnp.concatenate([small, jnp.zeros((-rows % 128, 128), f32)], axis=0).T
        router_out[...] = turned[: router_out.shape[0], :rows]
        gain_a_out[...] = turned[gain_lane : gain_lane + 1, :rows].reshape(rows)
        gain_e_out[...] = turned[gain_lane + 1 : gain_lane + 2, :rows].reshape(rows)


def finish(args, heads, buckets, experts, narrow_n):
    hid, _, _, _, gin, early, late, gout, _, _, small = args
    gain_lane = 30 if experts <= 16 else 126
    tokens, width = hid.shape
    steps = 4
    rows_n, units = gin.shape

    def rows(shape):
        return pl.BlockSpec((shape[0] // steps, shape[1]), lambda i: (i, 0))

    def whole(shape):
        return pl.BlockSpec(shape, lambda i: (0,) * len(shape))

    square, slab = (tokens, width), (rows_n, width)
    singles = [(experts, rows_n), (buckets // narrow_n, heads), (rows_n,), (rows_n,)]
    shapes = [square, square, (rows_n, units), gout.shape, slab, slab, slab, slab] + singles
    return pl.pallas_call(
        functools.partial(finish_kernel, heads, gain_lane),
        grid=(steps,),
        in_specs=[rows(item.shape) for item in args[:-1]] + [whole(small.shape)],
        out_specs=[rows(shape) for shape in shapes[:4]] + [whole(shape) for shape in shapes[4:]],
        out_shape=[jax.ShapeDtypeStruct(shape, f32) for shape in shapes],
        compiler_params=params(),
        name="finish",
    )(*args)


def body(
    tokens, lengths, routes, bucket_table, attn_gain, query_weight, key_weight, value_weight,
    output_weight, relative_bias, expert_gain, router_weight, experts_in, experts_out, cotangent,
):
    seq_count, span, width = tokens.shape
    narrow_n = lax.axis_size("narrow")
    wide_n = lax.axis_size("wide")
    seqs = seq_count // narrow_n
    heads = relative_bias.shape[1]
    buckets = relative_bias.shape[0]
    experts = router_weight.shape[1]
    tok_count = seq_count * span
    capacity = 5 * tok_count // (4 * experts)
    cap = -(-capacity // 16) * 16
    table = 2 * span * narrow_n
    flat_cot = cotangent.reshape(tok_count, width)
    tok_quad = tokens.reshape(narrow_n, seqs, span, width)
    (
        tok_seq, att_seq, att_pos, hidden, routed, cot_rows, q, k, v, invl, probs,
        slot_row, slot_col, offset_hot,
    ) = forward(
        (
            lengths, tok_quad, flat_cot, routes.reshape(seq_count, span), bucket_table,
            relative_bias.T, attn_gain, expert_gain,
            query_weight, key_weight, value_weight, output_weight,
        ),
        wide_n, capacity, cap, tok_quad.shape, table,
    )
    res, back_rows, gin, gin_early, gin_send, gout, gout_send, router_grad = run_experts(
        routed, slot_row, router_weight.T, cot_rows, experts_in[0], experts_out[0], experts
    )
    picked_res, hidden_grad, part, big, small, _, gin_late, gout_far = backward(
        (
            back_rows, slot_col, hidden, flat_cot, att_pos, att_seq, probs, invl, q, k, v, tok_seq,
            res, output_weight, query_weight, key_weight, value_weight, attn_gain, expert_gain,
            router_grad, offset_hot, gin_send, gout_send,
        ),
        wide_n, experts, tok_quad.shape, res.shape, table,
    )

    (
        layer_output, input_grad, grad_in, grad_out, grad_query, grad_key, grad_value, grad_output,
        grad_router, grad_relative, grad_first, grad_second,
    ) = finish(
        (
            hidden, picked_res, hidden_grad, part.reshape(tok_count, width), gin, gin_early, gin_late,
            gout, gout_far, big, small,
        ),
        heads, buckets, experts, narrow_n,
    )
    return (
        layer_output.reshape(seq_count, span, width),
        input_grad.reshape(seq_count, span, width),
        grad_first,
        grad_query,
        grad_key,
        grad_value,
        grad_output,
        grad_relative,
        grad_second,
        grad_router.T,
        grad_in[None],
        grad_out[None],
    )


def solution(mesh):
    token = P("wide", "narrow", None)
    expert = P("wide", None, None)
    row, vector = P("narrow", None), P("narrow")
    return jax.shard_map(
        body,
        mesh=mesh,
        in_specs=(token, P("wide"), token) + (P(),) * 9 + (expert, expert, token),
        out_specs=(
            token, token, vector, row, row, row, row, row, vector, row,
            P("wide", "narrow", None), P("wide", "narrow", None),
        ),
        check_vma=False,
    )
```

```python
import functools

import jax
import jax.numpy as jnp
from jax import lax
from jax.experimental import pallas as pl
from jax.experimental.pallas import tpu as pltpu
from jax.sharding import PartitionSpec as P

f32, bf16 = jnp.float32, jnp.bfloat16
epsilon = 1e-06
VMEM_BYTES = 62 * 1024 * 1024
NN = (((1,), (0,)), ((), ()))
NT = (((1,), (1,)), ((), ()))
TN = (((0,), (0,)), ((), ()))


def dot(a, b, dims=NN):
    return lax.dot_general(a, b, dims, preferred_element_type=f32)


def vmem():
    return pl.BlockSpec(memory_space=pltpu.VMEM)


def params(**kw):
    return pltpu.CompilerParams(vmem_limit_bytes=VMEM_BYTES, **kw)


def inverse_rms(field):
    return lax.rsqrt(jnp.mean(field * field, axis=-1, keepdims=True) + epsilon)


def half_masks(pair_width):
    lane = lax.broadcasted_iota(jnp.int32, (1, pair_width), 1)
    low = lane < pair_width // 2
    return low, (low.astype(f32).astype(bf16), (~low).astype(f32).astype(bf16))


MESH = pl.DeviceIdType.MESH
LOG2E = 1.4426950408889634


def hbm():
    return pl.BlockSpec(memory_space=pl.ANY)


def flipped(me, k, size):
    out, bit = me, 1
    while bit < size:
        out = out + ((k // bit) % 2) * (bit - 2 * bit * ((me // bit) % 2))
        bit *= 2
    return out


def remote(src, dst, sems, k, axis, peer):
    return pltpu.make_async_remote_copy(
        src_ref=src,
        dst_ref=dst,
        send_sem=sems.at[0, k],
        recv_sem=sems.at[1, k],
        device_id={axis: peer},
        device_id_type=MESH,
    )


def greet(narrow_n, wide_n):
    barrier = pltpu.get_barrier_semaphore()
    count = 0
    for axis, size in (("narrow", narrow_n), ("wide", wide_n)):
        if size > 1:
            me = lax.axis_index(axis)

            def greet(k, carry, axis=axis, size=size, me=me):
                pl.semaphore_signal(
                    barrier, inc=1, device_id={axis: flipped(me, k, size)}, device_id_type=MESH
                )
                return carry

            lax.fori_loop(1, size, greet, 0)
            count += size - 1
    return count


def enter(narrow_n, wide_n):
    count = greet(narrow_n, wide_n)
    pl.semaphore_wait(pltpu.get_barrier_semaphore(), count)


def expert_pick(expert, cap, slot_row):
    ids = lax.broadcasted_iota(jnp.int32, (cap, slot_row.shape[1]), 0) + expert * cap
    return (ids == slot_row).astype(f32).astype(bf16)


def token_slots(routes_ref, column_ref, experts, capacity, cap):
    seqs, span = routes_ref.shape
    routes = routes_ref[...]
    hot = jnp.concatenate([(routes == e).astype(f32) for e in range(experts)], axis=0)
    row = lax.broadcasted_iota(jnp.int32, (span, span), 0)
    ahead = (row < lax.broadcasted_iota(jnp.int32, (span, span), 1)).astype(f32).astype(bf16)
    size = experts * seqs
    row = lax.broadcasted_iota(jnp.int32, (size, size), 0)
    col = lax.broadcasted_iota(jnp.int32, (size, size), 1)
    above = ((row // seqs == col // seqs) & (col < row)).astype(f32).astype(bf16)
    counts = jnp.broadcast_to(jnp.sum(hot, axis=-1, keepdims=True), hot.shape).astype(bf16)
    position = dot(hot.astype(bf16), ahead) + dot(above, counts)
    slot = jnp.zeros((seqs, span), f32)
    for e in range(experts):
        here = position[e * seqs : (e + 1) * seqs]
        here = jnp.where(here < capacity, here + e * cap, experts * cap)
        slot = slot + hot[e * seqs : (e + 1) * seqs] * here
    turned = jnp.concatenate([slot] * (span // seqs), axis=0).T
    for s in range(seqs):
        column_ref[s * span : (s + 1) * span, :] = turned[:, s : s + 1].astype(jnp.int32)
    return jnp.concatenate([slot[s : s + 1] for s in range(seqs)], axis=1).astype(jnp.int32)


def forward_kernel(
    wide_n, capacity, lens_ref, tok_any, cot_any, routes_ref, table_ref, bias_ref, gain_a_ref, gain_e_ref,
    wq_any, wk_any, wv_any, wo_any,
    tokseq_any, attseq_any, att_any, hid_any, routed_any, cotrows_any, q_any, k_any, v_any, invl_any, p_any,
    slot_row_ref, slot_col_ref, hot_ref,
    tokbuf, tokpos, q_ref, k_ref, v_ref, invl_ref, attseq, attpos, hid_ref, routed_ref, cotsend,
    strip_ref, pbuf, vext, kext, diag_ref, cot_ref, wq_ref, wk_ref, wv_ref, wo_ref, insem, toksem, attsem, cotsem, psem, outsem,
):
    parts, seqs, span, width = tokbuf.shape
    total = parts * span
    heads = bias_ref.shape[0]
    pairs, table = heads // 2, diag_ref.shape[1]
    cap = cotsend.shape[1]
    n = lax.axis_index("narrow")
    w = lax.axis_index("wide")
    own = pltpu.make_async_copy(tok_any.at[n], tokbuf.at[n], outsem.at[0])
    position = pltpu.make_async_copy(tok_any, tokpos, outsem.at[1])
    cot_load, *qkv_loads, wo_load = [
        pltpu.make_async_copy(a, b, insem.at[i])
        for i, (a, b) in enumerate(
            (
                (cot_any, cot_ref), (wq_any, wq_ref), (wk_any, wk_ref), (wv_any, wv_ref),
                (wo_any, wo_ref),
            )
        )
    ]
    for copy in (cot_load, own, *qkv_loads, position, wo_load):
        copy.start()
    expected = greet(parts, wide_n)
    slot_row_ref[...] = token_slots(routes_ref, slot_col_ref, wide_n, capacity, cap)

    def cot_block(k):
        pick = expert_pick(flipped(w, k, wide_n), cap, slot_row_ref[...])
        cotsend[k] = dot(pick, cot_ref[...]).astype(bf16)

    def cot_early(k, carry):
        cot_block(k)
        return carry

    cot_load.wait()
    lax.fori_loop(wide_n // 2, wide_n, cot_early, 0)
    pl.semaphore_wait(pltpu.get_barrier_semaphore(), expected)

    def tok_copy(k):
        peer = flipped(n, k, parts)
        return remote(tok_any.at[peer], tokbuf.at[n], toksem, k, "narrow", peer)

    for k in (2, 3, 1):
        tok_copy(k).start()

    def cot_copy(k):
        peer = flipped(w, k, wide_n)
        return remote(cotsend.at[k], cotrows_any.at[k], cotsem, k, "wide", peer)

    def cot_start(k, carry):
        cot_copy(k).start()
        return carry

    def cot_step(k, carry):
        cot_block(k)
        cot_copy(k).start()
        return carry

    lax.fori_loop(wide_n // 2, wide_n, cot_start, 0)
    lax.fori_loop(1, wide_n // 2, cot_step, 0)
    cot_block(0)
    cot_own = pltpu.make_async_copy(cotsend.at[0], cotrows_any.at[0], outsem.at[2])
    cot_own.start()

    gain = gain_a_ref[...].astype(f32).reshape(1, width)
    own.wait()
    for copy in qkv_loads:
        copy.wait()
    for k in range(parts):
        src = flipped(n, k, parts)
        if k > 0:
            tok_copy(k).wait_recv()
        x = tokbuf[src].reshape(seqs * span, width).astype(f32)
        normed = (x * inverse_rms(x) * gain).astype(bf16)
        shape = (seqs, span, width)
        q_ref[src] = (dot(normed, wq_ref[...]) * LOG2E).astype(bf16).reshape(shape)
        k_ref[src] = dot(normed, wk_ref[...]).astype(bf16).reshape(shape)
        v_ref[src] = dot(normed, wv_ref[...]).astype(bf16).reshape(shape)
    outs = [
        pltpu.make_async_copy(a, b, outsem.at[i])
        for a, b, i in (
            (tokbuf, tokseq_any, 3), (q_ref, q_any, 4), (k_ref, k_any, 5), (v_ref, v_any, 6),
        )
    ]
    for copy in outs:
        copy.start()

    buckets, offsets = bias_ref.shape[1], table_ref.shape[0]
    ids = lax.broadcasted_iota(jnp.int32, (buckets, offsets), 0)
    found = (ids == table_ref[...].reshape(1, offsets)).astype(f32).astype(bf16)
    hot_ref[...] = jnp.zeros_like(hot_ref)
    hot_ref[:, :offsets] = found
    diag_ref[:heads, :] = dot(bias_ref[...], hot_ref[...]) * LOG2E

    low, masks = half_masks(128)
    lane = lax.broadcasted_iota(jnp.int32, (1, 128), 1)
    hot = [(lane == 64).astype(f32).astype(bf16), (lane == 0).astype(f32).astype(bf16)]
    for hh in range(2):
        ones = jnp.broadcast_to(masks[hh], (total, 128))
        vext[hh * total : (hh + 1) * total, 128:] = ones

    def att_copy(k, lanes):
        peer = flipped(n, k, parts)
        return remote(
            attseq.at[peer, :, :, lanes], attpos.at[n, :, :, lanes], attsem, k, "narrow", peer
        )

    def one_pair(pair, carry):
        lanes = pl.ds(pl.multiple_of(pair * 128, 128), 128)
        for hh in range(2):
            row = diag_ref[pl.ds(2 * pair + hh, 1), :]
            strip_ref[hh] = pltpu.roll(
                jnp.broadcast_to(row, (span, table)), table - span + 1, 1, stride=1, stride_axis=0
            )

        def one_sequence(s, inner):
            vp = v_ref[:, s, :, lanes].reshape(total, 128)
            kp = k_ref[:, s, :, lanes].reshape(total, 128).astype(f32)
            ids = lax.broadcasted_iota(jnp.int32, (total, 128), 0)
            push = jnp.where(ids < lens_ref[n * seqs + s], 0.0, -1e30)
            for hh in range(2):
                vext[hh * total : (hh + 1) * total, :128] = vp * masks[hh]
                kext[hh] = jnp.where(lane == 64 - 64 * hh, push, kp).astype(bf16)

            @pl.when(pair > 0)
            def _():
                pltpu.make_async_copy(pbuf.at[s], p_any.at[pair, s], psem.at[s]).wait()

            for block in range(parts // 2):
                rows = slice(block * 2 * span, (block + 1) * 2 * span)
                both = slice(2 * block, 2 * block + 2)
                qp = q_ref[both, s, :, lanes].reshape(2 * span, 128)
                for hh in range(2):
                    bias = jnp.concatenate(
                        [
                            strip_ref[hh, :, (parts - 1 - r) * span : (parts - 1 - r) * span + total]
                            for r in (2 * block, 2 * block + 1)
                        ],
                        axis=0,
                    )
                    scores = dot(qp * masks[hh] + hot[hh], kext[hh], NT) + bias
                    raised = jnp.exp2(scores - jnp.max(scores, axis=-1, keepdims=True))
                    pbuf[s, rows, hh * total : (hh + 1) * total] = raised.astype(bf16)
                mixed = dot(pbuf[s, rows, :], vext[...])
                inv = 1.0 / mixed[:, 128:]
                invl_ref[both, s, :, lanes] = inv.astype(bf16).reshape(2, span, 128)
                attseq[both, s, :, lanes] = (mixed[:, :128] * inv).astype(bf16).reshape(2, span, 128)
            pltpu.make_async_copy(pbuf.at[s], p_any.at[pair, s], psem.at[s]).start()
            return inner

        lax.fori_loop(0, seqs, one_sequence, 0)
        for k in range(parts - 1, 0, -1):
            att_copy(k, lanes).start()
        return carry

    lax.fori_loop(0, pairs, one_pair, 0)
    for a, b, i in ((invl_ref, invl_any, 7), (attseq, attseq_any, 11)):
        copy = pltpu.make_async_copy(a, b, outsem.at[i])
        copy.start()
        outs.append(copy)
    position.wait()
    wo_load.wait()
    gain = gain_e_ref[...].astype(f32).reshape(1, width)
    for k in range(parts):
        src = flipped(n, k, parts)
        if k > 0:
            att_copy(k, slice(None)).wait_recv()
            att = attpos[src].reshape(seqs * span, width)
        else:
            attpos[src] = attseq[src]
            att = attseq[src].reshape(seqs * span, width)
        rows = pl.ds(pl.multiple_of(src * seqs * span, seqs * span), seqs * span)
        hidden = tokpos[src].reshape(seqs * span, width).astype(f32) + dot(att, wo_ref[...])
        hid_ref[rows, :] = hidden
        copy = pltpu.make_async_copy(hid_ref.at[rows], hid_any.at[rows], outsem.at[12 + k])
        copy.start()
        outs.append(copy)
        routed_ref[rows, :] = (hidden * inverse_rms(hidden) * gain).astype(bf16)
    for a, b, i in ((attpos, att_any, 8), (routed_ref, routed_any, 10)):
        copy = pltpu.make_async_copy(a, b, outsem.at[i])
        copy.start()
        outs.append(copy)
    for k in range(1, parts):
        tok_copy(k).wait_send()
        att_copy(k, slice(None)).wait_send()
    for s in range(seqs):
        pltpu.make_async_copy(pbuf.at[s], p_any.at[0, s], psem.at[s]).wait()
    cot_own.wait()

    def cot_wait(k, carry):
        cot_copy(k).wait()
        return carry

    lax.fori_loop(1, wide_n, cot_wait, 0)
    for copy in outs:
        copy.wait()


def forward(args, wide_n, capacity, cap, quad, table):
    parts, seqs, span, width = quad
    heads, buckets = args[5].shape
    pairs = heads // 2
    total = parts * span
    tokens = parts * seqs * span
    shapes = [
        (quad, bf16), (quad, bf16), (quad, bf16), ((tokens, width), f32), ((tokens, width), bf16),
        ((wide_n, cap, width), bf16), (quad, bf16), (quad, bf16), (quad, bf16), (quad, bf16),
        ((pairs, seqs, total, 2 * total), bf16),
    ]
    small = [((1, tokens), jnp.int32), ((tokens, 1), jnp.int32), ((buckets, table), bf16)]
    return pl.pallas_call(
        functools.partial(forward_kernel, wide_n, capacity),
        in_specs=[pl.BlockSpec(memory_space=pltpu.SMEM), hbm(), hbm()] + [vmem()] * 5 + [hbm()] * 4,
        out_specs=[hbm()] * len(shapes) + [vmem()] * 3,
        out_shape=[jax.ShapeDtypeStruct(*item) for item in shapes + small],
        scratch_shapes=[
            pltpu.VMEM(quad, bf16),
            pltpu.VMEM(quad, bf16),
            pltpu.VMEM(quad, bf16),
            pltpu.VMEM(quad, bf16),
            pltpu.VMEM(quad, bf16),
            pltpu.VMEM(quad, bf16),
            pltpu.VMEM(quad, bf16),
            pltpu.VMEM(quad, bf16),
            pltpu.VMEM((tokens, width), f32),
            pltpu.VMEM((tokens, width), bf16),
            pltpu.VMEM((wide_n, cap, width), bf16),
            pltpu.VMEM((2, span, table), f32),
            pltpu.VMEM((seqs, total, 2 * total), bf16),
            pltpu.VMEM((2 * total, 256), bf16),
            pltpu.VMEM((2, total, 128), bf16),
            pltpu.VMEM((16, table), f32),
            pltpu.VMEM((tokens, width), bf16),
            *[pltpu.VMEM((width, width), bf16)] * 4,
            pltpu.SemaphoreType.DMA((5,)),
            pltpu.SemaphoreType.DMA((2, parts)),
            pltpu.SemaphoreType.DMA((2, parts)),
            pltpu.SemaphoreType.DMA((2, wide_n)),
            pltpu.SemaphoreType.DMA((seqs,)),
            pltpu.SemaphoreType.DMA((16,)),
        ],
        compiler_params=params(collective_id=1, has_side_effects=True),
        name="forward",
    )(*args)


def expert_kernel(
    experts, chunks, split, routed_ref, slot_ref, router_ref, cot_any, win_any, wout_any,
    res_any, back_any, gin_any, ginfar_any, ginsend_any, gout_any, goutsend_any, grouter_ref,
    send_ref, recv_ref, cot_ref, push_ref, win_ref, wout_ref, act_ref, pg_ref, res_ref,
    acc_res, acc_back, nearin_ref, nearout_ref, wr_ref, sendsem, backsem, sem, gradsem,
):
    wide_n, cap, width = send_ref.shape
    units = win_ref.shape[1]
    tile = 512
    w = lax.axis_index("wide")
    per = wide_n // chunks
    chunk_rows = per * cap
    loads = [
        pltpu.make_async_copy(a, b, sem.at[i])
        for i, (a, b) in enumerate(((cot_any, cot_ref), (win_any, win_ref), (wout_any, wout_ref)))
    ]
    for copy in loads:
        copy.start()
    expected = greet(4, wide_n)

    def send_copy(k):
        return remote(
            send_ref.at[k], recv_ref.at[k], sendsem, k, "wide", flipped(w, k, wide_n)
        )

    def back_copy(k):
        return remote(
            cot_ref.at[k], back_any.at[w], backsem, k, "wide", flipped(w, k, wide_n)
        )

    def turn(i):
        return (i % 2) * 2 + i // 2

    last = wide_n // 2 - 1
    inner = ((w // 2) % last + last - 1) // last

    def order(i):
        return i + inner * (turn(i) - i)

    def make_rows(i, carry):
        k = turn(i // per) * per + i % per
        pick = expert_pick(flipped(w, k, wide_n), cap, slot_ref[...])
        send_ref[k] = dot(pick, routed_ref[...]).astype(bf16)
        return carry

    def send_rows(i, carry):
        send_copy(turn(i // per) * per + i % per).start()
        return carry

    def send_step(i, carry):
        return send_rows(i, make_rows(i, carry))

    lax.fori_loop(1, wide_n // 2, make_rows, 0)
    pl.semaphore_wait(pltpu.get_barrier_semaphore(), expected)
    lax.fori_loop(1, wide_n // 2, send_rows, 0)
    lax.fori_loop(wide_n // 2, wide_n, send_step, 0)
    pick = expert_pick(w, cap, slot_ref[...])
    recv_ref[0] = dot(pick, routed_ref[...]).astype(bf16)
    for copy in loads:
        copy.wait()
    router = router_ref[...].astype(f32)
    blank = jnp.zeros((wr_ref.shape[0] - experts, width), f32)
    wr_ref[...] = jnp.concatenate([router, blank], axis=0).astype(bf16)
    lane = lax.broadcasted_iota(jnp.int32, (1, wr_ref.shape[0]), 1)
    hot = lane == w
    c0 = 0.7978845608028654
    c1 = c0 * 0.044715
    grouter_ref[...] = jnp.zeros_like(grouter_ref)

    def give(first):
        def one(j, carry):
            @pl.when(first + j > 0)
            def _():
                back_copy(first + j).start()

            return carry

        return one

    def one_chunk(step, carry):
        chunk = order(step)
        first = chunk * per

        def arrive(j, inner):
            @pl.when(first + j > 0)
            def _():
                send_copy(first + j).wait_recv()

            return inner

        lax.fori_loop(0, per, arrive, 0)

        @pl.when(inner * (step + 1) == chunks)
        def _():
            for earlier in (2, 1, 0):
                lax.fori_loop(0, per, give(earlier * per), 0)

        sources = pl.ds(first, per)
        here = pl.ds(pl.multiple_of(chunk * chunk_rows, chunk_rows), chunk_rows)
        x = recv_ref[sources].reshape(chunk_rows, width)
        cot = cot_ref[sources].reshape(chunk_rows, width).astype(f32)
        logits = jnp.where(lane < experts, dot(x, wr_ref[...], NT), -1e30)
        raised = jnp.exp(logits - jnp.max(logits, axis=-1, keepdims=True))
        probs = raised * (1.0 / jnp.sum(raised, axis=-1, keepdims=True))
        gate = jnp.sum(jnp.where(hot, probs, 0.0), axis=-1, keepdims=True)
        push_ref[here, :] = (gate * cot).astype(bf16)
        acc_res[...] = jnp.zeros_like(acc_res)
        acc_back[...] = jnp.zeros_like(acc_back)

        def hidden_tile(t, inner):
            cols = pl.ds(pl.multiple_of(t * tile, tile), tile)
            pre = dot(recv_ref[sources].reshape(chunk_rows, width), win_ref[:, cols])
            ag = dot(push_ref[here, :], wout_ref[cols, :], NT)
            sq = pre * pre
            th = jnp.tanh(pre * (c0 + c1 * sq))
            half = 0.5 + 0.5 * th
            act = (pre * half).astype(bf16)
            slope = half + pre * (0.5 - 0.5 * th * th) * (c0 + 3.0 * c1 * sq)
            pg = (ag * slope).astype(bf16)
            act_ref[here, cols] = act
            pg_ref[here, cols] = pg
            acc_res[...] += dot(act, wout_ref[cols, :])
            acc_back[...] += dot(pg, win_ref[:, cols], NT)
            return inner

        lax.fori_loop(0, units // tile, hidden_tile, 0)
        result = acc_res[...].astype(bf16).astype(f32)
        res_ref[sources] = (gate * result).astype(bf16).reshape(per, cap, width)
        gate_grad = jnp.sum(cot * result, axis=-1, keepdims=True)
        logit_grad = probs * (jnp.where(hot, gate_grad, 0.0) - gate * gate_grad)
        logit_grad = logit_grad.astype(bf16)
        back = acc_back[...].astype(bf16).astype(f32) + dot(logit_grad, wr_ref[...])
        cot_ref[sources] = back.astype(bf16).reshape(per, cap, width)
        grouter_ref[...] += dot(x, logit_grad, TN)

        @pl.when(step == chunks - 1)
        def _():
            lax.fori_loop(0, per, give(first), 0)

        @pl.when((1 - inner) * (step + 1) == chunks)
        def _():
            for earlier in (2, 1, 0):
                lax.fori_loop(0, per, give(earlier * per), 0)

        return carry

    lax.fori_loop(0, chunks, one_chunk, 0)
    own = pltpu.make_async_copy(cot_ref.at[0], back_any.at[w], sem.at[0])
    own.start()
    res_copy = pltpu.make_async_copy(res_ref, res_any, sem.at[1])
    res_copy.start()

    n = lax.axis_index("narrow")
    core, half = n % 2, n // 2
    in_rows, out_rows = width // 4, units // 4

    def slice_at(index, rows):
        return pl.ds(pl.multiple_of(index * rows, rows), rows)

    def near_copy(ref, near, rows, side, i, cols=slice(None)):
        return link(
            ref.at[slice_at(2 * side + 1 - core, rows), cols], near.at[side, :, cols],
            gradsem.at[0, i + side], gradsem.at[1, i + side], "narrow", flipped(n, 1, 4),
        )

    def near_add(ref, near, rows, side, i, cols=slice(None)):
        near_copy(ref, near, rows, side, i, cols).wait()
        at = slice_at(2 * side + core, rows)
        ref[at, cols] = (ref[at, cols].astype(f32) + near[side, :, cols].astype(f32)).astype(bf16)
        return at

    early, late = slice(0, split), slice(split, units)
    gin_far = link(
        win_ref.at[slice_at(2 * (1 - half) + core, in_rows), early], ginfar_any,
        gradsem.at[0, 6], gradsem.at[1, 6], "narrow", flipped(n, 2, 4),
    )

    def in_tile(t, carry):
        cols = pl.ds(pl.multiple_of(t * tile, tile), tile)
        win_ref[:, cols] = dot(
            recv_ref[...].reshape(wide_n * cap, width), pg_ref[:, cols], TN
        ).astype(bf16)

        @pl.when(t == split // tile - 1)
        def _():
            for side in range(2):
                near_copy(win_ref, nearin_ref, in_rows, side, 0, early).start()

        return carry

    def out_tile(t, carry):
        cols = pl.ds(pl.multiple_of(t * tile, tile), tile)
        wout_ref[cols, :] = dot(act_ref[:, cols], push_ref[...], TN).astype(bf16)

        @pl.when(t == 1)
        def _():
            near_add(win_ref, nearin_ref, in_rows, 1 - half, 0, early)
            gin_far.start()

        return carry

    lax.fori_loop(0, units // tile, in_tile, 0)
    for side in range(2):
        near_copy(win_ref, nearin_ref, in_rows, side, 4, late).start()
    lax.fori_loop(0, units // tile, out_tile, 0)
    for side in range(2):
        near_copy(wout_ref, nearout_ref, out_rows, side, 2).start()
    near_add(win_ref, nearin_ref, in_rows, half, 0, early)
    at = near_add(win_ref, nearin_ref, in_rows, half, 4, late)
    ends = [pltpu.make_async_copy(win_ref.at[at], gin_any, sem.at[2])]
    at = near_add(win_ref, nearin_ref, in_rows, 1 - half, 4, late)
    ends.append(pltpu.make_async_copy(win_ref.at[at, late], ginsend_any, sem.at[5]))
    at = near_add(wout_ref, nearout_ref, out_rows, 1 - half, 2)
    ends.append(pltpu.make_async_copy(wout_ref.at[at], goutsend_any, sem.at[3]))
    at = near_add(wout_ref, nearout_ref, out_rows, half, 2)
    ends.append(pltpu.make_async_copy(wout_ref.at[at], gout_any, sem.at[4]))
    for copy in ends:
        copy.start()

    def finish_step(k, carry):
        send_copy(k).wait_send()
        back_copy(k).wait()
        return carry

    lax.fori_loop(1, wide_n, finish_step, 0)
    own.wait()
    res_copy.wait()
    gin_far.wait()
    for copy in ends:
        copy.wait()


def run_experts(routed, slot_row, wr, cot_rows, win, wout, experts):
    wide_n, cap, width = cot_rows.shape
    units = win.shape[1]
    chunks, split = 4, 2 * units // 3
    slots = wide_n * cap
    block = (wide_n, cap, width)
    step = slots // chunks
    return pl.pallas_call(
        functools.partial(expert_kernel, experts, chunks, split),
        in_specs=[vmem()] * 3 + [hbm()] * 3,
        out_specs=[hbm()] * 7 + [vmem()],
        out_shape=[
            jax.ShapeDtypeStruct(block, bf16),
            jax.ShapeDtypeStruct(block, bf16),
            jax.ShapeDtypeStruct((width // 4, units), bf16),
            jax.ShapeDtypeStruct((width // 4, split), bf16),
            jax.ShapeDtypeStruct((width // 4, units - split), bf16),
            jax.ShapeDtypeStruct((units // 4, width), bf16),
            jax.ShapeDtypeStruct((units // 4, width), bf16),
            jax.ShapeDtypeStruct((width, 128), f32),
        ],
        scratch_shapes=[
            pltpu.VMEM(block, bf16),
            pltpu.VMEM(block, bf16),
            pltpu.VMEM(block, bf16),
            pltpu.VMEM((slots, width), bf16),
            pltpu.VMEM((width, units), bf16),
            pltpu.VMEM((units, width), bf16),
            pltpu.VMEM((slots, units), bf16),
            pltpu.VMEM((slots, units), bf16),
            pltpu.VMEM(block, bf16),
            pltpu.VMEM((step, width), f32),
            pltpu.VMEM((step, width), f32),
            pltpu.VMEM((2, width // 4, units), bf16),
            pltpu.VMEM((2, units // 4, width), bf16),
            pltpu.VMEM((128, width), bf16),
            pltpu.SemaphoreType.DMA((2, wide_n)),
            pltpu.SemaphoreType.DMA((2, wide_n)),
            pltpu.SemaphoreType.DMA((6,)),
            pltpu.SemaphoreType.DMA((2, 7)),
        ],
        compiler_params=params(collective_id=2, has_side_effects=True),
        name="experts",
    )(routed, slot_row, wr, cot_rows, win, wout)


def link(src, dst, send_sem, recv_sem, axis, peer):
    return pltpu.make_async_remote_copy(
        src_ref=src,
        dst_ref=dst,
        send_sem=send_sem,
        recv_sem=recv_sem,
        device_id={axis: peer},
        device_id_type=MESH,
    )


def padded(v):
    return -(-v // 16) * 16


class Sums:
    REFS = 8

    def __init__(self, wide_n, refs, sems):
        (
            self.terms, self.near, self.mine, self.half_in, self.quarter_in, self.piece_in,
            self.cross_in, self.whole,
        ) = refs
        self.narrow_sem, self.pair_sem, self.piece_sem, self.back_sem = sems
        self.wide_n = wide_n
        self.n, self.w = lax.axis_index("narrow"), lax.axis_index("wide")
        self.core, self.side = self.n % 2, self.n // 2
        self.ranks, slices, self.piece, _ = self.piece_in.shape
        self.direct = slices == 1
        self.cut = 1 if self.direct else 4
        self.rank = self.w // self.cut
        _, self.blocks, self.rows, _ = self.terms.shape
        self.total = self.mine.shape[1]

    def near_copy(self, side):
        return link(
            self.terms.at[2 * side + 1 - self.core], self.near.at[side],
            self.narrow_sem.at[0, side], self.narrow_sem.at[1, side],
            "narrow", flipped(self.n, 1, 4),
        )

    def cross_copy(self):
        if self.direct:
            source = self.terms.at[2 * (1 - self.side) + self.core]
        else:
            source = self.mine.at[1 - self.side, self.piece_at(self.rank)]
        return link(
            source, self.cross_in,
            self.narrow_sem.at[0, 2], self.narrow_sem.at[1, 2], "narrow", flipped(self.n, 2, 4),
        )

    def part_at(self, level, other):
        first, second = self.w % 2, (self.w // 2) % 2
        if level == 1:
            size, index = self.total // 2, first + other * (1 - 2 * first)
        else:
            size, index = self.total // 4, 2 * first + second + other * (1 - 2 * second)
        return pl.ds(pl.multiple_of(index * size, 16), size)

    def piece_at(self, rank):
        base = 0
        if not self.direct:
            base = (2 * (self.w % 2) + (self.w // 2) % 2) * (self.total // 4)
        return pl.ds(pl.multiple_of(base + rank * self.piece, 16), self.piece)

    def pair_copy(self, level):
        return link(
            self.mine.at[:, self.part_at(level, 1)],
            self.half_in if level == 1 else self.quarter_in,
            self.pair_sem.at[0, level - 1], self.pair_sem.at[1, level - 1],
            "wide", flipped(self.w, level, self.wide_n),
        )

    def peer(self, rank):
        return rank * self.cut + self.w % self.cut

    def piece_copy(self, k):
        rank = flipped(self.rank, k, self.ranks)
        return link(
            self.mine.at[:, self.piece_at(rank)], self.piece_in.at[k],
            self.piece_sem.at[0, k], self.piece_sem.at[1, k], "wide", self.peer(rank),
        )

    def piece_back(self, k):
        at = self.piece_at(self.rank)
        return link(
            self.whole.at[at], self.whole.at[at], self.back_sem.at[0, k], self.back_sem.at[1, k],
            "wide", self.peer(flipped(self.rank, k, self.ranks)),
        )

    def pair_back(self, level):
        at = self.part_at(level, 0)
        return link(
            self.whole.at[at], self.whole.at[at],
            self.pair_sem.at[0, level + 1], self.pair_sem.at[1, level + 1],
            "wide", flipped(self.w, level, self.wide_n),
        )

    def each(self, f):
        def step(k, carry):
            f(k)
            return carry

        lax.fori_loop(1, self.ranks, step, 0)

    def start(self):
        for side in (0, 1):
            self.near_copy(side).start()

    def near_total(self, side):
        self.near_copy(side).wait()
        return self.terms[2 * side + self.core].astype(f32) + self.near[side].astype(f32)

    def place(self, i, total):
        rows = self.blocks * self.rows
        self.mine[i, 0:rows] = total.astype(bf16).reshape(rows, 128)

    def to_far(self):
        total = self.near_total(1 - self.side)
        self.terms[2 * (1 - self.side) + self.core] = total.astype(bf16)
        self.cross_copy().start()

    def to_half(self):
        if self.direct:
            total = self.near_total(self.side)
            self.cross_copy().wait()
            self.place(0, total + self.cross_in[...].astype(f32))
            self.each(lambda k: self.piece_copy(k).start())
        else:
            for side in (0, 1):
                self.place(side, self.near_total(side))
            self.pair_copy(1).start()

    def take(self, level, ref):
        self.pair_copy(level).wait()
        at = self.part_at(level, 0)
        total = self.mine[:, at].astype(f32) + ref[...].astype(f32)
        self.mine[:, at] = total.astype(bf16)

    def to_quarter(self):
        self.take(1, self.half_in)
        self.pair_copy(2).start()

    def to_piece(self):
        self.take(2, self.quarter_in)
        self.each(lambda k: self.piece_copy(k).start())

    def pieces_total(self):
        self.each(lambda k: self.piece_copy(k).wait())

        def add(k, total):
            return total + self.piece_in[k].astype(f32)

        at = self.piece_at(self.rank)
        return lax.fori_loop(1, self.ranks, add, self.mine[:, at].astype(f32))

    def to_cross(self):
        self.mine[:, self.piece_at(self.rank)] = self.pieces_total().astype(bf16)
        self.cross_copy().start()

    def back_piece(self):
        at = self.piece_at(self.rank)
        if self.direct:
            total = self.pieces_total()[0]
        else:
            self.cross_copy().wait()
            total = self.mine[self.side, at].astype(f32) + self.cross_in[...].astype(f32)
        self.whole[at] = total.astype(bf16)
        self.each(lambda k: self.piece_back(k).start())

    def back_quarter(self):
        self.each(lambda k: self.piece_back(k).wait())
        self.pair_back(2).start()

    def back_half(self):
        self.pair_back(2).wait()
        self.pair_back(1).start()

    def finish(self):
        if self.direct:
            self.each(lambda k: self.piece_back(k).wait())
        else:
            self.pair_back(1).wait()

    def block(self, b):
        return self.whole[b * self.rows : (b + 1) * self.rows, :]

    @staticmethod
    def scratch(blocks, rows, wide_n, slices):
        cut = 1 if slices == 1 else 4
        ranks = wide_n // cut
        piece = padded(-(-blocks * rows // wide_n))
        total = wide_n * piece
        return [
            pltpu.VMEM((4, blocks, rows, 128), bf16),
            pltpu.VMEM((2, blocks, rows, 128), bf16),
            pltpu.VMEM((slices, total, 128), bf16),
            pltpu.VMEM((slices, 16 if slices == 1 else total // 2, 128), bf16),
            pltpu.VMEM((slices, 16 if slices == 1 else total // 4, 128), bf16),
            pltpu.VMEM((ranks, slices, piece, 128), bf16),
            pltpu.VMEM((blocks, rows, 128) if slices == 1 else (piece, 128), bf16),
            pltpu.VMEM((total, 128), bf16),
        ], [
            pltpu.SemaphoreType.DMA((2, 3)),
            pltpu.SemaphoreType.DMA((2, 4)),
            pltpu.SemaphoreType.DMA((2, ranks)),
            pltpu.SemaphoreType.DMA((2, ranks)),
        ]


GROUPS = ((0, 6), (0, 2), (2, 4), (4, 5), (5, 6))


def backward_kernel(
    wide_n, experts, back_any, slot_ref, hid_any, cot_any, att_any, attseq_any, p_any, invl_any,
    q_any, k_any, v_any, tok_any, res_any, wo_any, wq_any, wk_any, wv_any, gain_a_ref, gain_e_ref,
    router_ref, hot_ref, gin_any, gout_any,
    out_any, hgrad_any, part_any, big_any, small_any, resland_any, ginfar_any, goutfar_any,
    back_ref, hid_ref, cot_ref, attseq_ref, invl_ref, q_ref, k_ref, v_ref, tok_ref,
    agsend, agbuf, turned_ref, dk_ref, dv_ref, pbuf, acc_ref, diag_ref,
    kmask_ref, vext_ref, ds_ref, gains_ref, smallout, wo_ref, wq_ref, wk_ref, wv_ref, loadsem, psem, agsem, partsem,
    ressem, gradsem, weightsem, *rest,
):
    parts, seqs, span, width = tok_ref.shape
    total = parts * span
    block_rows = seqs * span
    pairs = width // 128
    slots = back_ref.shape[0] * back_ref.shape[1]
    rows_n = width // parts
    n, w = lax.axis_index("narrow"), lax.axis_index("wide")
    count = len(GROUPS)
    per = Sums.REFS
    group = [
        Sums(
            wide_n,
            rest[per * i : per * i + per],
            rest[per * count + 4 * i : per * count + 4 * i + 4],
        )
        for i in range(count)
    ]
    folds = 4 if experts <= 16 else 1
    fold_rows = rows_n // folds
    gain_lane = 30 if folds == 4 else 126
    small_terms, small_near, small_mine, small_in, small_sem, small_wide_sem = rest[
        per * count + 4 * count :
    ]

    def small_copy(k):
        peer = flipped(n, k, parts)
        return remote(small_terms.at[peer], small_near.at[k], small_sem, k, "narrow", peer)

    def small_wide(k):
        peer = flipped(w, k, wide_n)
        return remote(small_mine, small_in.at[k], small_wide_sem, k, "wide", peer)

    loads = [
        pltpu.make_async_copy(a, b, loadsem.at[i])
        for i, (a, b) in enumerate(
            (
                (back_any, back_ref), (hid_any, hid_ref), (cot_any, cot_ref), (att_any, k_ref),
                (attseq_any, attseq_ref), (invl_any, invl_ref), (q_any, q_ref), (v_any, v_ref),
                (tok_any, tok_ref),
            )
        )
    ]
    wo_load, *qkv_loads = [
        pltpu.make_async_copy(a, b, weightsem.at[i])
        for i, (a, b) in enumerate(
            ((wo_any, wo_ref), (wq_any, wq_ref), (wk_any, wk_ref), (wv_any, wv_ref))
        )
    ]
    for copy in (*loads[:3], wo_load, *loads[3:], *qkv_loads):
        copy.start()

    def block_of(phase):
        return n // 2 + phase * (1 - 2 * (n // 2))

    def step_of(i):
        late = i // 8
        phase = (1 - late) * (i // 4) + late * (i % 2)
        return phase, (1 - late) * (i % 4) + late * (i // 2)

    def p_copy(i):
        phase, pair = step_of(i)
        at = pl.ds(pl.multiple_of(block_of(phase) * 2 * span, 2 * span), 2 * span)
        return pltpu.make_async_copy(p_any.at[pair, :, at], pbuf.at[i % 2], psem.at[i % 2])

    out_half = gout_any.shape[0] // 2
    grad_copies = [
        link(a, b, gradsem.at[0, i], gradsem.at[1, i], "narrow", flipped(n, 2, parts))
        for i, (a, b) in enumerate(
            (
                (gin_any, ginfar_any),
                (gout_any.at[:out_half], goutfar_any.at[:out_half]),
                (gout_any.at[out_half:], goutfar_any.at[out_half:]),
            )
        )
    ]
    p_copy(0).start()
    expected = greet(parts, wide_n)

    def res_copy(k):
        return remote(
            res_any.at[k], resland_any.at[w], ressem, k, "wide", flipped(w, k, wide_n)
        )

    def res_start(k, carry):
        res_copy(k).start()
        return carry

    res_own = pltpu.make_async_copy(res_any.at[0], resland_any.at[w], loadsem.at[10])

    def ag_copy(k):
        peer = flipped(n, k, parts)
        return remote(agsend.at[peer], agbuf.at[n], agsem, k, "narrow", peer)

    def rows_of(src):
        return pl.ds(pl.multiple_of(src * block_rows, block_rows), block_rows)

    def picked(rows):
        ids = lax.broadcasted_iota(jnp.int32, (block_rows, slots), 1)
        pick = (ids == slot_ref[rows, :]).astype(f32).astype(bf16)
        return dot(pick, back_ref[...].reshape(slots, width))

    gain_a = gain_a_ref[...].astype(f32).reshape(1, width)
    gain_e = gain_e_ref[...].astype(f32).reshape(1, width)
    gains_ref[...] = jnp.zeros_like(gains_ref)
    for copy in (*loads[:3], wo_load):
        copy.wait()
    for k in range(parts - 1, -1, -1):
        src = flipped(n, k, parts)
        rows = rows_of(src)
        upstream = picked(rows)
        hidden = hid_ref[rows, :]
        inv = inverse_rms(hidden)
        scaled = upstream * gain_e
        inner = jnp.mean(scaled * hidden, axis=-1, keepdims=True)
        grad = cot_ref[rows, :].astype(f32) + inv * scaled - hidden * (inv * inv * inv * inner)
        gains_ref[1:2, :] += jnp.sum(upstream * hidden * inv, axis=0, keepdims=True)
        hid_ref[rows, :] = grad
        grad = grad.astype(bf16)
        cot_ref[rows, :] = grad
        grad = dot(grad, wo_ref[...], NT).astype(bf16).reshape(seqs, span, width)
        if k == parts - 1:
            pl.semaphore_wait(pltpu.get_barrier_semaphore(), expected)
        if k > 0:
            agsend[src] = grad
            ag_copy(k).start()
        else:
            agbuf[src] = grad
        if k == parts - 1:
            lax.fori_loop(1, wide_n, res_start, 0)
            res_own.start()
    for copy in grad_copies[:2]:
        copy.start()
    hid_copy = pltpu.make_async_copy(hid_ref, hgrad_any, loadsem.at[1])
    hid_copy.start()
    loads[3].wait()
    for h in range(2):
        cols = slice(h * 2 * rows_n, (h + 1) * 2 * rows_n)
        grad = dot(k_ref[...].reshape(parts * block_rows, width)[:, cols], cot_ref[...], TN)
        grad = grad.astype(bf16)
        for t in range(2):
            for b in range(pairs):
                group[0].terms[2 * h + t, b] = grad[
                    t * rows_n : (t + 1) * rows_n, b * 128 : (b + 1) * 128
                ]
    k_copy = pltpu.make_async_copy(k_any, k_ref, loadsem.at[9])
    k_copy.start()
    group[0].start()
    for copy in loads[4:]:
        copy.wait()
    for b in range(parts):
        x = tok_ref[b].reshape(block_rows, width).astype(f32)
        normed = x * inverse_rms(x) * gain_a
        turned_ref[:, b * block_rows : (b + 1) * block_rows] = normed.T.astype(bf16)
    diag_ref[...] = jnp.zeros_like(diag_ref)

    low, masks = half_masks(128)
    lane = lax.broadcasted_iota(jnp.int32, (1, 128), 1)
    strip = (parts + 2) * span

    def attention_pair(phase, pair, i):
        slot = i % 2
        block = block_of(phase)
        both = pl.ds(2 * block, 2)
        lanes = pl.ds(pl.multiple_of(pair * 128, 128), 128)
        p_copy(i).wait()

        @pl.when(i + 1 < 2 * pairs)
        def _():
            p_copy(i + 1).start()

        for s in range(seqs):
            kp = k_ref[:, s, :, lanes].reshape(total, 128)
            vp = v_ref[:, s, :, lanes].reshape(total, 128)
            for hh in range(2):
                ones = (lane // 2 == 32 - 32 * hh).astype(f32)
                kmask_ref[hh * total : (hh + 1) * total, :] = kp * masks[hh]
                vext_ref[hh] = jnp.where(ones > 0, ones, vp.astype(f32)).astype(bf16)
            dk = [0.0, 0.0]
            dv = [0.0, 0.0]
            qp = q_ref[both, s, :, lanes].reshape(2 * span, 128)
            inv = invl_ref[both, s, :, lanes].reshape(2 * span, 128).astype(f32)
            gp = agbuf[both, s, :, lanes].reshape(2 * span, 128).astype(f32)
            gp = (gp * inv).astype(bf16)
            gf = gp.astype(f32)
            agree = gf * attseq_ref[both, s, :, lanes].reshape(2 * span, 128).astype(f32)
            for hh in range(2):
                side = low if hh == 0 else ~low
                delta = -jnp.sum(jnp.where(side, agree, 0.0), axis=-1, keepdims=True)
                high = delta.astype(bf16).astype(f32)
                ext = jnp.where(lane == 64 - 64 * hh, high, 0.0)
                ext = jnp.where(lane == 65 - 64 * hh, delta - high, ext)
                ext = jnp.where(side, gf, ext).astype(bf16)
                raised = pbuf[slot, s, :, hh * total : (hh + 1) * total]
                score_grad = raised.astype(f32) * dot(ext, vext_ref[hh], NT)
                if s == 0:
                    acc_ref[hh] = score_grad
                else:
                    acc_ref[hh] += score_grad
                score_grad = score_grad.astype(bf16)
                ds_ref[:, hh * total : (hh + 1) * total] = score_grad
                dk[hh] = dot(qp, score_grad, TN)
                dv[hh] = dot(gp, raised, TN)
            dq = dot(ds_ref[...], kmask_ref[...])
            q_ref[both, s, :, lanes] = dq.astype(bf16).reshape(2, span, 128)
            upper = lax.broadcasted_iota(jnp.int32, (128, 1), 0) < 64
            dk = jnp.where(upper, dk[0], dk[1]) * (1.0 / LOG2E)
            dv = jnp.where(upper, dv[0], dv[1])
            here = slice(s * total, (s + 1) * total)
            if phase == 0:
                dk_ref[lanes, here] = dk
                dv_ref[lanes, here] = dv
            else:
                dk = (dk + dk_ref[lanes, here]).T
                dv = (dv + dv_ref[lanes, here]).T
                k_ref[:, s, :, lanes] = dk.astype(bf16).reshape(parts, span, 128)
                v_ref[:, s, :, lanes] = dv.astype(bf16).reshape(parts, span, 128)
        base = pl.multiple_of((parts - 2 - 2 * block) * span, span)
        for hh in range(2):
            upper, lower = acc_ref[hh, :span, :], acc_ref[hh, span:, :]
            zero = jnp.zeros((span, span), f32)
            upper = jnp.concatenate([zero, upper, zero], axis=1)
            lower = jnp.concatenate([lower, zero, zero], axis=1)
            both_rows = upper + lower
            small_sum = jnp.zeros((8, strip), f32)
            for a in range(span // 8):
                shift = span - 8 - 8 * a
                rows8 = both_rows[8 * a : 8 * a + 8]
                small_sum += rows8 if shift == 0 else pltpu.roll(rows8, shift, 1)
            line = small_sum[7:8]
            for a in range(7):
                line = line + pltpu.roll(small_sum[a : a + 1], 7 - a, 1)
            diag_ref[pl.ds(gain_lane - 14 + 2 * pair + hh, 1), pl.ds(base, strip)] += line

    for copy in (k_copy, *qkv_loads):
        copy.wait()
    ag_copy(1).wait_recv()

    def weight_group(g):
        first, last = GROUPS[g]
        cols = slice(first * 128, last * 128)
        size = last - first
        for i, ref in enumerate((q_ref, k_ref, v_ref)):
            field = ref[:, :, :, cols].reshape(parts * block_rows, size * 128)
            grad = dot(turned_ref[...], field).astype(bf16)
            for part in range(parts):
                for t in range(size):
                    group[g].terms[part, size * i + t] = grad[
                        part * rows_n : (part + 1) * rows_n, t * 128 : (t + 1) * 128
                    ]
        group[g].start()

    hooks = {
        1: [group[0].to_half],
        5: [lambda: weight_group(1)],
        6: [group[1].to_half],
        7: [lambda: weight_group(2), group[0].to_quarter, grad_copies[2].start],
        8: [group[2].to_half],
        9: [lambda: weight_group(3), group[0].to_piece, group[1].to_quarter],
        10: [group[3].to_half],
        11: [group[0].to_cross, group[2].to_quarter],
    }

    def attention_step(i, carry):
        phase, pair = step_of(i)

        @pl.when(i == 4)
        def _():
            for k in range(2, parts):
                ag_copy(k).wait_recv()

        for which in range(2):

            @pl.when(phase == which)
            def _(which=which):
                attention_pair(which, pair, i)

        for at, calls in hooks.items():

            @pl.when(i == at)
            def _(calls=calls):
                for call in calls:
                    call()

        return carry

    lax.fori_loop(0, 2 * pairs, attention_step, 0)
    weight_group(4)

    def part_copy(k):
        peer = flipped(n, k, parts)
        return remote(agsend.at[peer], part_any.at[n], partsem, k, "narrow", peer)

    for k in range(1, parts):
        ag_copy(k).wait_send()
    for k in (0, 3, 1, 2):
        src = flipped(n, k, parts)
        x = tok_ref[src].reshape(block_rows, width).astype(f32)
        inv = inverse_rms(x)
        upstream = dot(q_ref[src].reshape(block_rows, width), wq_ref[...], NT)
        upstream += dot(k_ref[src].reshape(block_rows, width), wk_ref[...], NT)
        upstream += dot(v_ref[src].reshape(block_rows, width), wv_ref[...], NT)
        scaled = upstream * gain_a
        inner = jnp.mean(scaled * x, axis=-1, keepdims=True)
        grad = inv * scaled - x * (inv * inv * inv * inner)
        gains_ref[0:1, :] += jnp.sum(upstream * x * inv, axis=0, keepdims=True)
        grad = grad.astype(bf16).reshape(seqs, span, width)
        agsend[src] = grad
        if k == 0:
            part_own = pltpu.make_async_copy(agsend.at[src], part_any.at[n], loadsem.at[3])
            part_own.start()
            group[4].to_far()
            group[1].to_piece()
        if k in (1, 3):
            part_copy(k).start()
        if k == 3:
            group[3].to_quarter()
            group[0].back_piece()
        if k == 1:
            group[4].to_half()
            group[2].to_piece()
            group[1].to_cross()

    pack = router_ref[...]
    for i in range(2):
        column = jnp.broadcast_to(gains_ref[i : i + 1, :], (128, width)).T
        pack = pack + jnp.where(lane == gain_lane + i, column, 0.0)
    relative = lax.dot_general(
        hot_ref[...].astype(f32), diag_ref[...], NT,
        precision=lax.Precision.HIGHEST, preferred_element_type=f32,
    )
    share = relative.shape[0] // parts
    for part in range(parts):
        slab = pack[part * rows_n : (part + 1) * rows_n]
        head = slab[:share] + relative[part * share : (part + 1) * share]
        slab = jnp.concatenate([head, slab[share:]], axis=0)
        folded = slab[:fold_rows]
        for fold in range(1, folds):
            folded += pltpu.roll(slab[fold * fold_rows : (fold + 1) * fold_rows], 32 * fold, 1)
        small_terms[part] = folded.astype(bf16)
    for k in range(1, parts):
        small_copy(k).start()
    part_copy(2).start()
    group[0].back_quarter()
    group[3].to_piece()
    res_own.wait()

    def res_wait(k, carry):
        res_copy(k).wait()
        return carry

    lax.fori_loop(1, wide_n, res_wait, 0)
    again = pltpu.make_async_copy(resland_any, back_ref, loadsem.at[0])
    again.start()

    def small_hop():
        total = small_terms[n].astype(f32)
        for k in range(1, parts):
            small_copy(k).wait()
            total += small_near[k].astype(f32)
        small_mine[...] = total.astype(bf16)

        def small_send(k, carry):
            small_wide(k).start()
            return carry

        lax.fori_loop(1, wide_n, small_send, 0)

    again.wait()
    outs = [part_own, hid_copy]
    for b in range(parts):
        rows = pl.ds(b * block_rows, block_rows)
        cot_ref[rows, :] = picked(rows).astype(bf16)
        if b == 0:
            group[4].back_piece()
            group[1].back_piece()
        if b == 1:
            small_hop()
            group[2].to_cross()
            group[0].back_half()
        if b == 2:
            group[1].back_quarter()
            group[3].to_cross()
    copy = pltpu.make_async_copy(cot_ref, out_any, loadsem.at[2])
    copy.start()
    outs.append(copy)
    group[2].back_piece()
    group[1].back_half()
    group[3].back_piece()

    def unpack(g):
        group[g].finish()
        first, last = GROUPS[g]
        size = last - first
        for b in range(group[g].blocks):
            i, at = (3, b) if g == 0 else (b // size, first + b % size)
            turned_ref[i * rows_n : (i + 1) * rows_n, at * 128 : (at + 1) * 128] = group[g].block(b)

    unpack(0)
    group[2].back_quarter()
    unpack(4)
    group[3].back_quarter()
    group[2].back_half()
    unpack(1)
    group[3].back_half()
    total = small_mine[...].astype(f32)
    for k in range(1, wide_n):
        small_wide(k).wait()
        total += small_in[k].astype(f32)
    for fold in range(folds):
        part = total if fold == 0 else pltpu.roll(total, 128 - 32 * fold, 1)
        smallout[fold * fold_rows : (fold + 1) * fold_rows, :] = part
    unpack(2)
    for k in range(1, parts):
        part_copy(k).wait()
    unpack(3)
    for copy in grad_copies:
        copy.wait()
    for a, b, i in ((turned_ref.at[:, :width], big_any, 11), (smallout, small_any, 12)):
        copy = pltpu.make_async_copy(a, b, loadsem.at[i])
        copy.start()
        outs.append(copy)
    for copy in outs:
        copy.wait()


def backward(args, wide_n, experts, quad, slots_shape, table):
    parts, seqs, span, width = quad
    total, tokens = parts * span, parts * seqs * span
    rows_n = width // parts
    fold_rows = rows_n // (4 if experts <= 16 else 1)
    square = pltpu.VMEM((tokens, width), f32)
    sums = [
        Sums.scratch(
            (1 if g == 0 else 3) * (last - first), rows_n, wide_n, 1 if g == len(GROUPS) - 1 else 2
        )
        for g, (first, last) in enumerate(GROUPS)
    ]
    return pl.pallas_call(
        functools.partial(backward_kernel, wide_n, experts),
        in_specs=[hbm(), vmem()] + [hbm()] * 15 + [vmem()] * 4 + [hbm()] * 2,
        out_specs=[hbm()] * 8,
        out_shape=[
            jax.ShapeDtypeStruct((tokens, width), bf16),
            jax.ShapeDtypeStruct((tokens, width), f32),
            jax.ShapeDtypeStruct(quad, bf16),
            jax.ShapeDtypeStruct((4 * rows_n, width), bf16),
            jax.ShapeDtypeStruct((rows_n, 128), f32),
            jax.ShapeDtypeStruct(slots_shape, bf16),
            jax.ShapeDtypeStruct(args[-2].shape, bf16),
            jax.ShapeDtypeStruct(args[-1].shape, bf16),
        ],
        scratch_shapes=[
            pltpu.VMEM(slots_shape, bf16),
            square,
            pltpu.VMEM((tokens, width), bf16),
            pltpu.VMEM(quad, bf16),
            pltpu.VMEM(quad, bf16),
            pltpu.VMEM(quad, bf16),
            pltpu.VMEM(quad, bf16),
            pltpu.VMEM(quad, bf16),
            pltpu.VMEM(quad, bf16),
            pltpu.VMEM(quad, bf16),
            pltpu.VMEM(quad, bf16),
            pltpu.VMEM((width, tokens), bf16),
            pltpu.VMEM((width, tokens), f32),
            pltpu.VMEM((width, tokens), f32),
            pltpu.VMEM((2, seqs, 2 * span, 2 * total), bf16),
            pltpu.VMEM((2, 2 * span, total), f32),
            pltpu.VMEM((128, table), f32),
            pltpu.VMEM((2 * total, 128), bf16),
            pltpu.VMEM((2, total, 128), bf16),
            pltpu.VMEM((2 * span, 2 * total), bf16),
            pltpu.VMEM((8, width), f32),
            pltpu.VMEM((rows_n, 128), f32),
            *[pltpu.VMEM((width, width), bf16)] * 4,
            pltpu.SemaphoreType.DMA((13,)),
            pltpu.SemaphoreType.DMA((2,)),
            pltpu.SemaphoreType.DMA((2, parts)),
            pltpu.SemaphoreType.DMA((2, parts)),
            pltpu.SemaphoreType.DMA((2, wide_n)),
            pltpu.SemaphoreType.DMA((2, 3)),
            pltpu.SemaphoreType.DMA((4,)),
        ]
        + [ref for refs, _ in sums for ref in refs]
        + [sem for _, sems in sums for sem in sems]
        + [
            pltpu.VMEM((parts, fold_rows, 128), bf16),
            pltpu.VMEM((parts, fold_rows, 128), bf16),
            pltpu.VMEM((fold_rows, 128), bf16),
            pltpu.VMEM((wide_n, fold_rows, 128), bf16),
            pltpu.SemaphoreType.DMA((2, parts)),
            pltpu.SemaphoreType.DMA((2, wide_n)),
        ],
        compiler_params=params(collective_id=3, has_side_effects=True),
        name="backward",
    )(*args)


def finish_kernel(
    heads, gain_lane, hid_ref, res_ref, hgrad_ref, part_ref, gin_ref, early_ref, late_ref,
    gout_ref, far_ref, big_ref, small_ref,
    out_ref, igrad_ref, gin_out, gout_out, wq_out, wk_out, wv_out, wo_out,
    router_out, relative_out, gain_a_out, gain_e_out,
):
    step = pl.program_id(0)
    out_ref[...] = hid_ref[...] + res_ref[...].astype(f32)
    igrad_ref[...] = hgrad_ref[...] + part_ref[...].astype(f32)
    gout_out[...] = gout_ref[...].astype(f32) + far_ref[...].astype(f32)
    split = early_ref.shape[1]
    gin_out[:, :split] = gin_ref[:, :split].astype(f32) + early_ref[...].astype(f32)
    gin_out[:, split:] = gin_ref[:, split:].astype(f32) + late_ref[...].astype(f32)
    for i, ref in enumerate((wq_out, wk_out, wv_out, wo_out)):

        @pl.when(step == i // 2)
        def _(ref=ref, i=i):
            size = ref.shape[0]
            ref[...] = big_ref[(i % 2) * size : (i % 2 + 1) * size, :].astype(f32)

    @pl.when(step == 0)
    def _():
        small = small_ref[...]
        share = relative_out.shape[0]
        relative_out[...] = small[:share, gain_lane - 14 : gain_lane - 14 + heads]
        rows = small.shape[0]
        turned = jnp.concatenate([small, jnp.zeros((-rows % 128, 128), f32)], axis=0).T
        router_out[...] = turned[: router_out.shape[0], :rows]
        gain_a_out[...] = turned[gain_lane : gain_lane + 1, :rows].reshape(rows)
        gain_e_out[...] = turned[gain_lane + 1 : gain_lane + 2, :rows].reshape(rows)


def finish(args, heads, buckets, experts, narrow_n):
    hid, _, _, _, gin, _, _, gout, _, _, small = args
    gain_lane = 30 if experts <= 16 else 126
    tokens, width = hid.shape
    steps = 2
    rows_n, units = gin.shape

    def rows(shape):
        return pl.BlockSpec((shape[0] // steps, shape[1]), lambda i: (i, 0))

    def whole(shape):
        return pl.BlockSpec(shape, lambda i: (0,) * len(shape))

    square, slab = (tokens, width), (rows_n, width)
    singles = [(experts, rows_n), (buckets // narrow_n, heads), (rows_n,), (rows_n,)]
    shapes = [square, square, (rows_n, units), gout.shape, slab, slab, slab, slab] + singles
    return pl.pallas_call(
        functools.partial(finish_kernel, heads, gain_lane),
        grid=(steps,),
        in_specs=[rows(item.shape) for item in args[:-1]] + [whole(small.shape)],
        out_specs=[rows(shape) for shape in shapes[:4]] + [whole(shape) for shape in shapes[4:]],
        out_shape=[jax.ShapeDtypeStruct(shape, f32) for shape in shapes],
        compiler_params=params(),
        name="finish",
    )(*args)


def body(
    tokens, lengths, routes, bucket_table, attn_gain, query_weight, key_weight, value_weight,
    output_weight, relative_bias, expert_gain, router_weight, experts_in, experts_out, cotangent,
):
    seq_count, span, width = tokens.shape
    narrow_n = lax.axis_size("narrow")
    wide_n = lax.axis_size("wide")
    seqs = seq_count // narrow_n
    heads = relative_bias.shape[1]
    buckets = relative_bias.shape[0]
    experts = router_weight.shape[1]
    tok_count = seq_count * span
    capacity = 5 * tok_count // (4 * experts)
    cap = -(-capacity // 16) * 16
    table = 2 * span * narrow_n
    flat_cot = cotangent.reshape(tok_count, width)
    tok_quad = tokens.reshape(narrow_n, seqs, span, width)
    (
        tok_seq, att_seq, att_pos, hidden, routed, cot_rows, q, k, v, invl, probs,
        slot_row, slot_col, offset_hot,
    ) = forward(
        (
            lengths, tok_quad, flat_cot, routes.reshape(seq_count, span), bucket_table,
            relative_bias.T, attn_gain, expert_gain,
            query_weight, key_weight, value_weight, output_weight,
        ),
        wide_n, capacity, cap, tok_quad.shape, table,
    )
    res, back_rows, gin, gin_early, gin_send, gout, gout_send, router_grad = run_experts(
        routed, slot_row, router_weight.T, cot_rows, experts_in[0], experts_out[0], experts
    )
    picked_res, hidden_grad, part, big, small, _, gin_late, gout_far = backward(
        (
            back_rows, slot_col, hidden, flat_cot, att_pos, att_seq, probs, invl, q, k, v, tok_seq,
            res, output_weight, query_weight, key_weight, value_weight, attn_gain, expert_gain,
            router_grad, offset_hot, gin_send, gout_send,
        ),
        wide_n, experts, tok_quad.shape, res.shape, table,
    )

    (
        layer_output, input_grad, grad_in, grad_out, grad_query, grad_key, grad_value, grad_output,
        grad_router, grad_relative, grad_first, grad_second,
    ) = finish(
        (
            hidden, picked_res, hidden_grad, part.reshape(tok_count, width), gin, gin_early, gin_late,
            gout, gout_far, big, small,
        ),
        heads, buckets, experts, narrow_n,
    )
    return (
        layer_output.reshape(seq_count, span, width),
        input_grad.reshape(seq_count, span, width),
        grad_first,
        grad_query,
        grad_key,
        grad_value,
        grad_output,
        grad_relative,
        grad_second,
        grad_router.T,
        grad_in[None],
        grad_out[None],
    )


def solution(mesh):
    token = P("wide", "narrow", None)
    expert = P("wide", None, None)
    row, vector = P("narrow", None), P("narrow")
    return jax.shard_map(
        body,
        mesh=mesh,
        in_specs=(token, P("wide"), token) + (P(),) * 9 + (expert, expert, token),
        out_specs=(
            token, token, vector, row, row, row, row, row, vector, row,
            P("wide", "narrow", None), P("wide", "narrow", None),
        ),
        check_vma=False,
    )
```

```python
import functools

import jax
import jax.numpy as jnp
from jax import lax
from jax.experimental import pallas as pl
from jax.experimental.pallas import tpu as pltpu
from jax.sharding import PartitionSpec as P

f32, bf16 = jnp.float32, jnp.bfloat16
epsilon = 1e-06
VMEM_BYTES = 62 * 1024 * 1024
NN = (((1,), (0,)), ((), ()))
NT = (((1,), (1,)), ((), ()))
TN = (((0,), (0,)), ((), ()))


def dot(a, b, dims=NN):
    return lax.dot_general(a, b, dims, preferred_element_type=f32)


def vmem():
    return pl.BlockSpec(memory_space=pltpu.VMEM)


def params(**kw):
    return pltpu.CompilerParams(vmem_limit_bytes=VMEM_BYTES, **kw)


def inverse_rms(field):
    return lax.rsqrt(jnp.mean(field * field, axis=-1, keepdims=True) + epsilon)


def half_masks(pair_width):
    lane = lax.broadcasted_iota(jnp.int32, (1, pair_width), 1)
    low = lane < pair_width // 2
    return low, (low.astype(f32).astype(bf16), (~low).astype(f32).astype(bf16))


MESH = pl.DeviceIdType.MESH
LOG2E = 1.4426950408889634


def hbm():
    return pl.BlockSpec(memory_space=pl.ANY)


def flipped(me, k, size):
    out, bit = me, 1
    while bit < size:
        out = out + ((k // bit) % 2) * (bit - 2 * bit * ((me // bit) % 2))
        bit *= 2
    return out


def remote(src, dst, sems, k, axis, peer):
    return pltpu.make_async_remote_copy(
        src_ref=src,
        dst_ref=dst,
        send_sem=sems.at[0, k],
        recv_sem=sems.at[1, k],
        device_id={axis: peer},
        device_id_type=MESH,
    )


def greet(narrow_n, wide_n):
    barrier = pltpu.get_barrier_semaphore()
    count = 0
    for axis, size in (("narrow", narrow_n), ("wide", wide_n)):
        if size > 1:
            me = lax.axis_index(axis)

            def greet(k, carry, axis=axis, size=size, me=me):
                pl.semaphore_signal(
                    barrier, inc=1, device_id={axis: flipped(me, k, size)}, device_id_type=MESH
                )
                return carry

            lax.fori_loop(1, size, greet, 0)
            count += size - 1
    return count


def enter(narrow_n, wide_n):
    count = greet(narrow_n, wide_n)
    pl.semaphore_wait(pltpu.get_barrier_semaphore(), count)


def expert_pick(expert, cap, slot_row):
    ids = lax.broadcasted_iota(jnp.int32, (cap, slot_row.shape[1]), 0) + expert * cap
    return (ids == slot_row).astype(f32).astype(bf16)


def token_slots(routes_ref, column_ref, experts, capacity, cap):
    seqs, span = routes_ref.shape
    routes = routes_ref[...]
    hot = jnp.concatenate([(routes == e).astype(f32) for e in range(experts)], axis=0)
    row = lax.broadcasted_iota(jnp.int32, (span, span), 0)
    ahead = (row < lax.broadcasted_iota(jnp.int32, (span, span), 1)).astype(f32).astype(bf16)
    size = experts * seqs
    row = lax.broadcasted_iota(jnp.int32, (size, size), 0)
    col = lax.broadcasted_iota(jnp.int32, (size, size), 1)
    above = ((row // seqs == col // seqs) & (col < row)).astype(f32).astype(bf16)
    counts = jnp.broadcast_to(jnp.sum(hot, axis=-1, keepdims=True), hot.shape).astype(bf16)
    position = dot(hot.astype(bf16), ahead) + dot(above, counts)
    slot = jnp.zeros((seqs, span), f32)
    for e in range(experts):
        here = position[e * seqs : (e + 1) * seqs]
        here = jnp.where(here < capacity, here + e * cap, experts * cap)
        slot = slot + hot[e * seqs : (e + 1) * seqs] * here
    turned = jnp.concatenate([slot] * (span // seqs), axis=0).T
    for s in range(seqs):
        column_ref[s * span : (s + 1) * span, :] = turned[:, s : s + 1].astype(jnp.int32)
    return jnp.concatenate([slot[s : s + 1] for s in range(seqs)], axis=1).astype(jnp.int32)


def forward_kernel(
    wide_n, capacity, lens_ref, tok_any, cot_any, routes_ref, table_ref, bias_ref, gain_a_ref, gain_e_ref,
    wq_any, wk_any, wv_any, wo_any,
    tokseq_any, attseq_any, att_any, hid_any, routed_any, cotrows_any, q_any, k_any, v_any, invl_any, p_any,
    slot_row_ref, slot_col_ref, hot_ref,
    tokbuf, tokpos, q_ref, k_ref, v_ref, invl_ref, attseq, attpos, hid_ref, routed_ref, cotsend,
    strip_ref, pbuf, vext, kext, diag_ref, cot_ref, wq_ref, wk_ref, wv_ref, wo_ref, insem, toksem, attsem, cotsem, psem, outsem,
):
    parts, seqs, span, width = tokbuf.shape
    total = parts * span
    heads = bias_ref.shape[0]
    pairs, table = heads // 2, diag_ref.shape[1]
    cap = cotsend.shape[1]
    n = lax.axis_index("narrow")
    w = lax.axis_index("wide")
    own = pltpu.make_async_copy(tok_any.at[n], tokbuf.at[n], outsem.at[0])
    position = pltpu.make_async_copy(tok_any, tokpos, outsem.at[1])
    cot_load, *qkv_loads, wo_load = [
        pltpu.make_async_copy(a, b, insem.at[i])
        for i, (a, b) in enumerate(
            (
                (cot_any, cot_ref), (wq_any, wq_ref), (wk_any, wk_ref), (wv_any, wv_ref),
                (wo_any, wo_ref),
            )
        )
    ]
    for copy in (cot_load, own, *qkv_loads, position, wo_load):
        copy.start()
    expected = greet(parts, wide_n)
    slot_row_ref[...] = token_slots(routes_ref, slot_col_ref, wide_n, capacity, cap)

    def cot_block(k):
        pick = expert_pick(flipped(w, k, wide_n), cap, slot_row_ref[...])
        cotsend[k] = dot(pick, cot_ref[...]).astype(bf16)

    def cot_early(k, carry):
        cot_block(k)
        return carry

    cot_load.wait()
    lax.fori_loop(wide_n // 2, wide_n, cot_early, 0)
    pl.semaphore_wait(pltpu.get_barrier_semaphore(), expected)

    def tok_copy(k):
        peer = flipped(n, k, parts)
        return remote(tok_any.at[peer], tokbuf.at[n], toksem, k, "narrow", peer)

    for k in (2, 3, 1):
        tok_copy(k).start()

    def cot_copy(k):
        peer = flipped(w, k, wide_n)
        return remote(cotsend.at[k], cotrows_any.at[k], cotsem, k, "wide", peer)

    def cot_start(k, carry):
        cot_copy(k).start()
        return carry

    def cot_step(k, carry):
        cot_block(k)
        cot_copy(k).start()
        return carry

    lax.fori_loop(wide_n // 2, wide_n, cot_start, 0)
    lax.fori_loop(1, wide_n // 2, cot_step, 0)
    cot_block(0)
    cot_own = pltpu.make_async_copy(cotsend.at[0], cotrows_any.at[0], outsem.at[2])
    cot_own.start()

    gain = gain_a_ref[...].astype(f32).reshape(1, width)
    own.wait()
    for copy in qkv_loads:
        copy.wait()
    for k in range(parts):
        src = flipped(n, k, parts)
        if k > 0:
            tok_copy(k).wait_recv()
        x = tokbuf[src].reshape(seqs * span, width).astype(f32)
        normed = (x * inverse_rms(x) * gain).astype(bf16)
        shape = (seqs, span, width)
        q_ref[src] = (dot(normed, wq_ref[...]) * LOG2E).astype(bf16).reshape(shape)
        k_ref[src] = dot(normed, wk_ref[...]).astype(bf16).reshape(shape)
        v_ref[src] = dot(normed, wv_ref[...]).astype(bf16).reshape(shape)
    outs = [
        pltpu.make_async_copy(a, b, outsem.at[i])
        for a, b, i in (
            (tokbuf, tokseq_any, 3), (q_ref, q_any, 4), (k_ref, k_any, 5), (v_ref, v_any, 6),
        )
    ]
    for copy in outs:
        copy.start()

    buckets, offsets = bias_ref.shape[1], table_ref.shape[0]
    ids = lax.broadcasted_iota(jnp.int32, (buckets, offsets), 0)
    found = (ids == table_ref[...].reshape(1, offsets)).astype(f32).astype(bf16)
    hot_ref[...] = jnp.zeros_like(hot_ref)
    hot_ref[:, :offsets] = found
    diag_ref[:heads, :] = dot(bias_ref[...], hot_ref[...]) * LOG2E

    low, masks = half_masks(128)
    lane = lax.broadcasted_iota(jnp.int32, (1, 128), 1)
    hot = [(lane == 64).astype(f32).astype(bf16), (lane == 0).astype(f32).astype(bf16)]
    for hh in range(2):
        ones = jnp.broadcast_to(masks[hh], (total, 128))
        vext[hh * total : (hh + 1) * total, 128:] = ones

    def att_copy(k, lanes):
        peer = flipped(n, k, parts)
        return remote(
            attseq.at[peer, :, :, lanes], attpos.at[n, :, :, lanes], attsem, k, "narrow", peer
        )

    def one_pair(pair, carry):
        lanes = pl.ds(pl.multiple_of(pair * 128, 128), 128)
        for hh in range(2):
            row = diag_ref[pl.ds(2 * pair + hh, 1), :]
            strip_ref[hh] = pltpu.roll(
                jnp.broadcast_to(row, (span, table)), table - span + 1, 1, stride=1, stride_axis=0
            )

        def one_sequence(s, inner):
            vp = v_ref[:, s, :, lanes].reshape(total, 128)
            kp = k_ref[:, s, :, lanes].reshape(total, 128).astype(f32)
            ids = lax.broadcasted_iota(jnp.int32, (total, 128), 0)
            push = jnp.where(ids < lens_ref[n * seqs + s], 0.0, -1e30)
            for hh in range(2):
                vext[hh * total : (hh + 1) * total, :128] = vp * masks[hh]
                kext[hh] = jnp.where(lane == 64 - 64 * hh, push, kp).astype(bf16)

            @pl.when(pair > 0)
            def _():
                pltpu.make_async_copy(pbuf.at[s], p_any.at[pair, s], psem.at[s]).wait()

            for block in range(parts // 2):
                rows = slice(block * 2 * span, (block + 1) * 2 * span)
                both = slice(2 * block, 2 * block + 2)
                qp = q_ref[both, s, :, lanes].reshape(2 * span, 128)
                for hh in range(2):
                    bias = jnp.concatenate(
                        [
                            strip_ref[hh, :, (parts - 1 - r) * span : (parts - 1 - r) * span + total]
                            for r in (2 * block, 2 * block + 1)
                        ],
                        axis=0,
                    )
                    scores = dot(qp * masks[hh] + hot[hh], kext[hh], NT) + bias
                    raised = jnp.exp2(scores - jnp.max(scores, axis=-1, keepdims=True))
                    pbuf[s, rows, hh * total : (hh + 1) * total] = raised.astype(bf16)
                mixed = dot(pbuf[s, rows, :], vext[...])
                inv = 1.0 / mixed[:, 128:]
                invl_ref[both, s, :, lanes] = inv.astype(bf16).reshape(2, span, 128)
                attseq[both, s, :, lanes] = (mixed[:, :128] * inv).astype(bf16).reshape(2, span, 128)
            pltpu.make_async_copy(pbuf.at[s], p_any.at[pair, s], psem.at[s]).start()
            return inner

        lax.fori_loop(0, seqs, one_sequence, 0)
        for k in range(parts - 1, 0, -1):
            att_copy(k, lanes).start()
        return carry

    lax.fori_loop(0, pairs, one_pair, 0)
    for a, b, i in ((invl_ref, invl_any, 7), (attseq, attseq_any, 11)):
        copy = pltpu.make_async_copy(a, b, outsem.at[i])
        copy.start()
        outs.append(copy)
    position.wait()
    wo_load.wait()
    gain = gain_e_ref[...].astype(f32).reshape(1, width)
    for k in range(parts):
        src = flipped(n, k, parts)
        if k > 0:
            att_copy(k, slice(None)).wait_recv()
            att = attpos[src].reshape(seqs * span, width)
        else:
            attpos[src] = attseq[src]
            att = attseq[src].reshape(seqs * span, width)
        rows = pl.ds(pl.multiple_of(src * seqs * span, seqs * span), seqs * span)
        hidden = tokpos[src].reshape(seqs * span, width).astype(f32) + dot(att, wo_ref[...])
        hid_ref[rows, :] = hidden
        copy = pltpu.make_async_copy(hid_ref.at[rows], hid_any.at[rows], outsem.at[12 + k])
        copy.start()
        outs.append(copy)
        routed_ref[rows, :] = (hidden * inverse_rms(hidden) * gain).astype(bf16)
    for a, b, i in ((attpos, att_any, 8), (routed_ref, routed_any, 10)):
        copy = pltpu.make_async_copy(a, b, outsem.at[i])
        copy.start()
        outs.append(copy)
    for k in range(1, parts):
        tok_copy(k).wait_send()
        att_copy(k, slice(None)).wait_send()
    for s in range(seqs):
        pltpu.make_async_copy(pbuf.at[s], p_any.at[0, s], psem.at[s]).wait()
    cot_own.wait()

    def cot_wait(k, carry):
        cot_copy(k).wait()
        return carry

    lax.fori_loop(1, wide_n, cot_wait, 0)
    for copy in outs:
        copy.wait()


def forward(args, wide_n, capacity, cap, quad, table):
    parts, seqs, span, width = quad
    heads, buckets = args[5].shape
    pairs = heads // 2
    total = parts * span
    tokens = parts * seqs * span
    shapes = [
        (quad, bf16), (quad, bf16), (quad, bf16), ((tokens, width), f32), ((tokens, width), bf16),
        ((wide_n, cap, width), bf16), (quad, bf16), (quad, bf16), (quad, bf16), (quad, bf16),
        ((pairs, seqs, total, 2 * total), bf16),
    ]
    small = [((1, tokens), jnp.int32), ((tokens, 1), jnp.int32), ((buckets, table), bf16)]
    return pl.pallas_call(
        functools.partial(forward_kernel, wide_n, capacity),
        in_specs=[pl.BlockSpec(memory_space=pltpu.SMEM), hbm(), hbm()] + [vmem()] * 5 + [hbm()] * 4,
        out_specs=[hbm()] * len(shapes) + [vmem()] * 3,
        out_shape=[jax.ShapeDtypeStruct(*item) for item in shapes + small],
        scratch_shapes=[
            pltpu.VMEM(quad, bf16),
            pltpu.VMEM(quad, bf16),
            pltpu.VMEM(quad, bf16),
            pltpu.VMEM(quad, bf16),
            pltpu.VMEM(quad, bf16),
            pltpu.VMEM(quad, bf16),
            pltpu.VMEM(quad, bf16),
            pltpu.VMEM(quad, bf16),
            pltpu.VMEM((tokens, width), f32),
            pltpu.VMEM((tokens, width), bf16),
            pltpu.VMEM((wide_n, cap, width), bf16),
            pltpu.VMEM((2, span, table), f32),
            pltpu.VMEM((seqs, total, 2 * total), bf16),
            pltpu.VMEM((2 * total, 256), bf16),
            pltpu.VMEM((2, total, 128), bf16),
            pltpu.VMEM((16, table), f32),
            pltpu.VMEM((tokens, width), bf16),
            *[pltpu.VMEM((width, width), bf16)] * 4,
            pltpu.SemaphoreType.DMA((5,)),
            pltpu.SemaphoreType.DMA((2, parts)),
            pltpu.SemaphoreType.DMA((2, parts)),
            pltpu.SemaphoreType.DMA((2, wide_n)),
            pltpu.SemaphoreType.DMA((seqs,)),
            pltpu.SemaphoreType.DMA((16,)),
        ],
        compiler_params=params(collective_id=1, has_side_effects=True),
        name="forward",
    )(*args)


def expert_kernel(
    experts, chunks, split, routed_ref, slot_ref, router_ref, cot_any, win_any, wout_any,
    res_any, back_any, gin_any, ginfar_any, ginsend_any, gout_any, goutsend_any, grouter_ref,
    send_ref, recv_ref, cot_ref, push_ref, win_ref, wout_ref, act_ref, pg_ref, res_ref,
    acc_res, acc_back, nearin_ref, nearout_ref, wr_ref, sendsem, backsem, sem, gradsem,
):
    wide_n, cap, width = send_ref.shape
    units = win_ref.shape[1]
    tile = 512
    w = lax.axis_index("wide")
    per = wide_n // chunks
    chunk_rows = per * cap
    loads = [
        pltpu.make_async_copy(a, b, sem.at[i])
        for i, (a, b) in enumerate(((cot_any, cot_ref), (win_any, win_ref), (wout_any, wout_ref)))
    ]
    for copy in loads:
        copy.start()
    expected = greet(4, wide_n)

    def send_copy(k):
        return remote(
            send_ref.at[k], recv_ref.at[k], sendsem, k, "wide", flipped(w, k, wide_n)
        )

    def back_copy(k):
        return remote(
            cot_ref.at[k], back_any.at[w], backsem, k, "wide", flipped(w, k, wide_n)
        )

    def turn(i):
        return (i % 2) * 2 + i // 2

    last = wide_n // 2 - 1
    inner = ((w // 2) % last + last - 1) // last

    def order(i):
        return i + inner * (turn(i) - i)

    def make_rows(i, carry):
        k = turn(i // per) * per + i % per
        pick = expert_pick(flipped(w, k, wide_n), cap, slot_ref[...])
        send_ref[k] = dot(pick, routed_ref[...]).astype(bf16)
        return carry

    def send_rows(i, carry):
        send_copy(turn(i // per) * per + i % per).start()
        return carry

    def send_step(i, carry):
        return send_rows(i, make_rows(i, carry))

    lax.fori_loop(1, wide_n // 2, make_rows, 0)
    pl.semaphore_wait(pltpu.get_barrier_semaphore(), expected)
    lax.fori_loop(1, wide_n // 2, send_rows, 0)
    lax.fori_loop(wide_n // 2, wide_n, send_step, 0)
    pick = expert_pick(w, cap, slot_ref[...])
    recv_ref[0] = dot(pick, routed_ref[...]).astype(bf16)
    for copy in loads:
        copy.wait()
    router = router_ref[...].astype(f32)
    blank = jnp.zeros((wr_ref.shape[0] - experts, width), f32)
    wr_ref[...] = jnp.concatenate([router, blank], axis=0).astype(bf16)
    lane = lax.broadcasted_iota(jnp.int32, (1, wr_ref.shape[0]), 1)
    hot = lane == w
    c0 = 0.7978845608028654
    c1 = c0 * 0.044715
    grouter_ref[...] = jnp.zeros_like(grouter_ref)

    def give(first):
        def one(j, carry):
            @pl.when(first + j > 0)
            def _():
                back_copy(first + j).start()

            return carry

        return one

    def one_chunk(step, carry):
        chunk = order(step)
        first = chunk * per

        def arrive(j, inner):
            @pl.when(first + j > 0)
            def _():
                send_copy(first + j).wait_recv()

            return inner

        lax.fori_loop(0, per, arrive, 0)

        @pl.when(inner * (step + 1) == chunks)
        def _():
            for earlier in (2, 1, 0):
                lax.fori_loop(0, per, give(earlier * per), 0)

        sources = pl.ds(first, per)
        here = pl.ds(pl.multiple_of(chunk * chunk_rows, chunk_rows), chunk_rows)
        x = recv_ref[sources].reshape(chunk_rows, width)
        cot = cot_ref[sources].reshape(chunk_rows, width).astype(f32)
        logits = jnp.where(lane < experts, dot(x, wr_ref[...], NT), -1e30)
        raised = jnp.exp(logits - jnp.max(logits, axis=-1, keepdims=True))
        probs = raised * (1.0 / jnp.sum(raised, axis=-1, keepdims=True))
        gate = jnp.sum(jnp.where(hot, probs, 0.0), axis=-1, keepdims=True)
        push_ref[here, :] = (gate * cot).astype(bf16)
        acc_res[...] = jnp.zeros_like(acc_res)
        acc_back[...] = jnp.zeros_like(acc_back)

        def hidden_tile(t, inner):
            cols = pl.ds(pl.multiple_of(t * tile, tile), tile)
            pre = dot(recv_ref[sources].reshape(chunk_rows, width), win_ref[:, cols])
            ag = dot(push_ref[here, :], wout_ref[cols, :], NT)
            sq = pre * pre
            th = jnp.tanh(pre * (c0 + c1 * sq))
            half = 0.5 + 0.5 * th
            act = (pre * half).astype(bf16)
            slope = half + pre * (0.5 - 0.5 * th * th) * (c0 + 3.0 * c1 * sq)
            pg = (ag * slope).astype(bf16)
            act_ref[here, cols] = act
            pg_ref[here, cols] = pg
            acc_res[...] += dot(act, wout_ref[cols, :])
            acc_back[...] += dot(pg, win_ref[:, cols], NT)
            return inner

        lax.fori_loop(0, units // tile, hidden_tile, 0)
        result = acc_res[...].astype(bf16).astype(f32)
        res_ref[sources] = (gate * result).astype(bf16).reshape(per, cap, width)
        gate_grad = jnp.sum(cot * result, axis=-1, keepdims=True)
        logit_grad = probs * (jnp.where(hot, gate_grad, 0.0) - gate * gate_grad)
        logit_grad = logit_grad.astype(bf16)
        back = acc_back[...].astype(bf16).astype(f32) + dot(logit_grad, wr_ref[...])
        cot_ref[sources] = back.astype(bf16).reshape(per, cap, width)
        grouter_ref[...] += dot(x, logit_grad, TN)

        @pl.when(step == chunks - 1)
        def _():
            lax.fori_loop(0, per, give(first), 0)

        @pl.when((1 - inner) * (step + 1) == chunks)
        def _():
            for earlier in (2, 1, 0):
                lax.fori_loop(0, per, give(earlier * per), 0)

        return carry

    lax.fori_loop(0, chunks, one_chunk, 0)
    own = pltpu.make_async_copy(cot_ref.at[0], back_any.at[w], sem.at[0])
    own.start()
    res_copy = pltpu.make_async_copy(res_ref, res_any, sem.at[1])
    res_copy.start()

    n = lax.axis_index("narrow")
    core, half = n % 2, n // 2
    in_rows, out_rows = width // 4, units // 4

    def slice_at(index, rows):
        return pl.ds(pl.multiple_of(index * rows, rows), rows)

    def near_copy(ref, near, rows, side, i, cols=slice(None)):
        return link(
            ref.at[slice_at(2 * side + 1 - core, rows), cols], near.at[side, :, cols],
            gradsem.at[0, i + side], gradsem.at[1, i + side], "narrow", flipped(n, 1, 4),
        )

    def near_add(ref, near, rows, side, i, cols=slice(None)):
        near_copy(ref, near, rows, side, i, cols).wait()
        at = slice_at(2 * side + core, rows)
        ref[at, cols] = (ref[at, cols].astype(f32) + near[side, :, cols].astype(f32)).astype(bf16)
        return at

    early, late = slice(0, split), slice(split, units)
    gin_far = link(
        win_ref.at[slice_at(2 * (1 - half) + core, in_rows), early], ginfar_any,
        gradsem.at[0, 6], gradsem.at[1, 6], "narrow", flipped(n, 2, 4),
    )

    def in_tile(t, carry):
        cols = pl.ds(pl.multiple_of(t * tile, tile), tile)
        win_ref[:, cols] = dot(
            recv_ref[...].reshape(wide_n * cap, width), pg_ref[:, cols], TN
        ).astype(bf16)

        @pl.when(t == split // tile - 1)
        def _():
            for side in range(2):
                near_copy(win_ref, nearin_ref, in_rows, side, 0, early).start()

        return carry

    def out_tile(t, carry):
        cols = pl.ds(pl.multiple_of(t * tile, tile), tile)
        wout_ref[cols, :] = dot(act_ref[:, cols], push_ref[...], TN).astype(bf16)

        @pl.when(t == 1)
        def _():
            near_add(win_ref, nearin_ref, in_rows, 1 - half, 0, early)
            gin_far.start()

        return carry

    lax.fori_loop(0, units // tile, in_tile, 0)
    for side in range(2):
        near_copy(win_ref, nearin_ref, in_rows, side, 4, late).start()
    lax.fori_loop(0, units // tile, out_tile, 0)
    for side in range(2):
        near_copy(wout_ref, nearout_ref, out_rows, side, 2).start()
    near_add(win_ref, nearin_ref, in_rows, half, 0, early)
    at = near_add(win_ref, nearin_ref, in_rows, half, 4, late)
    ends = [pltpu.make_async_copy(win_ref.at[at], gin_any, sem.at[2])]
    at = near_add(win_ref, nearin_ref, in_rows, 1 - half, 4, late)
    ends.append(pltpu.make_async_copy(win_ref.at[at, late], ginsend_any, sem.at[5]))
    at = near_add(wout_ref, nearout_ref, out_rows, 1 - half, 2)
    ends.append(pltpu.make_async_copy(wout_ref.at[at], goutsend_any, sem.at[3]))
    at = near_add(wout_ref, nearout_ref, out_rows, half, 2)
    ends.append(pltpu.make_async_copy(wout_ref.at[at], gout_any, sem.at[4]))
    for copy in ends:
        copy.start()

    def finish_step(k, carry):
        send_copy(k).wait_send()
        back_copy(k).wait()
        return carry

    lax.fori_loop(1, wide_n, finish_step, 0)
    own.wait()
    res_copy.wait()
    gin_far.wait()
    for copy in ends:
        copy.wait()


def run_experts(routed, slot_row, wr, cot_rows, win, wout, experts):
    wide_n, cap, width = cot_rows.shape
    units = win.shape[1]
    chunks, split = 4, 2 * units // 3
    slots = wide_n * cap
    block = (wide_n, cap, width)
    step = slots // chunks
    return pl.pallas_call(
        functools.partial(expert_kernel, experts, chunks, split),
        in_specs=[vmem()] * 3 + [hbm()] * 3,
        out_specs=[hbm()] * 7 + [vmem()],
        out_shape=[
            jax.ShapeDtypeStruct(block, bf16),
            jax.ShapeDtypeStruct(block, bf16),
            jax.ShapeDtypeStruct((width // 4, units), bf16),
            jax.ShapeDtypeStruct((width // 4, split), bf16),
            jax.ShapeDtypeStruct((width // 4, units - split), bf16),
            jax.ShapeDtypeStruct((units // 4, width), bf16),
            jax.ShapeDtypeStruct((units // 4, width), bf16),
            jax.ShapeDtypeStruct((width, 128), f32),
        ],
        scratch_shapes=[
            pltpu.VMEM(block, bf16),
            pltpu.VMEM(block, bf16),
            pltpu.VMEM(block, bf16),
            pltpu.VMEM((slots, width), bf16),
            pltpu.VMEM((width, units), bf16),
            pltpu.VMEM((units, width), bf16),
            pltpu.VMEM((slots, units), bf16),
            pltpu.VMEM((slots, units), bf16),
            pltpu.VMEM(block, bf16),
            pltpu.VMEM((step, width), f32),
            pltpu.VMEM((step, width), f32),
            pltpu.VMEM((2, width // 4, units), bf16),
            pltpu.VMEM((2, units // 4, width), bf16),
            pltpu.VMEM((128, width), bf16),
            pltpu.SemaphoreType.DMA((2, wide_n)),
            pltpu.SemaphoreType.DMA((2, wide_n)),
            pltpu.SemaphoreType.DMA((6,)),
            pltpu.SemaphoreType.DMA((2, 7)),
        ],
        compiler_params=params(collective_id=2, has_side_effects=True),
        name="experts",
    )(routed, slot_row, wr, cot_rows, win, wout)


def link(src, dst, send_sem, recv_sem, axis, peer):
    return pltpu.make_async_remote_copy(
        src_ref=src,
        dst_ref=dst,
        send_sem=send_sem,
        recv_sem=recv_sem,
        device_id={axis: peer},
        device_id_type=MESH,
    )


def padded(v):
    return -(-v // 16) * 16


class Sums:
    REFS = 8

    def __init__(self, wide_n, refs, sems):
        (
            self.terms, self.near, self.mine, self.half_in, self.quarter_in, self.piece_in,
            self.cross_in, self.whole,
        ) = refs
        self.narrow_sem, self.pair_sem, self.piece_sem, self.back_sem = sems
        self.wide_n = wide_n
        self.n, self.w = lax.axis_index("narrow"), lax.axis_index("wide")
        self.core, self.side = self.n % 2, self.n // 2
        self.ranks, slices, self.piece, _ = self.piece_in.shape
        self.direct = slices == 1
        self.cut = 1 if self.direct else 4
        self.rank = self.w // self.cut
        _, self.blocks, self.rows, _ = self.terms.shape
        self.total = self.mine.shape[1]

    def near_copy(self, side):
        return link(
            self.terms.at[2 * side + 1 - self.core], self.near.at[side],
            self.narrow_sem.at[0, side], self.narrow_sem.at[1, side],
            "narrow", flipped(self.n, 1, 4),
        )

    def cross_copy(self):
        if self.direct:
            source = self.terms.at[2 * (1 - self.side) + self.core]
        else:
            source = self.mine.at[1 - self.side, self.piece_at(self.rank)]
        return link(
            source, self.cross_in,
            self.narrow_sem.at[0, 2], self.narrow_sem.at[1, 2], "narrow", flipped(self.n, 2, 4),
        )

    def part_at(self, level, other):
        first, second = self.w % 2, (self.w // 2) % 2
        if level == 1:
            size, index = self.total // 2, first + other * (1 - 2 * first)
        else:
            size, index = self.total // 4, 2 * first + second + other * (1 - 2 * second)
        return pl.ds(pl.multiple_of(index * size, 16), size)

    def piece_at(self, rank):
        base = 0
        if not self.direct:
            base = (2 * (self.w % 2) + (self.w // 2) % 2) * (self.total // 4)
        return pl.ds(pl.multiple_of(base + rank * self.piece, 16), self.piece)

    def pair_copy(self, level):
        return link(
            self.mine.at[:, self.part_at(level, 1)],
            self.half_in if level == 1 else self.quarter_in,
            self.pair_sem.at[0, level - 1], self.pair_sem.at[1, level - 1],
            "wide", flipped(self.w, level, self.wide_n),
        )

    def peer(self, rank):
        return rank * self.cut + self.w % self.cut

    def piece_copy(self, k):
        rank = flipped(self.rank, k, self.ranks)
        return link(
            self.mine.at[:, self.piece_at(rank)], self.piece_in.at[k],
            self.piece_sem.at[0, k], self.piece_sem.at[1, k], "wide", self.peer(rank),
        )

    def piece_back(self, k):
        at = self.piece_at(self.rank)
        return link(
            self.whole.at[at], self.whole.at[at], self.back_sem.at[0, k], self.back_sem.at[1, k],
            "wide", self.peer(flipped(self.rank, k, self.ranks)),
        )

    def pair_back(self, level):
        at = self.part_at(level, 0)
        return link(
            self.whole.at[at], self.whole.at[at],
            self.pair_sem.at[0, level + 1], self.pair_sem.at[1, level + 1],
            "wide", flipped(self.w, level, self.wide_n),
        )

    def each(self, f):
        def step(k, carry):
            f(k)
            return carry

        lax.fori_loop(1, self.ranks, step, 0)

    def start(self):
        for side in (0, 1):
            self.near_copy(side).start()

    def near_total(self, side):
        self.near_copy(side).wait()
        return self.terms[2 * side + self.core].astype(f32) + self.near[side].astype(f32)

    def place(self, i, total):
        rows = self.blocks * self.rows
        self.mine[i, 0:rows] = total.astype(bf16).reshape(rows, 128)

    def to_far(self):
        total = self.near_total(1 - self.side)
        self.terms[2 * (1 - self.side) + self.core] = total.astype(bf16)
        self.cross_copy().start()

    def to_half(self):
        if self.direct:
            total = self.near_total(self.side)
            self.cross_copy().wait()
            self.place(0, total + self.cross_in[...].astype(f32))
            self.each(lambda k: self.piece_copy(k).start())
        else:
            for side in (0, 1):
                self.place(side, self.near_total(side))
            self.pair_copy(1).start()

    def take(self, level, ref):
        self.pair_copy(level).wait()
        at = self.part_at(level, 0)
        total = self.mine[:, at].astype(f32) + ref[...].astype(f32)
        self.mine[:, at] = total.astype(bf16)

    def to_quarter(self):
        self.take(1, self.half_in)
        self.pair_copy(2).start()

    def to_piece(self):
        self.take(2, self.quarter_in)
        self.each(lambda k: self.piece_copy(k).start())

    def pieces_total(self):
        self.each(lambda k: self.piece_copy(k).wait())

        def add(k, total):
            return total + self.piece_in[k].astype(f32)

        at = self.piece_at(self.rank)
        return lax.fori_loop(1, self.ranks, add, self.mine[:, at].astype(f32))

    def to_cross(self):
        self.mine[:, self.piece_at(self.rank)] = self.pieces_total().astype(bf16)
        self.cross_copy().start()

    def back_piece(self):
        at = self.piece_at(self.rank)
        if self.direct:
            total = self.pieces_total()[0]
        else:
            self.cross_copy().wait()
            total = self.mine[self.side, at].astype(f32) + self.cross_in[...].astype(f32)
        self.whole[at] = total.astype(bf16)
        self.each(lambda k: self.piece_back(k).start())

    def back_quarter(self):
        self.each(lambda k: self.piece_back(k).wait())
        self.pair_back(2).start()

    def back_half(self):
        self.pair_back(2).wait()
        self.pair_back(1).start()

    def finish(self):
        if self.direct:
            self.each(lambda k: self.piece_back(k).wait())
        else:
            self.pair_back(1).wait()

    def block(self, b):
        return self.whole[b * self.rows : (b + 1) * self.rows, :]

    @staticmethod
    def scratch(blocks, rows, wide_n, slices):
        cut = 1 if slices == 1 else 4
        ranks = wide_n // cut
        piece = padded(-(-blocks * rows // wide_n))
        total = wide_n * piece
        return [
            pltpu.VMEM((4, blocks, rows, 128), bf16),
            pltpu.VMEM((2, blocks, rows, 128), bf16),
            pltpu.VMEM((slices, total, 128), bf16),
            pltpu.VMEM((slices, 16 if slices == 1 else total // 2, 128), bf16),
            pltpu.VMEM((slices, 16 if slices == 1 else total // 4, 128), bf16),
            pltpu.VMEM((ranks, slices, piece, 128), bf16),
            pltpu.VMEM((blocks, rows, 128) if slices == 1 else (piece, 128), bf16),
            pltpu.VMEM((total, 128), bf16),
        ], [
            pltpu.SemaphoreType.DMA((2, 3)),
            pltpu.SemaphoreType.DMA((2, 4)),
            pltpu.SemaphoreType.DMA((2, ranks)),
            pltpu.SemaphoreType.DMA((2, ranks)),
        ]


GROUPS = ((0, 6), (0, 2), (2, 4), (4, 5), (5, 6))


def backward_kernel(
    wide_n, experts, back_any, slot_ref, hid_any, cot_any, att_any, attseq_any, p_any, invl_any,
    q_any, k_any, v_any, tok_any, res_any, wo_any, wq_any, wk_any, wv_any, gain_a_ref, gain_e_ref,
    router_ref, hot_ref, gin_any, gout_any,
    out_any, hgrad_any, part_any, big_any, small_any, resland_any, ginfar_any, goutfar_any,
    back_ref, hid_ref, cot_ref, attseq_ref, invl_ref, q_ref, k_ref, v_ref, tok_ref,
    agsend, agbuf, turned_ref, dk_ref, dv_ref, pbuf, acc_ref, diag_ref,
    kmask_ref, vext_ref, ds_ref, gains_ref, smallout, wo_ref, wq_ref, wk_ref, wv_ref, loadsem, psem, agsem, partsem,
    ressem, gradsem, weightsem, *rest,
):
    parts, seqs, span, width = tok_ref.shape
    total = parts * span
    block_rows = seqs * span
    pairs = width // 128
    slots = back_ref.shape[0] * back_ref.shape[1]
    rows_n = width // parts
    n, w = lax.axis_index("narrow"), lax.axis_index("wide")
    count = len(GROUPS)
    per = Sums.REFS
    group = [
        Sums(
            wide_n,
            rest[per * i : per * i + per],
            rest[per * count + 4 * i : per * count + 4 * i + 4],
        )
        for i in range(count)
    ]
    folds = 4 if experts <= 16 else 1
    fold_rows = rows_n // folds
    gain_lane = 30 if folds == 4 else 126
    small_terms, small_near, small_mine, small_in, small_sem, small_wide_sem = rest[
        per * count + 4 * count :
    ]

    def small_copy(k):
        peer = flipped(n, k, parts)
        return remote(small_terms.at[peer], small_near.at[k], small_sem, k, "narrow", peer)

    def small_wide(k):
        peer = flipped(w, k, wide_n)
        return remote(small_mine, small_in.at[k], small_wide_sem, k, "wide", peer)

    loads = [
        pltpu.make_async_copy(a, b, loadsem.at[i])
        for i, (a, b) in enumerate(
            (
                (back_any, back_ref), (hid_any, hid_ref), (cot_any, cot_ref), (att_any, k_ref),
                (attseq_any, attseq_ref), (invl_any, invl_ref), (q_any, q_ref), (v_any, v_ref),
                (tok_any, tok_ref),
            )
        )
    ]
    wo_load, *qkv_loads = [
        pltpu.make_async_copy(a, b, weightsem.at[i])
        for i, (a, b) in enumerate(
            ((wo_any, wo_ref), (wq_any, wq_ref), (wk_any, wk_ref), (wv_any, wv_ref))
        )
    ]
    for copy in (*loads[:3], wo_load, *loads[3:], *qkv_loads):
        copy.start()

    def block_of(phase):
        return n // 2 + phase * (1 - 2 * (n // 2))

    def step_of(i):
        late = i // 8
        phase = (1 - late) * (i // 4) + late * (i % 2)
        return phase, (1 - late) * (i % 4) + late * (i // 2)

    def p_copy(i):
        phase, pair = step_of(i)
        at = pl.ds(pl.multiple_of(block_of(phase) * 2 * span, 2 * span), 2 * span)
        return pltpu.make_async_copy(p_any.at[pair, :, at], pbuf.at[i % 2], psem.at[i % 2])

    out_half = gout_any.shape[0] // 2
    grad_copies = [
        link(a, b, gradsem.at[0, i], gradsem.at[1, i], "narrow", flipped(n, 2, parts))
        for i, (a, b) in enumerate(
            (
                (gin_any, ginfar_any),
                (gout_any.at[:out_half], goutfar_any.at[:out_half]),
                (gout_any.at[out_half:], goutfar_any.at[out_half:]),
            )
        )
    ]
    p_copy(0).start()
    expected = greet(parts, wide_n)

    def res_copy(k):
        return remote(
            res_any.at[k], resland_any.at[w], ressem, k, "wide", flipped(w, k, wide_n)
        )

    def res_start(k, carry):
        res_copy(k).start()
        return carry

    res_own = pltpu.make_async_copy(res_any.at[0], resland_any.at[w], loadsem.at[10])

    def ag_copy(k):
        peer = flipped(n, k, parts)
        return remote(agsend.at[peer], agbuf.at[n], agsem, k, "narrow", peer)

    def rows_of(src):
        return pl.ds(pl.multiple_of(src * block_rows, block_rows), block_rows)

    def picked(rows):
        ids = lax.broadcasted_iota(jnp.int32, (block_rows, slots), 1)
        pick = (ids == slot_ref[rows, :]).astype(f32).astype(bf16)
        return dot(pick, back_ref[...].reshape(slots, width))

    gain_a = gain_a_ref[...].astype(f32).reshape(1, width)
    gain_e = gain_e_ref[...].astype(f32).reshape(1, width)
    gains_ref[...] = jnp.zeros_like(gains_ref)
    for copy in (*loads[:3], wo_load):
        copy.wait()
    for k in range(parts - 1, -1, -1):
        src = flipped(n, k, parts)
        rows = rows_of(src)
        upstream = picked(rows)
        hidden = hid_ref[rows, :]
        inv = inverse_rms(hidden)
        scaled = upstream * gain_e
        inner = jnp.mean(scaled * hidden, axis=-1, keepdims=True)
        grad = cot_ref[rows, :].astype(f32) + inv * scaled - hidden * (inv * inv * inv * inner)
        gains_ref[1:2, :] += jnp.sum(upstream * hidden * inv, axis=0, keepdims=True)
        hid_ref[rows, :] = grad
        grad = grad.astype(bf16)
        cot_ref[rows, :] = grad
        grad = dot(grad, wo_ref[...], NT).astype(bf16).reshape(seqs, span, width)
        if k == parts - 1:
            pl.semaphore_wait(pltpu.get_barrier_semaphore(), expected)
        if k > 0:
            agsend[src] = grad
            ag_copy(k).start()
        else:
            agbuf[src] = grad
        if k == parts - 1:
            lax.fori_loop(1, wide_n, res_start, 0)
            res_own.start()
    for copy in grad_copies:
        copy.start()
    hid_copy = pltpu.make_async_copy(hid_ref, hgrad_any, loadsem.at[1])
    hid_copy.start()
    loads[3].wait()
    for h in range(2):
        cols = slice(h * 2 * rows_n, (h + 1) * 2 * rows_n)
        grad = dot(k_ref[...].reshape(parts * block_rows, width)[:, cols], cot_ref[...], TN)
        grad = grad.astype(bf16)
        for t in range(2):
            for b in range(pairs):
                group[0].terms[2 * h + t, b] = grad[
                    t * rows_n : (t + 1) * rows_n, b * 128 : (b + 1) * 128
                ]
    k_copy = pltpu.make_async_copy(k_any, k_ref, loadsem.at[9])
    k_copy.start()
    group[0].start()
    for copy in loads[4:]:
        copy.wait()
    for b in range(parts):
        x = tok_ref[b].reshape(block_rows, width).astype(f32)
        normed = x * inverse_rms(x) * gain_a
        turned_ref[:, b * block_rows : (b + 1) * block_rows] = normed.T.astype(bf16)
    diag_ref[...] = jnp.zeros_like(diag_ref)

    low, masks = half_masks(128)
    lane = lax.broadcasted_iota(jnp.int32, (1, 128), 1)
    strip = (parts + 2) * span

    def attention_pair(phase, pair, i):
        slot = i % 2
        block = block_of(phase)
        both = pl.ds(2 * block, 2)
        lanes = pl.ds(pl.multiple_of(pair * 128, 128), 128)
        p_copy(i).wait()

        @pl.when(i + 1 < 2 * pairs)
        def _():
            p_copy(i + 1).start()

        for s in range(seqs):
            kp = k_ref[:, s, :, lanes].reshape(total, 128)
            vp = v_ref[:, s, :, lanes].reshape(total, 128)
            for hh in range(2):
                ones = (lane // 2 == 32 - 32 * hh).astype(f32)
                kmask_ref[hh * total : (hh + 1) * total, :] = kp * masks[hh]
                vext_ref[hh] = jnp.where(ones > 0, ones, vp.astype(f32)).astype(bf16)
            dk = [0.0, 0.0]
            dv = [0.0, 0.0]
            qp = q_ref[both, s, :, lanes].reshape(2 * span, 128)
            inv = invl_ref[both, s, :, lanes].reshape(2 * span, 128).astype(f32)
            gp = agbuf[both, s, :, lanes].reshape(2 * span, 128).astype(f32)
            gp = (gp * inv).astype(bf16)
            gf = gp.astype(f32)
            agree = gf * attseq_ref[both, s, :, lanes].reshape(2 * span, 128).astype(f32)
            for hh in range(2):
                side = low if hh == 0 else ~low
                delta = -jnp.sum(jnp.where(side, agree, 0.0), axis=-1, keepdims=True)
                high = delta.astype(bf16).astype(f32)
                ext = jnp.where(lane == 64 - 64 * hh, high, 0.0)
                ext = jnp.where(lane == 65 - 64 * hh, delta - high, ext)
                ext = jnp.where(side, gf, ext).astype(bf16)
                raised = pbuf[slot, s, :, hh * total : (hh + 1) * total]
                score_grad = raised.astype(f32) * dot(ext, vext_ref[hh], NT)
                if s == 0:
                    acc_ref[hh] = score_grad
                else:
                    acc_ref[hh] += score_grad
                score_grad = score_grad.astype(bf16)
                ds_ref[:, hh * total : (hh + 1) * total] = score_grad
                dk[hh] = dot(qp, score_grad, TN)
                dv[hh] = dot(gp, raised, TN)
            dq = dot(ds_ref[...], kmask_ref[...])
            q_ref[both, s, :, lanes] = dq.astype(bf16).reshape(2, span, 128)
            upper = lax.broadcasted_iota(jnp.int32, (128, 1), 0) < 64
            dk = jnp.where(upper, dk[0], dk[1]) * (1.0 / LOG2E)
            dv = jnp.where(upper, dv[0], dv[1])
            here = slice(s * total, (s + 1) * total)
            if phase == 0:
                dk_ref[lanes, here] = dk
                dv_ref[lanes, here] = dv
            else:
                dk = (dk + dk_ref[lanes, here]).T
                dv = (dv + dv_ref[lanes, here]).T
                k_ref[:, s, :, lanes] = dk.astype(bf16).reshape(parts, span, 128)
                v_ref[:, s, :, lanes] = dv.astype(bf16).reshape(parts, span, 128)
        base = pl.multiple_of((parts - 2 - 2 * block) * span, span)
        for hh in range(2):
            upper, lower = acc_ref[hh, :span, :], acc_ref[hh, span:, :]
            zero = jnp.zeros((span, span), f32)
            upper = jnp.concatenate([zero, upper, zero], axis=1)
            lower = jnp.concatenate([lower, zero, zero], axis=1)
            both_rows = upper + lower
            small_sum = jnp.zeros((8, strip), f32)
            for a in range(span // 8):
                shift = span - 8 - 8 * a
                rows8 = both_rows[8 * a : 8 * a + 8]
                small_sum += rows8 if shift == 0 else pltpu.roll(rows8, shift, 1)
            line = small_sum[7:8]
            for a in range(7):
                line = line + pltpu.roll(small_sum[a : a + 1], 7 - a, 1)
            diag_ref[pl.ds(gain_lane - 14 + 2 * pair + hh, 1), pl.ds(base, strip)] += line

    for copy in (k_copy, *qkv_loads):
        copy.wait()
    ag_copy(1).wait_recv()

    def weight_group(g):
        first, last = GROUPS[g]
        cols = slice(first * 128, last * 128)
        size = last - first
        for i, ref in enumerate((q_ref, k_ref, v_ref)):
            field = ref[:, :, :, cols].reshape(parts * block_rows, size * 128)
            grad = dot(turned_ref[...], field).astype(bf16)
            for part in range(parts):
                for t in range(size):
                    group[g].terms[part, size * i + t] = grad[
                        part * rows_n : (part + 1) * rows_n, t * 128 : (t + 1) * 128
                    ]
        group[g].start()

    hooks = {
        1: [group[0].to_half],
        5: [lambda: weight_group(1)],
        6: [group[1].to_half],
        7: [lambda: weight_group(2), group[0].to_quarter],
        8: [group[2].to_half],
        9: [lambda: weight_group(3), group[0].to_piece, group[1].to_quarter],
        10: [group[3].to_half],
        11: [group[0].to_cross, group[2].to_quarter],
    }

    def attention_step(i, carry):
        phase, pair = step_of(i)

        @pl.when(i == 4)
        def _():
            for k in range(2, parts):
                ag_copy(k).wait_recv()

        for which in range(2):

            @pl.when(phase == which)
            def _(which=which):
                attention_pair(which, pair, i)

        for at, calls in hooks.items():

            @pl.when(i == at)
            def _(calls=calls):
                for call in calls:
                    call()

        return carry

    lax.fori_loop(0, 2 * pairs, attention_step, 0)
    weight_group(4)

    def part_copy(k):
        peer = flipped(n, k, parts)
        return remote(agsend.at[peer], part_any.at[n], partsem, k, "narrow", peer)

    for k in range(1, parts):
        ag_copy(k).wait_send()
    for k in (0, 3, 1, 2):
        src = flipped(n, k, parts)
        x = tok_ref[src].reshape(block_rows, width).astype(f32)
        inv = inverse_rms(x)
        upstream = dot(q_ref[src].reshape(block_rows, width), wq_ref[...], NT)
        upstream += dot(k_ref[src].reshape(block_rows, width), wk_ref[...], NT)
        upstream += dot(v_ref[src].reshape(block_rows, width), wv_ref[...], NT)
        scaled = upstream * gain_a
        inner = jnp.mean(scaled * x, axis=-1, keepdims=True)
        grad = inv * scaled - x * (inv * inv * inv * inner)
        gains_ref[0:1, :] += jnp.sum(upstream * x * inv, axis=0, keepdims=True)
        grad = grad.astype(bf16).reshape(seqs, span, width)
        agsend[src] = grad
        if k == 0:
            part_own = pltpu.make_async_copy(agsend.at[src], part_any.at[n], loadsem.at[3])
            part_own.start()
            group[4].to_far()
            group[1].to_piece()
        if k in (1, 3):
            part_copy(k).start()
        if k == 3:
            group[3].to_quarter()
            group[0].back_piece()
        if k == 1:
            group[4].to_half()
            group[2].to_piece()
            group[1].to_cross()

    pack = router_ref[...]
    for i in range(2):
        column = jnp.broadcast_to(gains_ref[i : i + 1, :], (128, width)).T
        pack = pack + jnp.where(lane == gain_lane + i, column, 0.0)
    relative = lax.dot_general(
        hot_ref[...].astype(f32), diag_ref[...], NT,
        precision=lax.Precision.HIGHEST, preferred_element_type=f32,
    )
    share = relative.shape[0] // parts
    for part in range(parts):
        slab = pack[part * rows_n : (part + 1) * rows_n]
        head = slab[:share] + relative[part * share : (part + 1) * share]
        slab = jnp.concatenate([head, slab[share:]], axis=0)
        folded = slab[:fold_rows]
        for fold in range(1, folds):
            folded += pltpu.roll(slab[fold * fold_rows : (fold + 1) * fold_rows], 32 * fold, 1)
        small_terms[part] = folded.astype(bf16)
    for k in range(1, parts):
        small_copy(k).start()
    part_copy(2).start()
    group[0].back_quarter()
    group[3].to_piece()
    res_own.wait()

    def res_wait(k, carry):
        res_copy(k).wait()
        return carry

    lax.fori_loop(1, wide_n, res_wait, 0)
    again = pltpu.make_async_copy(resland_any, back_ref, loadsem.at[0])
    again.start()

    def small_hop():
        total = small_terms[n].astype(f32)
        for k in range(1, parts):
            small_copy(k).wait()
            total += small_near[k].astype(f32)
        small_mine[...] = total.astype(bf16)

        def small_send(k, carry):
            small_wide(k).start()
            return carry

        lax.fori_loop(1, wide_n, small_send, 0)

    again.wait()
    outs = [part_own, hid_copy]
    for b in range(parts):
        rows = pl.ds(b * block_rows, block_rows)
        cot_ref[rows, :] = picked(rows).astype(bf16)
        if b == 0:
            group[4].back_piece()
            group[1].back_piece()
        if b == 1:
            small_hop()
            group[2].to_cross()
            group[0].back_half()
        if b == 2:
            group[1].back_quarter()
            group[3].to_cross()
    copy = pltpu.make_async_copy(cot_ref, out_any, loadsem.at[2])
    copy.start()
    outs.append(copy)
    group[2].back_piece()
    group[1].back_half()
    group[3].back_piece()

    def unpack(g):
        group[g].finish()
        first, last = GROUPS[g]
        size = last - first
        for b in range(group[g].blocks):
            i, at = (3, b) if g == 0 else (b // size, first + b % size)
            turned_ref[i * rows_n : (i + 1) * rows_n, at * 128 : (at + 1) * 128] = group[g].block(b)

    unpack(0)
    group[2].back_quarter()
    unpack(4)
    group[3].back_quarter()
    group[2].back_half()
    unpack(1)
    group[3].back_half()
    total = small_mine[...].astype(f32)
    for k in range(1, wide_n):
        small_wide(k).wait()
        total += small_in[k].astype(f32)
    for fold in range(folds):
        part = total if fold == 0 else pltpu.roll(total, 128 - 32 * fold, 1)
        smallout[fold * fold_rows : (fold + 1) * fold_rows, :] = part
    unpack(2)
    for k in range(1, parts):
        part_copy(k).wait()
    unpack(3)
    for copy in grad_copies:
        copy.wait()
    for a, b, i in ((turned_ref.at[:, :width], big_any, 11), (smallout, small_any, 12)):
        copy = pltpu.make_async_copy(a, b, loadsem.at[i])
        copy.start()
        outs.append(copy)
    for copy in outs:
        copy.wait()


def backward(args, wide_n, experts, quad, slots_shape, table):
    parts, seqs, span, width = quad
    total, tokens = parts * span, parts * seqs * span
    rows_n = width // parts
    fold_rows = rows_n // (4 if experts <= 16 else 1)
    square = pltpu.VMEM((tokens, width), f32)
    sums = [
        Sums.scratch(
            (1 if g == 0 else 3) * (last - first), rows_n, wide_n, 1 if g == len(GROUPS) - 1 else 2
        )
        for g, (first, last) in enumerate(GROUPS)
    ]
    return pl.pallas_call(
        functools.partial(backward_kernel, wide_n, experts),
        in_specs=[hbm(), vmem()] + [hbm()] * 15 + [vmem()] * 4 + [hbm()] * 2,
        out_specs=[hbm()] * 8,
        out_shape=[
            jax.ShapeDtypeStruct((tokens, width), bf16),
            jax.ShapeDtypeStruct((tokens, width), f32),
            jax.ShapeDtypeStruct(quad, bf16),
            jax.ShapeDtypeStruct((4 * rows_n, width), bf16),
            jax.ShapeDtypeStruct((rows_n, 128), f32),
            jax.ShapeDtypeStruct(slots_shape, bf16),
            jax.ShapeDtypeStruct(args[-2].shape, bf16),
            jax.ShapeDtypeStruct(args[-1].shape, bf16),
        ],
        scratch_shapes=[
            pltpu.VMEM(slots_shape, bf16),
            square,
            pltpu.VMEM((tokens, width), bf16),
            pltpu.VMEM(quad, bf16),
            pltpu.VMEM(quad, bf16),
            pltpu.VMEM(quad, bf16),
            pltpu.VMEM(quad, bf16),
            pltpu.VMEM(quad, bf16),
            pltpu.VMEM(quad, bf16),
            pltpu.VMEM(quad, bf16),
            pltpu.VMEM(quad, bf16),
            pltpu.VMEM((width, tokens), bf16),
            pltpu.VMEM((width, tokens), f32),
            pltpu.VMEM((width, tokens), f32),
            pltpu.VMEM((2, seqs, 2 * span, 2 * total), bf16),
            pltpu.VMEM((2, 2 * span, total), f32),
            pltpu.VMEM((128, table), f32),
            pltpu.VMEM((2 * total, 128), bf16),
            pltpu.VMEM((2, total, 128), bf16),
            pltpu.VMEM((2 * span, 2 * total), bf16),
            pltpu.VMEM((8, width), f32),
            pltpu.VMEM((rows_n, 128), f32),
            *[pltpu.VMEM((width, width), bf16)] * 4,
            pltpu.SemaphoreType.DMA((13,)),
            pltpu.SemaphoreType.DMA((2,)),
            pltpu.SemaphoreType.DMA((2, parts)),
            pltpu.SemaphoreType.DMA((2, parts)),
            pltpu.SemaphoreType.DMA((2, wide_n)),
            pltpu.SemaphoreType.DMA((2, 3)),
            pltpu.SemaphoreType.DMA((4,)),
        ]
        + [ref for refs, _ in sums for ref in refs]
        + [sem for _, sems in sums for sem in sems]
        + [
            pltpu.VMEM((parts, fold_rows, 128), bf16),
            pltpu.VMEM((parts, fold_rows, 128), bf16),
            pltpu.VMEM((fold_rows, 128), bf16),
            pltpu.VMEM((wide_n, fold_rows, 128), bf16),
            pltpu.SemaphoreType.DMA((2, parts)),
            pltpu.SemaphoreType.DMA((2, wide_n)),
        ],
        compiler_params=params(collective_id=3, has_side_effects=True),
        name="backward",
    )(*args)


def finish_kernel(
    heads, gain_lane, hid_ref, res_ref, hgrad_ref, part_ref, gin_ref, early_ref, late_ref,
    gout_ref, far_ref, big_ref, small_ref,
    out_ref, igrad_ref, gin_out, gout_out, wq_out, wk_out, wv_out, wo_out,
    router_out, relative_out, gain_a_out, gain_e_out,
):
    step = pl.program_id(0)
    out_ref[...] = hid_ref[...] + res_ref[...].astype(f32)
    igrad_ref[...] = hgrad_ref[...] + part_ref[...].astype(f32)
    gout_out[...] = gout_ref[...].astype(f32) + far_ref[...].astype(f32)
    split = early_ref.shape[1]
    gin_out[:, :split] = gin_ref[:, :split].astype(f32) + early_ref[...].astype(f32)
    gin_out[:, split:] = gin_ref[:, split:].astype(f32) + late_ref[...].astype(f32)
    for i, ref in enumerate((wq_out, wk_out, wv_out, wo_out)):

        @pl.when(step == i // 2)
        def _(ref=ref, i=i):
            size = ref.shape[0]
            ref[...] = big_ref[(i % 2) * size : (i % 2 + 1) * size, :].astype(f32)

    @pl.when(step == 0)
    def _():
        small = small_ref[...]
        share = relative_out.shape[0]
        relative_out[...] = small[:share, gain_lane - 14 : gain_lane - 14 + heads]
        rows = small.shape[0]
        turned = jnp.concatenate([small, jnp.zeros((-rows % 128, 128), f32)], axis=0).T
        router_out[...] = turned[: router_out.shape[0], :rows]
        gain_a_out[...] = turned[gain_lane : gain_lane + 1, :rows].reshape(rows)
        gain_e_out[...] = turned[gain_lane + 1 : gain_lane + 2, :rows].reshape(rows)


def finish(args, heads, buckets, experts, narrow_n):
    hid, _, _, _, gin, _, _, gout, _, _, small = args
    gain_lane = 30 if experts <= 16 else 126
    tokens, width = hid.shape
    steps = 2
    rows_n, units = gin.shape

    def rows(shape):
        return pl.BlockSpec((shape[0] // steps, shape[1]), lambda i: (i, 0))

    def whole(shape):
        return pl.BlockSpec(shape, lambda i: (0,) * len(shape))

    square, slab = (tokens, width), (rows_n, width)
    singles = [(experts, rows_n), (buckets // narrow_n, heads), (rows_n,), (rows_n,)]
    shapes = [square, square, (rows_n, units), gout.shape, slab, slab, slab, slab] + singles
    return pl.pallas_call(
        functools.partial(finish_kernel, heads, gain_lane),
        grid=(steps,),
        in_specs=[rows(item.shape) for item in args[:-1]] + [whole(small.shape)],
        out_specs=[rows(shape) for shape in shapes[:4]] + [whole(shape) for shape in shapes[4:]],
        out_shape=[jax.ShapeDtypeStruct(shape, f32) for shape in shapes],
        compiler_params=params(),
        name="finish",
    )(*args)


def body(
    tokens, lengths, routes, bucket_table, attn_gain, query_weight, key_weight, value_weight,
    output_weight, relative_bias, expert_gain, router_weight, experts_in, experts_out, cotangent,
):
    seq_count, span, width = tokens.shape
    narrow_n = lax.axis_size("narrow")
    wide_n = lax.axis_size("wide")
    seqs = seq_count // narrow_n
    heads = relative_bias.shape[1]
    buckets = relative_bias.shape[0]
    experts = router_weight.shape[1]
    tok_count = seq_count * span
    capacity = 5 * tok_count // (4 * experts)
    cap = -(-capacity // 16) * 16
    table = 2 * span * narrow_n
    flat_cot = cotangent.reshape(tok_count, width)
    tok_quad = tokens.reshape(narrow_n, seqs, span, width)
    (
        tok_seq, att_seq, att_pos, hidden, routed, cot_rows, q, k, v, invl, probs,
        slot_row, slot_col, offset_hot,
    ) = forward(
        (
            lengths, tok_quad, flat_cot, routes.reshape(seq_count, span), bucket_table,
            relative_bias.T, attn_gain, expert_gain,
            query_weight, key_weight, value_weight, output_weight,
        ),
        wide_n, capacity, cap, tok_quad.shape, table,
    )
    res, back_rows, gin, gin_early, gin_send, gout, gout_send, router_grad = run_experts(
        routed, slot_row, router_weight.T, cot_rows, experts_in[0], experts_out[0], experts
    )
    picked_res, hidden_grad, part, big, small, _, gin_late, gout_far = backward(
        (
            back_rows, slot_col, hidden, flat_cot, att_pos, att_seq, probs, invl, q, k, v, tok_seq,
            res, output_weight, query_weight, key_weight, value_weight, attn_gain, expert_gain,
            router_grad, offset_hot, gin_send, gout_send,
        ),
        wide_n, experts, tok_quad.shape, res.shape, table,
    )

    (
        layer_output, input_grad, grad_in, grad_out, grad_query, grad_key, grad_value, grad_output,
        grad_router, grad_relative, grad_first, grad_second,
    ) = finish(
        (
            hidden, picked_res, hidden_grad, part.reshape(tok_count, width), gin, gin_early, gin_late,
            gout, gout_far, big, small,
        ),
        heads, buckets, experts, narrow_n,
    )
    return (
        layer_output.reshape(seq_count, span, width),
        input_grad.reshape(seq_count, span, width),
        grad_first,
        grad_query,
        grad_key,
        grad_value,
        grad_output,
        grad_relative,
        grad_second,
        grad_router.T,
        grad_in[None],
        grad_out[None],
    )


def solution(mesh):
    token = P("wide", "narrow", None)
    expert = P("wide", None, None)
    row, vector = P("narrow", None), P("narrow")
    return jax.shard_map(
        body,
        mesh=mesh,
        in_specs=(token, P("wide"), token) + (P(),) * 9 + (expert, expert, token),
        out_specs=(
            token, token, vector, row, row, row, row, row, vector, row,
            P("wide", "narrow", None), P("wide", "narrow", None),
        ),
        check_vma=False,
    )
```
